32 devices in a mesh: stem: 4 (over y, x), tm: 8 (over z, core).
Axes of the slice: x: 2, y: 2, z: 4, core: 2. Of those that a mesh axis runs over, the one named last changes fastest.
Arguments:
- mixture: bfloat16 [2, 1024, 1024], P(None, 'tm'), may hold values from 0 to 13
- seg_lengths: int32 [4], replicated, may hold values from 1 to 128, 256 in all
- frame_mask: int32 [1024], P('tm'), may hold values 0 or 1
- conv_first: bfloat16 [4, 16, 2, 5, 5], P('stem'), may hold values from -0.875 to 0.875
- encoder_gain_vector: float32 [4, 16], P('stem'), may hold values from 0.1 to 1.9
- shift_first: float32 [4, 16], P('stem'), may hold values from -1.75 to 1.75
- conv_second: bfloat16 [4, 32, 16, 5, 5], P('stem'), may hold values from -0.3125 to 0.3125
- gain_second: float32 [4, 32], P('stem'), may hold values from 0.1 to 1.9
- shift_second: float32 [4, 32], P('stem'), may hold values from -1.75 to 1.75
- deconv_second: bfloat16 [4, 16, 32, 5, 5], P('stem'), may hold values from -0.4375 to 0.4375
- bias_second: float32 [4, 16], P('stem'), may hold values from -1.75 to 1.75
- decoder_gain_vector: float32 [4, 16], P('stem'), may hold values from 0.1 to 1.9
- shift_third: float32 [4, 16], P('stem'), may hold values from -1.75 to 1.75
- deconv_first: bfloat16 [4, 2, 32, 5, 5], P('stem'), may hold values from -0.4375 to 0.4375
- bias_first: float32 [4, 2], P('stem'), may hold values from -3 to 3
- cotangent: bfloat16 [4, 2, 1024, 1024], P(None, None, 'tm', 'stem'), may hold values from -6 to 6
Outputs:
- estimates: bfloat16 [4, 2, 1024, 1024], P(None, None, 'tm', 'stem')
- mixture_grad: float32 [2, 1024, 1024], P(None, 'tm', 'stem')
- conv_first_grad: float32 [4, 16, 2, 5, 5], P('stem')
- gain_first_grad: float32 [4, 16], P('stem')
- shift_first_grad: float32 [4, 16], P('stem')
- conv_second_grad: float32 [4, 32, 16, 5, 5], P('stem')
- gain_second_grad: float32 [4, 32], P('stem')
- shift_second_grad: float32 [4, 32], P('stem')
- deconv_second_grad: float32 [4, 16, 32, 5, 5], P('stem')
- bias_second_grad: float32 [4, 16], P('stem')
- gain_third_grad: float32 [4, 16], P('stem')
- shift_third_grad: float32 [4, 16], P('stem')
- deconv_first_grad: float32 [4, 2, 32, 5, 5], P('stem')
- bias_first_grad: float32 [4, 2], P('stem')
The draws below stay inside these ranges and needn't reach their ends.
Inputs may be any that keep to these rules, and one draw needn't show every extreme that they name: `seg_lengths`: they sum to 256 and the longest is 128.
All inputs are finite; a program needn't handle non-finite values. No bound on the sum of `frame_mask` on one device may be relied on, other than what follows from the above.
Results may differ from the reference program's by a relative error of at most 0.02.
Values may be sent and summed in bfloat16 or wider, within the bound.
No kernel may reach another device: no remote copies, remote signals or barrier semaphores. Data moves between devices by JAX's collectives and lax.ppermute only.
A program may use at most 448 MiB of HBM per device.

```python
import math
import jax
import jax.numpy as jnp
import numpy as np
from jax import lax

BINS = 1024
CH1 = 16
CH2 = 32
SEG_LONG = 512
STEMS = 4
FRAMES = 1024
SEGS = 4


def draw_mixture(key, part):
    first_key = jax.random.fold_in(key, 0)
    frame_ramp = 1.0 + 2.0 * jnp.arange(FRAMES, dtype=jnp.float32)[None, :, None] / FRAMES
    return (jax.random.uniform(first_key, (2, FRAMES, BINS), jnp.float32, 0.1, 1.5) * frame_ramp).astype(jnp.bfloat16)


def set_ends(drawn, key, least, high):
    longest = drawn.shape.index(max(drawn.shape))
    spots = []
    for shift in (0, 1):
        where = [jax.random.randint(jax.random.fold_in(key, axis), (), 0, length) for axis, length in enumerate(drawn.shape)]
        where[longest] = (where[longest] + shift) % drawn.shape[longest]
        spots.append(tuple(where))
    return drawn.at[spots[0]].set(least).at[spots[1]].set(high)


def block_scale(key, dims, cuts, least, top_value):
    def one(position, parts):
        draws = jax.random.uniform(jax.random.fold_in(jax.random.fold_in(key, 6), position), (parts,), jnp.float32, least / len(cuts), top_value / len(cuts))
        return jnp.repeat(jnp.exp(draws), dims[position] // parts).reshape((-1,) + (1,) * (len(dims) - position - 1))

    factor_of = one(*cuts[0])
    for cut in cuts[1:]:
        factor_of = factor_of * one(*cut)
    return factor_of


def split_up(amount, total, most, lean):
    weights = [(1 << 20) // math.isqrt(rank ** lean) + 1 for rank in range(2, amount + 1)]
    surplus, given = total - most - (amount - 1), [1] * (amount - 1)
    while surplus > 0:
        movable = [i for i in range(amount - 1) if given[i] < most]
        whole, budget = sum([weights[i] for i in movable]), surplus
        for i in movable:
            extra = min(most - given[i], max(1, budget * weights[i] // whole), surplus)
            given[i] = given[i] + extra
            surplus = surplus - extra
    return np.array([most] + given)


def ragged(stream_key, count, total, reach, skew):
    if count == 2:
        one = jax.random.randint(stream_key, (), max(1, total - reach), min(reach, total - 1) + 1)
        return jnp.stack([one, total - one])
    tallies = jnp.asarray(split_up(count, total, reach, skew), jnp.int32)
    pairs = (count - 1) // 2
    source_of, receiver = tallies[1:1 + 2 * pairs:2], tallies[2:2 + 2 * pairs:2]
    margin = jnp.minimum(source_of - 1, reach - receiver)
    passed = jax.random.randint(jax.random.fold_in(stream_key, 1), (pairs,), 0, 1 << 20) % (margin + 1)
    tallies = tallies.at[1:1 + 2 * pairs:2].set(source_of - passed).at[2:2 + 2 * pairs:2].set(receiver + passed)
    return tallies[jax.random.permutation(jax.random.fold_in(stream_key, 2), count)]


def scatter_about(key, dims, scale, limit, cuts=(), kind=jnp.bfloat16):
    array = jax.random.normal(key, dims, jnp.float32) * scale
    if len(cuts) > 0:
        array = block_scale(key, dims, cuts, -0.22, 0.18) * array
    return jnp.clip(array, min=-limit, max=limit).astype(kind)


def setup_inputs(seed: int = 0) -> dict:
    key_list = jax.random.split(jax.random.key(seed), 17)
    mixture = draw_mixture(jax.random.fold_in(key_list[16], 71), 0)
    seg_lengths = ragged(key_list[1], SEGS, FRAMES // 4, SEG_LONG // 4, 1).astype(jnp.int32)
    frame_mask = set_ends((jax.random.randint(key_list[2], (FRAMES,), 0, 8) < 7).astype(jnp.int32), jax.random.fold_in(key_list[2], 1), 0, 1)
    conv_first = scatter_about(key_list[3], (STEMS, CH1, 2, 5, 5), 50 ** -0.5, 0.875, ((0, 4),))
    encoder_gain_vector = jnp.clip(1.0 + 0.18 * jax.random.normal(key_list[4], (STEMS, CH1), jnp.float32), 0.1, 1.9)
    shift_first = scatter_about(key_list[5], (STEMS, CH1), 0.3, 1.75, ((0, 4),), jnp.float32)
    conv_second = scatter_about(key_list[6], (STEMS, CH2, CH1, 5, 5), (CH1 * 25) ** -0.5, 0.3125, ((0, 4),))
    gain_second = jnp.clip(1.0 + 0.18 * jax.random.normal(key_list[7], (STEMS, CH2), jnp.float32), 0.1, 1.9)
    shift_second = scatter_about(key_list[8], (STEMS, CH2), 0.3, 1.75, ((0, 4),), jnp.float32)
    deconv_second = scatter_about(key_list[9], (STEMS, CH1, CH2, 5, 5), (CH2 * 25 // 4) ** -0.5, 0.4375, ((0, 4),))
    bias_second = scatter_about(key_list[10], (STEMS, CH1), 0.3, 1.75, ((0, 4),), jnp.float32)
    decoder_gain_vector = jnp.clip(1.0 + 0.18 * jax.random.normal(key_list[11], (STEMS, CH1), jnp.float32), 0.1, 1.9)
    shift_third = scatter_about(key_list[12], (STEMS, CH1), 0.3, 1.75, ((0, 4),), jnp.float32)
    deconv_first = scatter_about(key_list[13], (STEMS, 2, 2 * CH1, 5, 5), (2 * CH1 * 25 // 4) ** -0.5, 0.4375, ((0, 4),))
    bias_first = scatter_about(key_list[14], (STEMS, 2), 0.5, 3.0, ((0, 4),), jnp.float32)
    cotangent = scatter_about(key_list[15], (STEMS, 2, FRAMES, BINS), 1.0, 6.0, ((2, 8), (3, 4)))
    return {"mixture": mixture, "seg_lengths": seg_lengths, "frame_mask": frame_mask, "conv_first": conv_first, "encoder_gain_vector": encoder_gain_vector, "shift_first": shift_first, "conv_second": conv_second, "gain_second": gain_second, "shift_second": shift_second, "deconv_second": deconv_second, "bias_second": bias_second, "decoder_gain_vector": decoder_gain_vector, "shift_third": shift_third, "deconv_first": deconv_first, "bias_first": bias_first, "cotangent": cotangent}


@jax.custom_vjp
def low(v):
    return lax.optimization_barrier(v.astype(jnp.bfloat16)).astype(jnp.float32)

@jax.custom_vjp
def low_back(v):
    return v

def low_keep(v):
    return (low(v), None)

def low_pass(kept, grad):
    return (grad,)

def back_keep(v):
    return (v, None)

def back_low(kept, grad):
    return (low(grad),)
low.defvjp(low_keep, low_pass)
low_back.defvjp(back_keep, back_low)
NORM_EPS = 0.001
RATIO_EPS = 1e-10
CONV_LAYOUT = ('NCHW', 'OIHW', 'NCHW')
HIGH_PRECISION = lax.Precision.HIGHEST

def edge_flags(seg_lengths, device_index, coarse, frame_step):
    starts = 4 * (jnp.cumsum(seg_lengths, dtype=jnp.int32) - seg_lengths)
    frames = (device_index * coarse + jnp.arange(-1, coarse + 1, dtype=jnp.int32)) * (2 * frame_step)
    left_ok = 1.0 - jnp.any(frames[:, None] == starts[None, :], axis=1).astype(jnp.float32)
    right_ok = 1.0 - jnp.any((frames + 2 * frame_step)[:, None] == starts[None, :], axis=1).astype(jnp.float32)
    return (left_ok, right_ok)

def bins_down(input_values, kernel):
    return lax.conv_general_dilated(input_values[None], kernel[:, :, None, :], (1, 2), ((0, 0), (1, 2)), dimension_numbers=CONV_LAYOUT, precision=HIGH_PRECISION)[0]

def bins_up(input_values, kernel):
    return lax.conv_general_dilated(input_values[None], jnp.flip(kernel, 2)[:, :, None, :], (1, 1), ((0, 0), (3, 2)), lhs_dilation=(1, 2), dimension_numbers=CONV_LAYOUT, precision=HIGH_PRECISION)[0]

def down_apply(padded, kernel, left_ok, right_ok, rim_width):
    row_count = padded.shape[1] - 2 * rim_width
    coarse = row_count // 2
    inner_left = left_ok[1:coarse + 1][None, :, None]
    inner_right = right_ok[1:coarse + 1][None, :, None]

    def frame_tap(offset):
        return padded[:, offset - 1 + rim_width:offset - 1 + rim_width + row_count:2]
    middle = bins_down(frame_tap(1), kernel[:, :, 1]) + bins_down(frame_tap(2), kernel[:, :, 2])
    outer_left = inner_left * bins_down(frame_tap(0), kernel[:, :, 0])
    outer_right = inner_right * (bins_down(frame_tap(3), kernel[:, :, 3]) + bins_down(frame_tap(4), kernel[:, :, 4]))
    return middle + outer_left + outer_right

def up_apply(padded, kernel, left_ok, right_ok, rim_width):
    coarse = padded.shape[1] - 2 * rim_width
    inner_left = left_ok[1:coarse + 1][None, :, None]
    inner_right = right_ok[1:coarse + 1][None, :, None]
    current = padded[:, rim_width:rim_width + coarse]
    previous = padded[:, rim_width - 1:rim_width - 1 + coarse]
    following = padded[:, rim_width + 1:rim_width + 1 + coarse]
    even_rows = bins_up(current, kernel[:, :, 1]) + inner_left * bins_up(previous, kernel[:, :, 3])
    odd_rows = inner_right * bins_up(following, kernel[:, :, 0]) + bins_up(current, kernel[:, :, 2]) + inner_left * bins_up(previous, kernel[:, :, 4])
    return jnp.stack([even_rows, odd_rows], 2).reshape(even_rows.shape[0], 2 * coarse, even_rows.shape[2])

def frame_pad(input_values, rim_width):
    return jnp.pad(input_values, ((0, 0), (rim_width, rim_width), (0, 0)))

def masked_norm(input_values, kept_row_mask, gain_vector, shift_vector):
    overall_count = jnp.sum(kept_row_mask) * input_values.shape[2]
    weighted = input_values * kept_row_mask[None, :, None]
    norm_average = lax.optimization_barrier(jnp.sum(weighted, axis=(1, 2))) / overall_count
    square_mean = lax.optimization_barrier(jnp.sum(weighted * input_values, axis=(1, 2))) / overall_count
    norm_inverse_scale = lax.rsqrt(square_mean - norm_average * norm_average + NORM_EPS)
    return (input_values - norm_average[:, None, None]) * norm_inverse_scale[:, None, None] * gain_vector[:, None, None] + shift_vector[:, None, None]

def network(mix_values, stem_params, flags_one, flags_two, single_keep_mask, keep_two):
    conv_first, encoder_gain_vector, shift_first, conv_second, gain_second, shift_second, deconv_second, bias_second, decoder_gain_vector, shift_third, deconv_first, bias_first = stem_params
    pre_one = low_back(down_apply(frame_pad(mix_values, 2), conv_first, flags_one[0], flags_one[1], 2))
    act_one = low(jax.nn.silu(masked_norm(pre_one, single_keep_mask, encoder_gain_vector, shift_first)))
    pre_two = low_back(down_apply(frame_pad(act_one, 2), conv_second, flags_two[0], flags_two[1], 2))
    act_two = low(jax.nn.silu(masked_norm(pre_two, keep_two, gain_second, shift_second)))
    up_pre = low_back(up_apply(frame_pad(act_two, 1), deconv_second, flags_two[0], flags_two[1], 1)) + bias_second[:, None, None]
    norm_three = low(masked_norm(jax.nn.softplus(up_pre), single_keep_mask, decoder_gain_vector, shift_third))
    joined = jnp.concatenate([norm_three, act_one], 0)
    logits = low_back(up_apply(frame_pad(joined, 1), deconv_first, flags_one[0], flags_one[1], 1)) + bias_first[:, None, None]
    return low_back(low(jax.nn.sigmoid(logits)))

def reference(mixture, seg_lengths, frame_mask, conv_first, encoder_gain_vector, shift_first, conv_second, gain_second, shift_second, deconv_second, bias_second, decoder_gain_vector, shift_third, deconv_first, bias_first, cotangent):
    frame_total = mixture.shape[1]
    flags_one = edge_flags(seg_lengths, 0, frame_total // 2, 1)
    flags_two = edge_flags(seg_lengths, 0, frame_total // 4, 2)
    single_keep_mask = lax.optimization_barrier(jnp.min(frame_mask.reshape(-1, 2), axis=1)).astype(jnp.float32)
    keep_two = lax.optimization_barrier(jnp.min(frame_mask.reshape(-1, 4), axis=1)).astype(jnp.float32)
    mix_values = mixture.astype(jnp.float32)
    params = (conv_first.astype(jnp.float32), encoder_gain_vector.astype(jnp.float32), shift_first.astype(jnp.float32), conv_second.astype(jnp.float32), gain_second.astype(jnp.float32), shift_second.astype(jnp.float32), deconv_second.astype(jnp.float32), bias_second.astype(jnp.float32), decoder_gain_vector.astype(jnp.float32), shift_third.astype(jnp.float32), deconv_first.astype(jnp.float32), bias_first.astype(jnp.float32))

    def forward(mix_in, param_values):

        def one_stem(stem_params):
            return network(mix_in, stem_params, flags_one, flags_two, single_keep_mask, keep_two)
        mask_values = lax.map(jax.checkpoint(one_stem), param_values)
        squares = mask_values * mask_values
        power_total = lax.optimization_barrier(jnp.sum(squares, axis=0)) + RATIO_EPS
        return mix_in[None] * (squares / power_total[None])
    estimates, pullback = jax.vjp(forward, mix_values, params)
    mixture_grad, param_grads = pullback(cotangent.astype(jnp.float32))
    return (estimates.astype(jnp.bfloat16), mixture_grad, param_grads[0], param_grads[1], param_grads[2], param_grads[3], param_grads[4], param_grads[5], param_grads[6], param_grads[7], param_grads[8], param_grads[9], param_grads[10], param_grads[11])
```

```python
import jax
import jax.numpy as jnp
from jax import lax
from jax.experimental import pallas as pl
from jax.experimental.pallas import tpu as pltpu
from jax.sharding import PartitionSpec as P

NORM_EPS = 0.001
RATIO_EPS = 1e-10
BF = jnp.bfloat16
F32 = jnp.float32
TAPS = 5
L = 128
M = 32
NJ = 32
R = M * NJ
CHUNK = 256
COLS0 = 1024
COLS1 = 1920
COLS1B = 1536
COLS2 = 1152
GROUPS1 = ((0, 1), (256, 2), (512, 0), (768, 3), (1024, 4))
FULL = pl.BlockSpec(memory_space=pltpu.VMEM)
SCALAR = pl.BlockSpec(memory_space=pltpu.SMEM)


def lane(shape):
    return lax.broadcasted_iota(jnp.int32, shape, 1)


def sub(shape):
    return lax.broadcasted_iota(jnp.int32, shape, 0)


def rows(j, count=M):
    return pl.ds(pl.multiple_of(j * count, count), count)


def run(kernel, name, outs, args, scratch=(), scalars=0, flops=0):
    bytes_all = sum(a.size * a.dtype.itemsize for a in args)
    shapes = [jax.ShapeDtypeStruct(s, d) for s, d in outs]
    bytes_all += sum(s.size * s.dtype.itemsize for s in shapes)
    return pl.pallas_call(
        kernel,
        out_shape=shapes,
        in_specs=[SCALAR] * scalars + [FULL] * (len(args) - scalars),
        out_specs=[FULL] * len(outs),
        scratch_shapes=[pltpu.VMEM(s, d) for s, d in scratch],
        compiler_params=pltpu.CompilerParams(vmem_limit_bytes=48 << 20),
        cost_estimate=pl.CostEstimate(flops=flops, bytes_accessed=bytes_all, transcendentals=0),
        name=name,
    )(*args)


def for_blocks(fn, count=NJ):
    def body(j, carry):
        fn(j)
        return carry

    lax.fori_loop(0, count, body, 0)


def for_blocks_rims(fn):
    def body(j, carry):
        fn(j, True, True)
        return carry

    fn(0, False, True)
    lax.fori_loop(1, NJ - 1, body, 0)
    fn(NJ - 1, True, False)


def from_prev(value, rim, flag):
    rim = jnp.concatenate([rim] * (M // 8), axis=0)
    return jnp.where(sub(value.shape) == 0, rim, pltpu.roll(value, 1, 0)) * flag


def from_next(value, rim, flag):
    rim = jnp.concatenate([rim] * (M // 8), axis=0)
    return jnp.where(sub(value.shape) == M - 1, rim, pltpu.roll(value, M - 1, 0)) * flag


def widen(source, out):
    def group(g):
        for k in range(source.shape[1] // L):
            at = slice(L * k, L * k + L)
            tile = source[rows(g, 8), at]
            for i in range(8):
                out[rows(8 * g + i, 8), at] = jnp.broadcast_to(tile[i : i + 1], (8, L))

    for_blocks(group, NJ // 8)


def mask_bf(cond):
    return jnp.where(cond, 1.0, 0.0).astype(BF)


def fill_rims(cat, parts, low, high):
    def one(j, has_prev, has_next):
        for target, after, before in parts:
            value = None
            if has_next:
                value = cat[rows(j + 1), after : after + L] * low
            if has_prev:
                other = cat[rows(j - 1), before : before + L] * high
                value = other if value is None else value + other
            cat[rows(j), target : target + L] = value

    for_blocks_rims(one)


def rims_1(cat, groups, base):
    at = lane((M, L))
    fill_rims(
        cat,
        [(base + L * k, g, g + L) for k, g in enumerate(groups)],
        mask_bf(at < 32),
        mask_bf(at >= 112),
    )


def rims_2(cat):
    at = lane((M, L))
    fill_rims(
        cat,
        [(768 + L * k, 256 * k, 256 * k + L) for k in range(3)],
        mask_bf(at < 32),
        mask_bf(at >= 96),
    )


def rims_0(cat):
    at = lane((M, L)) % 32
    fill_rims(cat, [(512 + L * k, L * k, L * k) for k in range(4)], mask_bf(at < 2), mask_bf(at == 31))


def matmul(left, right, transposed=False):
    return lax.dot_general(
        left, right, (((1,), (1 if transposed else 0,)), ((), ())), preferred_element_type=F32
    )


def for_chunks(fn, size=CHUNK):
    def body(r, carry):
        fn(pl.ds(pl.multiple_of(r * size, size), size))
        return carry

    lax.fori_loop(0, R // size, body, 0)


def sum8(value):
    total = value[0:8]
    for k in range(1, value.shape[0] // 8):
        total = total + value[8 * k : 8 * k + 8]
    return total


def fold(stats, period):
    step = L // 2
    while step >= period:
        stats = stats + pltpu.roll(stats, step, 1)
        step //= 2
    return stats


def stack_rows(values):
    at = sub((8, L))
    tile = jnp.zeros((8, L), F32)
    for k, value in enumerate(values):
        tile = jnp.where(at == k, value, tile)
    return tile


def total_rows(value):
    return jnp.sum(value, axis=0, keepdims=True)


def norm_terms(moments, count):
    mean = moments[0:1] / count
    return mean, lax.rsqrt(moments[1:2] / count - mean * mean + NORM_EPS)


def silu(v):
    return v / (1.0 + jnp.exp(-v))


def silu_slope(v):
    s = 1.0 / (1.0 + jnp.exp(-v))
    return s * (1.0 + v * (1.0 - s))


def softplus(v):
    return jnp.maximum(v, 0.0) + jnp.log1p(jnp.exp(-jnp.abs(v)))


def softplus_slope(r):
    return jnp.where(r < 0.05, r * (1.0 - r * (0.5 - r * (1.0 / 6.0))), 1.0 - jnp.exp(-r))


def tile_2(w, tap, q, half):
    at = lane((16, L)) // 32
    tile = jnp.zeros((16, L), F32)
    for k in range(4):
        b = q - 2 * (4 * half + k) + 1
        if 0 <= b < TAPS:
            start = (tap * TAPS + b) * 16
            tile = jnp.where(at == k, w[start : start + 16, :], tile)
    return tile.astype(BF)


def matrix_2_down(w, t):
    zero = jnp.zeros((16, L), BF)
    for k, (base, tap) in enumerate(GROUPS1):
        for half in range(2):
            at = slice(L * half, L * half + L)
            for q in range(16):
                t[base + 16 * q : base + 16 * q + 16, at] = tile_2(w, tap, q, half)
            for part in range(8):
                q = {0: 16, 1: 17, 7: -1}.get(part)
                start = 1280 + L * k + 16 * part
                t[start : start + 16, at] = zero if q is None else tile_2(w, tap, q, half)


def matrix_2_up(w, t):
    zero = jnp.zeros((16, L), BF)
    at = lane((16, L))
    for row in range(2):
        for k, tap in enumerate((row + 1, row + 3, row - 1)):
            for q in range(16):
                span = slice(row * 256 + q * 16, row * 256 + q * 16 + 16)
                for half in range(2):
                    cols = slice(256 * k + L * half, 256 * k + L * half + L)
                    t[span, cols] = tile_2(w, tap, q, half) if 0 <= tap < TAPS else zero
                rim = zero
                if 0 <= tap < TAPS and q in (0, 1, 15):
                    b = {0: 3, 1: 4, 15: 0}[q]
                    start = (tap * TAPS + b) * 16
                    cond = at < 32 if q == 15 else at >= 96
                    rim = jnp.where(cond, w[start : start + 16, :], 0.0).astype(BF)
                t[span, 768 + L * k : 768 + L * k + L] = rim


def band(w, tap, channel, offset):
    tile = jnp.zeros((32, L), F32)
    for b in range(TAPS):
        start = (tap * 2 + channel) * TAPS + b
        tile = jnp.where(offset == b, w[start : start + 1, :], tile)
    return tile.astype(BF)


def matrix_1_down(w, t, col):
    q, zero = sub((32, L)), jnp.zeros((32, L), BF)
    for half in range(2):
        p = 8 * half + lane((32, L)) // 16
        inner = q - 2 * p + 1
        rim = jnp.where(q == 31, -2 * p, jnp.where(q == 0, 33 - 2 * p, jnp.where(q == 1, 34 - 2 * p, -9)))
        for row in range(2):
            cols = slice(col + row * 256 + half * L, col + row * 256 + half * L + L)
            for part, frame in enumerate((0, 1, 2, 3, None, -1, 4, 5)):
                tap = -1 if frame is None else frame - 2 * row + 1
                for c in range(2):
                    start = part * 64 + c * 32
                    ok = 0 <= tap < TAPS
                    t[start : start + 32, cols] = band(w, tap, c, inner) if ok else zero
                    t[512 + start : 544 + start, cols] = band(w, tap, c, rim) if ok else zero


def matrix_1_up(w, t, col):
    q, zero = sub((32, L)), jnp.zeros((32, L), BF)
    at = lane((32, L))
    rim = jnp.where(at < 16, q - 31, jnp.where(at >= 112, q + 3, -9))
    for frame in range(4):
        taps = (frame + 1, frame - 1, frame + 3, frame - 3)
        for c in range(2):
            span = slice(frame * 64 + c * 32, frame * 64 + c * 32 + 32)
            for k, tap in enumerate(taps):
                ok = 0 <= tap < TAPS
                for half in range(2):
                    p = 8 * half + at // 16
                    start = col + 256 * k + L * half
                    t[span, start : start + L] = band(w, tap, c, q - 2 * p + 1) if ok else zero
                start = col + 1024 + L * k
                t[span, start : start + L] = band(w, tap, c, rim) if ok else zero


def matrices_first(w1c, t1a):
    matrix_1_down(w1c, t1a, 0)


def matrices_forward(w2c, w2d, w1d, t2a_c, t2b_d, t1b_d):
    matrix_2_down(w2c, t2a_c)
    matrix_2_up(w2d, t2b_d)
    matrix_1_up(w1d.at[0], t1b_d, 0)
    matrix_1_up(w1d.at[1], t1b_d, COLS1B)


def matrices_back(w1c, w2c, w2d, w1d, t1a_d, t2a_d, t2b_c, t1b_c):
    matrix_1_down(w1d.at[0], t1a_d, 0)
    matrix_1_down(w1d.at[1], t1a_d, 512)
    matrix_2_down(w2d, t2a_d)
    matrix_2_up(w2c, t2b_c)
    matrix_1_up(w1c, t1b_c, 0)


def correlate(coarse, fine, d):
    def part(rs, first):
        value = lax.dot_general(
            coarse(rs), fine[rs, :], (((0,), (0,)), ((), ())), preferred_element_type=F32
        )
        d[...] = value if first else d[...] + value

    part(pl.ds(0, CHUNK), True)

    def body(r, carry):
        part(pl.ds(pl.multiple_of(r * CHUNK, CHUNK), CHUNK), False)
        return carry

    lax.fori_loop(1, R // CHUNK, body, 0)


def weight_2(d, out):
    at = lane((32, L))
    for k, (base, tap) in enumerate(GROUPS1):
        total = jnp.zeros((32, L), F32)
        for p in range(8):
            span = slice(32 * p, 32 * p + 32)
            tiles = [d[span, base : base + L], d[span, base + L : base + 256]]
            tiles.append(d[span, 1280 + L * k : 1280 + L * k + L])
            if p == 0:
                value = jnp.where(at < 16, pltpu.roll(tiles[2], 16, 1), pltpu.roll(tiles[0], 16, 1))
            else:
                which, off = divmod(32 * p - 16, L)
                value = pltpu.roll(tiles[which], L - off, 1)
                if off + 80 > L:
                    value = jnp.where(at < L - off, value, pltpu.roll(tiles[which + 1], L - off, 1))
            total = total + value
        out[tap * 32 : tap * 32 + 32, :] = total


def weight_1(d, out, start):
    at = lane((16, L)) % 32
    sums = [jnp.zeros((16, L), F32) for _ in range(3)]
    for row in range(2):
        for k, tile in enumerate((2, 0, 1) if row == 0 else (0, 1, 3)):
            for p in range(16):
                first = row * 256 + p * 16
                span = slice(first, first + 16)
                value = pltpu.roll(d[span, L * tile : L * tile + L], (1 - 2 * p) % L, 1)
                if p in (0, 15):
                    rim = d[span, 512 + L * tile : 512 + L * tile + L]
                    rim = pltpu.roll(rim, L - 31 if p == 0 else 3, 1)
                    value = jnp.where(at == 0 if p == 0 else at >= 3, rim, value)
                sums[k] = sums[k] + value
    for k in range(3):
        out[start + 16 * k : start + 16 * k + 16, :] = sums[k]


def weight_2_kernel(coarse, fine, out, d):
    correlate(lambda rs: coarse[rs, :], fine, d)
    weight_2(d, out)


def weight_1_first(coarse, fine, out, d):
    correlate(lambda rs: coarse[rs, :], fine, d)
    weight_1(d, out, 0)


def weight_1_joined(low, cat1, fine, out, d):
    correlate(lambda rs: low[rs, :], fine, d)
    weight_1(d, out, 0)
    correlate(lambda rs: cat1[rs, 0:512], fine, d)
    weight_1(d, out, 48)


def spread(scr, store):
    at = lane((M, L)) // 32
    for half in range(2):
        parts = [scr[k % 2, pl.ds(2 * half + k // 2, M, stride=4), :] for k in range(4)]
        for block in range(4):
            value = parts[block]
            for k in range(4):
                if k != block:
                    value = jnp.where(at == k, pltpu.roll(parts[k], (32 * (k - block)) % L, 1), value)
            store(block, half, value)


def gather(blocks, scr):
    at = lane((M, L)) // 32
    for half in range(2):
        parts = [blocks(block, half) for block in range(4)]
        for k in range(4):
            value = parts[k]
            for block in range(4):
                if block != k:
                    value = jnp.where(
                        at == block, pltpu.roll(parts[block], (32 * (block - k)) % L, 1), value
                    )
            scr[k % 2, pl.ds(2 * half + k // 2, M, stride=4), :] = value


def layout_kernel(mix, cot, aux, x0, c0, first, last, scr, wide, ends):
    def place(out, block, row):
        def store(k, half, value):
            at = slice(L * half, L * half + L)
            out[rows(block + k), at] = value.astype(BF)
            wide[rows(row + k), at] = value

        return store

    def mix_tile(t):
        for c in range(2):
            scr[c] = mix[c, :, pl.ds(pl.multiple_of(t * L, L), L)].astype(F32)
        spread(scr, place(x0, 4 * t, 4 * t))

    for_blocks(mix_tile, NJ // 4)
    tiles = cot.shape[3] // L

    def cot_tile(t):
        for c in range(2):
            scr[c] = cot[t // tiles, c, :, pl.ds(pl.multiple_of((t % tiles) * L, L), L)].astype(F32)
        spread(scr, place(c0, 4 * t, NJ + 4 * t))

    for_blocks(cot_tile, NJ // 4)
    ends[...] = jnp.zeros(ends.shape, F32)
    end_rows(wide, ends.at[0], ends.at[1], blocks=2 * NJ)
    for k, m in enumerate((0, M - 1)):
        for i in range(3):
            ends[k, 2 * NJ + i : 2 * NJ + i + 1, 0:L] = aux[2 + i, m : m + 1, :]
    first[...] = ends[0].astype(BF)
    last[...] = ends[1].astype(BF)


def columns_0(cat, read, left, right, aux):
    a, a_next = aux[0], aux[1]

    def one(j):
        for half in range(2):
            value = read(j, half)
            cat[rows(j), L * half : L * half + L] = value.astype(BF)
            if half == 1:
                moved = from_prev(value, left[rows(j, 8), L : 2 * L], a)
                cat[rows(j), 256:384] = moved.astype(BF)
            else:
                moved = from_next(value, right[rows(j, 8), 0:L], a_next)
                cat[rows(j), 384:512] = moved.astype(BF)

    for_blocks(one)
    rims_0(cat)


def block_sums(j, z, aux, sums):
    s1, s2 = sums
    for k in range(4):
        value = z[rows(j), L * k : L * k + L]
        kept = value * aux[2 + k // 2]
        s1 = s1 + sum8(kept)
        s2 = s2 + sum8(kept * value)
    return s1, s2


def end_rows(z, first, last, apply=lambda v: v, blocks=NJ):
    def group(g):
        for k in range(z.shape[1] // L):
            at = slice(L * k, L * k + L)
            place = sub((8, L))
            top = low = jnp.zeros((8, L), F32)
            for i in range(8):
                start = pl.multiple_of((8 * g + i) * M, M)
                top = jnp.where(place == i, z[pl.ds(start, 8), at][0:1], top)
                low = jnp.where(place == i, z[pl.ds(start + M - 8, 8), at][7:8], low)
            first[rows(g, 8), at] = apply(top)
            last[rows(g, 8), at] = apply(low)

    for_blocks(group, blocks // 8)


def conv_one_kernel(x0, left, right, aux, t, cat, z, mom, first, last, hx, kept, lf, rf, lw, rw):
    lf[...] = left[...].astype(F32)
    rf[...] = right[...].astype(F32)
    hx[:, 0:L] = rf[0 : 2 * NJ, 0:L]
    hx[:, L : 2 * L] = lf[0 : 2 * NJ, L : 2 * L]
    kept[...] = jnp.zeros(kept.shape, F32)
    kept[0:3, :] = lf[2 * NJ : 2 * NJ + 3, 0:L]
    kept[3:6, :] = rf[2 * NJ : 2 * NJ + 3, 0:L]
    widen(lf.at[0:NJ], lw)
    widen(rf.at[0:NJ], rw)
    columns_0(cat, lambda j, h: x0[rows(j), L * h : L * h + L].astype(F32), lw, rw, aux)

    def chunk(rs):
        z[rs, :] = matmul(cat[rs, :], t[...])

    for_chunks(chunk)

    end_rows(z, first, last)

    def sums(j, carry):
        return block_sums(j, z, aux, carry)

    zero = jnp.zeros((8, L), F32)
    s1, s2 = lax.fori_loop(0, NJ, sums, (zero, zero))
    stats = fold(stack_rows([total_rows(s1), total_rows(s2)]), 16)
    count_one = total_rows(aux[2] + aux[3])
    count_two = total_rows(aux[4])
    at = sub((8, L))
    stats = jnp.where(at == 2, count_one * (NJ * 16.0), stats)
    mom[...] = jnp.where(at == 3, count_two * (NJ * 8.0), stats)


def conv_two_kernel(z1, left, right, mom1, prm, aux, t, cat, ends, z2, mom, first, last, ef, lw, rw):
    mean, scale = norm_terms(mom1, mom1[2:3])
    gain, shift = prm[0:1], prm[1:2]

    def act(value):
        return silu((value - mean) * scale * gain + shift)

    a, a_next = aux[0], aux[1]
    for k in range(4):
        ef[0, :, L * k : L * k + L] = act(left[:, L * k : L * k + L])
        ef[1, :, L * k : L * k + L] = act(right[:, L * k : L * k + L])
    widen(ef.at[0], lw)
    widen(ef.at[1], rw)

    def one(j):
        for k in range(4):
            at = slice(L * k, L * k + L)
            value = act(z1[rows(j), at])
            cat[rows(j), at] = value.astype(BF)
            if k >= 2:
                moved = from_prev(value, lw[rows(j, 8), at], a)
                cat[rows(j), 256 + L * k : 384 + L * k] = moved.astype(BF)
            moved = from_next(value, rw[rows(j, 8), at], a_next)
            cat[rows(j), 768 + L * k : 896 + L * k] = moved.astype(BF)

    for_blocks(one)
    end_rows(z1, ef.at[2], ef.at[3], act)
    ends[...] = ef[...].astype(BF)
    rims_1(cat, [g for g, _ in GROUPS1], 1280)

    def chunk(rs):
        z2[rs, :] = matmul(cat[rs, :], t[...])

    for_chunks(chunk)

    end_rows(z2, first, last)

    def sums(j, carry):
        s1, s2 = carry
        for k in range(2):
            value = z2[rows(j), L * k : L * k + L]
            kept = value * aux[4]
            s1 = s1 + sum8(kept)
            s2 = s2 + sum8(kept * value)
        return s1, s2

    zero = jnp.zeros((8, L), F32)
    s1, s2 = lax.fori_loop(0, NJ, sums, (zero, zero))
    mom[...] = fold(stack_rows([total_rows(s1), total_rows(s2)]), 32)


def columns_2(cat, read, left, right, aux, own=None):
    a, a_next = aux[0], aux[1]

    def one(j):
        for k in range(2):
            at = slice(L * k, L * k + L)
            value = read(j, k)
            low = value.astype(BF)
            cat[rows(j), at] = low
            if own is not None:
                own[rows(j), at] = low
            moved = from_prev(value, left[rows(j, 8), at], a)
            cat[rows(j), 256 + L * k : 384 + L * k] = moved.astype(BF)
            moved = from_next(value, right[rows(j, 8), at], a_next)
            cat[rows(j), 512 + L * k : 640 + L * k] = moved.astype(BF)

    for_blocks(one)
    rims_2(cat)


def up_two_kernel(z2, left, right, mom1, mom2, prm, aux, t, act2, rect, mom, first, last, cat, lf, rf, lw, rw):
    mean, scale = norm_terms(mom2, mom1[3:4])
    gain, shift, bias = prm[2:3], prm[3:4], prm[6:7]

    def act(value):
        return silu((value - mean) * scale * gain + shift)

    for k in range(2):
        at = slice(L * k, L * k + L)
        lf[:, at] = act(left[:, at])
        rf[:, at] = act(right[:, at])
    widen(lf, lw)
    widen(rf, rw)
    columns_2(cat, lambda j, k: act(z2[rows(j), L * k : L * k + L]), lw, rw, aux, act2)

    def chunk(rs):
        rect[rs, :] = matmul(cat[rs, :], t[...], True)

    for_chunks(chunk)

    def sums(j, carry):
        s1, s2 = carry
        for k in range(4):
            at = slice(L * k, L * k + L)
            value = softplus(rect[rows(j), at] + bias)
            rect[rows(j), at] = value
            kept = value * aux[2 + k // 2]
            s1 = s1 + sum8(kept)
            s2 = s2 + sum8(kept * value)
        return s1, s2

    zero = jnp.zeros((8, L), F32)
    s1, s2 = lax.fori_loop(0, NJ, sums, (zero, zero))
    end_rows(rect, first, last)
    mom[...] = fold(stack_rows([total_rows(s1), total_rows(s2)]), 16)


def columns_1b(cat, read, left, right, aux, own=None):
    a, a_next = aux[0], aux[1]

    def one(j):
        for k in range(4):
            at = slice(L * k, L * k + L)
            value = read(j, k)
            low = value.astype(BF)
            cat[rows(j), at] = low
            if own is not None:
                own[rows(j), at] = low
            if k >= 2:
                moved = from_prev(value, left[rows(j, 8), at], a)
                cat[rows(j), 256 + L * k : 384 + L * k] = moved.astype(BF)
            else:
                moved = from_next(value, right[rows(j, 8), at], a_next)
                cat[rows(j), 768 + L * k : 896 + L * k] = moved.astype(BF)

    for_blocks(one)
    rims_1(cat, (0, 256, 512, 768), 1024)


def edge_columns(own, prev, after):
    at = lane((NJ, L))
    place = sub((NJ, L))
    parts = [own, prev, after]
    groups = [own[:, 0:256], own[:, 256:512], prev, after]
    for g in groups:
        low = jnp.where((place == NJ - 1) | (at >= 32), 0.0, pltpu.roll(g[:, 0:L], NJ - 1, 0))
        high = jnp.where((place == 0) | (at < 112), 0.0, pltpu.roll(g[:, L : 2 * L], 1, 0))
        parts.append(low + high)
    return jnp.concatenate(parts, axis=1).astype(BF)


def sigmoid(v):
    return 1.0 / (1.0 + jnp.exp(-v))


def up_one_kernel(
    rect, left, right, mom1, mom3, prm, aux, cat1, ends1, t, own, sig, sigh, mask, cat, lf, rf, ef, hf,
    lw, rw,
):
    mean, scale = norm_terms(mom3, mom1[2:3])
    gain, shift, bias = prm[4:5], prm[5:6], prm[7:8]

    def norm(value):
        return (value - mean) * scale * gain + shift

    for k in range(4):
        at = slice(L * k, L * k + L)
        lf[:, at] = norm(left[:, at])
        rf[:, at] = norm(right[:, at])
    widen(lf, lw)
    widen(rf, rw)
    columns_1b(cat, lambda j, k: norm(rect[rows(j), L * k : L * k + L]), lw, rw, aux, own)
    end_rows(rect, ef.at[0], ef.at[1], norm)
    wide = jnp.concatenate([bias, bias], axis=1)
    zero = jnp.zeros((NJ, 256), F32)
    a, a_end = aux[0, 0:1, 0:1], aux[1, M - 1 : M, 0:1]
    e1 = [ends1[k].astype(F32) for k in range(4)]
    edges = [
        (
            edge_columns(lf[...], zero, ef[0, :, 0:256] * a),
            edge_columns(e1[0], zero, e1[2][:, 0:256] * a),
        ),
        (
            edge_columns(rf[...], ef[1, :, 256:512] * a_end, zero),
            edge_columns(e1[1], e1[3][:, 256:512] * a_end, zero),
        ),
    ]
    for k, half in ((0, 1), (1, 0)):
        value = matmul(edges[k][0], t[:, 0:COLS1B], True)
        value = value + matmul(edges[k][1], t[:, COLS1B : 2 * COLS1B], True)
        sigh[:, L * half : L * half + L] = sigmoid(value[:, L * half : L * half + L] + bias)

    def chunk(rs):
        value = matmul(cat[rs, :], t[:, 0:COLS1B], True)
        value = value + matmul(cat1[rs, 0:1024], t[:, COLS1B : COLS1B + 1024], True)
        value = value + matmul(cat1[rs, 1280:1792], t[:, COLS1B + 1024 : 2 * COLS1B], True)
        sig[rs, :] = sigmoid(value + wide)

    for_chunks(chunk)
    per = R // mask.shape[0]
    blocks = NJ // mask.shape[0]
    for s in range(mask.shape[0]):
        mask[s, 0:per, :] = sig[s * per : (s + 1) * per, :].astype(BF)
        hf[...] = jnp.zeros(hf.shape, F32)
        hf[0:blocks, :] = sigh[s * blocks : (s + 1) * blocks, :]
        mask[s, per : per + 16, :] = hf[...].astype(BF)


def ratio_terms(masks):
    squares = [m * m for m in masks]
    power = squares[0]
    for s in squares[1:]:
        power = power + s
    inverse = 1.0 / (power + RATIO_EPS)
    return [s * inverse for s in squares], inverse


def mask_back(masks, cots, mix):
    ratios, inverse = ratio_terms(masks)
    direct = cots[0] * ratios[0]
    for c, r in zip(cots[1:], ratios[1:]):
        direct = direct + c * r
    common = 2.0 * mix * inverse
    return [m * common * (c - direct) for m, c in zip(masks, cots)], direct


def mask_kernel(index, masks, c0, x0, hx, grad, direct, hf):
    stems = masks.shape[0]
    per, blocks = R // stems, NJ // stems
    mine = index[0]

    def one(j):
        for half in range(2):
            at = slice(L * half, L * half + L)
            m = [masks[s, rows(j), at].astype(F32) for s in range(stems)]
            c = [c0[rows(s * blocks + j), at].astype(F32) for s in range(stems)]
            x = x0[rows(mine * blocks + j), at].astype(F32)
            grads, own = mask_back(m, c, x)
            direct[rows(j), at] = own
            for s in range(stems):
                grad[s, rows(j), at] = grads[s].astype(BF)

    for_blocks(one, blocks)
    m = [masks[s, per : per + 16, :].astype(F32)[0:blocks] for s in range(stems)]
    c = [hx[NJ + s * blocks : NJ + (s + 1) * blocks, :] for s in range(stems)]
    grads, _ = mask_back(m, c, hx[rows(mine, blocks), :])
    for s in range(stems):
        hf[...] = jnp.zeros(hf.shape, F32)
        hf[0:blocks, :] = grads[s]
        grad[s, per : per + 16, :] = hf[...].astype(BF)


def estimate_kernel(index, masks, x0, out, scr, est):
    stems = masks.shape[0]
    blocks = NJ // stems
    mine = index[0]

    def one(j):
        for half in range(2):
            at = slice(L * half, L * half + L)
            m = [masks[s, rows(j), at].astype(F32) for s in range(stems)]
            x = x0[rows(mine * blocks + j), at].astype(F32)
            ratios, _ = ratio_terms(m)
            for s in range(stems):
                est[s, rows(j), at] = x * ratios[s]

    for_blocks(one, blocks)
    for s in range(stems):
        for t in range(blocks // 4):
            gather(
                lambda block, half, s=s, t=t: est[s, rows(4 * t + block), L * half : L * half + L], scr
            )
            for c in range(2):
                out[s, c, :, L * t : L * t + L] = scr[c].astype(BF)


def down_one_back_kernel(
    grad, sig, sigh, aux, t, rect, mom1, mom3, cat, g3, gact, mom, bias, first, last, hf, zf, hw
):
    stems = grad.shape[0]
    per, blocks = R // stems, NJ // stems
    for s in range(stems):
        span = slice(s * blocks, (s + 1) * blocks)
        value = grad[s, per : per + 16, :].astype(F32)[0:blocks]
        own = sigh[span, :]
        hf[span, :] = value * own * (1.0 - own)
    zf[...] = jnp.zeros(zf.shape, F32)

    def read(j, half):
        at = slice(L * half, L * half + L)
        own = sig[rows(j), at]
        value = grad[j // blocks, rows(j % blocks), at].astype(F32) * own * (1.0 - own)
        zf[...] = zf[...] + sum8(value)
        return value

    widen(hf, hw)
    columns_0(cat, read, hw, hw, aux)
    bias[...] = zf[...]

    def chunk(rs):
        value = matmul(cat[rs, :], t[...])
        g3[rs, :] = value[:, 0:512]
        gact[rs, :] = value[:, 512:1024]

    for_chunks(chunk)
    mean, scale = norm_terms(mom3, mom1[2:3])

    end_rows(g3, first, last)

    def sums(j, carry):
        s1, s2 = carry
        for k in range(4):
            at = slice(L * k, L * k + L)
            value = g3[rows(j), at]
            s1 = s1 + sum8(value)
            s2 = s2 + sum8(value * (rect[rows(j), at] - mean))
        return s1, s2

    zero = jnp.zeros((8, L), F32)
    s1, s2 = lax.fori_loop(0, NJ, sums, (zero, zero))
    mom[...] = fold(stack_rows([total_rows(s1), total_rows(s2) * scale]), 16)


def norm_back(g, xhat, kept, moments, count, factor):
    return factor * (g - kept * ((moments[0:1] + xhat * moments[1:2]) / count))


def up_two_back_kernel(
    g3, left, right, mom4, mom1, mom3, mom2, prm, aux, kept, rect, rleft, rright, t, z2,
    cat, g2, mom, first, last, lf, rf, lw, rw,
):
    count = mom1[2:3]
    mean, scale = norm_terms(mom3, count)
    factor = scale * prm[4:5]

    def back(g, r, keep):
        xhat = (r - mean) * scale
        return norm_back(g, xhat, keep, mom4, count, factor) * softplus_slope(r)

    for k in range(4):
        at = slice(L * k, L * k + L)
        row = k // 2
        lf[:, at] = back(left[:, at], rleft[:, at], kept[row : row + 1, :])
        rf[:, at] = back(right[:, at], rright[:, at], kept[3 + row : 4 + row, :])
    widen(lf, lw)
    widen(rf, rw)
    a, a_next = aux[0], aux[1]

    def one(j, total):
        for k in range(4):
            at = slice(L * k, L * k + L)
            value = back(g3[rows(j), at], rect[rows(j), at], aux[2 + k // 2])
            total = total + sum8(value)
            cat[rows(j), at] = value.astype(BF)
            if k >= 2:
                moved = from_prev(value, lw[rows(j, 8), at], a)
                cat[rows(j), 256 + L * k : 384 + L * k] = moved.astype(BF)
            moved = from_next(value, rw[rows(j, 8), at], a_next)
            cat[rows(j), 768 + L * k : 896 + L * k] = moved.astype(BF)
        return total

    zero = jnp.zeros((8, L), F32)
    bias = lax.fori_loop(0, NJ, one, zero)
    rims_1(cat, [g for g, _ in GROUPS1], 1280)

    def chunk(rs):
        g2[rs, :] = matmul(cat[rs, :], t[...])

    for_chunks(chunk)
    mean2, scale2 = norm_terms(mom2, mom1[3:4])
    gain, shift = prm[2:3], prm[3:4]

    def sums(j, carry):
        s1, s2 = carry
        for k in range(2):
            at = slice(L * k, L * k + L)
            xhat = (z2[rows(j), at] - mean2) * scale2
            value = g2[rows(j), at] * silu_slope(xhat * gain + shift)
            g2[rows(j), at] = value
            s1 = s1 + sum8(value)
            s2 = s2 + sum8(value * xhat)
        return s1, s2

    s1, s2 = lax.fori_loop(0, NJ, sums, (zero, zero))
    stats = fold(stack_rows([total_rows(s1), total_rows(s2)]), 32)
    bias = fold(stack_rows([total_rows(bias)] * 3), 16)
    end_rows(g2, first, last)
    mom[...] = jnp.where(sub((8, L)) == 2, bias, stats)


def down_two_back_kernel(
    g2, left, right, mom5, mom1, mom2, prm, aux, kept, z2, zleft, zright, t, gact, z1,
    own, g1, mom, first, last, cat, lf, rf, lw, rw,
):
    count = mom1[3:4]
    mean, scale = norm_terms(mom2, count)
    factor = scale * prm[2:3]

    def back(g, z, keep):
        return norm_back(g, (z - mean) * scale, keep, mom5, count, factor)

    for k in range(2):
        at = slice(L * k, L * k + L)
        lf[:, at] = back(left[:, at], zleft[:, at], kept[2:3, :])
        rf[:, at] = back(right[:, at], zright[:, at], kept[5:6, :])

    def read(j, k):
        at = slice(L * k, L * k + L)
        return back(g2[rows(j), at], z2[rows(j), at], aux[4])

    widen(lf, lw)
    widen(rf, rw)
    columns_2(cat, read, lw, rw, aux, own)

    def chunk(rs):
        g1[rs, :] = matmul(cat[rs, :], t[...], True) + gact[rs, :]

    for_chunks(chunk)
    mean1, scale1 = norm_terms(mom1, mom1[2:3])
    gain, shift = prm[0:1], prm[1:2]

    def sums(j, carry):
        s1, s2 = carry
        for k in range(4):
            at = slice(L * k, L * k + L)
            xhat = (z1[rows(j), at] - mean1) * scale1
            value = g1[rows(j), at] * silu_slope(xhat * gain + shift)
            g1[rows(j), at] = value
            s1 = s1 + sum8(value)
            s2 = s2 + sum8(value * xhat)
        return s1, s2

    zero = jnp.zeros((8, L), F32)
    s1, s2 = lax.fori_loop(0, NJ, sums, (zero, zero))
    end_rows(g1, first, last)
    mom[...] = fold(stack_rows([total_rows(s1), total_rows(s2)]), 16)


def up_one_back_kernel(
    g1, left, right, mom6, mom1, prm, aux, kept, z1, zleft, zright, t, own, net, cat, lf, rf,
    lw, rw,
):
    count = mom1[2:3]
    mean, scale = norm_terms(mom1, count)
    factor = scale * prm[0:1]

    def back(g, z, keep):
        return norm_back(g, (z - mean) * scale, keep, mom6, count, factor)

    for k in range(4):
        at = slice(L * k, L * k + L)
        row = k // 2
        lf[:, at] = back(left[:, at], zleft[:, at], kept[row : row + 1, :])
        rf[:, at] = back(right[:, at], zright[:, at], kept[3 + row : 4 + row, :])

    def read(j, k):
        at = slice(L * k, L * k + L)
        return back(g1[rows(j), at], z1[rows(j), at], aux[2 + k // 2])

    widen(lf, lw)
    widen(rf, rw)
    columns_1b(cat, read, lw, rw, aux, own)

    def chunk(rs):
        net[rs, :] = matmul(cat[rs, :], t[...], True).astype(BF)

    for_chunks(chunk)


def mixture_kernel(parts, direct, out, scr):
    stems = parts.shape[0]

    def tile(t):
        def block(k, half):
            at = slice(L * half, L * half + L)
            value = parts[0, rows(4 * t + k), at].astype(F32)
            for s in range(1, stems):
                value = value + parts[s, rows(4 * t + k), at].astype(F32)
            return value + direct[rows(4 * t + k), at]

        gather(block, scr)
        for c in range(2):
            out[c, :, pl.ds(pl.multiple_of(t * L, L), L)] = scr[c]

    for_blocks(tile, NJ // stems // 4)


def sum_over(values, axis):
    count = lax.axis_size(axis)
    if count & (count - 1):
        return lax.psum(values, axis)
    step = 1
    while step < count:
        radix = 2 if step == 1 or count // step == 2 else 4
        moved = [
            lax.ppermute(values, axis, [(i, i ^ (step * k)) for i in range(count)])
            for k in range(1, radix)
        ]
        for m in moved:
            values = values + m
        step *= radix
    return values


def from_left(values, axis):
    count = lax.axis_size(axis)
    return lax.ppermute(values, axis, [(i, i + 1) for i in range(count - 1)])


def from_right(values, axis):
    count = lax.axis_size(axis)
    return lax.ppermute(values, axis, [(i + 1, i) for i in range(count - 1)])


def swap(values, axis):
    return lax.all_to_all(values, axis, 0, 0, tiled=True)


def flags(seg_lengths, frame_mask, position, total):
    order = jnp.arange(seg_lengths.shape[0])
    earlier = order[None, :] < order[:, None]
    starts = 4 * jnp.sum(jnp.where(earlier, seg_lengths[None, :], 0), axis=1)
    frames = (position * M + jnp.arange(M + 1, dtype=jnp.int32)) * 4
    shut = jnp.any(frames[:, None] == starts[None, :], axis=1) | (frames == total)
    a = 1.0 - shut.astype(F32)
    keep_one = jnp.min(frame_mask.reshape(M, 2, 2), axis=2).astype(F32)
    keep_two = jnp.min(frame_mask.reshape(M, 4), axis=1).astype(F32)
    columns = jnp.stack([a[:M], a[1:], keep_one[:, 0], keep_one[:, 1], keep_two])
    return jnp.broadcast_to(columns[:, :, None], (5, M, L))


def per_device(
    mixture,
    seg_lengths,
    frame_mask,
    conv_first,
    encoder_gain_vector,
    shift_first,
    conv_second,
    gain_second,
    shift_second,
    deconv_second,
    bias_second,
    decoder_gain_vector,
    shift_third,
    deconv_first,
    bias_first,
    cotangent,
):
    position = lax.axis_index("tm")
    stems = lax.axis_size("stem")
    index = lax.axis_index("stem").astype(jnp.int32).reshape(1)
    frames = mixture.shape[1]
    per, blocks = R // stems, NJ // stems
    aux = flags(seg_lengths, frame_mask, position, frames * lax.axis_size("tm"))
    prm = jnp.stack(
        [
            jnp.tile(encoder_gain_vector[0], 8),
            jnp.tile(shift_first[0], 8),
            jnp.tile(gain_second[0], 4),
            jnp.tile(shift_second[0], 4),
            jnp.tile(decoder_gain_vector[0], 8),
            jnp.tile(shift_third[0], 8),
            jnp.tile(bias_second[0], 8),
            jnp.tile(jnp.repeat(bias_first[0], 32), 2),
        ]
    )
    w1c = jnp.tile(conv_first[0].transpose(2, 1, 3, 0).reshape(50, 16).astype(F32), (1, 8))
    w1d = deconv_first[0].transpose(2, 0, 3, 1).reshape(50, 2, 16).astype(F32)
    w1d = jnp.tile(w1d.transpose(1, 0, 2), (1, 1, 8))
    w2c = jnp.tile(conv_second[0].transpose(2, 3, 1, 0).reshape(400, 32).astype(F32), (1, 4))
    w2d = jnp.tile(deconv_second[0].transpose(2, 3, 0, 1).reshape(400, 32).astype(F32), (1, 4))

    x0, c0, first, last = run(
        layout_kernel,
        "layout",
        [((R, 256), BF), ((R, 256), BF), ((2 * NJ + 16, 256), BF), ((2 * NJ + 16, 256), BF)],
        [mixture, cotangent, aux],
        [((2, frames, L), F32), ((2 * R, 256), F32), ((2, 2 * NJ + 16, 256), F32)],
    )
    left0, right0 = from_left(last, "tm"), from_right(first, "tm")
    (t1a_c,) = run(matrices_first, "matrices_first", [((COLS0, 512), BF)], [w1c])
    t2a_c, t2b_d, t1b_d = run(
        matrices_forward,
        "matrices_forward",
        [((COLS1, 256), BF), ((512, COLS2), BF), ((256, 2 * COLS1B), BF)],
        [w2c, w2d, w1d],
    )
    t1a_d, t2a_d, t2b_c, t1b_c = run(
        matrices_back,
        "matrices_back",
        [((COLS0, 1024), BF), ((COLS1, 256), BF), ((512, COLS2), BF), ((256, COLS1B), BF)],
        [w1c, w2c, w2d, w1d],
    )
    wide = lambda lanes: [((8 * NJ, lanes), F32)] * 2
    halo = lambda lanes: [((NJ, lanes), F32), ((NJ, lanes), F32)]
    mom_out = [((8, L), F32)]
    cat0, z1, mom1, first, last, hx, kept = run(
        conv_one_kernel,
        "conv_one",
        [((R, COLS0), BF), ((R, 512), F32)] + mom_out + halo(512) + [((2 * NJ, 256), F32)] + mom_out,
        [x0, left0, right0, aux, t1a_c],
        [((2 * NJ + 16, 256), F32)] * 2 + wide(256),
        flops=2 * R * COLS0 * 512,
    )
    h1l, h1r = from_left(last, "tm"), from_right(first, "tm")
    mom1 = sum_over(mom1, "tm")
    cat1, ends1, z2, mom2, first, last = run(
        conv_two_kernel,
        "conv_two",
        [((R, COLS1), BF), ((4, NJ, 512), BF), ((R, 256), F32)] + mom_out + halo(256),
        [z1, h1l, h1r, mom1, prm, aux, t2a_c],
        [((4, NJ, 512), F32)] + wide(512),
        flops=2 * R * COLS1 * 256,
    )
    h2l, h2r = from_left(last, "tm"), from_right(first, "tm")
    mom2 = sum_over(mom2, "tm")
    act2, rect, mom3, first, last = run(
        up_two_kernel,
        "up_two",
        [((R, 256), BF), ((R, 512), F32)] + mom_out + halo(512),
        [z2, h2l, h2r, mom1, mom2, prm, aux, t2b_d],
        [((R, COLS2), BF)] + halo(256) + wide(256),
        flops=2 * R * COLS2 * 512,
    )
    h3l, h3r = from_left(last, "tm"), from_right(first, "tm")
    mom3 = sum_over(mom3, "tm")
    low3, sig, sigh, mask = run(
        up_one_kernel,
        "up_one",
        [((R, 512), BF), ((R, 256), F32), ((NJ, 256), F32), ((stems, per + 16, 256), BF)],
        [rect, h3l, h3r, mom1, mom3, prm, aux, cat1, ends1, t1b_d],
        [((R, COLS1B), BF)] + halo(512) + [((2, NJ, 512), F32), ((16, 256), F32)] + wide(512),
        flops=2 * R * 2 * COLS1B * 256,
    )
    masks = swap(mask, "stem")
    grad, direct = run(
        mask_kernel,
        "mask",
        [((stems, per + 16, 256), BF), ((per, 256), F32)],
        [index, masks, c0, x0, hx],
        [((16, 256), F32)],
        scalars=1,
    )
    grad = swap(grad, "stem")
    (estimates,) = run(
        estimate_kernel,
        "estimate",
        [((stems, 2, frames, blocks * 32), BF)],
        [index, masks, x0],
        [((2, frames, L), F32), ((stems, per, 256), F32)],
        scalars=1,
    )
    cat0g, g3, gact, mom4, bias_one, first, last = run(
        down_one_back_kernel,
        "down_one_back",
        [((R, COLS0), BF), ((R, 512), F32), ((R, 512), F32)] + mom_out + mom_out + halo(512),
        [grad, sig, sigh, aux, t1a_d, rect, mom1, mom3],
        [((NJ, 256), F32), ((8, L), F32), ((8 * NJ, 256), F32)],
        flops=2 * R * COLS0 * 1024,
    )
    h4l, h4r = from_left(last, "tm"), from_right(first, "tm")
    mom4 = sum_over(mom4, "tm")
    (w1d_grad,) = run(
        weight_1_joined,
        "weight_up_one",
        [((96, L), F32)],
        [low3, cat1, cat0g],
        [((512, COLS0), F32)],
        flops=2 * R * COLS0 * 1024,
    )
    cat1g, g2, mom5, first, last = run(
        up_two_back_kernel,
        "up_two_back",
        [((R, COLS1), BF), ((R, 256), F32)] + mom_out + halo(256),
        [g3, h4l, h4r, mom4, mom1, mom3, mom2, prm, aux, kept, rect, h3l, h3r, t2a_d, z2],
        halo(512) + wide(512),
        flops=2 * R * COLS1 * 256,
    )
    h5l, h5r = from_left(last, "tm"), from_right(first, "tm")
    mom5 = sum_over(mom5, "tm")
    (w2d_grad,) = run(
        weight_2_kernel,
        "weight_up_two",
        [((160, L), F32)],
        [act2, cat1g],
        [((256, COLS1), F32)],
        flops=2 * R * COLS1 * 256,
    )
    low2, g1, mom6, first, last = run(
        down_two_back_kernel,
        "down_two_back",
        [((R, 256), BF), ((R, 512), F32)] + mom_out + halo(512),
        [g2, h5l, h5r, mom5, mom1, mom2, prm, aux, kept, z2, h2l, h2r, t2b_c, gact, z1],
        [((R, COLS2), BF)] + halo(256) + wide(256),
        flops=2 * R * COLS2 * 512,
    )
    h6l, h6r = from_left(last, "tm"), from_right(first, "tm")
    mom6 = sum_over(mom6, "tm")
    (w2c_grad,) = run(
        weight_2_kernel,
        "weight_down_two",
        [((160, L), F32)],
        [low2, cat1],
        [((256, COLS1), F32)],
        flops=2 * R * COLS1 * 256,
    )
    low1, net = run(
        up_one_back_kernel,
        "up_one_back",
        [((R, 512), BF), ((R, 256), BF)],
        [g1, h6l, h6r, mom6, mom1, prm, aux, kept, z1, h1l, h1r, t1b_c],
        [((R, COLS1B), BF)] + halo(512) + wide(512),
        flops=2 * R * COLS1B * 256,
    )
    parts = swap(net.reshape(stems, per, 256), "stem")
    (w1c_grad,) = run(
        weight_1_first,
        "weight_down_one",
        [((48, L), F32)],
        [low1, cat0],
        [((512, COLS0), F32)],
        flops=2 * R * COLS0 * 512,
    )
    (mixture_grad,) = run(
        mixture_kernel,
        "mixture",
        [((2, frames, blocks * 32), F32)],
        [parts, direct],
        [((2, frames, L), F32)],
    )
    early = sum_over(jnp.concatenate([w1d_grad, w2d_grad, w2c_grad, bias_one]), "tm")
    w1c_grad = sum_over(w1c_grad, "tm")

    def outer(tiles):
        taps = tiles.reshape(3, 16, 2, 2, 32)[..., :TAPS].transpose(1, 3, 0, 2, 4)
        return taps.reshape(16, 2, 6, TAPS)[:, :, 1:]

    def inner(tiles):
        return tiles[:, :80].reshape(TAPS, 32, TAPS, 16).transpose(1, 3, 0, 2)

    w1d_grad = jnp.concatenate([outer(early[0:48]), outer(early[48:96])]).transpose(1, 0, 2, 3)
    return (
        estimates,
        mixture_grad,
        outer(w1c_grad)[None],
        mom6[1, :16][None],
        mom6[0, :16][None],
        inner(early[256:416])[None],
        mom5[1, :32][None],
        mom5[0, :32][None],
        inner(early[96:256]).transpose(1, 0, 2, 3)[None],
        mom5[2, :16][None],
        mom4[1, :16][None],
        mom4[0, :16][None],
        w1d_grad[None],
        early[416:424].reshape(8, 2, 2, 32).sum((0, 1, 3))[None],
    )


def solution(mesh):
    in_specs = (
        P(None, "tm", None),
        P(),
        P("tm"),
        P("stem", None, None, None, None),
        P("stem", None),
        P("stem", None),
        P("stem", None, None, None, None),
        P("stem", None),
        P("stem", None),
        P("stem", None, None, None, None),
        P("stem", None),
        P("stem", None),
        P("stem", None),
        P("stem", None, None, None, None),
        P("stem", None),
        P(None, None, "tm", "stem"),
    )
    out_specs = (
        P(None, None, "tm", "stem"),
        P(None, "tm", "stem"),
        P("stem", None, None, None, None),
        P("stem", None),
        P("stem", None),
        P("stem", None, None, None, None),
        P("stem", None),
        P("stem", None),
        P("stem", None, None, None, None),
        P("stem", None),
        P("stem", None),
        P("stem", None),
        P("stem", None, None, None, None),
        P("stem", None),
    )
    return jax.shard_map(
        per_device, mesh=mesh, in_specs=in_specs, out_specs=out_specs, check_vma=False
    )
```

```python
import jax
import jax.numpy as jnp
from jax import lax
from jax.experimental import pallas as pl
from jax.experimental.pallas import tpu as pltpu
from jax.sharding import PartitionSpec as P

NORM_EPS = 0.001
RATIO_EPS = 1e-10
BF = jnp.bfloat16
F32 = jnp.float32
TAPS = 5
L = 128
M = 32
NJ = 32
R = M * NJ
CHUNK = 256
COLS0 = 1024
COLS1 = 1920
COLS1B = 1536
COLS2 = 1152
GROUPS1 = ((0, 1024, 1), (256, 1152, 2), (512, 1280, 0), (768, 1408, 3), (1536, 1792, 4))
FULL = pl.BlockSpec(memory_space=pltpu.VMEM)
SCALAR = pl.BlockSpec(memory_space=pltpu.SMEM)
FAR = pl.BlockSpec(memory_space=pltpu.HBM)


class Far:
    def __init__(self, array, columns=None):
        self.array, self.columns = array, columns


class Arriving:
    def __init__(self, source, target, sem):
        self.copy, self.target, self.waited = pltpu.make_async_copy(source, target, sem), target, False
        self.copy.start()

    def get(self):
        if not self.waited:
            self.copy.wait()
            self.waited = True
        return self.target


class Leaving:
    def __init__(self, target, sem):
        self.target, self.sem, self.copy = target, sem, None

    def put(self, source):
        self.copy = pltpu.make_async_copy(source, self.target, self.sem)
        self.copy.start()


def run(kernel, name, outs, args, scratch=(), flops=0):
    arrays = [a.array if isinstance(a, Far) else a for a in args]
    far_in = [k for k, a in enumerate(args) if isinstance(a, Far)]
    far_out = [k for k, o in enumerate(outs) if len(o) == 3]
    n_in, n_out, n_own = len(args), len(outs), len(scratch)
    placed = [
        pltpu.with_memory_space_constraint(a.array, pltpu.HBM) if isinstance(a, Far) else a for a in args
    ]
    landing = []
    for k in far_in:
        shape = args[k].array.shape
        if args[k].columns is not None:
            shape = (shape[0], args[k].columns)
        landing.append(pltpu.VMEM(shape, args[k].array.dtype))

    def body(*refs):
        ins, results = list(refs[:n_in]), list(refs[n_in : n_in + n_out])
        own = refs[n_in + n_out : n_in + n_out + n_own]
        targets = refs[n_in + n_out + n_own : n_in + n_out + n_own + len(far_in)]
        sems = refs[-1]
        for i, k in enumerate(far_in):
            source = ins[k] if args[k].columns is None else ins[k].at[:, 0 : args[k].columns]
            ins[k] = Arriving(source, targets[i], sems.at[i])
        for i, k in enumerate(far_out):
            results[k] = Leaving(results[k], sems.at[len(far_in) + i])
        kernel(*ins, *results, *own)
        for k in far_in:
            ins[k].get()
        for k in far_out:
            results[k].copy.wait()

    in_specs = []
    for a in args:
        if isinstance(a, Far):
            in_specs.append(FAR)
        else:
            in_specs.append(SCALAR if a.dtype == jnp.int32 else FULL)
    bytes_all = sum(a.size * a.dtype.itemsize for a in arrays)
    bytes_all += sum(jnp.zeros((), o[1]).dtype.itemsize * o[0][0] * o[0][-1] for o in outs)
    return pl.pallas_call(
        body,
        out_shape=[
            pltpu.HBM(o[0], o[1]) if len(o) == 3 else jax.ShapeDtypeStruct(o[0], o[1]) for o in outs
        ],
        in_specs=in_specs,
        out_specs=[FAR if len(o) == 3 else FULL for o in outs],
        scratch_shapes=[pltpu.VMEM(s, d) for s, d in scratch]
        + landing
        + [pltpu.SemaphoreType.DMA((max(1, len(far_in) + len(far_out)),))],
        compiler_params=pltpu.CompilerParams(vmem_limit_bytes=24 << 20),
        cost_estimate=pl.CostEstimate(flops=flops, bytes_accessed=bytes_all, transcendentals=0),
        name=name,
    )(*placed)


def lane(shape):
    return lax.broadcasted_iota(jnp.int32, shape, 1)


def sub(shape):
    return lax.broadcasted_iota(jnp.int32, shape, 0)


def rows(j, count=M):
    return pl.ds(pl.multiple_of(j * count, count), count)


def tiles(width):
    return [slice(L * k, L * k + L) for k in range(width // L)]


def for_blocks(fn, count=NJ):
    def body(j, carry):
        fn(j)
        return carry

    lax.fori_loop(0, count, body, 0)


def for_blocks_rims(fn):
    def body(j, carry):
        fn(j, True, True)
        return carry

    fn(0, False, True)
    lax.fori_loop(1, NJ - 1, body, 0)
    fn(NJ - 1, True, False)


def from_prev(value, rim, flag):
    rim = jnp.concatenate([rim] * (M // 8), axis=0)
    return jnp.where(sub(value.shape) == 0, rim, pltpu.roll(value, 1, 0)) * flag


def from_next(value, rim, flag):
    rim = jnp.concatenate([rim] * (M // 8), axis=0)
    return jnp.where(sub(value.shape) == M - 1, rim, pltpu.roll(value, M - 1, 0)) * flag


def widen(source, out):
    def group(g):
        for at in tiles(source.shape[1]):
            tile = source[rows(g, 8), at]
            for i in range(8):
                out[rows(8 * g + i, 8), at] = jnp.broadcast_to(tile[i : i + 1], (8, L))

    for_blocks(group, NJ // 8)


def mask_bf(cond):
    return jnp.where(cond, 1.0, 0.0).astype(BF)


def fill_rims(cat, parts, low, high):
    def one(j, has_prev, has_next):
        for target, after, before in parts:
            value = None
            if has_next:
                value = cat[rows(j + 1), after : after + L] * low
            if has_prev:
                other = cat[rows(j - 1), before : before + L] * high
                value = other if value is None else value + other
            cat[rows(j), target : target + L] = value

    for_blocks_rims(one)


def rims_1(cat, groups):
    at = lane((M, L))
    parts = [(rim, base, base + L) for base, rim, _ in groups]
    fill_rims(cat, parts, mask_bf(at < 32), mask_bf(at >= 112))


def rims_2(cat):
    at = lane((M, L))
    parts = [(768 + L * k, 256 * k, 256 * k + L) for k in range(3)]
    fill_rims(cat, parts, mask_bf(at < 32), mask_bf(at >= 96))


def rims_0(cat):
    at = lane((M, L)) % 32
    fill_rims(cat, [(512 + L * k, L * k, L * k) for k in range(4)], mask_bf(at < 2), mask_bf(at == 31))


def matmul(left, right, transposed=False):
    return lax.dot_general(
        left, right, (((1,), (1 if transposed else 0,)), ((), ())), preferred_element_type=F32
    )


def for_chunks(fn, size=CHUNK):
    def body(r, carry):
        fn(pl.ds(pl.multiple_of(r * size, size), size))
        return carry

    lax.fori_loop(0, R // size, body, 0)


def sum8(value):
    total = value[0:8]
    for k in range(1, value.shape[0] // 8):
        total = total + value[8 * k : 8 * k + 8]
    return total


def sum_blocks(fn):
    def body(j, carry):
        return fn(j, *carry)

    zero = jnp.zeros((8, L), F32)
    return [total_rows(s) for s in lax.fori_loop(0, NJ, body, (zero, zero))]


def fold(stats, period):
    step = L // 2
    while step >= period:
        stats = stats + pltpu.roll(stats, step, 1)
        step //= 2
    return stats


def stack_rows(values):
    at = sub((8, L))
    tile = jnp.zeros((8, L), F32)
    for k, value in enumerate(values):
        tile = jnp.where(at == k, value, tile)
    return tile


def total_rows(value):
    return jnp.sum(value, axis=0, keepdims=True)


def norm_terms(moments, count):
    mean = moments[0:1] / count
    return mean, lax.rsqrt(moments[1:2] / count - mean * mean + NORM_EPS)


def silu(v):
    return v / (1.0 + jnp.exp(-v))


def silu_slope(v):
    s = 1.0 / (1.0 + jnp.exp(-v))
    return s * (1.0 + v * (1.0 - s))


def sigmoid(v):
    return 1.0 / (1.0 + jnp.exp(-v))


def softplus(v):
    return jnp.maximum(v, 0.0) + jnp.log1p(jnp.exp(-jnp.abs(v)))


def softplus_slope(r):
    return jnp.where(r < 0.05, r * (1.0 - r * (0.5 - r * (1.0 / 6.0))), 1.0 - jnp.exp(-r))


def end_rows(z, group_out, blocks=NJ):
    def group(g):
        for at in tiles(z.shape[1]):
            place = sub((8, L))
            top = low = jnp.zeros((8, L), F32)
            for i in range(8):
                start = pl.multiple_of((8 * g + i) * M, M)
                top = jnp.where(place == i, z[pl.ds(start, 8), at][0:1], top)
                low = jnp.where(place == i, z[pl.ds(start + M - 8, 8), at][7:8], low)
            group_out(rows(g, 8), at, top, low)

    for_blocks(group, blocks // 8)


def pack_ends(z, index, cross, core, blocks=NJ):
    even = index[1] == 0

    def group_out(rs, at, top, low):
        cross[rs, at] = jnp.where(even, top, low)
        core[rs, at] = jnp.where(even, low, top)

    end_rows(z, group_out, blocks)


def pack_moments(mom, cross, value):
    mom[...] = value
    cross[NJ : NJ + 8, 0:L] = value


def sides(index, cross, core, at):
    even = index[1] == 0
    a, b = cross[0:NJ, at], core[0:NJ, at]
    return jnp.where(even, a, b), jnp.where(even, b, a)


def tile_2(w, tap, q, half):
    at = lane((16, L)) // 32
    tile = jnp.zeros((16, L), F32)
    for k in range(4):
        b = q - 2 * (4 * half + k) + 1
        if 0 <= b < TAPS:
            start = (tap * TAPS + b) * 16
            tile = jnp.where(at == k, w[start : start + 16, :], tile)
    return tile.astype(BF)


def matrix_2_down(w, t):
    zero = jnp.zeros((16, L), BF)
    for base, rim, tap in GROUPS1:
        for half in range(2):
            at = slice(L * half, L * half + L)
            for q in range(16):
                t[base + 16 * q : base + 16 * q + 16, at] = tile_2(w, tap, q, half)
            for part in range(8):
                q = {0: 16, 1: 17, 7: -1}.get(part)
                start = rim + 16 * part
                t[start : start + 16, at] = zero if q is None else tile_2(w, tap, q, half)


def matrix_2_up(w, t):
    zero = jnp.zeros((16, L), BF)
    at = lane((16, L))
    for row in range(2):
        for k, tap in enumerate((row + 1, row + 3, row - 1)):
            for q in range(16):
                span = slice(row * 256 + q * 16, row * 256 + q * 16 + 16)
                for half in range(2):
                    cols = slice(256 * k + L * half, 256 * k + L * half + L)
                    t[span, cols] = tile_2(w, tap, q, half) if 0 <= tap < TAPS else zero
                rim = zero
                if 0 <= tap < TAPS and q in (0, 1, 15):
                    b = {0: 3, 1: 4, 15: 0}[q]
                    start = (tap * TAPS + b) * 16
                    cond = at < 32 if q == 15 else at >= 96
                    rim = jnp.where(cond, w[start : start + 16, :], 0.0).astype(BF)
                t[span, 768 + L * k : 768 + L * k + L] = rim


def band(w, tap, channel, offset):
    tile = jnp.zeros((32, L), F32)
    for b in range(TAPS):
        start = (tap * 2 + channel) * TAPS + b
        tile = jnp.where(offset == b, w[start : start + 1, :], tile)
    return tile.astype(BF)


def matrix_1_down(w, t, col):
    q, zero = sub((32, L)), jnp.zeros((32, L), BF)
    for half in range(2):
        p = 8 * half + lane((32, L)) // 16
        inner = q - 2 * p + 1
        rim = jnp.where(q == 31, -2 * p, jnp.where(q == 0, 33 - 2 * p, jnp.where(q == 1, 34 - 2 * p, -9)))
        for row in range(2):
            cols = slice(col + row * 256 + half * L, col + row * 256 + half * L + L)
            for part, frame in enumerate((0, 1, 2, 3, None, -1, 4, 5)):
                tap = -1 if frame is None else frame - 2 * row + 1
                for c in range(2):
                    start = part * 64 + c * 32
                    ok = 0 <= tap < TAPS
                    t[start : start + 32, cols] = band(w, tap, c, inner) if ok else zero
                    t[512 + start : 544 + start, cols] = band(w, tap, c, rim) if ok else zero


def matrix_1_up(w, t, col):
    q, zero = sub((32, L)), jnp.zeros((32, L), BF)
    at = lane((32, L))
    rim = jnp.where(at < 16, q - 31, jnp.where(at >= 112, q + 3, -9))
    for frame in range(4):
        taps = (frame + 1, frame - 1, frame + 3, frame - 3)
        for c in range(2):
            span = slice(frame * 64 + c * 32, frame * 64 + c * 32 + 32)
            for k, tap in enumerate(taps):
                ok = 0 <= tap < TAPS
                for half in range(2):
                    p = 8 * half + at // 16
                    start = col + 256 * k + L * half
                    t[span, start : start + L] = band(w, tap, c, q - 2 * p + 1) if ok else zero
                start = col + 1024 + L * k
                t[span, start : start + L] = band(w, tap, c, rim) if ok else zero


def matrices_first(w1c, t1a):
    matrix_1_down(w1c, t1a, 0)


def matrices_forward(w2c, w2d, w1d, t2a_c, t2b_d, t1b_d, a, b, c):
    matrix_2_down(w2c, a)
    t2a_c.put(a)
    matrix_2_up(w2d, b)
    t2b_d.put(b)
    matrix_1_up(w1d.at[0], c, 0)
    matrix_1_up(w1d.at[1], c, COLS1B)
    t1b_d.put(c)


def matrices_back(w1c, w2c, w2d, w1d, t1a_d, t2a_d, t2b_c, t1b_c, a, b, c, d):
    w1c, w2c, w2d, w1d = [w.get() for w in (w1c, w2c, w2d, w1d)]
    matrix_1_down(w1d.at[0], a, 0)
    matrix_1_down(w1d.at[1], a, 512)
    t1a_d.put(a)
    matrix_2_down(w2d, b)
    t2a_d.put(b)
    matrix_2_up(w2c, c)
    t2b_c.put(c)
    matrix_1_up(w1c, d, 0)
    t1b_c.put(d)


def correlate(coarse, fine, d):
    def part(rs, first):
        value = lax.dot_general(
            coarse[rs, :], fine[rs, :], (((0,), (0,)), ((), ())), preferred_element_type=F32
        )
        d[...] = value if first else d[...] + value

    part(pl.ds(0, CHUNK), True)

    def body(r, carry):
        part(pl.ds(pl.multiple_of(r * CHUNK, CHUNK), CHUNK), False)
        return carry

    lax.fori_loop(1, R // CHUNK, body, 0)


def weight_2(d, out):
    at = lane((32, L))
    sums = {}
    for base, rim, tap in GROUPS1:
        total = jnp.zeros((32, L), F32)
        for p in range(8):
            span = slice(32 * p, 32 * p + 32)
            parts = [d[span, base : base + L], d[span, base + L : base + 256], d[span, rim : rim + L]]
            if p == 0:
                value = jnp.where(at < 16, pltpu.roll(parts[2], 16, 1), pltpu.roll(parts[0], 16, 1))
            else:
                which, off = divmod(32 * p - 16, L)
                value = pltpu.roll(parts[which], L - off, 1)
                if off + 80 > L:
                    value = jnp.where(at < L - off, value, pltpu.roll(parts[which + 1], L - off, 1))
            total = total + value
        sums[tap] = total
    out[0:32, :] = jnp.where(at < 80, sums[0], pltpu.roll(sums[4], 80, 1))
    out[32:64, :] = jnp.where(at < 80, sums[1], pltpu.roll(sums[4], 32, 1))
    out[64:96, :] = sums[2]
    out[96:128, :] = sums[3]


def weight_1(d, out, start):
    at = lane((16, L)) % 32
    result = jnp.zeros((16, L), F32)
    for k in range(3):
        total = jnp.zeros((16, L), F32)
        for row in range(2):
            tile = (2, 0, 1)[k] if row == 0 else (0, 1, 3)[k]
            for p in range(16):
                first = row * 256 + p * 16
                span = slice(first, first + 16)
                value = pltpu.roll(d[span, L * tile : L * tile + L], (1 - 2 * p) % L, 1)
                if p in (0, 15):
                    rim = d[span, 512 + L * tile : 512 + L * tile + L]
                    rim = pltpu.roll(rim, L - 31 if p == 0 else 3, 1)
                    value = jnp.where(at == 0 if p == 0 else at >= 3, rim, value)
                total = total + value
        if k > 0:
            total = pltpu.roll(total, 8 * k, 1)
        result = jnp.where((at >= 8 * k) & (at < 8 * k + TAPS), total, result)
    out[start : start + 16, :] = result


def weight_2_kernel(coarse, fine, out, d):
    correlate(ready(coarse), ready(fine), d)
    weight_2(d, out)


def weight_1_first(coarse, fine, out, d):
    correlate(ready(coarse), ready(fine), d)
    weight_1(d, out, 0)


def weight_1_joined(low, cat1, fine, out, d):
    correlate(ready(low), ready(fine), d)
    weight_1(d, out, 0)
    correlate(ready(cat1), ready(fine), d)
    weight_1(d, out, 16)


def ready(ref):
    return ref.get() if isinstance(ref, Arriving) else ref


def spread(scr, store):
    at = lane((M, L)) // 32
    for half in range(2):
        parts = [scr[k % 2, pl.ds(2 * half + k // 2, M, stride=4), :] for k in range(4)]
        for block in range(4):
            value = parts[block]
            for k in range(4):
                if k != block:
                    value = jnp.where(at == k, pltpu.roll(parts[k], (32 * (k - block)) % L, 1), value)
            store(block, half, value)


def gather(blocks, scr):
    at = lane((M, L)) // 32
    for half in range(2):
        parts = [blocks(block, half) for block in range(4)]
        for k in range(4):
            value = parts[k]
            for block in range(4):
                if block != k:
                    value = jnp.where(
                        at == block, pltpu.roll(parts[block], (32 * (block - k)) % L, 1), value
                    )
            scr[k % 2, pl.ds(2 * half + k // 2, M, stride=4), :] = value


def layout_kernel(index, frame_mask, mix, cot, cross, core, x0, c0, scr, wide, xf, cf, ends):
    def place(out, block, row):
        def store(k, half, value):
            at = slice(L * half, L * half + L)
            out[rows(block + k), at] = value.astype(BF)
            wide[rows(row + k), at] = value

        return store

    m = mix.get()

    def mix_tile(t):
        for c in range(2):
            scr[c] = m[c, :, pl.ds(pl.multiple_of(t * L, L), L)].astype(F32)
        spread(scr, place(xf, 4 * t, 4 * t))

    for_blocks(mix_tile, NJ // 4)
    x0.put(xf)
    g = cot.get()
    per_stem = g.shape[3] // L

    def cot_tile(t):
        for c in range(2):
            lanes = pl.ds(pl.multiple_of((t % per_stem) * L, L), L)
            scr[c] = g[t // per_stem, c, :, lanes].astype(F32)
        spread(scr, place(cf, 4 * t, NJ + 4 * t))

    for_blocks(cot_tile, NJ // 4)
    c0.put(cf)
    ends[...] = jnp.zeros(ends.shape, F32)
    pack_ends(wide, index, ends.at[0], ends.at[1], 2 * NJ)
    even = index[1] == 0

    def least(first, count):
        value = frame_mask[first]
        for k in range(1, count):
            value = jnp.minimum(value, frame_mask[first + k])
        return value.astype(F32)

    for i, (first, count) in enumerate(((0, 2), (2, 2), (0, 4))):
        top, low = least(first, count), least(4 * M - 4 + first, count)
        row = 2 * NJ + i
        ends[0, row : row + 1, :] = jnp.full((1, 2 * L), jnp.where(even, top, low))
        ends[1, row : row + 1, :] = jnp.full((1, 2 * L), jnp.where(even, low, top))
    cross[...] = ends[0].astype(BF)
    core[...] = ends[1].astype(BF)


def columns_0(cat, blocks, read, left, right, aux):
    a, a_next = aux[0], aux[1]
    for which, (first, count) in enumerate(blocks):

        def one(i, which=which, first=first):
            j = first + i
            for half in range(2):
                value = read(which, j, half)
                cat[rows(j), L * half : L * half + L] = value.astype(BF)
                if half == 1:
                    moved = from_prev(value, left[rows(j, 8), L : 2 * L], a)
                    cat[rows(j), 256:384] = moved.astype(BF)
                else:
                    moved = from_next(value, right[rows(j, 8), 0:L], a_next)
                    cat[rows(j), 384:512] = moved.astype(BF)

        for_blocks(one, count)
    rims_0(cat)


def conv_one_kernel(
    index, x0, cross_in, core_in, aux, t,
    z, cross, core, mom, hx, kept, zfar, catfar, cat, lf, rf, lw, rw,
):
    even = index[1] == 0
    a, b = cross_in[...].astype(F32), core_in[...].astype(F32)
    lf[...] = jnp.where(even, a, b)
    rf[...] = jnp.where(even, b, a)
    hx[:, 0:L] = rf[0 : 2 * NJ, 0:L]
    hx[:, L : 2 * L] = lf[0 : 2 * NJ, L : 2 * L]
    kept[...] = jnp.zeros(kept.shape, F32)
    kept[0:3, :] = lf[2 * NJ : 2 * NJ + 3, 0:L]
    kept[3:6, :] = rf[2 * NJ : 2 * NJ + 3, 0:L]
    widen(lf.at[0:NJ], lw)
    widen(rf.at[0:NJ], rw)
    x = ready(x0)
    read = lambda which, j, h: x[rows(j), L * h : L * h + L].astype(F32)
    columns_0(cat, [(0, NJ)], read, lw, rw, aux)
    catfar.put(cat)
    weights = ready(t)

    def chunk(rs):
        z[rs, :] = matmul(cat[rs, :], weights[...])

    for_chunks(chunk)
    zfar.put(z)
    pack_ends(z, index, cross, core)

    def sums(j, s1, s2):
        for k, at in enumerate(tiles(512)):
            value = z[rows(j), at]
            part = value * aux[2 + k // 2]
            s1 = s1 + sum8(part)
            s2 = s2 + sum8(part * value)
        return s1, s2

    stats = fold(stack_rows(sum_blocks(sums)), 16)
    at = sub((8, L))
    stats = jnp.where(at == 2, total_rows(aux[2] + aux[3]) * (NJ * 16.0), stats)
    stats = jnp.where(at == 3, total_rows(aux[4]) * (NJ * 8.0), stats)
    pack_moments(mom, cross, stats)


def conv_two_kernel(
    index, z1, cross_in, core_in, mom1, prm, aux, t,
    z2, cross, core, mom, ends, h1, zfar, catfar, cat, ef, hf, lw, rw,
):
    mean, scale = norm_terms(mom1, mom1[2:3])
    gain, shift = prm[0:1], prm[1:2]

    def act(value):
        return silu((value - mean) * scale * gain + shift)

    a, a_next = aux[0], aux[1]
    for at in tiles(512):
        left, right = sides(index, cross_in, core_in, at)
        hf[0, :, at] = left
        hf[1, :, at] = right
        ef[0, :, at] = act(left)
        ef[1, :, at] = act(right)
    h1.put(hf)
    widen(ef.at[0], lw)
    widen(ef.at[1], rw)

    def one(j):
        for k, at in enumerate(tiles(512)):
            value = act(z1[rows(j), at])
            cat[rows(j), at] = value.astype(BF)
            if k >= 2:
                moved = from_prev(value, lw[rows(j, 8), at], a)
                cat[rows(j), 256 + L * k : 384 + L * k] = moved.astype(BF)
            start = 768 + L * k if k < 2 else 1280 + L * k
            moved = from_next(value, rw[rows(j, 8), at], a_next)
            cat[rows(j), start : start + L] = moved.astype(BF)

    for_blocks(one)
    rims_1(cat, GROUPS1)
    catfar.put(cat)
    weights = ready(t)

    def chunk(rs):
        z2[rs, :] = matmul(cat[rs, :], weights[...])

    for_chunks(chunk)
    zfar.put(z2)
    pack_ends(z2, index, cross, core)

    def sums(j, s1, s2):
        for at in tiles(256):
            value = z2[rows(j), at]
            part = value * aux[4]
            s1 = s1 + sum8(part)
            s2 = s2 + sum8(part * value)
        return s1, s2

    pack_moments(mom, cross, fold(stack_rows(sum_blocks(sums)), 32))

    def group_out(rs, at, top, low):
        ef[2, rs, at] = act(top)
        ef[3, rs, at] = act(low)

    end_rows(z1, group_out)
    ends[...] = ef[...].astype(BF)


def columns_2(cat, read, left, right, aux):
    a, a_next = aux[0], aux[1]

    def one(j):
        for k, at in enumerate(tiles(256)):
            value = read(j, at)
            cat[rows(j), at] = value.astype(BF)
            moved = from_prev(value, left[rows(j, 8), at], a)
            cat[rows(j), 256 + L * k : 384 + L * k] = moved.astype(BF)
            moved = from_next(value, right[rows(j, 8), at], a_next)
            cat[rows(j), 512 + L * k : 640 + L * k] = moved.astype(BF)

    for_blocks(one)
    rims_2(cat)


def up_two_kernel(
    index, z2, cross_in, core_in, mom1, mom2, prm, aux, t,
    rect, cross, core, mom, h2, act2, rectfar, cat, hf, lf, rf, lw, rw,
):
    mean, scale = norm_terms(mom2, mom1[3:4])
    gain, shift, bias = prm[2:3], prm[3:4], prm[6:7]

    def act(value):
        return silu((value - mean) * scale * gain + shift)

    for at in tiles(256):
        left, right = sides(index, cross_in, core_in, at)
        hf[0, :, at] = left
        hf[1, :, at] = right
        lf[:, at] = act(left)
        rf[:, at] = act(right)
    h2.put(hf)
    widen(lf, lw)
    widen(rf, rw)
    columns_2(cat, lambda j, at: act(z2[rows(j), at]), lw, rw, aux)
    act2.put(cat.at[:, 0:256])
    weights = ready(t)

    def chunk(rs):
        rect[rs, :] = matmul(cat[rs, :], weights[...], True)

    for_chunks(chunk)

    def sums(j, s1, s2):
        for k, at in enumerate(tiles(512)):
            value = softplus(rect[rows(j), at] + bias)
            rect[rows(j), at] = value
            part = value * aux[2 + k // 2]
            s1 = s1 + sum8(part)
            s2 = s2 + sum8(part * value)
        return s1, s2

    stats = sum_blocks(sums)
    rectfar.put(rect)
    pack_moments(mom, cross, fold(stack_rows(stats), 16))
    pack_ends(rect, index, cross, core)


def columns_1b(cat, read, left, right, aux):
    a, a_next = aux[0], aux[1]

    def one(j):
        for k, at in enumerate(tiles(512)):
            value = read(j, k, at)
            cat[rows(j), at] = value.astype(BF)
            if k >= 2:
                moved = from_prev(value, left[rows(j, 8), at], a)
                cat[rows(j), 256 + L * k : 384 + L * k] = moved.astype(BF)
            else:
                moved = from_next(value, right[rows(j, 8), at], a_next)
                cat[rows(j), 768 + L * k : 896 + L * k] = moved.astype(BF)

    for_blocks(one)
    rims_1(cat, GROUPS1[:4])


def edge_columns(own, prev, after):
    at = lane((NJ, L))
    place = sub((NJ, L))
    parts = [own, prev, after]
    groups = [own[:, 0:256], own[:, 256:512], prev, after]
    for g in groups:
        low = jnp.where((place == NJ - 1) | (at >= 32), 0.0, pltpu.roll(g[:, 0:L], NJ - 1, 0))
        high = jnp.where((place == 0) | (at < 112), 0.0, pltpu.roll(g[:, L : 2 * L], 1, 0))
        parts.append(low + high)
    return jnp.concatenate(parts, axis=1).astype(BF)


def quarter_blocks(index, stems):
    count = NJ // stems
    return [((index[0] ^ k) * count, count) for k in range(stems)]


def up_one_kernel(
    index, rect, cross_in, core_in, mom1, mom3, prm, aux, ends1, cat1, t,
    m0, m1, m2, m3, h3, low3, sig, sigh, cat, hf, lf, rf, ef, ff, sf, shf, lw, rw,
):
    mean, scale = norm_terms(mom3, mom1[2:3])
    gain, shift, bias = prm[4:5], prm[5:6], prm[7:8]

    def norm(value):
        return (value - mean) * scale * gain + shift

    for at in tiles(512):
        left, right = sides(index, cross_in, core_in, at)
        hf[0, :, at] = left
        hf[1, :, at] = right
        lf[:, at] = norm(left)
        rf[:, at] = norm(right)
    h3.put(hf)
    widen(lf, lw)
    widen(rf, rw)
    columns_1b(cat, lambda j, k, at: norm(rect[rows(j), at]), lw, rw, aux)
    low3.put(cat.at[:, 0:512])

    def group_out(rs, at, top, low):
        ef[0, rs, at] = norm(top)
        ef[1, rs, at] = norm(low)

    end_rows(rect, group_out)
    wide = jnp.concatenate([bias, bias], axis=1)
    zero = jnp.zeros((NJ, 256), F32)
    a, a_end = aux[0, 0:1, 0:1], aux[1, M - 1 : M, 0:1]
    e1 = [ends1[k].astype(F32) for k in range(4)]
    edges = [
        (
            edge_columns(lf[...], zero, ef[0, :, 0:256] * a),
            edge_columns(e1[0], zero, e1[2][:, 0:256] * a),
        ),
        (
            edge_columns(rf[...], ef[1, :, 256:512] * a_end, zero),
            edge_columns(e1[1], e1[3][:, 256:512] * a_end, zero),
        ),
    ]
    weights, other = ready(t), ready(cat1)
    for k, half in ((0, 1), (1, 0)):
        value = matmul(edges[k][0], weights[:, 0:COLS1B], True)
        value = value + matmul(edges[k][1], weights[:, COLS1B : 2 * COLS1B], True)
        shf[:, L * half : L * half + L] = sigmoid(value[:, L * half : L * half + L] + bias)
    sigh.put(shf)
    masks = (m0, m1, m2, m3)
    per = R // len(masks)
    for mask, (first, count) in zip(masks, quarter_blocks(index, len(masks))):
        rs = rows(lax.div(first, count), per)
        value = matmul(cat[rs, :], weights[:, 0:COLS1B], True)
        value = value + matmul(other[rs, :], weights[:, COLS1B : 2 * COLS1B], True)
        value = sigmoid(value + wide)
        sf[rs, :] = value
        mask[0:per, :] = value.astype(BF)
        ff[...] = jnp.zeros(ff.shape, F32)
        ff[0:count, :] = shf[rows(lax.div(first, count), count), :]
        mask[per : per + 16, :] = ff[...].astype(BF)
    sig.put(sf)


def ratio_terms(masks):
    squares = [m * m for m in masks]
    power = squares[0]
    for s in squares[1:]:
        power = power + s
    inverse = 1.0 / (power + RATIO_EPS)
    return [s * inverse for s in squares], inverse


def mask_back(masks, cots, mix):
    ratios, inverse = ratio_terms(masks)
    direct = cots[0] * ratios[0]
    for c, r in zip(cots[1:], ratios[1:]):
        direct = direct + c * r
    common = 2.0 * mix * inverse
    return [m * common * (c - direct) for m, c in zip(masks, cots)], direct


def mask_kernel(index, m0, m1, m2, m3, c0, x0, hx, g0, g1, g2, g3, direct, df, ff):
    masks, grads = (m0, m1, m2, m3), (g0, g1, g2, g3)
    stems = len(masks)
    per, blocks = R // stems, NJ // stems
    mine = index[0]
    cots, mix, rim = ready(c0), ready(x0), ready(hx)

    def one(j):
        for at in tiles(256):
            m = [masks[s][rows(j), at].astype(F32) for s in range(stems)]
            c = [cots[rows((mine ^ s) * blocks + j), at].astype(F32) for s in range(stems)]
            x = mix[rows(mine * blocks + j), at].astype(F32)
            values, own = mask_back(m, c, x)
            df[rows(j), at] = own
            for s in range(stems):
                grads[s][rows(j), at] = values[s].astype(BF)

    for_blocks(one, blocks)
    direct.put(df)
    m = [masks[s][per : per + 16, :].astype(F32)[0:blocks] for s in range(stems)]
    c = [rim[rows(stems + (mine ^ s), blocks), :] for s in range(stems)]
    values, _ = mask_back(m, c, rim[rows(mine, blocks), :])
    for s in range(stems):
        ff[...] = jnp.zeros(ff.shape, F32)
        ff[0:blocks, :] = values[s]
        grads[s][per : per + 16, :] = ff[...].astype(BF)


def estimate_kernel(index, m0, m1, m2, m3, x0, out, scr, est):
    masks = (m0, m1, m2, m3)
    stems = len(masks)
    blocks = NJ // stems
    mine = index[0]
    mix = ready(x0)

    def one(j):
        for at in tiles(256):
            m = [masks[s][rows(j), at].astype(F32) for s in range(stems)]
            x = mix[rows(mine * blocks + j), at].astype(F32)
            ratios, _ = ratio_terms(m)
            for s in range(stems):
                est[s, rows(j), at] = x * ratios[s]

    for_blocks(one, blocks)
    for s in range(stems):
        for t in range(blocks // 4):
            gather(
                lambda block, half, s=s, t=t: est[s, rows(4 * t + block), L * half : L * half + L], scr
            )
            for c in range(2):
                out[mine ^ s, c, :, L * t : L * t + L] = scr[c].astype(BF)


def down_one_back_kernel(
    index, q0, q1, q2, q3, sigh, sig, aux, mom1, mom3, rect, t,
    g3, cat, cross, core, mom, bias, gact, gf, hf, zf, hw,
):
    grads = (q0, q1, q2, q3)
    blocks = quarter_blocks(index, len(grads))
    per = R // len(grads)
    rim = ready(sigh)
    for grad, (first, count) in zip(grads, blocks):
        span = rows(lax.div(first, count), count)
        value = grad[per : per + 16, :].astype(F32)[0:count]
        own = rim[span, :]
        hf[span, :] = value * own * (1.0 - own)
    zf[...] = jnp.zeros(zf.shape, F32)
    widen(hf, hw)
    sigs = ready(sig)

    def read(which, j, half):
        at = slice(L * half, L * half + L)
        own = sigs[rows(j), at]
        value = grads[which][rows(j - blocks[which][0]), at].astype(F32) * own * (1.0 - own)
        zf[...] = zf[...] + sum8(value)
        return value

    columns_0(cat, blocks, read, hw, hw, aux)
    bias[...] = zf[...]
    weights = ready(t)

    def chunk(rs):
        value = matmul(cat[rs, :], weights[...])
        g3[rs, :] = value[:, 0:512]
        gf[rs, :] = value[:, 512:1024]

    for_chunks(chunk)
    gact.put(gf)
    mean, scale = norm_terms(mom3, mom1[2:3])
    pack_ends(g3, index, cross, core)
    r = ready(rect)

    def sums(j, s1, s2):
        for at in tiles(512):
            value = g3[rows(j), at]
            s1 = s1 + sum8(value)
            s2 = s2 + sum8(value * (r[rows(j), at] - mean))
        return s1, s2

    s1, s2 = sum_blocks(sums)
    pack_moments(mom, cross, fold(stack_rows([s1, s2 * scale]), 16))


def norm_back(g, xhat, kept, moments, count, factor):
    return factor * (g - kept * ((moments[0:1] + xhat * moments[1:2]) / count))


def up_two_back_kernel(
    index, g3, cross_in, core_in, mom4, mom1, mom3, mom2, prm, aux, kept, rect, h3, t, z2,
    g2, cat, cross, core, mom, lf, rf, lw, rw,
):
    count = mom1[2:3]
    mean, scale = norm_terms(mom3, count)
    factor = scale * prm[4:5]
    inverse = 1.0 / count

    def back(g, r, keep):
        xhat = (r - mean) * scale
        value = factor * (g - keep * ((mom4[0:1] + xhat * mom4[1:2]) * inverse))
        return value * softplus_slope(r)

    r, h = ready(rect), ready(h3)
    for k, at in enumerate(tiles(512)):
        left, right = sides(index, cross_in, core_in, at)
        row = k // 2
        lf[:, at] = back(left, h[0, :, at], kept[row : row + 1, :])
        rf[:, at] = back(right, h[1, :, at], kept[3 + row : 4 + row, :])
    widen(lf, lw)
    widen(rf, rw)
    a, a_next = aux[0], aux[1]

    def one(j, total):
        for k, at in enumerate(tiles(512)):
            value = back(g3[rows(j), at], r[rows(j), at], aux[2 + k // 2])
            total = total + sum8(value)
            cat[rows(j), at] = value.astype(BF)
            if k >= 2:
                moved = from_prev(value, lw[rows(j, 8), at], a)
                cat[rows(j), 256 + L * k : 384 + L * k] = moved.astype(BF)
            start = 768 + L * k if k < 2 else 1280 + L * k
            moved = from_next(value, rw[rows(j, 8), at], a_next)
            cat[rows(j), start : start + L] = moved.astype(BF)
        return total

    bias = lax.fori_loop(0, NJ, one, jnp.zeros((8, L), F32))
    rims_1(cat, GROUPS1)
    weights = ready(t)

    def chunk(rs):
        g2[rs, :] = matmul(cat[rs, :], weights[...])

    for_chunks(chunk)
    mean2, scale2 = norm_terms(mom2, mom1[3:4])
    gain, shift = prm[2:3], prm[3:4]
    z = ready(z2)

    def sums(j, s1, s2):
        for at in tiles(256):
            xhat = (z[rows(j), at] - mean2) * scale2
            value = g2[rows(j), at] * silu_slope(xhat * gain + shift)
            g2[rows(j), at] = value
            s1 = s1 + sum8(value)
            s2 = s2 + sum8(value * xhat)
        return s1, s2

    stats = fold(stack_rows(sum_blocks(sums)), 32)
    pack_ends(g2, index, cross, core)
    bias = fold(stack_rows([total_rows(bias)] * 3), 16)
    pack_moments(mom, cross, jnp.where(sub((8, L)) == 2, bias, stats))


def down_two_back_kernel(
    index, g2, cross_in, core_in, mom5, mom1, mom2, prm, aux, kept, z2, h2, t, gact, z1,
    g1, low2, cross, core, mom, cat, lf, rf, lw, rw,
):
    count = mom1[3:4]
    mean, scale = norm_terms(mom2, count)
    factor = scale * prm[2:3]
    inverse = 1.0 / count

    def back(g, z, keep):
        xhat = (z - mean) * scale
        return factor * (g - keep * ((mom5[0:1] + xhat * mom5[1:2]) * inverse))

    z, h = ready(z2), ready(h2)
    for at in tiles(256):
        left, right = sides(index, cross_in, core_in, at)
        lf[:, at] = back(left, h[0, :, at], kept[2:3, :])
        rf[:, at] = back(right, h[1, :, at], kept[5:6, :])
    widen(lf, lw)
    widen(rf, rw)
    columns_2(cat, lambda j, at: back(g2[rows(j), at], z[rows(j), at], aux[4]), lw, rw, aux)
    low2[...] = cat[:, 0:256]
    weights, added = ready(t), ready(gact)

    def chunk(rs):
        g1[rs, :] = matmul(cat[rs, :], weights[...], True) + added[rs, :]

    for_chunks(chunk)
    mean1, scale1 = norm_terms(mom1, mom1[2:3])
    gain, shift = prm[0:1], prm[1:2]
    z = ready(z1)

    def sums(j, s1, s2):
        for at in tiles(512):
            xhat = (z[rows(j), at] - mean1) * scale1
            value = g1[rows(j), at] * silu_slope(xhat * gain + shift)
            g1[rows(j), at] = value
            s1 = s1 + sum8(value)
            s2 = s2 + sum8(value * xhat)
        return s1, s2

    stats = fold(stack_rows(sum_blocks(sums)), 16)
    pack_ends(g1, index, cross, core)
    pack_moments(mom, cross, stats)


def up_one_back_kernel(
    index, g1, cross_in, core_in, mom6, mom1, prm, aux, kept, z1, h1, t,
    n0, n1, n2, n3, low1, cat, lf, rf, lw, rw,
):
    count = mom1[2:3]
    mean, scale = norm_terms(mom1, count)
    factor = scale * prm[0:1]
    inverse = 1.0 / count

    def back(g, z, keep):
        xhat = (z - mean) * scale
        return factor * (g - keep * ((mom6[0:1] + xhat * mom6[1:2]) * inverse))

    z, h = ready(z1), ready(h1)
    for k, at in enumerate(tiles(512)):
        left, right = sides(index, cross_in, core_in, at)
        row = k // 2
        lf[:, at] = back(left, h[0, :, at], kept[row : row + 1, :])
        rf[:, at] = back(right, h[1, :, at], kept[3 + row : 4 + row, :])
    widen(lf, lw)
    widen(rf, rw)
    columns_1b(
        cat, lambda j, k, at: back(g1[rows(j), at], z[rows(j), at], aux[2 + k // 2]), lw, rw, aux
    )
    low1[...] = cat[:, 0:512]
    weights = ready(t)
    nets = (n0, n1, n2, n3)
    per = R // len(nets)
    for net, (first, blocks) in zip(nets, quarter_blocks(index, len(nets))):
        rs = rows(lax.div(first, blocks), per)
        net[...] = matmul(cat[rs, :], weights[...], True).astype(BF)


def mixture_kernel(p0, p1, p2, p3, direct, out, scr):
    parts = (p0, p1, p2, p3)
    own = ready(direct)

    def tile(t):
        def block(k, half):
            at = slice(L * half, L * half + L)
            value = own[rows(4 * t + k), at]
            for part in parts:
                value = value + part[rows(4 * t + k), at].astype(F32)
            return value

        gather(block, scr)
        for c in range(2):
            out[c, :, pl.ds(pl.multiple_of(t * L, L), L)] = scr[c]

    for_blocks(tile, NJ // len(parts) // 4)


def pairs(count, offset):
    there = [(i, (i + offset) % count) for i in range(0, count, 2)]
    return there + [(b, a) for a, b in there]


def flip(values, axis, bit):
    return lax.ppermute(values, axis, [(i, i ^ bit) for i in range(lax.axis_size(axis))])


def sum_over(values, axis):
    count = lax.axis_size(axis)
    if count & (count - 1):
        return lax.psum(values, axis)
    step = 1
    while step < count:
        radix = 2 if step == 1 or count // step == 2 else 4
        moved = [flip(values, axis, step * k) for k in range(1, radix)]
        for m in moved:
            values = values + m
        step *= radix
    return values


def sum_halves(values, axis, odd):
    count = lax.axis_size(axis)
    half = values.shape[0] // 2
    top, low = values[:half], values[half:]
    mine = jnp.where(odd, low, top) + flip(jnp.where(odd, top, low), axis, 1)
    if count == 8:
        moved = [flip(mine, axis, bit) for bit in (2, 4, 6)]
        mine = mine + moved[0] + moved[1] + moved[2]
    else:
        step = 2
        while step < count:
            mine = mine + flip(mine, axis, step)
            step *= 2
    other = flip(mine, axis, 1)
    return jnp.where(odd, jnp.concatenate([other, mine]), jnp.concatenate([mine, other]))


def exchange(cross, core, mom, axis):
    count = lax.axis_size(axis)
    near = lax.ppermute(cross, axis, pairs(count, -1))
    if count == 8:
        far = lax.ppermute(mom, axis, pairs(count, 3))
        across = flip(mom, axis, 4)
        inside = flip(core, axis, 1)
        part = mom + near[NJ:, 0:L] + far + across
        return near, inside, part + flip(part, axis, 1)
    return near, flip(core, axis, 1), sum_over(mom, axis)


def swap(blocks, axis):
    return [blocks[0]] + [flip(blocks[k], axis, k) for k in range(1, len(blocks))]


def flags(seg_lengths, frame_mask, position, total):
    order = jnp.arange(seg_lengths.shape[0])
    earlier = order[None, :] < order[:, None]
    starts = 4 * jnp.sum(jnp.where(earlier, seg_lengths[None, :], 0), axis=1)
    frames = (position * M + jnp.arange(M + 1, dtype=jnp.int32)) * 4
    shut = jnp.any(frames[:, None] == starts[None, :], axis=1) | (frames == total)
    a = 1.0 - shut.astype(F32)
    keep_one = jnp.min(frame_mask.reshape(M, 2, 2), axis=2).astype(F32)
    keep_two = jnp.min(frame_mask.reshape(M, 4), axis=1).astype(F32)
    columns = jnp.stack([a[:M], a[1:], keep_one[:, 0], keep_one[:, 1], keep_two])
    return jnp.broadcast_to(columns[:, :, None], (5, M, L))


def per_device(
    mixture,
    seg_lengths,
    frame_mask,
    conv_first,
    encoder_gain_vector,
    shift_first,
    conv_second,
    gain_second,
    shift_second,
    deconv_second,
    bias_second,
    decoder_gain_vector,
    shift_third,
    deconv_first,
    bias_first,
    cotangent,
):
    position = lax.axis_index("tm")
    stems = lax.axis_size("stem")
    odd = position % 2
    index = jnp.stack([lax.axis_index("stem"), odd]).astype(jnp.int32)
    frames = mixture.shape[1]
    per, blocks = R // stems, NJ // stems
    aux = flags(seg_lengths, frame_mask, position, frames * lax.axis_size("tm"))
    prm = jnp.stack(
        [
            jnp.tile(encoder_gain_vector[0], 8),
            jnp.tile(shift_first[0], 8),
            jnp.tile(gain_second[0], 4),
            jnp.tile(shift_second[0], 4),
            jnp.tile(decoder_gain_vector[0], 8),
            jnp.tile(shift_third[0], 8),
            jnp.tile(bias_second[0], 8),
            jnp.tile(jnp.repeat(bias_first[0], 32), 2),
        ]
    )
    w1c = jnp.tile(conv_first[0].transpose(2, 1, 3, 0).reshape(50, 16).astype(F32), (1, 8))
    w1d = deconv_first[0].transpose(2, 0, 3, 1).reshape(50, 2, 16).astype(F32)
    w1d = jnp.tile(w1d.transpose(1, 0, 2), (1, 1, 8))
    w2c = jnp.tile(conv_second[0].transpose(2, 3, 1, 0).reshape(400, 32).astype(F32), (1, 4))
    w2d = jnp.tile(deconv_second[0].transpose(2, 3, 0, 1).reshape(400, 32).astype(F32), (1, 4))

    edge = 2 * NJ + 16
    cross, core, x0, c0 = run(
        layout_kernel,
        "layout",
        [((edge, 256), BF), ((edge, 256), BF), ((R, 256), BF, True), ((R, 256), BF, True)],
        [index, frame_mask, Far(mixture), Far(cotangent)],
        [((2, frames, L), F32), ((2 * R, 256), F32), ((R, 256), BF), ((R, 256), BF)]
        + [((2, edge, 256), F32)],
    )
    near = lax.ppermute(cross, "tm", pairs(lax.axis_size("tm"), -1))
    inside = flip(core, "tm", 1)
    (t1a_c,) = run(matrices_first, "matrices_first", [((COLS0, 512), BF)], [w1c])
    t2a_c, t2b_d, t1b_d = run(
        matrices_forward,
        "matrices_forward",
        [((COLS1, 256), BF, True), ((512, COLS2), BF, True), ((256, 2 * COLS1B), BF, True)],
        [w2c, w2d, w1d],
        [((COLS1, 256), BF), ((512, COLS2), BF), ((256, 2 * COLS1B), BF)],
    )
    t1a_d, t2a_d, t2b_c, t1b_c = run(
        matrices_back,
        "matrices_back",
        [((COLS0, 1024), BF, True), ((COLS1, 256), BF, True), ((512, COLS2), BF, True)]
        + [((256, COLS1B), BF, True)],
        [Far(w1c), Far(w2c), Far(w2d), Far(w1d)],
        [((COLS0, 1024), BF), ((COLS1, 256), BF), ((512, COLS2), BF), ((256, COLS1B), BF)],
    )

    def packet(lanes):
        return [((NJ + 8, lanes), F32), ((NJ, lanes), F32), ((8, L), F32)]

    def rim(lanes):
        return [((NJ, lanes), F32)] * 2

    def wide(lanes):
        return [((8 * NJ, lanes), F32)] * 2

    z1, cross, core, mom, hx, kept, z1_far, cat0 = run(
        conv_one_kernel,
        "conv_one",
        [((R, 512), F32)] + packet(512)
        + [((2 * NJ, 256), F32), ((8, L), F32), ((R, 512), F32, True), ((R, COLS0), BF, True)],
        [index, Far(x0), near, inside, aux, t1a_c],
        [((R, COLS0), BF), ((edge, 256), F32), ((edge, 256), F32)] + wide(256),
        flops=2 * R * COLS0 * 512,
    )
    near, inside, mom1 = exchange(cross, core, mom, "tm")
    z2, cross, core, mom, ends1, h1, z2_far, cat1 = run(
        conv_two_kernel,
        "conv_two",
        [((R, 256), F32)] + packet(256)
        + [((4, NJ, 512), BF), ((2, NJ, 512), F32, True), ((R, 256), F32, True), ((R, COLS1), BF, True)],
        [index, z1, near, inside, mom1, prm, aux, Far(t2a_c)],
        [((R, COLS1), BF), ((4, NJ, 512), F32), ((2, NJ, 512), F32)] + wide(512),
        flops=2 * R * COLS1 * 256,
    )
    near, inside, mom2 = exchange(cross, core, mom, "tm")
    rect, cross, core, mom, h2, act2, rect_far = run(
        up_two_kernel,
        "up_two",
        [((R, 512), F32)] + packet(512)
        + [((2, NJ, 256), F32, True), ((R, 256), BF, True), ((R, 512), F32, True)],
        [index, z2, near, inside, mom1, mom2, prm, aux, Far(t2b_d)],
        [((R, COLS2), BF), ((2, NJ, 256), F32)] + rim(256) + wide(256),
        flops=2 * R * COLS2 * 512,
    )
    near, inside, mom3 = exchange(cross, core, mom, "tm")
    *masks, h3, low3, sig, sigh = run(
        up_one_kernel,
        "up_one",
        [((per + 16, 256), BF)] * stems
        + [((2, NJ, 512), F32, True), ((R, 512), BF, True), ((R, 256), F32, True), ((NJ, 256), F32, True)],
        [index, rect, near, inside, mom1, mom3, prm, aux, ends1, Far(cat1, COLS1B), Far(t1b_d)],
        [((R, COLS1B), BF), ((2, NJ, 512), F32)] + rim(512)
        + [((2, NJ, 512), F32), ((16, 256), F32), ((R, 256), F32), ((NJ, 256), F32)] + wide(512),
        flops=2 * R * 2 * COLS1B * 256,
    )
    masks = swap(masks, "stem")
    *grads, direct = run(
        mask_kernel,
        "mask",
        [((per + 16, 256), BF)] * stems + [((per, 256), F32, True)],
        [index, *masks, Far(c0), Far(x0), Far(hx)],
        [((per, 256), F32), ((16, 256), F32)],
    )
    grads = swap(grads, "stem")
    (estimates,) = run(
        estimate_kernel,
        "estimate",
        [((stems, 2, frames, blocks * 32), BF)],
        [index, *masks, Far(x0)],
        [((2, frames, L), F32), ((stems, per, 256), F32)],
    )
    g3, cat0g, cross, core, mom, bias_one, gact = run(
        down_one_back_kernel,
        "down_one_back",
        [((R, 512), F32), ((R, COLS0), BF)] + packet(512) + [((8, L), F32), ((R, 512), F32, True)],
        [index, *grads, Far(sigh), Far(sig), aux, mom1, mom3, Far(rect_far), Far(t1a_d)],
        [((R, 512), F32), ((NJ, 256), F32), ((8, L), F32), ((8 * NJ, 256), F32)],
        flops=2 * R * COLS0 * 1024,
    )
    near, inside, mom4 = exchange(cross, core, mom, "tm")
    (w1d_grad,) = run(
        weight_1_joined,
        "weight_up_one",
        [((32, L), F32)],
        [Far(low3), Far(cat1, 512), cat0g],
        [((512, COLS0), F32)],
        flops=2 * R * COLS0 * 1024,
    )
    g2, cat1g, cross, core, mom = run(
        up_two_back_kernel,
        "up_two_back",
        [((R, 256), F32), ((R, COLS1), BF)] + packet(256),
        [index, g3, near, inside, mom4, mom1, mom3, mom2, prm, aux, kept]
        + [Far(rect_far), Far(h3), Far(t2a_d), Far(z2_far)],
        rim(512) + wide(512),
        flops=2 * R * COLS1 * 256,
    )
    near, inside, mom5 = exchange(cross, core, mom, "tm")
    (w2d_grad,) = run(
        weight_2_kernel,
        "weight_up_two",
        [((128, L), F32)],
        [Far(act2), cat1g],
        [((256, COLS1), F32)],
        flops=2 * R * COLS1 * 256,
    )
    g1, low2, cross, core, mom = run(
        down_two_back_kernel,
        "down_two_back",
        [((R, 512), F32), ((R, 256), BF)] + packet(512),
        [index, g2, near, inside, mom5, mom1, mom2, prm, aux, kept]
        + [Far(z2_far), Far(h2), Far(t2b_c), Far(gact), Far(z1_far)],
        [((R, COLS2), BF)] + rim(256) + wide(256),
        flops=2 * R * COLS2 * 512,
    )
    near, inside, mom6 = exchange(cross, core, mom, "tm")
    (w2c_grad,) = run(
        weight_2_kernel,
        "weight_down_two",
        [((128, L), F32)],
        [low2, Far(cat1)],
        [((256, COLS1), F32)],
        flops=2 * R * COLS1 * 256,
    )
    *nets, low1 = run(
        up_one_back_kernel,
        "up_one_back",
        [((per, 256), BF)] * stems + [((R, 512), BF)],
        [index, g1, near, inside, mom6, mom1, prm, aux, kept, Far(z1_far), Far(h1), Far(t1b_c)],
        [((R, COLS1B), BF)] + rim(512) + wide(512),
        flops=2 * R * COLS1B * 256,
    )
    nets = swap(nets, "stem")
    (w1c_grad,) = run(
        weight_1_first,
        "weight_down_one",
        [((16, L), F32)],
        [low1, Far(cat0)],
        [((512, COLS0), F32)],
        flops=2 * R * COLS0 * 512,
    )
    (mixture_grad,) = run(
        mixture_kernel,
        "mixture",
        [((2, frames, blocks * 32), F32)],
        [*nets, Far(direct)],
        [((2, frames, L), F32)],
    )
    spare = jnp.zeros((8, L), F32)
    early = sum_halves(jnp.concatenate([w1d_grad, bias_one, spare, w2d_grad]), "tm", odd)
    w2c_grad = sum_halves(w2c_grad, "tm", odd)
    w1c_grad = sum_over(w1c_grad, "tm")

    def outer(packed):
        taps = packed.reshape(16, 2, 2, 4, 8)[:, :, :, :3, :TAPS].transpose(0, 2, 3, 1, 4)
        return taps.reshape(16, 2, 6, TAPS)[:, :, 1:]

    def inner(packed):
        last = jnp.concatenate([packed[0:32, 80:], packed[32:64, 80:112]], axis=1)
        taps = jnp.concatenate([packed[:, :80].reshape(4, 32, 80), last[None]])
        return taps.reshape(TAPS, 32, TAPS, 16).transpose(1, 3, 0, 2)

    w1d_grad = jnp.concatenate([outer(early[0:16]), outer(early[16:32])]).transpose(1, 0, 2, 3)
    return (
        estimates,
        mixture_grad,
        outer(w1c_grad)[None],
        mom6[1, :16][None],
        mom6[0, :16][None],
        inner(w2c_grad)[None],
        mom5[1, :32][None],
        mom5[0, :32][None],
        inner(early[48:176]).transpose(1, 0, 2, 3)[None],
        mom5[2, :16][None],
        mom4[1, :16][None],
        mom4[0, :16][None],
        w1d_grad[None],
        early[32:40].reshape(8, 2, 2, 32).sum((0, 1, 3))[None],
    )


def solution(mesh):
    in_specs = (
        P(None, "tm", None),
        P(),
        P("tm"),
        P("stem", None, None, None, None),
        P("stem", None),
        P("stem", None),
        P("stem", None, None, None, None),
        P("stem", None),
        P("stem", None),
        P("stem", None, None, None, None),
        P("stem", None),
        P("stem", None),
        P("stem", None),
        P("stem", None, None, None, None),
        P("stem", None),
        P(None, None, "tm", "stem"),
    )
    out_specs = (
        P(None, None, "tm", "stem"),
        P(None, "tm", "stem"),
        P("stem", None, None, None, None),
        P("stem", None),
        P("stem", None),
        P("stem", None, None, None, None),
        P("stem", None),
        P("stem", None),
        P("stem", None, None, None, None),
        P("stem", None),
        P("stem", None),
        P("stem", None),
        P("stem", None, None, None, None),
        P("stem", None),
    )
    return jax.shard_map(
        per_device, mesh=mesh, in_specs=in_specs, out_specs=out_specs, check_vma=False
    )
```

```python
import jax
import jax.numpy as jnp
from jax import lax
from jax.experimental import pallas as pl
from jax.experimental.pallas import tpu as pltpu
from jax.sharding import PartitionSpec as P

NORM_EPS = 0.001
RATIO_EPS = 1e-10
BF = jnp.bfloat16
F32 = jnp.float32
TAPS = 5
L = 128
M = 32
NJ = 32
R = M * NJ
CHUNK = 256
UNROLL = 4
COLS0 = 1024
COLS1 = 1920
COLS1B = 1536
COLS2 = 1152
GROUPS1 = ((0, 1024, 1), (256, 1152, 2), (512, 1280, 0), (768, 1408, 3), (1536, 1792, 4))
FULL = pl.BlockSpec(memory_space=pltpu.VMEM)
SCALAR = pl.BlockSpec(memory_space=pltpu.SMEM)
FAR = pl.BlockSpec(memory_space=pltpu.HBM)


class Far:
    def __init__(self, array, columns=None):
        self.array, self.columns = array, columns


class Arriving:
    def __init__(self, source, target, sem):
        self.copy, self.target, self.waited = pltpu.make_async_copy(source, target, sem), target, False
        self.copy.start()

    def get(self):
        if not self.waited:
            self.copy.wait()
            self.waited = True
        return self.target


class Leaving:
    def __init__(self, target, sems):
        self.target, self.sems, self.copies = target, sems, []

    def put(self, source, part=None):
        target = self.target if part is None else self.target.at[part]
        source = source if part is None else source.at[part]
        copy = pltpu.make_async_copy(source, target, self.sems.at[len(self.copies)])
        copy.start()
        self.copies.append(copy)

    def wait(self):
        for copy in self.copies:
            copy.wait()


PARTS = 6


def run(kernel, name, outs, args, scratch=(), flops=0, fetch=(), token=None):
    n_args = len(args)
    args = list(args) + list(fetch) + ([] if token is None else [token])
    n_made = len(outs)
    outs = list(outs)
    for f in fetch:
        outs.append(((f.array.shape[0], f.columns or f.array.shape[1]) + f.array.shape[2:], f.array.dtype))
    arrays = [a.array if isinstance(a, Far) else a for a in args]
    if token is not None:
        outs.append((token.shape, token.dtype))
    far_in = [k for k, a in enumerate(args[:n_args]) if isinstance(a, Far)]
    far_out = [k for k, o in enumerate(outs) if len(o) == 3]
    n_in, n_out, n_own = len(args), len(outs), len(scratch)
    placed = [
        pltpu.with_memory_space_constraint(a.array, pltpu.HBM) if isinstance(a, Far) else a for a in args
    ]
    landing = []
    for k in far_in:
        shape = args[k].array.shape
        if args[k].columns is not None:
            shape = (shape[0], args[k].columns)
        landing.append(pltpu.VMEM(shape, args[k].array.dtype))

    def body(*refs):
        ins, results = list(refs[:n_in]), list(refs[n_in : n_in + n_out])
        own = refs[n_in + n_out : n_in + n_out + n_own]
        targets = refs[n_in + n_out + n_own : n_in + n_out + n_own + len(far_in)]
        in_sems, out_sems = refs[-2:]

        def cut(k):
            return ins[k] if args[k].columns is None else ins[k].at[:, 0 : args[k].columns]

        for i, k in enumerate(far_in):
            ins[k] = Arriving(cut(k), targets[i], in_sems.at[i])
        fetched = [
            Arriving(cut(n_args + i), results[n_made + i], in_sems.at[len(far_in) + i]) for i in range(len(fetch))
        ]
        for i, k in enumerate(far_out):
            results[k] = Leaving(results[k], out_sems.at[i])
        if token is not None:
            results[-1][...] = ins[-1][...]
        kernel(*ins[:n_args], *results[:n_made], *own)
        for k in far_in:
            ins[k].get()
        for f in fetched:
            f.get()
        for k in far_out:
            results[k].wait()

    in_specs = []
    for a in args:
        if isinstance(a, Far):
            in_specs.append(FAR)
        else:
            in_specs.append(SCALAR if a.dtype == jnp.int32 else FULL)
    bytes_all = sum(a.size * a.dtype.itemsize for a in arrays)
    bytes_all += sum(jnp.zeros((), o[1]).dtype.itemsize * o[0][0] * o[0][-1] for o in outs)
    return pl.pallas_call(
        body,
        out_shape=[
            pltpu.HBM(o[0], o[1]) if len(o) == 3 else jax.ShapeDtypeStruct(o[0], o[1]) for o in outs
        ],
        in_specs=in_specs,
        out_specs=[FAR if len(o) == 3 else FULL for o in outs],
        scratch_shapes=[pltpu.VMEM(s, d) for s, d in scratch]
        + landing
        + [
            pltpu.SemaphoreType.DMA((max(1, len(far_in) + len(fetch)),)),
            pltpu.SemaphoreType.DMA((max(1, len(far_out)), PARTS)),
        ],
        compiler_params=pltpu.CompilerParams(vmem_limit_bytes=24 << 20),
        cost_estimate=pl.CostEstimate(flops=flops, bytes_accessed=bytes_all, transcendentals=0),
        name=name,
    )(*placed)


def lane(shape):
    return lax.broadcasted_iota(jnp.int32, shape, 1)


def sub(shape):
    return lax.broadcasted_iota(jnp.int32, shape, 0)


def rows(j, count=M):
    return pl.ds(pl.multiple_of(j * count, count), count)


def tiles(width):
    return [slice(L * k, L * k + L) for k in range(width // L)]


def for_blocks(fn, count=NJ):
    step = UNROLL if isinstance(count, int) and count % UNROLL == 0 else 1

    def body(j, carry):
        for i in range(step):
            fn(j * step + i)
        return carry

    lax.fori_loop(0, count // step, body, 0)


def for_blocks_rims(fn):
    def body(j, carry):
        fn(j, True, True)
        return carry

    fn(0, False, True)
    lax.fori_loop(1, NJ - 1, body, 0)
    fn(NJ - 1, True, False)


def from_prev(value, rim, flag):
    rim = jnp.concatenate([rim] * (M // 8), axis=0)
    return jnp.where(sub(value.shape) == 0, rim, pltpu.roll(value, 1, 0)) * flag


def from_next(value, rim, flag):
    rim = jnp.concatenate([rim] * (M // 8), axis=0)
    return jnp.where(sub(value.shape) == M - 1, rim, pltpu.roll(value, M - 1, 0)) * flag


def widen(source, out):
    def group(g):
        for at in tiles(source.shape[1]):
            tile = source[rows(g, 8), at]
            for i in range(8):
                out[rows(8 * g + i, 8), at] = jnp.broadcast_to(tile[i : i + 1], (8, L))

    for_blocks(group, NJ // 8)


def mask_bf(cond):
    return jnp.where(cond, 1.0, 0.0).astype(BF)


def fill_rims(cat, parts, low, high):
    def one(j, has_prev, has_next):
        for target, after, before in parts:
            value = None
            if has_next:
                value = cat[rows(j + 1), after : after + L] * low
            if has_prev:
                other = cat[rows(j - 1), before : before + L] * high
                value = other if value is None else value + other
            cat[rows(j), target : target + L] = value

    for_blocks_rims(one)


def rims_1(cat, groups):
    at = lane((M, L))
    parts = [(rim, base, base + L) for base, rim, _ in groups]
    fill_rims(cat, parts, mask_bf(at < 32), mask_bf(at >= 112))


def rims_2(cat):
    at = lane((M, L))
    parts = [(768 + L * k, 256 * k, 256 * k + L) for k in range(3)]
    fill_rims(cat, parts, mask_bf(at < 32), mask_bf(at >= 96))


def rims_0(cat):
    at = lane((M, L)) % 32
    fill_rims(cat, [(512 + L * k, L * k, L * k) for k in range(4)], mask_bf(at < 2), mask_bf(at == 31))


def matmul(left, right, transposed=False):
    return lax.dot_general(
        left, right, (((1,), (1 if transposed else 0,)), ((), ())), preferred_element_type=F32
    )


def quarters(fn):
    for k in range(4):
        fn(slice(R // 4 * k, R // 4 * (k + 1)))


def for_chunks(fn, size=CHUNK):
    def body(r, carry):
        fn(pl.ds(pl.multiple_of(r * size, size), size))
        return carry

    lax.fori_loop(0, R // size, body, 0)


def sum8(value):
    total = value[0:8]
    for k in range(1, value.shape[0] // 8):
        total = total + value[8 * k : 8 * k + 8]
    return total


def sum_blocks(fn):
    def body(j, carry):
        for i in range(UNROLL):
            carry = fn(j * UNROLL + i, *carry)
        return carry

    zero = jnp.zeros((8, L), F32)
    return [total_rows(s) for s in lax.fori_loop(0, NJ // UNROLL, body, (zero, zero))]


def fold(stats, period):
    step = L // 2
    while step >= period:
        stats = stats + pltpu.roll(stats, step, 1)
        step //= 2
    return stats


def stack_rows(values):
    at = sub((8, L))
    tile = jnp.zeros((8, L), F32)
    for k, value in enumerate(values):
        tile = jnp.where(at == k, value, tile)
    return tile


def total_rows(value):
    return jnp.sum(value, axis=0, keepdims=True)


def norm_terms(moments, count):
    mean = moments[0:1] / count
    return mean, lax.rsqrt(moments[1:2] / count - mean * mean + NORM_EPS)


def silu(v):
    return v / (1.0 + jnp.exp(-v))


def silu_slope(v):
    s = 1.0 / (1.0 + jnp.exp(-v))
    return s * (1.0 + v * (1.0 - s))


def sigmoid(v):
    return 1.0 / (1.0 + jnp.exp(-v))


def softplus(v):
    return jnp.maximum(v, 0.0) + jnp.log1p(jnp.exp(-jnp.abs(v)))


def softplus_slope(r):
    return jnp.where(r < 0.05, r * (1.0 - r * (0.5 - r * (1.0 / 6.0))), 1.0 - jnp.exp(-r))


def end_rows(z, group_out, blocks=NJ):
    def group(g):
        for at in tiles(z.shape[1]):
            place = sub((8, L))
            top = low = jnp.zeros((8, L), F32)
            for i in range(8):
                start = pl.multiple_of((8 * g + i) * M, M)
                top = jnp.where(place == i, z[pl.ds(start, 8), at][0:1], top)
                low = jnp.where(place == i, z[pl.ds(start + M - 8, 8), at][7:8], low)
            group_out(rows(g, 8), at, top, low)

    for_blocks(group, blocks // 8)


def pack_ends(z, index, cross, core, blocks=NJ):
    even = index[1] == 0

    def group_out(rs, at, top, low):
        cross[rs, at] = jnp.where(even, top, low)
        core[rs, at] = jnp.where(even, low, top)

    end_rows(z, group_out, blocks)


def pack_moments(mom, cross, value):
    mom[...] = value
    cross[NJ : NJ + 8, 0:L] = value


def sides(index, cross, core, at):
    even = index[1] == 0
    a, b = cross[0:NJ, at], core[0:NJ, at]
    return jnp.where(even, a, b), jnp.where(even, b, a)


def tile_2(w, tap, q, half):
    at = lane((16, L)) // 32
    tile = jnp.zeros((16, L), F32)
    for k in range(4):
        b = q - 2 * (4 * half + k) + 1
        if 0 <= b < TAPS:
            start = (tap * TAPS + b) * 16
            tile = jnp.where(at == k, w[start : start + 16, :], tile)
    return tile.astype(BF)


def repeat_lanes(w, out):
    for k in range(w.shape[0] // 16):
        span = slice(16 * k, 16 * k + 16)
        out[span, :] = jnp.concatenate([w[span, :].astype(F32)] * (L // 32), axis=1)


def matrix_2_down(narrow, t, w):
    repeat_lanes(narrow, w)
    zero = jnp.zeros((16, L), BF)
    for base, rim, tap in GROUPS1:
        for half in range(2):
            at = slice(L * half, L * half + L)
            for q in range(16):
                t[base + 16 * q : base + 16 * q + 16, at] = tile_2(w, tap, q, half)
            for part in range(8):
                q = {0: 16, 1: 17, 7: -1}.get(part)
                start = rim + 16 * part
                t[start : start + 16, at] = zero if q is None else tile_2(w, tap, q, half)


def matrix_2_up(narrow, t, w):
    repeat_lanes(narrow, w)
    zero = jnp.zeros((16, L), BF)
    at = lane((16, L))
    for row in range(2):
        for k, tap in enumerate((row + 1, row + 3, row - 1)):
            for q in range(16):
                span = slice(row * 256 + q * 16, row * 256 + q * 16 + 16)
                for half in range(2):
                    cols = slice(256 * k + L * half, 256 * k + L * half + L)
                    t[span, cols] = tile_2(w, tap, q, half) if 0 <= tap < TAPS else zero
                rim = zero
                if 0 <= tap < TAPS and q in (0, 1, 15):
                    b = {0: 3, 1: 4, 15: 0}[q]
                    start = (tap * TAPS + b) * 16
                    cond = at < 32 if q == 15 else at >= 96
                    rim = jnp.where(cond, w[start : start + 16, :], 0.0).astype(BF)
                t[span, 768 + L * k : 768 + L * k + L] = rim


def band(w, tap, channel, offset):
    tile = jnp.zeros((32, L), F32)
    for b in range(TAPS):
        start = (tap * TAPS + b) * 2 + channel
        tile = jnp.where(offset == b, w[start : start + 1, :], tile)
    return tile.astype(BF)


def matrix_1_down(w, t, col):
    q, zero = sub((32, L)), jnp.zeros((32, L), BF)
    for half in range(2):
        p = 8 * half + lane((32, L)) // 16
        inner = q - 2 * p + 1
        rim = jnp.where(q == 31, -2 * p, jnp.where(q == 0, 33 - 2 * p, jnp.where(q == 1, 34 - 2 * p, -9)))
        for row in range(2):
            cols = slice(col + row * 256 + half * L, col + row * 256 + half * L + L)
            for part, frame in enumerate((0, 1, 2, 3, None, -1, 4, 5)):
                tap = -1 if frame is None else frame - 2 * row + 1
                for c in range(2):
                    start = part * 64 + c * 32
                    ok = 0 <= tap < TAPS
                    t[start : start + 32, cols] = band(w, tap, c, inner) if ok else zero
                    t[512 + start : 544 + start, cols] = band(w, tap, c, rim) if ok else zero


def matrix_1_up(w, t, col):
    q, zero = sub((32, L)), jnp.zeros((32, L), BF)
    at = lane((32, L))
    rim = jnp.where(at < 16, q - 31, jnp.where(at >= 112, q + 3, -9))
    for frame in range(4):
        taps = (frame + 1, frame - 1, frame + 3, frame - 3)
        for c in range(2):
            span = slice(frame * 64 + c * 32, frame * 64 + c * 32 + 32)
            for k, tap in enumerate(taps):
                ok = 0 <= tap < TAPS
                for half in range(2):
                    p = 8 * half + at // 16
                    start = col + 256 * k + L * half
                    t[span, start : start + L] = band(w, tap, c, q - 2 * p + 1) if ok else zero
                start = col + 1024 + L * k
                t[span, start : start + L] = band(w, tap, c, rim) if ok else zero


def window_0(w1c, t):
    matrix_1_down(w1c, t, 0)


def window_1(w2c, t, w):
    matrix_2_down(w2c, t, w)


def window_2(w2d, t, w):
    matrix_2_up(w2d, t, w)


def window_3(w1d, t):
    matrix_1_up(w1d.at[0], t, 0)
    matrix_1_up(w1d.at[1], t, COLS1B)


def window_swap(spare, out):
    out[...] = spare[...]


def correlate(coarse, fine, d):
    def part(rs, first):
        value = lax.dot_general(
            coarse[rs, :], fine[rs, :], (((0,), (0,)), ((), ())), preferred_element_type=F32
        )
        d[...] = value if first else d[...] + value

    part(pl.ds(0, CHUNK), True)

    def body(r, carry):
        part(pl.ds(pl.multiple_of(r * CHUNK, CHUNK), CHUNK), False)
        return carry

    lax.fori_loop(1, R // CHUNK, body, 0)


def weight_2(d, out):
    at = lane((32, L))
    sums = {}
    for base, rim, tap in GROUPS1:
        total = jnp.zeros((32, L), F32)
        for p in range(8):
            span = slice(32 * p, 32 * p + 32)
            parts = [d[span, base : base + L], d[span, base + L : base + 256], d[span, rim : rim + L]]
            if p == 0:
                value = jnp.where(at < 16, pltpu.roll(parts[2], 16, 1), pltpu.roll(parts[0], 16, 1))
            else:
                which, off = divmod(32 * p - 16, L)
                value = pltpu.roll(parts[which], L - off, 1)
                if off + 80 > L:
                    value = jnp.where(at < L - off, value, pltpu.roll(parts[which + 1], L - off, 1))
            total = total + value
        sums[tap] = total
    out[0:32, :] = jnp.where(at < 80, sums[0], pltpu.roll(sums[4], 80, 1))
    out[32:64, :] = jnp.where(at < 80, sums[1], pltpu.roll(sums[4], 32, 1))
    out[64:96, :] = sums[2]
    out[96:128, :] = sums[3]


def weight_1(d, out, start):
    at = lane((16, L)) % 32
    result = jnp.zeros((16, L), F32)
    for k in range(3):
        total = jnp.zeros((16, L), F32)
        for row in range(2):
            tile = (2, 0, 1)[k] if row == 0 else (0, 1, 3)[k]
            for p in range(16):
                first = row * 256 + p * 16
                span = slice(first, first + 16)
                value = pltpu.roll(d[span, L * tile : L * tile + L], (1 - 2 * p) % L, 1)
                if p in (0, 15):
                    rim = d[span, 512 + L * tile : 512 + L * tile + L]
                    rim = pltpu.roll(rim, L - 31 if p == 0 else 3, 1)
                    value = jnp.where(at == 0 if p == 0 else at >= 3, rim, value)
                total = total + value
        if k > 0:
            total = pltpu.roll(total, 8 * k, 1)
        result = jnp.where((at >= 8 * k) & (at < 8 * k + TAPS), total, result)
    out[start : start + 16, :] = result


def window_4(low, act, fine, w2d, t, out, d, w, kept):
    matrix_2_down(w2d, t, w)
    correlate(ready(low), ready(fine), d)
    weight_1(d, kept, 0)
    correlate(ready(act), ready(fine), d)
    weight_1(d, kept, 16)
    out.put(kept)


def window_5(coarse, fine, w2c, t, out, d, w, kept):
    matrix_2_up(w2c, t, w)
    correlate(ready(coarse), ready(fine), d)
    weight_2(d, kept)
    out.put(kept)


def window_6(coarse, fine, w1c, t, out, d, kept):
    matrix_1_up(w1c, t, 0)
    correlate(ready(coarse), ready(fine), d)
    weight_2(d, kept)
    out.put(kept)


HALF = 160


def window_7(index, coarse, fine, bias, w1d, w2d, w2c, keep, give, d, first):
    correlate(ready(coarse), ready(fine), d)
    weight_1(d, first, 0)
    even = index[1] == 0
    up_two, up_one, down_two = ready(w2d), ready(w1d), ready(w2c)
    spare = jnp.zeros((8, L), F32)

    def place(span, a, b):
        keep[span, :] = jnp.where(even, a, b)
        give[span, :] = jnp.where(even, b, a)

    place(slice(0, 128), up_two[...], down_two[...])
    place(slice(128, 144), up_one[0:16, :], first[...])
    place(slice(144, 160), up_one[16:32, :], jnp.concatenate([bias[...], spare]))


def unpack_kernel(index, mine, other, w1c, w2c, w2d, w1d, bias):
    even = index[1] == 0
    a, b = mine[...], other[...]
    up, down = jnp.where(even, a, b), jnp.where(even, b, a)
    for half, out in ((up, w2d), (down, w2c)):
        turned = half[0:128].T
        moved = [turned] + [pltpu.roll(turned, L - 32 * tap, 1) for tap in range(1, 4)]
        for tap in range(TAPS):
            for b in range(TAPS):
                if tap < 4:
                    value = moved[tap][16 * b : 16 * b + 16]
                else:
                    value = moved[b // 3][80 + 16 * (b % 3) : 96 + 16 * (b % 3)]
                out[tap * TAPS + b] = value[:, 0:32]
    tall = jnp.concatenate([up[128:160], down[128:144], jnp.zeros((80, L), F32)]).T
    other_tall = pltpu.roll(tall, L - 32, 1)
    for tap in range(TAPS):
        for b in range(TAPS):
            for c in range(2):
                row = (tap + 1) % 2 * 64 + c * 32 + (tap + 1) // 2 * 8 + b
                w1d[tap * TAPS + b, c : c + 1, :] = tall[row : row + 1, 0:32]
                w1c[tap * TAPS + b, c : c + 1, :] = other_tall[row : row + 1, 0:16]
    total = total_rows(down[144:152])
    total = jnp.broadcast_to(total, (8, L))
    total = total + pltpu.roll(total, 64, 1)
    for step in (16, 8, 4, 2, 1):
        total = total + pltpu.roll(total, L - step, 1)
    bias[...] = jnp.where(lane((8, L)) == 0, total, pltpu.roll(total, L - 31, 1))


def ready(ref):
    return ref.get() if isinstance(ref, Arriving) else ref


def spread(scr, store):
    at = lane((M, L)) // 32
    for half in range(2):
        parts = [scr[k % 2, pl.ds(2 * half + k // 2, M, stride=4), :] for k in range(4)]
        for block in range(4):
            value = parts[block]
            for k in range(4):
                if k != block:
                    value = jnp.where(at == k, pltpu.roll(parts[k], (32 * (k - block)) % L, 1), value)
            store(block, half, value)


def gather(blocks, scr):
    at = lane((M, L)) // 32
    for half in range(2):
        parts = [blocks(block, half) for block in range(4)]
        for k in range(4):
            value = parts[k]
            for block in range(4):
                if block != k:
                    value = jnp.where(
                        at == block, pltpu.roll(parts[block], (32 * (block - k)) % L, 1), value
                    )
            scr[k % 2, pl.ds(2 * half + k // 2, M, stride=4), :] = value


def layout_kernel(index, frame_mask, mix, cot, cross, core, xf, x0, c0, scr, wide, cf, ends):
    def place(out, block, row):
        def store(k, half, value):
            at = slice(L * half, L * half + L)
            out[rows(block + k), at] = value.astype(BF)
            wide[rows(row + k), at] = value

        return store

    m = mix.get()

    def mix_tile(t):
        for c in range(2):
            scr[c] = m[c, :, pl.ds(pl.multiple_of(t * L, L), L)].astype(F32)
        spread(scr, place(xf, 4 * t, 4 * t))

    for_blocks(mix_tile, NJ // 4)
    x0.put(xf)
    g = cot.get()
    per_stem = g.shape[3] // L

    def cot_tile(t):
        for c in range(2):
            lanes = pl.ds(pl.multiple_of((t % per_stem) * L, L), L)
            scr[c] = g[t // per_stem, c, :, lanes].astype(F32)
        spread(scr, place(cf, 4 * t, NJ + 4 * t))

    for_blocks(cot_tile, NJ // 4)
    c0.put(cf)
    ends[...] = jnp.zeros(ends.shape, F32)
    pack_ends(wide, index, ends.at[0], ends.at[1], 2 * NJ)
    even = index[1] == 0

    def least(first, count):
        value = frame_mask[first]
        for k in range(1, count):
            value = jnp.minimum(value, frame_mask[first + k])
        return value.astype(F32)

    for i, (first, count) in enumerate(((0, 2), (2, 2), (0, 4))):
        top, low = least(first, count), least(4 * M - 4 + first, count)
        row = 2 * NJ + i
        ends[0, row : row + 1, :] = jnp.full((1, 2 * L), jnp.where(even, top, low))
        ends[1, row : row + 1, :] = jnp.full((1, 2 * L), jnp.where(even, low, top))
    cross[...] = ends[0].astype(BF)
    core[...] = ends[1].astype(BF)


def columns_0(cat, blocks, read, left, right, aux):
    a, a_next = aux[0], aux[1]
    for which, (first, count) in enumerate(blocks):

        def one(i, which=which, first=first):
            j = first + i
            for half in range(2):
                value = read(which, j, half)
                cat[rows(j), L * half : L * half + L] = value.astype(BF)
                if half == 1:
                    moved = from_prev(value, left[rows(j, 8), L : 2 * L], a)
                    cat[rows(j), 256:384] = moved.astype(BF)
                else:
                    moved = from_next(value, right[rows(j, 8), 0:L], a_next)
                    cat[rows(j), 384:512] = moved.astype(BF)

        for_blocks(one, count)
    rims_0(cat)


def conv_one_kernel(
    index, x0, cross_in, core_in, aux, t,
    cross, core, mom, kept, hxfar, zfar, catfar, z, hx, cat, lf, rf, lw, rw,
):
    even = index[1] == 0
    a, b = cross_in[...].astype(F32), core_in[...].astype(F32)
    lf[...] = jnp.where(even, a, b)
    rf[...] = jnp.where(even, b, a)
    hx[:, 0:L] = rf[0 : 2 * NJ, 0:L]
    hx[:, L : 2 * L] = lf[0 : 2 * NJ, L : 2 * L]
    hxfar.put(hx)
    kept[...] = jnp.zeros(kept.shape, F32)
    kept[0:3, :] = lf[2 * NJ : 2 * NJ + 3, 0:L]
    kept[3:6, :] = rf[2 * NJ : 2 * NJ + 3, 0:L]
    widen(lf.at[0:NJ], lw)
    widen(rf.at[0:NJ], rw)
    x = ready(x0)
    read = lambda which, j, h: x[rows(j), L * h : L * h + L].astype(F32)
    columns_0(cat, [(0, NJ)], read, lw, rw, aux)
    catfar.put(cat)
    weights = ready(t)

    def chunk(rs):
        z[rs, :] = matmul(cat[rs, :], weights[...])
        zfar.put(z, (rs, slice(None)))

    quarters(chunk)
    pack_ends(z, index, cross, core)

    def sums(j, s1, s2):
        for k, at in enumerate(tiles(512)):
            value = z[rows(j), at]
            part = value * aux[2 + k // 2]
            s1 = s1 + sum8(part)
            s2 = s2 + sum8(part * value)
        return s1, s2

    stats = fold(stack_rows(sum_blocks(sums)), 16)
    at = sub((8, L))
    stats = jnp.where(at == 2, total_rows(aux[2] + aux[3]) * (NJ * 16.0), stats)
    stats = jnp.where(at == 3, total_rows(aux[4]) * (NJ * 8.0), stats)
    pack_moments(mom, cross, stats)


def conv_two_kernel(
    index, z1, cross_in, core_in, mom1, prm, aux, t,
    cross, core, mom, ends, h1, zfar, catfar, z2, cat, ef, eb, hf, lw, rw,
):
    mean, scale = norm_terms(mom1, mom1[2:3])
    gain, shift = prm[0:1], prm[1:2]

    def act(value):
        return silu((value - mean) * scale * gain + shift)

    a, a_next = aux[0], aux[1]
    for at in tiles(512):
        left, right = sides(index, cross_in, core_in, at)
        hf[0, :, at] = left
        hf[1, :, at] = right
        ef[0, :, at] = act(left)
        ef[1, :, at] = act(right)
    h1.put(hf)
    widen(ef.at[0], lw)
    widen(ef.at[1], rw)

    def one(j):
        for k, at in enumerate(tiles(512)):
            value = act(z1[rows(j), at])
            cat[rows(j), at] = value.astype(BF)
            if k >= 2:
                moved = from_prev(value, lw[rows(j, 8), at], a)
                cat[rows(j), 256 + L * k : 384 + L * k] = moved.astype(BF)
            start = 768 + L * k if k < 2 else 1280 + L * k
            moved = from_next(value, rw[rows(j, 8), at], a_next)
            cat[rows(j), start : start + L] = moved.astype(BF)

    for_blocks(one)
    catfar.put(cat, (slice(None), slice(0, 1024)))
    catfar.put(cat, (slice(None), slice(1536, 1792)))
    rims_1(cat, GROUPS1)
    catfar.put(cat, (slice(None), slice(1024, 1536)))
    catfar.put(cat, (slice(None), slice(1792, 1920)))
    def group_out(rs, at, top, low):
        ef[2, rs, at] = act(top)
        ef[3, rs, at] = act(low)

    end_rows(z1, group_out)
    eb[...] = ef[...].astype(BF)
    ends.put(eb)
    weights = ready(t)

    def chunk(rs):
        z2[rs, :] = matmul(cat[rs, :], weights[...])
        zfar.put(z2, (rs, slice(None)))

    quarters(chunk)
    pack_ends(z2, index, cross, core)

    def sums(j, s1, s2):
        for at in tiles(256):
            value = z2[rows(j), at]
            part = value * aux[4]
            s1 = s1 + sum8(part)
            s2 = s2 + sum8(part * value)
        return s1, s2

    pack_moments(mom, cross, fold(stack_rows(sum_blocks(sums)), 32))


def columns_2(cat, read, left, right, aux):
    a, a_next = aux[0], aux[1]

    def one(j):
        for k, at in enumerate(tiles(256)):
            value = read(j, at)
            cat[rows(j), at] = value.astype(BF)
            moved = from_prev(value, left[rows(j, 8), at], a)
            cat[rows(j), 256 + L * k : 384 + L * k] = moved.astype(BF)
            moved = from_next(value, right[rows(j, 8), at], a_next)
            cat[rows(j), 512 + L * k : 640 + L * k] = moved.astype(BF)

    for_blocks(one)
    rims_2(cat)


def up_two_kernel(
    index, z2, cross_in, core_in, mom1, mom2, prm, aux, t,
    cross, core, mom, h2, act2, rectfar, rect, cat, hf, lf, rf, lw, rw,
):
    mean, scale = norm_terms(mom2, mom1[3:4])
    gain, shift, bias = prm[2:3], prm[3:4], prm[6:7]

    def act(value):
        return silu((value - mean) * scale * gain + shift)

    for at in tiles(256):
        left, right = sides(index, cross_in, core_in, at)
        hf[0, :, at] = left
        hf[1, :, at] = right
        lf[:, at] = act(left)
        rf[:, at] = act(right)
    h2.put(hf)
    widen(lf, lw)
    widen(rf, rw)
    columns_2(cat, lambda j, at: act(z2[rows(j), at]), lw, rw, aux)
    act2.put(cat.at[:, 0:256])
    weights = ready(t)

    def chunk(rs):
        rect[rs, :] = matmul(cat[rs, :], weights[...], True)

    for_chunks(chunk)

    def sums(j, s1, s2):
        for k, at in enumerate(tiles(512)):
            value = softplus(rect[rows(j), at] + bias)
            rect[rows(j), at] = value
            part = value * aux[2 + k // 2]
            s1 = s1 + sum8(part)
            s2 = s2 + sum8(part * value)
        return s1, s2

    stats = sum_blocks(sums)
    rectfar.put(rect)
    pack_moments(mom, cross, fold(stack_rows(stats), 16))
    pack_ends(rect, index, cross, core)


def columns_1b(cat, read, left, right, aux):
    a, a_next = aux[0], aux[1]

    def one(j):
        for k, at in enumerate(tiles(512)):
            value = read(j, k, at)
            cat[rows(j), at] = value.astype(BF)
            if k >= 2:
                moved = from_prev(value, left[rows(j, 8), at], a)
                cat[rows(j), 256 + L * k : 384 + L * k] = moved.astype(BF)
            else:
                moved = from_next(value, right[rows(j, 8), at], a_next)
                cat[rows(j), 768 + L * k : 896 + L * k] = moved.astype(BF)

    for_blocks(one)
    rims_1(cat, GROUPS1[:4])


def edge_columns(own, prev, after):
    at = lane((NJ, L))
    place = sub((NJ, L))
    parts = [own, prev, after]
    groups = [own[:, 0:256], own[:, 256:512], prev, after]
    for g in groups:
        low = jnp.where((place == NJ - 1) | (at >= 32), 0.0, pltpu.roll(g[:, 0:L], NJ - 1, 0))
        high = jnp.where((place == 0) | (at < 112), 0.0, pltpu.roll(g[:, L : 2 * L], 1, 0))
        parts.append(low + high)
    return jnp.concatenate(parts, axis=1).astype(BF)


def quarter_blocks(index, stems):
    count = NJ // stems
    return [((index[0] ^ k) * count, count) for k in range(stems)]


def up_one_kernel(
    index, rect, cross_in, core_in, mom1, mom3, prm, aux, ends1, cat1, t,
    m0, m1, m2, m3, h3, low3, sig, sigh, cat, hf, lf, rf, ef, ff, sf, shf, lw, rw,
):
    mean, scale = norm_terms(mom3, mom1[2:3])
    gain, shift, bias = prm[4:5], prm[5:6], prm[7:8]

    def norm(value):
        return (value - mean) * scale * gain + shift

    for at in tiles(512):
        left, right = sides(index, cross_in, core_in, at)
        hf[0, :, at] = left
        hf[1, :, at] = right
        lf[:, at] = norm(left)
        rf[:, at] = norm(right)
    h3.put(hf)
    widen(lf, lw)
    widen(rf, rw)
    columns_1b(cat, lambda j, k, at: norm(rect[rows(j), at]), lw, rw, aux)
    low3.put(cat.at[:, 0:512])

    def group_out(rs, at, top, low):
        ef[0, rs, at] = norm(top)
        ef[1, rs, at] = norm(low)

    end_rows(rect, group_out)
    wide = jnp.concatenate([bias, bias], axis=1)
    zero = jnp.zeros((NJ, 256), F32)
    a, a_end = aux[0, 0:1, 0:1], aux[1, M - 1 : M, 0:1]
    e1 = [ends1[k].astype(F32) for k in range(4)]
    edges = [
        (
            edge_columns(lf[...], zero, ef[0, :, 0:256] * a),
            edge_columns(e1[0], zero, e1[2][:, 0:256] * a),
        ),
        (
            edge_columns(rf[...], ef[1, :, 256:512] * a_end, zero),
            edge_columns(e1[1], e1[3][:, 256:512] * a_end, zero),
        ),
    ]
    weights, other = ready(t), ready(cat1)
    for k, half in ((0, 1), (1, 0)):
        value = matmul(edges[k][0], weights[:, 0:COLS1B], True)
        value = value + matmul(edges[k][1], weights[:, COLS1B : 2 * COLS1B], True)
        shf[:, L * half : L * half + L] = sigmoid(value[:, L * half : L * half + L] + bias)
    sigh.put(shf)
    masks = (m0, m1, m2, m3)
    per = R // len(masks)
    for mask, (first, count) in zip(masks, quarter_blocks(index, len(masks))):
        rs = rows(lax.div(first, count), per)
        value = matmul(cat[rs, :], weights[:, 0:COLS1B], True)
        value = value + matmul(other[rs, :], weights[:, COLS1B : 2 * COLS1B], True)
        value = sigmoid(value + wide)
        sf[rs, :] = value
        mask[0:per, :] = value.astype(BF)
        ff[...] = jnp.zeros(ff.shape, F32)
        ff[0:count, :] = shf[rows(lax.div(first, count), count), :]
        mask[per : per + 16, :] = ff[...].astype(BF)
    sig.put(sf)


def ratio_terms(masks):
    squares = [m * m for m in masks]
    power = squares[0]
    for s in squares[1:]:
        power = power + s
    inverse = 1.0 / (power + RATIO_EPS)
    return [s * inverse for s in squares], inverse


def mask_back(masks, cots, mix):
    ratios, inverse = ratio_terms(masks)
    direct = cots[0] * ratios[0]
    for c, r in zip(cots[1:], ratios[1:]):
        direct = direct + c * r
    common = 2.0 * mix * inverse
    return [m * common * (c - direct) for m, c in zip(masks, cots)], direct


def mask_kernel(index, m0, m1, m2, m3, c0, x0, hx, g0, g1, g2, g3, direct, df, ff):
    masks, grads = (m0, m1, m2, m3), (g0, g1, g2, g3)
    stems = len(masks)
    per, blocks = R // stems, NJ // stems
    mine = index[0]
    cots, mix, rim = ready(c0), ready(x0), ready(hx)

    def one(j):
        for at in tiles(256):
            m = [masks[s][rows(j), at].astype(F32) for s in range(stems)]
            c = [cots[rows((mine ^ s) * blocks + j), at].astype(F32) for s in range(stems)]
            x = mix[rows(mine * blocks + j), at].astype(F32)
            values, own = mask_back(m, c, x)
            df[rows(j), at] = own
            for s in range(stems):
                grads[s][rows(j), at] = values[s].astype(BF)

    for_blocks(one, blocks)
    direct.put(df)
    m = [masks[s][per : per + 16, :].astype(F32)[0:blocks] for s in range(stems)]
    c = [rim[rows(stems + (mine ^ s), blocks), :] for s in range(stems)]
    values, _ = mask_back(m, c, rim[rows(mine, blocks), :])
    for s in range(stems):
        ff[...] = jnp.zeros(ff.shape, F32)
        ff[0:blocks, :] = values[s]
        grads[s][per : per + 16, :] = ff[...].astype(BF)


def estimate_kernel(index, m0, m1, m2, m3, x0, w1d, out, t, scr, est):
    masks = (m0, m1, m2, m3)
    stems = len(masks)
    blocks = NJ // stems
    mine = index[0]
    matrix_1_down(w1d.at[0], t, 0)
    matrix_1_down(w1d.at[1], t, 512)
    mix = ready(x0)

    def one(j):
        for at in tiles(256):
            m = [masks[s][rows(j), at].astype(F32) for s in range(stems)]
            x = mix[rows(mine * blocks + j), at].astype(F32)
            ratios, _ = ratio_terms(m)
            for s in range(stems):
                est[s, rows(j), at] = x * ratios[s]

    for_blocks(one, blocks)
    for s in range(stems):
        for t in range(blocks // 4):
            gather(
                lambda block, half, s=s, t=t: est[s, rows(4 * t + block), L * half : L * half + L], scr
            )
            for c in range(2):
                out[mine ^ s, c, :, L * t : L * t + L] = scr[c].astype(BF)


def down_one_back_kernel(
    index, q0, q1, q2, q3, sigh, sig, aux, mom1, mom3, rect, t,
    g3, cat, cross, core, mom, bias, gact, gf, hf, zf, hw,
):
    grads = (q0, q1, q2, q3)
    blocks = quarter_blocks(index, len(grads))
    per = R // len(grads)
    rim = ready(sigh)
    for grad, (first, count) in zip(grads, blocks):
        span = rows(lax.div(first, count), count)
        value = grad[per : per + 16, :].astype(F32)[0:count]
        own = rim[span, :]
        hf[span, :] = value * own * (1.0 - own)
    zf[...] = jnp.zeros(zf.shape, F32)
    widen(hf, hw)
    sigs = ready(sig)

    def read(which, j, half):
        at = slice(L * half, L * half + L)
        own = sigs[rows(j), at]
        value = grads[which][rows(j - blocks[which][0]), at].astype(F32) * own * (1.0 - own)
        zf[...] = zf[...] + sum8(value)
        return value

    columns_0(cat, blocks, read, hw, hw, aux)
    bias[...] = zf[...]
    weights = ready(t)

    def chunk(rs):
        value = matmul(cat[rs, :], weights[...])
        g3[rs, :] = value[:, 0:512]
        gf[rs, :] = value[:, 512:1024]
        gact.put(gf, (rs, slice(None)))

    quarters(chunk)
    mean, scale = norm_terms(mom3, mom1[2:3])
    pack_ends(g3, index, cross, core)
    r = ready(rect)

    def sums(j, s1, s2):
        for at in tiles(512):
            value = g3[rows(j), at]
            s1 = s1 + sum8(value)
            s2 = s2 + sum8(value * (r[rows(j), at] - mean))
        return s1, s2

    s1, s2 = sum_blocks(sums)
    pack_moments(mom, cross, fold(stack_rows([s1, s2 * scale]), 16))


def norm_back(g, xhat, kept, moments, count, factor):
    return factor * (g - kept * ((moments[0:1] + xhat * moments[1:2]) / count))


def up_two_back_kernel(
    index, g3, cross_in, core_in, mom4, mom1, mom3, mom2, prm, aux, kept, rect, h3, t, z2,
    g2, cat, cross, core, mom, lf, rf, lw, rw,
):
    count = mom1[2:3]
    mean, scale = norm_terms(mom3, count)
    factor = scale * prm[4:5]
    inverse = 1.0 / count

    def back(g, r, keep):
        xhat = (r - mean) * scale
        value = factor * (g - keep * ((mom4[0:1] + xhat * mom4[1:2]) * inverse))
        return value * softplus_slope(r)

    r, h = ready(rect), ready(h3)
    for k, at in enumerate(tiles(512)):
        left, right = sides(index, cross_in, core_in, at)
        row = k // 2
        lf[:, at] = back(left, h[0, :, at], kept[row : row + 1, :])
        rf[:, at] = back(right, h[1, :, at], kept[3 + row : 4 + row, :])
    widen(lf, lw)
    widen(rf, rw)
    a, a_next = aux[0], aux[1]

    def one(j, total):
        for k, at in enumerate(tiles(512)):
            value = back(g3[rows(j), at], r[rows(j), at], aux[2 + k // 2])
            total = total + sum8(value)
            cat[rows(j), at] = value.astype(BF)
            if k >= 2:
                moved = from_prev(value, lw[rows(j, 8), at], a)
                cat[rows(j), 256 + L * k : 384 + L * k] = moved.astype(BF)
            start = 768 + L * k if k < 2 else 1280 + L * k
            moved = from_next(value, rw[rows(j, 8), at], a_next)
            cat[rows(j), start : start + L] = moved.astype(BF)
        return total

    def four(j, total):
        for i in range(UNROLL):
            total = one(j * UNROLL + i, total)
        return total

    bias = lax.fori_loop(0, NJ // UNROLL, four, jnp.zeros((8, L), F32))
    rims_1(cat, GROUPS1)
    weights = ready(t)

    def chunk(rs):
        g2[rs, :] = matmul(cat[rs, :], weights[...])

    for_chunks(chunk)
    mean2, scale2 = norm_terms(mom2, mom1[3:4])
    gain, shift = prm[2:3], prm[3:4]
    z = ready(z2)

    def sums(j, s1, s2):
        for at in tiles(256):
            xhat = (z[rows(j), at] - mean2) * scale2
            value = g2[rows(j), at] * silu_slope(xhat * gain + shift)
            g2[rows(j), at] = value
            s1 = s1 + sum8(value)
            s2 = s2 + sum8(value * xhat)
        return s1, s2

    stats = fold(stack_rows(sum_blocks(sums)), 32)
    pack_ends(g2, index, cross, core)
    bias = fold(stack_rows([total_rows(bias)] * 3), 16)
    pack_moments(mom, cross, jnp.where(sub((8, L)) == 2, bias, stats))


def down_two_back_kernel(
    index, g2, cross_in, core_in, mom5, mom1, mom2, prm, aux, kept, z2, h2, t, gact, z1,
    g1, low2, cross, core, mom, cat, lf, rf, lw, rw,
):
    count = mom1[3:4]
    mean, scale = norm_terms(mom2, count)
    factor = scale * prm[2:3]
    inverse = 1.0 / count

    def back(g, z, keep):
        xhat = (z - mean) * scale
        return factor * (g - keep * ((mom5[0:1] + xhat * mom5[1:2]) * inverse))

    z, h = ready(z2), ready(h2)
    for at in tiles(256):
        left, right = sides(index, cross_in, core_in, at)
        lf[:, at] = back(left, h[0, :, at], kept[2:3, :])
        rf[:, at] = back(right, h[1, :, at], kept[5:6, :])
    widen(lf, lw)
    widen(rf, rw)
    columns_2(cat, lambda j, at: back(g2[rows(j), at], z[rows(j), at], aux[4]), lw, rw, aux)
    low2[...] = cat[:, 0:256]
    weights, added = ready(t), ready(gact)

    def chunk(rs):
        g1[rs, :] = matmul(cat[rs, :], weights[...], True) + added[rs, :]

    for_chunks(chunk)
    mean1, scale1 = norm_terms(mom1, mom1[2:3])
    gain, shift = prm[0:1], prm[1:2]
    z = ready(z1)

    def sums(j, s1, s2):
        for at in tiles(512):
            xhat = (z[rows(j), at] - mean1) * scale1
            value = g1[rows(j), at] * silu_slope(xhat * gain + shift)
            g1[rows(j), at] = value
            s1 = s1 + sum8(value)
            s2 = s2 + sum8(value * xhat)
        return s1, s2

    stats = fold(stack_rows(sum_blocks(sums)), 16)
    pack_ends(g1, index, cross, core)
    pack_moments(mom, cross, stats)


def up_one_back_kernel(
    index, g1, cross_in, core_in, mom6, mom1, prm, aux, kept, z1, h1, t,
    n0, n1, n2, n3, low1, cat, lf, rf, lw, rw,
):
    count = mom1[2:3]
    mean, scale = norm_terms(mom1, count)
    factor = scale * prm[0:1]
    inverse = 1.0 / count

    def back(g, z, keep):
        xhat = (z - mean) * scale
        return factor * (g - keep * ((mom6[0:1] + xhat * mom6[1:2]) * inverse))

    z, h = ready(z1), ready(h1)
    for k, at in enumerate(tiles(512)):
        left, right = sides(index, cross_in, core_in, at)
        row = k // 2
        lf[:, at] = back(left, h[0, :, at], kept[row : row + 1, :])
        rf[:, at] = back(right, h[1, :, at], kept[3 + row : 4 + row, :])
    widen(lf, lw)
    widen(rf, rw)
    columns_1b(
        cat, lambda j, k, at: back(g1[rows(j), at], z[rows(j), at], aux[2 + k // 2]), lw, rw, aux
    )
    low1[...] = cat[:, 0:512]
    weights = ready(t)
    nets = (n0, n1, n2, n3)
    per = R // len(nets)
    for net, (first, blocks) in zip(nets, quarter_blocks(index, len(nets))):
        rs = rows(lax.div(first, blocks), per)
        net[...] = matmul(cat[rs, :], weights[...], True).astype(BF)


def mixture_kernel(p0, p1, p2, p3, direct, out, scr):
    parts = (p0, p1, p2, p3)
    own = ready(direct)

    def tile(t):
        def block(k, half):
            at = slice(L * half, L * half + L)
            value = own[rows(4 * t + k), at]
            for part in parts:
                value = value + part[rows(4 * t + k), at].astype(F32)
            return value

        gather(block, scr)
        for c in range(2):
            out[c, :, pl.ds(pl.multiple_of(t * L, L), L)] = scr[c]

    for_blocks(tile, NJ // len(parts) // 4)


def pairs(count, offset):
    there = [(i, (i + offset) % count) for i in range(0, count, 2)]
    return there + [(b, a) for a, b in there]


def flip(values, axis, bit):
    return lax.ppermute(values, axis, [(i, i ^ bit) for i in range(lax.axis_size(axis))])


def sum_over(values, axis):
    count = lax.axis_size(axis)
    if count & (count - 1):
        return lax.psum(values, axis)
    step = 1
    while step < count:
        radix = 2 if step == 1 or count // step == 2 else 4
        moved = [flip(values, axis, step * k) for k in range(1, radix)]
        for m in moved:
            values = values + m
        step *= radix
    return values


def sum_halves(keep, give, axis):
    count = lax.axis_size(axis)
    mine = keep + flip(give, axis, 1)
    if count == 8:
        low = mine.astype(BF)
        moved = [flip(low, axis, bit) for bit in (2, 4, 6)]
        mine = low.astype(F32) + moved[0].astype(F32) + moved[1].astype(F32) + moved[2].astype(F32)
    else:
        step = 2
        while step < count:
            mine = mine + flip(mine, axis, step)
            step *= 2
    return mine, flip(mine, axis, 1)


def exchange(cross, core, mom, axis, beside):
    count = lax.axis_size(axis)
    near = lax.ppermute(cross, axis, pairs(count, -1))
    if count == 8:
        far = lax.ppermute(mom, axis, pairs(count, 3))
        across = flip(mom, axis, 4)
        inside = flip(core, axis, 1)
        *made, mom = beside(mom)
        part = mom + near[NJ:, 0:L] + far + across
        return near, inside, part + flip(part, axis, 1), made
    inside = flip(core, axis, 1)
    *made, mom = beside(mom)
    return near, inside, sum_over(mom, axis), made


def swap(blocks, axis):
    return [blocks[0]] + [flip(blocks[k], axis, k) for k in range(1, len(blocks))]


def flags(seg_lengths, frame_mask, position, total):
    order = jnp.arange(seg_lengths.shape[0])
    earlier = order[None, :] < order[:, None]
    starts = 4 * jnp.sum(jnp.where(earlier, seg_lengths[None, :], 0), axis=1)
    frames = (position * M + jnp.arange(M + 1, dtype=jnp.int32)) * 4
    shut = jnp.any(frames[:, None] == starts[None, :], axis=1) | (frames == total)
    a = 1.0 - shut.astype(F32)
    keep_one = jnp.min(frame_mask.reshape(M, 2, 2), axis=2).astype(F32)
    keep_two = jnp.min(frame_mask.reshape(M, 4), axis=1).astype(F32)
    columns = jnp.stack([a[:M], a[1:], keep_one[:, 0], keep_one[:, 1], keep_two])
    return jnp.broadcast_to(columns[:, :, None], (5, M, L))


def per_device(
    mixture,
    seg_lengths,
    frame_mask,
    conv_first,
    encoder_gain_vector,
    shift_first,
    conv_second,
    gain_second,
    shift_second,
    deconv_second,
    bias_second,
    decoder_gain_vector,
    shift_third,
    deconv_first,
    bias_first,
    cotangent,
):
    position = lax.axis_index("tm")
    stems = lax.axis_size("stem")
    odd = position % 2
    index = jnp.stack([lax.axis_index("stem"), odd]).astype(jnp.int32)
    frames = mixture.shape[1]
    per, blocks = R // stems, NJ // stems
    aux = flags(seg_lengths, frame_mask, position, frames * lax.axis_size("tm"))
    prm = jnp.stack(
        [
            jnp.tile(encoder_gain_vector[0], 8),
            jnp.tile(shift_first[0], 8),
            jnp.tile(gain_second[0], 4),
            jnp.tile(shift_second[0], 4),
            jnp.tile(decoder_gain_vector[0], 8),
            jnp.tile(shift_third[0], 8),
            jnp.tile(bias_second[0], 8),
            jnp.tile(jnp.repeat(bias_first[0], 32), 2),
        ]
    )
    w1c = jnp.tile(conv_first[0].transpose(2, 3, 1, 0).reshape(50, 16).astype(F32), (1, 8))
    w1d = deconv_first[0].transpose(2, 3, 0, 1).reshape(50, 2, 16).astype(F32)
    w1d = jnp.tile(w1d.transpose(1, 0, 2), (1, 1, 8))
    w2c = conv_second[0].transpose(2, 3, 1, 0).reshape(400, 32)
    w2d = deconv_second[0].transpose(2, 3, 0, 1).reshape(400, 32)
    edge = 2 * NJ + 16

    def packet(lanes):
        return [((NJ + 8, lanes), F32), ((NJ, lanes), F32), ((8, L), F32)]

    def rim(lanes):
        return [((NJ, lanes), F32)] * 2

    def wide(lanes):
        return [((8 * NJ, lanes), F32)] * 2

    def far(*shape, kind=F32):
        return [(shape, kind, True)]

    cross, core, x0, x0_far, c0 = run(
        layout_kernel,
        "layout",
        [((edge, 256), BF), ((edge, 256), BF), ((R, 256), BF)] + far(R, 256, kind=BF) + far(R, 256, kind=BF),
        [index, frame_mask, Far(mixture), Far(cotangent)],
        [((2, frames, L), F32), ((2 * R, 256), F32), ((R, 256), BF), ((2, edge, 256), F32)],
    )
    near = lax.ppermute(cross, "tm", pairs(lax.axis_size("tm"), -1))
    inside = flip(core, "tm", 1)
    (t,) = run(window_0, "window_0", [((COLS0, 512), BF)], [w1c])
    cross, core, mom, kept, hx, z1, cat0 = run(
        conv_one_kernel,
        "conv_one",
        packet(512) + [((8, L), F32)] + far(2 * NJ, 256) + far(R, 512) + far(R, COLS0, kind=BF),
        [index, x0, near, inside, aux, t],
        [((R, 512), F32), ((2 * NJ, 256), F32), ((R, COLS0), BF), ((edge, 256), F32), ((edge, 256), F32)]
        + wide(256),
        flops=2 * R * COLS0 * 512,
    )
    near, inside, mom1, (t, z1_here) = exchange(
        cross, core, mom, "tm",
        lambda token: run(
            window_1, "window_1", [((COLS1, 256), BF)], [w2c], [((400, L), F32)], fetch=[Far(z1)], token=token
        ),
    )
    cross, core, mom, ends1, h1, z2, cat1 = run(
        conv_two_kernel,
        "conv_two",
        packet(256) + far(4, NJ, 512, kind=BF) + far(2, NJ, 512) + far(R, 256) + far(R, COLS1, kind=BF),
        [index, z1_here, near, inside, mom1, prm, aux, t],
        [((R, 256), F32), ((R, COLS1), BF), ((4, NJ, 512), F32), ((4, NJ, 512), BF), ((2, NJ, 512), F32)]
        + wide(512),
        flops=2 * R * COLS1 * 256,
    )
    near, inside, mom2, (t, z2_here) = exchange(
        cross, core, mom, "tm",
        lambda token: run(
            window_2, "window_2", [((512, COLS2), BF)], [w2d], [((400, L), F32)], fetch=[Far(z2)], token=token
        ),
    )
    cross, core, mom, h2, act2, rect = run(
        up_two_kernel,
        "up_two",
        packet(512) + far(2, NJ, 256) + far(R, 256, kind=BF) + far(R, 512),
        [index, z2_here, near, inside, mom1, mom2, prm, aux, t],
        [((R, 512), F32), ((R, COLS2), BF), ((2, NJ, 256), F32)] + rim(256) + wide(256),
        flops=2 * R * COLS2 * 512,
    )
    near, inside, mom3, (t, rect_here, cat1_here, ends1_here) = exchange(
        cross, core, mom, "tm",
        lambda token: run(
            window_3,
            "window_3",
            [((256, 2 * COLS1B), BF)],
            [w1d],
            fetch=[Far(rect), Far(cat1, COLS1B), Far(ends1)],
            token=token,
        ),
    )
    *masks, h3, low3, sig, sigh = run(
        up_one_kernel,
        "up_one",
        [((per + 16, 256), BF)] * stems
        + far(2, NJ, 512) + far(R, 512, kind=BF) + far(R, 256) + far(NJ, 256),
        [index, rect_here, near, inside, mom1, mom3, prm, aux, ends1_here, cat1_here, t],
        [((R, COLS1B), BF), ((2, NJ, 512), F32)] + rim(512)
        + [((2, NJ, 512), F32), ((16, 256), F32), ((R, 256), F32), ((NJ, 256), F32)] + wide(512),
        flops=2 * R * 2 * COLS1B * 256,
    )
    _, c0_here, x0_here, hx_here = run(
        window_swap, "window_swap", [((8, L), F32)], [mom3], fetch=[Far(c0), Far(x0_far), Far(hx)]
    )
    masks = swap(masks, "stem")
    *grads, direct = run(
        mask_kernel,
        "mask",
        [((per + 16, 256), BF)] * stems + far(per, 256),
        [index, *masks, c0_here, x0_here, hx_here],
        [((per, 256), F32), ((16, 256), F32)],
    )
    grads = swap(grads, "stem")
    estimates, t, sig_here, sigh_here, rect_here = run(
        estimate_kernel,
        "estimate",
        [((stems, 2, frames, blocks * 32), BF), ((COLS0, 1024), BF)],
        [index, *masks, Far(x0_far), w1d],
        [((2, frames, L), F32), ((stems, per, 256), F32)],
        fetch=[Far(sig), Far(sigh), Far(rect)],
    )
    g3, cat0g, cross, core, mom, bias_one, gact = run(
        down_one_back_kernel,
        "down_one_back",
        [((R, 512), F32), ((R, COLS0), BF)] + packet(512) + [((8, L), F32)] + far(R, 512),
        [index, *grads, sigh_here, sig_here, aux, mom1, mom3, rect_here, t],
        [((R, 512), F32), ((NJ, 256), F32), ((8, L), F32), ((8 * NJ, 256), F32)],
        flops=2 * R * COLS0 * 1024,
    )
    near, inside, mom4, (t, w1d_grad, rect_here, h3_here, z2_here) = exchange(
        cross, core, mom, "tm",
        lambda token: run(
            window_4,
            "window_4",
            [((COLS1, 256), BF)] + far(32, L),
            [Far(low3), Far(cat1, 512), cat0g, w2d],
            [((512, COLS0), F32), ((400, L), F32), ((32, L), F32)],
            flops=2 * R * COLS0 * 1024,
            fetch=[Far(rect), Far(h3), Far(z2)],
            token=token,
        ),
    )
    g2, cat1g, cross, core, mom = run(
        up_two_back_kernel,
        "up_two_back",
        [((R, 256), F32), ((R, COLS1), BF)] + packet(256),
        [index, g3, near, inside, mom4, mom1, mom3, mom2, prm, aux, kept, rect_here, h3_here, t, z2_here],
        rim(512) + wide(512),
        flops=2 * R * COLS1 * 256,
    )
    near, inside, mom5, (t, w2d_grad, z2_here, h2_here, gact_here, z1_here) = exchange(
        cross, core, mom, "tm",
        lambda token: run(
            window_5,
            "window_5",
            [((512, COLS2), BF)] + far(128, L),
            [Far(act2), cat1g, w2c],
            [((256, COLS1), F32), ((400, L), F32), ((128, L), F32)],
            flops=2 * R * COLS1 * 256,
            fetch=[Far(z2), Far(h2), Far(gact), Far(z1)],
            token=token,
        ),
    )
    g1, low2, cross, core, mom = run(
        down_two_back_kernel,
        "down_two_back",
        [((R, 512), F32), ((R, 256), BF)] + packet(512),
        [index, g2, near, inside, mom5, mom1, mom2, prm, aux, kept, z2_here, h2_here, t, gact_here, z1_here],
        [((R, COLS2), BF)] + rim(256) + wide(256),
        flops=2 * R * COLS2 * 512,
    )
    near, inside, mom6, (t, w2c_grad, z1_here, h1_here, cat0_here) = exchange(
        cross, core, mom, "tm",
        lambda token: run(
            window_6,
            "window_6",
            [((256, COLS1B), BF)] + far(128, L),
            [low2, Far(cat1), w1c],
            [((256, COLS1), F32), ((128, L), F32)],
            flops=2 * R * COLS1 * 256,
            fetch=[Far(z1), Far(h1), Far(cat0)],
            token=token,
        ),
    )
    *nets, low1 = run(
        up_one_back_kernel,
        "up_one_back",
        [((per, 256), BF)] * stems + [((R, 512), BF)],
        [index, g1, near, inside, mom6, mom1, prm, aux, kept, z1_here, h1_here, t],
        [((R, COLS1B), BF)] + rim(512) + wide(512),
        flops=2 * R * COLS1B * 256,
    )
    nets = swap(nets, "stem")
    keep, give, direct_here = run(
        window_7,
        "window_7",
        [((HALF, L), F32), ((HALF, L), F32)],
        [index, low1, cat0_here, bias_one, Far(w1d_grad), Far(w2d_grad), Far(w2c_grad)],
        [((512, COLS0), F32), ((16, L), F32)],
        flops=2 * R * COLS0 * 512,
        fetch=[Far(direct)],
    )
    (mixture_grad,) = run(
        mixture_kernel,
        "mixture",
        [((2, frames, blocks * 32), F32)],
        [*nets, direct_here],
        [((2, frames, L), F32)],
    )
    mine, other = sum_halves(keep, give, "tm")
    w1c_grad, w2c_grad, w2d_grad, w1d_grad, bias_one = run(
        unpack_kernel,
        "unpack",
        [((25, 2, 16), F32), ((25, 16, 32), F32), ((25, 16, 32), F32), ((25, 2, 32), F32), ((8, L), F32)],
        [index, mine, other],
    )

    def turned(grad, order):
        return grad.reshape((TAPS, TAPS) + grad.shape[1:]).transpose(order)[None]

    return (
        estimates,
        mixture_grad,
        turned(w1c_grad, (3, 2, 0, 1)),
        mom6[1, :16][None],
        mom6[0, :16][None],
        turned(w2c_grad, (3, 2, 0, 1)),
        mom5[1, :32][None],
        mom5[0, :32][None],
        turned(w2d_grad, (2, 3, 0, 1)),
        mom5[2, :16][None],
        mom4[1, :16][None],
        mom4[0, :16][None],
        turned(w1d_grad, (2, 3, 0, 1)),
        bias_one[0:1, 0:2],
    )


def solution(mesh):
    in_specs = (
        P(None, "tm", None),
        P(),
        P("tm"),
        P("stem", None, None, None, None),
        P("stem", None),
        P("stem", None),
        P("stem", None, None, None, None),
        P("stem", None),
        P("stem", None),
        P("stem", None, None, None, None),
        P("stem", None),
        P("stem", None),
        P("stem", None),
        P("stem", None, None, None, None),
        P("stem", None),
        P(None, None, "tm", "stem"),
    )
    out_specs = (
        P(None, None, "tm", "stem"),
        P(None, "tm", "stem"),
        P("stem", None, None, None, None),
        P("stem", None),
        P("stem", None),
        P("stem", None, None, None, None),
        P("stem", None),
        P("stem", None),
        P("stem", None, None, None, None),
        P("stem", None),
        P("stem", None),
        P("stem", None),
        P("stem", None, None, None, None),
        P("stem", None),
    )
    return jax.shard_map(
        per_device, mesh=mesh, in_specs=in_specs, out_specs=out_specs, check_vma=False
    )
```

```python
import jax
import jax.numpy as jnp
from jax import lax
from jax.experimental import pallas as pl
from jax.experimental.pallas import tpu as pltpu
from jax.sharding import PartitionSpec as P

NORM_EPS = 0.001
RATIO_EPS = 1e-10
BF = jnp.bfloat16
F32 = jnp.float32
TAPS = 5
L = 128
M = 32
NJ = 32
R = M * NJ
CHUNK = 512
UNROLL = 4
COLS0 = 1024
COLS1 = 1920
COLS1B = 1536
COLS2 = 1152
GROUPS1 = ((0, 1024, 1), (256, 1152, 2), (512, 1280, 0), (768, 1408, 3), (1536, 1792, 4))
FULL = pl.BlockSpec(memory_space=pltpu.VMEM)
SCALAR = pl.BlockSpec(memory_space=pltpu.SMEM)
FAR = pl.BlockSpec(memory_space=pltpu.HBM)


class Far:
    def __init__(self, array, columns=None, parts=1):
        self.array, self.columns, self.parts = array, columns, parts


class Arriving:
    def __init__(self, source, target, sems, parts=1):
        self.target, self.waited, self.copies = target, 0, []
        size = target.shape[0] // parts
        for k in range(parts):
            span = pl.ds(k * size, size)
            here = (source, target) if parts == 1 else (source.at[span], target.at[span])
            self.copies.append(pltpu.make_async_copy(*here, sems.at[k]))
            self.copies[-1].start()

    def get(self, part=None):
        last = len(self.copies) if part is None else part + 1
        for copy in self.copies[self.waited : last]:
            copy.wait()
        self.waited = max(self.waited, last)
        return self.target


class Leaving:
    def __init__(self, target, sems):
        self.target, self.sems, self.copies = target, sems, []

    def put(self, source, part=None):
        target = self.target if part is None else self.target.at[part]
        source = source if part is None else source.at[part]
        copy = pltpu.make_async_copy(source, target, self.sems.at[len(self.copies)])
        copy.start()
        self.copies.append(copy)

    def wait(self):
        for copy in self.copies:
            copy.wait()


PARTS = 6


def run(kernel, name, outs, args, scratch=(), flops=0, fetch=(), store=(), token=None):
    n_args = len(args)
    args = list(args) + list(fetch) + list(store) + ([] if token is None else [token])
    n_made = len(outs)
    outs = list(outs)
    for f in fetch:
        outs.append(((f.array.shape[0], f.columns or f.array.shape[1]) + f.array.shape[2:], f.array.dtype))
    arrays = [a.array if isinstance(a, Far) else a for a in args]
    n_stored = len(outs)
    outs += [(a.shape, a.dtype, True) for a in store]
    if token is not None:
        outs.append((token.shape, token.dtype))
    far_in = [k for k, a in enumerate(args[:n_args]) if isinstance(a, Far)]
    far_out = [k for k, o in enumerate(outs) if len(o) == 3]
    n_in, n_out, n_own = len(args), len(outs), len(scratch)
    placed = [
        pltpu.with_memory_space_constraint(a.array, pltpu.HBM) if isinstance(a, Far) else a for a in args
    ]
    landing = []
    for k in far_in:
        shape = args[k].array.shape
        if args[k].columns is not None:
            shape = (shape[0], args[k].columns)
        landing.append(pltpu.VMEM(shape, args[k].array.dtype))

    def body(*refs):
        ins, results = list(refs[:n_in]), list(refs[n_in : n_in + n_out])
        own = refs[n_in + n_out : n_in + n_out + n_own]
        targets = refs[n_in + n_out + n_own : n_in + n_out + n_own + len(far_in)]
        in_sems, out_sems = refs[-2:]

        def cut(k):
            return ins[k] if args[k].columns is None else ins[k].at[:, 0 : args[k].columns]

        for i, k in enumerate(far_in):
            ins[k] = Arriving(cut(k), targets[i], in_sems.at[i], args[k].parts)
        fetched = [
            Arriving(cut(n_args + i), results[n_made + i], in_sems.at[len(far_in) + i]) for i in range(len(fetch))
        ]
        for i, k in enumerate(far_out):
            results[k] = Leaving(results[k], out_sems.at[i])
        for i in range(len(store)):
            results[n_stored + i].put(ins[n_args + len(fetch) + i])
        if token is not None:
            results[-1][...] = ins[-1][...]
        kernel(*ins[:n_args], *results[:n_made], *own)
        for k in far_in:
            ins[k].get()
        for f in fetched:
            f.get()
        for k in far_out:
            results[k].wait()

    in_specs = []
    for a in args:
        if isinstance(a, Far):
            in_specs.append(FAR)
        else:
            in_specs.append(SCALAR if a.dtype == jnp.int32 else FULL)
    bytes_all = sum(a.size * a.dtype.itemsize for a in arrays)
    bytes_all += sum(jnp.zeros((), o[1]).dtype.itemsize * o[0][0] * o[0][-1] for o in outs)
    return pl.pallas_call(
        body,
        out_shape=[
            pltpu.HBM(o[0], o[1]) if len(o) == 3 else jax.ShapeDtypeStruct(o[0], o[1]) for o in outs
        ],
        in_specs=in_specs,
        out_specs=[FAR if len(o) == 3 else FULL for o in outs],
        scratch_shapes=[pltpu.VMEM(s, d) for s, d in scratch]
        + landing
        + [
            pltpu.SemaphoreType.DMA((max(1, len(far_in) + len(fetch)), PARTS)),
            pltpu.SemaphoreType.DMA((max(1, len(far_out)), PARTS)),
        ],
        compiler_params=pltpu.CompilerParams(vmem_limit_bytes=24 << 20),
        cost_estimate=pl.CostEstimate(flops=flops, bytes_accessed=bytes_all, transcendentals=0),
        name=name,
    )(*placed)


def lane(shape):
    return lax.broadcasted_iota(jnp.int32, shape, 1)


def sub(shape):
    return lax.broadcasted_iota(jnp.int32, shape, 0)


def rows(j, count=M):
    return pl.ds(pl.multiple_of(j * count, count), count)


def tiles(width):
    return [slice(L * k, L * k + L) for k in range(width // L)]


def for_blocks(fn, count=NJ):
    step = UNROLL if isinstance(count, int) and count % UNROLL == 0 else 1

    def body(j, carry):
        for i in range(step):
            fn(j * step + i)
        return carry

    lax.fori_loop(0, count // step, body, 0)


def put_all(stores):
    for ref, span, at, value in stores:
        ref[span, at] = value


def for_blocks_rims(fn):
    group = 5

    def several(first, count, has_prev, has_next):
        stores = []
        for i in range(count):
            stores += fn(first + i, has_prev, has_next)
        put_all(stores)

    def body(g, carry):
        several(group * g + 1, group, True, True)
        return carry

    several(0, 1, False, True)
    lax.fori_loop(0, (NJ - 2) // group, body, 0)
    several(NJ - 1, 1, True, False)


def from_prev(value, rim, flag):
    rim = jnp.concatenate([rim] * (M // 8), axis=0)
    return jnp.where(sub(value.shape) == 0, rim, pltpu.roll(value, 1, 0)) * flag


def from_next(value, rim, flag):
    rim = jnp.concatenate([rim] * (M // 8), axis=0)
    return jnp.where(sub(value.shape) == M - 1, rim, pltpu.roll(value, M - 1, 0)) * flag


def widen(source, out):
    def group(g):
        for at in tiles(source.shape[1]):
            tile = source[rows(g, 8), at]
            for i in range(8):
                out[rows(8 * g + i, 8), at] = jnp.broadcast_to(tile[i : i + 1], (8, L))

    for_blocks(group, NJ // 8)


def mask_bf(cond):
    return jnp.where(cond, 1.0, 0.0).astype(BF)


def fill_rims(cat, parts, low):
    zero = jnp.zeros((M, L), BF)
    cond = mask_bf(low) > 0.5

    def one(j, has_prev, has_next):
        stores = []
        for target, after, before in parts:
            value = cat[rows(j + 1), after : after + L] if has_next else zero
            other = cat[rows(j - 1), before : before + L] if has_prev else zero
            stores.append((cat, rows(j), slice(target, target + L), jnp.where(cond, value, other)))
        return stores

    for_blocks_rims(one)


def rims_1(cat, groups):
    fill_rims(cat, [(rim, base, base + L) for base, rim, _ in groups], lane((M, L)) < 32)


def rims_2(cat):
    fill_rims(cat, [(768 + L * k, 256 * k, 256 * k + L) for k in range(3)], lane((M, L)) < 32)


def rims_0(cat):
    fill_rims(cat, [(512 + L * k, L * k, L * k) for k in range(4)], lane((M, L)) % 32 < 2)


def matmul(left, right, transposed=False):
    return lax.dot_general(
        left, right, (((1,), (1 if transposed else 0,)), ((), ())), preferred_element_type=F32
    )


def quarters(fn):
    for k in range(4):
        fn(slice(R // 4 * k, R // 4 * (k + 1)))


def for_chunks(fn, size=CHUNK):
    def body(r, carry):
        fn(pl.ds(pl.multiple_of(r * size, size), size))
        return carry

    lax.fori_loop(0, R // size, body, 0)


def product_sums(cat, weights, transposed, use, done=None, size=256):
    sums = (jnp.zeros((8, L), F32), jnp.zeros((8, L), F32))

    def part(r, sums):
        rs = rows(r, size)
        value = matmul(cat[rs, :], weights[...], transposed)
        for i in range(size // M):
            for k, at in enumerate(tiles(value.shape[1])):
                if k % 4 == 0:
                    stores = []
                sums = use(r * (size // M) + i, k, at, value[M * i : M * i + M, at], *sums, stores)
                if k % 4 == 3 or k == value.shape[1] // L - 1:
                    put_all(stores)
        if done is not None:
            done(rs)
        return sums

    if done is None:
        sums = lax.fori_loop(0, R // size, part, sums)
    else:
        for r in range(R // size):
            sums = part(r, sums)
    return [total_rows(v) for v in sums]


def sum8(value):
    total = value[0:8]
    for k in range(1, value.shape[0] // 8):
        total = total + value[8 * k : 8 * k + 8]
    return total


def sum_blocks(fn):
    def body(j, carry):
        for i in range(UNROLL):
            carry = fn(j * UNROLL + i, *carry)
        return carry

    zero = jnp.zeros((8, L), F32)
    return [total_rows(s) for s in lax.fori_loop(0, NJ // UNROLL, body, (zero, zero))]


def fold(stats, period):
    step = L // 2
    while step >= period:
        stats = stats + pltpu.roll(stats, step, 1)
        step //= 2
    return stats


def stack_rows(values):
    at = sub((8, L))
    tile = jnp.zeros((8, L), F32)
    for k, value in enumerate(values):
        tile = jnp.where(at == k, value, tile)
    return tile


def total_rows(value):
    return jnp.sum(value, axis=0, keepdims=True)


def norm_terms(moments, count):
    mean = moments[0:1] / count
    return mean, lax.rsqrt(moments[1:2] / count - mean * mean + NORM_EPS)


def silu(v):
    return v / (1.0 + jnp.exp(-v))


def silu_slope(v):
    s = 1.0 / (1.0 + jnp.exp(-v))
    return s * (1.0 + v * (1.0 - s))


def sigmoid(v):
    return 1.0 / (1.0 + jnp.exp(-v))


def softplus(v):
    return jnp.maximum(v, 0.0) + jnp.log1p(jnp.exp(-jnp.abs(v)))


def softplus_slope(r):
    return jnp.where(r < 0.05, r * (1.0 - r * (0.5 - r * (1.0 / 6.0))), 1.0 - jnp.exp(-r))


def end_rows(z, group_out, blocks=NJ):
    def group(g):
        for at in tiles(z.shape[1]):
            place = sub((8, L))
            top = low = jnp.zeros((8, L), F32)
            for i in range(8):
                start = pl.multiple_of((8 * g + i) * M, M)
                top = jnp.where(place == i, z[pl.ds(start, 8), at][0:1], top)
                low = jnp.where(place == i, z[pl.ds(start + M - 8, 8), at][7:8], low)
            group_out(rows(g, 8), at, top, low)

    for_blocks(group, blocks // 8)


def pack_ends(z, index, cross, core, blocks=NJ):
    even = index[1] == 0

    def group_out(rs, at, top, low):
        cross[rs, at] = jnp.where(even, top, low)
        core[rs, at] = jnp.where(even, low, top)

    end_rows(z, group_out, blocks)


def pack_moments(mom, cross, value):
    mom[...] = value
    cross[NJ : NJ + 8, 0:L] = value


def sides(index, cross, core, at):
    even = index[1] == 0
    a, b = cross[0:NJ, at], core[0:NJ, at]
    return jnp.where(even, a, b), jnp.where(even, b, a)


def tile_2(w, tap, q, half):
    at = lane((16, L)) // 32
    tile = jnp.zeros((16, L), F32)
    for k in range(4):
        b = q - 2 * (4 * half + k) + 1
        if 0 <= b < TAPS:
            start = (tap * TAPS + b) * 16
            tile = jnp.where(at == k, w[start : start + 16, :], tile)
    return tile.astype(BF)


def repeat_lanes(w, out):
    for k in range(w.shape[0] // 16):
        span = slice(16 * k, 16 * k + 16)
        out[span, :] = jnp.concatenate([w[span, :].astype(F32)] * (L // 32), axis=1)


def matrix_2_down(narrow, t, w):
    repeat_lanes(narrow, w)
    zero = jnp.zeros((16, L), BF)
    for base, rim, tap in GROUPS1:
        for half in range(2):
            at = slice(L * half, L * half + L)
            for q in range(16):
                t[base + 16 * q : base + 16 * q + 16, at] = tile_2(w, tap, q, half)
            for part in range(8):
                q = {0: 16, 1: 17, 7: -1}.get(part)
                start = rim + 16 * part
                t[start : start + 16, at] = zero if q is None else tile_2(w, tap, q, half)


def matrix_2_up(narrow, t, w):
    repeat_lanes(narrow, w)
    zero = jnp.zeros((16, L), BF)
    at = lane((16, L))
    for row in range(2):
        for k, tap in enumerate((row + 1, row + 3, row - 1)):
            for q in range(16):
                span = slice(row * 256 + q * 16, row * 256 + q * 16 + 16)
                for half in range(2):
                    cols = slice(256 * k + L * half, 256 * k + L * half + L)
                    t[span, cols] = tile_2(w, tap, q, half) if 0 <= tap < TAPS else zero
                rim = zero
                if 0 <= tap < TAPS and q in (0, 1, 15):
                    b = {0: 3, 1: 4, 15: 0}[q]
                    start = (tap * TAPS + b) * 16
                    cond = at < 32 if q == 15 else at >= 96
                    rim = jnp.where(cond, w[start : start + 16, :], 0.0).astype(BF)
                t[span, 768 + L * k : 768 + L * k + L] = rim


def band(w, tap, channel, offset):
    tile = jnp.zeros((32, L), F32)
    for b in range(TAPS):
        start = (tap * TAPS + b) * 2 + channel
        tile = jnp.where(offset == b, w[start : start + 1, :], tile)
    return tile.astype(BF)


def matrix_1_down(w, t, col):
    q, zero = sub((32, L)), jnp.zeros((32, L), BF)
    for half in range(2):
        p = 8 * half + lane((32, L)) // 16
        inner = q - 2 * p + 1
        rim = jnp.where(q == 31, -2 * p, jnp.where(q == 0, 33 - 2 * p, jnp.where(q == 1, 34 - 2 * p, -9)))
        for row in range(2):
            cols = slice(col + row * 256 + half * L, col + row * 256 + half * L + L)
            for part, frame in enumerate((0, 1, 2, 3, None, -1, 4, 5)):
                tap = -1 if frame is None else frame - 2 * row + 1
                for c in range(2):
                    start = part * 64 + c * 32
                    ok = 0 <= tap < TAPS
                    t[start : start + 32, cols] = band(w, tap, c, inner) if ok else zero
                    t[512 + start : 544 + start, cols] = band(w, tap, c, rim) if ok else zero


def matrix_1_up(w, t, col):
    q, zero = sub((32, L)), jnp.zeros((32, L), BF)
    at = lane((32, L))
    rim = jnp.where(at < 16, q - 31, jnp.where(at >= 112, q + 3, -9))
    for frame in range(4):
        taps = (frame + 1, frame - 1, frame + 3, frame - 3)
        for c in range(2):
            span = slice(frame * 64 + c * 32, frame * 64 + c * 32 + 32)
            for k, tap in enumerate(taps):
                ok = 0 <= tap < TAPS
                for half in range(2):
                    p = 8 * half + at // 16
                    start = col + 256 * k + L * half
                    t[span, start : start + L] = band(w, tap, c, q - 2 * p + 1) if ok else zero
                start = col + 1024 + L * k
                t[span, start : start + L] = band(w, tap, c, rim) if ok else zero


def window_0(w1c, t):
    matrix_1_down(w1c, t, 0)


def window_1(w2c, t, w):
    matrix_2_down(w2c, t, w)


def window_2(w2d, t, w):
    matrix_2_up(w2d, t, w)


def window_3(w1d, t):
    matrix_1_up(w1d.at[0], t, 0)
    matrix_1_up(w1d.at[1], t, COLS1B)


def window_swap(w2d, out, t, w):
    matrix_2_down(w2d, t, w)
    out.put(t)


def correlate(coarse, fine, d):
    for k in range(R // CHUNK):
        span = slice(CHUNK * k, CHUNK * k + CHUNK)
        left, right = ready(coarse, k), ready(fine, k)
        value = lax.dot_general(
            left[span, :], right[span, :], (((0,), (0,)), ((), ())), preferred_element_type=F32
        )
        d[...] = value if k == 0 else d[...] + value


def weight_2(d, out):
    at = lane((32, L))
    sums = {}
    for base, rim, tap in GROUPS1:
        total = jnp.zeros((32, L), F32)
        for p in range(8):
            span = slice(32 * p, 32 * p + 32)
            parts = [d[span, base : base + L], d[span, base + L : base + 256], d[span, rim : rim + L]]
            if p == 0:
                value = jnp.where(at < 16, pltpu.roll(parts[2], 16, 1), pltpu.roll(parts[0], 16, 1))
            else:
                which, off = divmod(32 * p - 16, L)
                value = pltpu.roll(parts[which], L - off, 1)
                if off + 80 > L:
                    value = jnp.where(at < L - off, value, pltpu.roll(parts[which + 1], L - off, 1))
            total = total + value
        sums[tap] = total
    out[0:32, :] = jnp.where(at < 80, sums[0], pltpu.roll(sums[4], 80, 1))
    out[32:64, :] = jnp.where(at < 80, sums[1], pltpu.roll(sums[4], 32, 1))
    out[64:96, :] = sums[2]
    out[96:128, :] = sums[3]


def weight_1(d, out, start):
    at = lane((16, L)) % 32
    result = jnp.zeros((16, L), F32)
    for k in range(3):
        total = jnp.zeros((16, L), F32)
        for row in range(2):
            tile = (2, 0, 1)[k] if row == 0 else (0, 1, 3)[k]
            for p in range(16):
                first = row * 256 + p * 16
                span = slice(first, first + 16)
                value = pltpu.roll(d[span, L * tile : L * tile + L], (1 - 2 * p) % L, 1)
                if p in (0, 15):
                    rim = d[span, 512 + L * tile : 512 + L * tile + L]
                    rim = pltpu.roll(rim, L - 31 if p == 0 else 3, 1)
                    value = jnp.where(at == 0 if p == 0 else at >= 3, rim, value)
                total = total + value
        if k > 0:
            total = pltpu.roll(total, 8 * k, 1)
        result = jnp.where((at >= 8 * k) & (at < 8 * k + TAPS), total, result)
    out[start : start + 16, :] = result


def window_4(low, act, fine, out, d, kept):
    correlate(low, fine, d)
    weight_1(d, kept, 0)
    correlate(act, fine, d)
    weight_1(d, kept, 16)
    out.put(kept)


def window_5(coarse, fine, w2c, t, out, d, w, kept):
    matrix_2_up(w2c, t, w)
    correlate(coarse, fine, d)
    weight_2(d, kept)
    out.put(kept)


HALF = 144


def window_6(index, coarse, fine, w1c, w1d, w2d, t, keep, give, d, kept):
    matrix_1_up(w1c, t, 0)
    correlate(coarse, fine, d)
    weight_2(d, kept)
    even = index[1] == 0
    up_two, up_one = ready(w2d), ready(w1d)

    def place(span, a, b):
        keep[span, :] = jnp.where(even, a, b)
        give[span, :] = jnp.where(even, b, a)

    place(slice(0, 128), up_two[...], kept[...])
    place(slice(128, 144), up_one[0:16, :], up_one[16:32, :])


def window_7(coarse, fine, keep, got, bias, low, d, first):
    correlate(coarse, fine, d)
    weight_1(d, first, 0)
    low[0:HALF, :] = (keep[...] + got[...]).astype(BF)
    low[HALF : HALF + 16, :] = first[...].astype(BF)
    low[HALF + 16 : HALF + 32, :] = jnp.concatenate([bias[...], jnp.zeros((8, L), F32)]).astype(BF)


def unpack_kernel(index, mine, other, w1c, w2c, w2d, w1d, bias):
    even = index[1] == 0
    a, b = mine[...], other[...]
    up, down = jnp.where(even, a, b), jnp.where(even, b, a)
    own = a[HALF:] + b[HALF:]
    for half, out in ((up, w2d), (down, w2c)):
        turned = half[0:128].T
        moved = [turned] + [pltpu.roll(turned, L - 32 * tap, 1) for tap in range(1, 4)]
        for tap in range(TAPS):
            for b in range(TAPS):
                if tap < 4:
                    value = moved[tap][16 * b : 16 * b + 16]
                else:
                    value = moved[b // 3][80 + 16 * (b % 3) : 96 + 16 * (b % 3)]
                out[tap * TAPS + b] = value[:, 0:32]
    tall = jnp.concatenate([up[128:144], down[128:144], own[0:16], jnp.zeros((80, L), F32)]).T
    other_tall = pltpu.roll(tall, L - 32, 1)
    for tap in range(TAPS):
        for b in range(TAPS):
            for c in range(2):
                row = (tap + 1) % 2 * 64 + c * 32 + (tap + 1) // 2 * 8 + b
                w1d[tap * TAPS + b, c : c + 1, :] = tall[row : row + 1, 0:32]
                w1c[tap * TAPS + b, c : c + 1, :] = other_tall[row : row + 1, 0:16]
    total = total_rows(own[16:24])
    total = jnp.broadcast_to(total, (8, L))
    total = total + pltpu.roll(total, 64, 1)
    for step in (16, 8, 4, 2, 1):
        total = total + pltpu.roll(total, L - step, 1)
    bias[...] = jnp.where(lane((8, L)) == 0, total, pltpu.roll(total, L - 31, 1))


def ready(ref, part=None):
    return ref.get(part) if isinstance(ref, Arriving) else ref


def spread(scr, store):
    at = lane((M, L)) // 32
    for half in range(2):
        parts = [scr[k % 2, pl.ds(2 * half + k // 2, M, stride=4), :] for k in range(4)]
        for block in range(4):
            value = parts[block]
            for k in range(4):
                if k != block:
                    value = jnp.where(at == k, pltpu.roll(parts[k], (32 * (k - block)) % L, 1), value)
            store(block, half, value)


def gather(blocks, scr):
    at = lane((M, L)) // 32
    for half in range(2):
        parts = [blocks(block, half) for block in range(4)]
        for k in range(4):
            value = parts[k]
            for block in range(4):
                if block != k:
                    value = jnp.where(
                        at == block, pltpu.roll(parts[block], (32 * (block - k)) % L, 1), value
                    )
            scr[k % 2, pl.ds(2 * half + k // 2, M, stride=4), :] = value


def layout_kernel(index, frame_mask, mix, cot, cross, core, x0, c0, scr, wide, ends):
    def place(out, block, row):
        def store(k, half, value):
            at = slice(L * half, L * half + L)
            out[rows(block + k), at] = value.astype(BF)
            wide[rows(row + k), at] = value

        return store

    m = mix.get()

    def mix_tile(t):
        for c in range(2):
            scr[c] = m[c, :, pl.ds(pl.multiple_of(t * L, L), L)].astype(F32)
        spread(scr, place(x0, 4 * t, 4 * t))

    for_blocks(mix_tile, NJ // 4)
    g = cot.get()
    per_stem = g.shape[3] // L

    def cot_tile(t):
        for c in range(2):
            lanes = pl.ds(pl.multiple_of((t % per_stem) * L, L), L)
            scr[c] = g[t // per_stem, c, :, lanes].astype(F32)
        spread(scr, place(c0, 4 * t, NJ + 4 * t))

    for_blocks(cot_tile, NJ // 4)
    ends[...] = jnp.zeros(ends.shape, F32)
    pack_ends(wide, index, ends.at[0], ends.at[1], 2 * NJ)
    even = index[1] == 0

    def least(first, count):
        value = frame_mask[first]
        for k in range(1, count):
            value = jnp.minimum(value, frame_mask[first + k])
        return value.astype(F32)

    for i, (first, count) in enumerate(((0, 2), (2, 2), (0, 4))):
        top, low = least(first, count), least(4 * M - 4 + first, count)
        row = 2 * NJ + i
        ends[0, row : row + 1, :] = jnp.full((1, 2 * L), jnp.where(even, top, low))
        ends[1, row : row + 1, :] = jnp.full((1, 2 * L), jnp.where(even, low, top))
    cross[...] = ends[0].astype(BF)
    core[...] = ends[1].astype(BF)


def columns_0(cat, blocks, read, left, right, aux):
    a, a_next = aux[0], aux[1]
    for which, (first, count) in enumerate(blocks):

        def one(i, which=which, first=first):
            j = first + i
            span, stores = rows(j), []
            for half in range(2):
                value = read(which, j, half)
                stores.append((cat, span, slice(L * half, L * half + L), value.astype(BF)))
                if half == 1:
                    moved = from_prev(value, left[rows(j, 8), L : 2 * L], a)
                    stores.append((cat, span, slice(256, 384), moved.astype(BF)))
                else:
                    moved = from_next(value, right[rows(j, 8), 0:L], a_next)
                    stores.append((cat, span, slice(384, 512), moved.astype(BF)))
            put_all(stores)

        for_blocks(one, count)
    rims_0(cat)


def conv_one_kernel(
    index, x0, cross_in, core_in, aux, t,
    cross, core, mom, kept, hx, cat, zfar, z, lf, rf, lw, rw,
):
    even = index[1] == 0
    a, b = cross_in[...].astype(F32), core_in[...].astype(F32)
    lf[...] = jnp.where(even, a, b)
    rf[...] = jnp.where(even, b, a)
    hx[:, 0:L] = rf[0 : 2 * NJ, 0:L]
    hx[:, L : 2 * L] = lf[0 : 2 * NJ, L : 2 * L]
    kept[...] = jnp.zeros(kept.shape, F32)
    kept[0:3, :] = lf[2 * NJ : 2 * NJ + 3, 0:L]
    kept[3:6, :] = rf[2 * NJ : 2 * NJ + 3, 0:L]
    widen(lf.at[0:NJ], lw)
    widen(rf.at[0:NJ], rw)
    x = ready(x0)
    read = lambda which, j, h: x[rows(j), L * h : L * h + L].astype(F32)
    columns_0(cat, [(0, NJ)], read, lw, rw, aux)
    weights = ready(t)

    def use(j, k, at, value, s1, s2, stores):
        stores.append((z, rows(j), at, value))
        part = value * aux[2 + k // 2]
        return s1 + sum8(part), s2 + sum8(part * value)

    stats = product_sums(cat, weights, False, use, lambda rs: zfar.put(z, (rs, slice(None))))
    pack_ends(z, index, cross, core)
    stats = fold(stack_rows(stats), 16)
    at = sub((8, L))
    stats = jnp.where(at == 2, total_rows(aux[2] + aux[3]) * (NJ * 16.0), stats)
    stats = jnp.where(at == 3, total_rows(aux[4]) * (NJ * 8.0), stats)
    pack_moments(mom, cross, stats)


def conv_two_kernel(
    index, z1, cross_in, core_in, mom1, prm, aux, t,
    cross, core, mom, eb, hf, zfar, catfar, z2, cat, ef, lw, rw,
):
    mean, scale = norm_terms(mom1, mom1[2:3])
    gain, shift = prm[0:1], prm[1:2]

    def act(value):
        return silu((value - mean) * scale * gain + shift)

    a, a_next = aux[0], aux[1]
    for at in tiles(512):
        left, right = sides(index, cross_in, core_in, at)
        hf[0, :, at] = left
        hf[1, :, at] = right
        ef[0, :, at] = act(left)
        ef[1, :, at] = act(right)
    widen(ef.at[0], lw)
    widen(ef.at[1], rw)

    def one(j):
        span, stores = rows(j), []
        for k, at in enumerate(tiles(512)):
            value = act(z1[span, at])
            stores.append((cat, span, at, value.astype(BF)))
            if k >= 2:
                moved = from_prev(value, lw[rows(j, 8), at], a)
                stores.append((cat, span, slice(256 + L * k, 384 + L * k), moved.astype(BF)))
            start = 768 + L * k if k < 2 else 1280 + L * k
            moved = from_next(value, rw[rows(j, 8), at], a_next)
            stores.append((cat, span, slice(start, start + L), moved.astype(BF)))
        put_all(stores)

    for_blocks(one)
    catfar.put(cat, (slice(None), slice(0, 1024)))
    catfar.put(cat, (slice(None), slice(1536, 1792)))
    rims_1(cat, GROUPS1)
    catfar.put(cat, (slice(None), slice(1024, 1536)))
    catfar.put(cat, (slice(None), slice(1792, 1920)))
    def group_out(rs, at, top, low):
        ef[2, rs, at] = act(top)
        ef[3, rs, at] = act(low)

    end_rows(z1, group_out)
    eb[...] = ef[...].astype(BF)
    weights = ready(t)

    def use(j, k, at, value, s1, s2, stores):
        stores.append((z2, rows(j), at, value))
        part = value * aux[4]
        return s1 + sum8(part), s2 + sum8(part * value)

    stats = product_sums(cat, weights, False, use, lambda rs: zfar.put(z2, (rs, slice(None))))
    pack_ends(z2, index, cross, core)
    pack_moments(mom, cross, fold(stack_rows(stats), 32))


def columns_2(cat, read, left, right, aux):
    a, a_next = aux[0], aux[1]

    def one(j):
        span, stores = rows(j), []
        for k, at in enumerate(tiles(256)):
            value = read(j, at)
            stores.append((cat, span, at, value.astype(BF)))
            moved = from_prev(value, left[rows(j, 8), at], a)
            stores.append((cat, span, slice(256 + L * k, 384 + L * k), moved.astype(BF)))
            moved = from_next(value, right[rows(j, 8), at], a_next)
            stores.append((cat, span, slice(512 + L * k, 640 + L * k), moved.astype(BF)))
        put_all(stores)

    for_blocks(one)
    rims_2(cat)


def up_two_kernel(
    index, z2, cross_in, core_in, mom1, mom2, prm, aux, t,
    cross, core, mom, hf, act2, rectfar, rect, cat, lf, rf, lw, rw,
):
    mean, scale = norm_terms(mom2, mom1[3:4])
    gain, shift, bias = prm[2:3], prm[3:4], prm[6:7]

    def act(value):
        return silu((value - mean) * scale * gain + shift)

    for at in tiles(256):
        left, right = sides(index, cross_in, core_in, at)
        hf[0, :, at] = left
        hf[1, :, at] = right
        lf[:, at] = act(left)
        rf[:, at] = act(right)
    widen(lf, lw)
    widen(rf, rw)
    columns_2(cat, lambda j, at: act(z2[rows(j), at]), lw, rw, aux)
    act2[...] = cat[:, 0:256]
    weights = ready(t)

    def use(j, k, at, value, s1, s2, stores):
        value = softplus(value + bias)
        stores.append((rect, rows(j), at, value))
        part = value * aux[2 + k // 2]
        return s1 + sum8(part), s2 + sum8(part * value)

    stats = product_sums(cat, weights, True, use, lambda rs: rectfar.put(rect, (rs, slice(None))))
    pack_moments(mom, cross, fold(stack_rows(stats), 16))
    pack_ends(rect, index, cross, core)


def columns_1b(cat, read, left, right, aux):
    a, a_next = aux[0], aux[1]

    def one(j):
        span, stores = rows(j), []
        for k, at in enumerate(tiles(512)):
            value = read(j, k, at)
            stores.append((cat, span, at, value.astype(BF)))
            if k >= 2:
                moved = from_prev(value, left[rows(j, 8), at], a)
                stores.append((cat, span, slice(256 + L * k, 384 + L * k), moved.astype(BF)))
            else:
                moved = from_next(value, right[rows(j, 8), at], a_next)
                stores.append((cat, span, slice(768 + L * k, 896 + L * k), moved.astype(BF)))
        put_all(stores)

    for_blocks(one)
    rims_1(cat, GROUPS1[:4])


def edge_columns(own, prev, after):
    at = lane((NJ, L))
    place = sub((NJ, L))
    parts = [own, prev, after]
    groups = [own[:, 0:256], own[:, 256:512], prev, after]
    for g in groups:
        low = jnp.where((place == NJ - 1) | (at >= 32), 0.0, pltpu.roll(g[:, 0:L], NJ - 1, 0))
        high = jnp.where((place == 0) | (at < 112), 0.0, pltpu.roll(g[:, L : 2 * L], 1, 0))
        parts.append(low + high)
    return jnp.concatenate(parts, axis=1).astype(BF)


def quarter_blocks(index, stems):
    count = NJ // stems
    return [((index[0] ^ k) * count, count) for k in range(stems)]


def up_one_kernel(
    index, rect, cross_in, core_in, mom1, mom3, prm, aux, ends1, cat1, t,
    m0, m1, m2, m3, hf, low3, sf, shf, cat, lf, rf, ef, ff, lw, rw,
):
    mean, scale = norm_terms(mom3, mom1[2:3])
    gain, shift, bias = prm[4:5], prm[5:6], prm[7:8]

    def norm(value):
        return (value - mean) * scale * gain + shift

    for at in tiles(512):
        left, right = sides(index, cross_in, core_in, at)
        hf[0, :, at] = left
        hf[1, :, at] = right
        lf[:, at] = norm(left)
        rf[:, at] = norm(right)
    widen(lf, lw)
    widen(rf, rw)
    columns_1b(cat, lambda j, k, at: norm(rect[rows(j), at]), lw, rw, aux)
    low3[...] = cat[:, 0:512]

    def group_out(rs, at, top, low):
        ef[0, rs, at] = norm(top)
        ef[1, rs, at] = norm(low)

    end_rows(rect, group_out)
    wide = jnp.concatenate([bias, bias], axis=1)
    zero = jnp.zeros((NJ, 256), F32)
    a, a_end = aux[0, 0:1, 0:1], aux[1, M - 1 : M, 0:1]
    e1 = [ends1[k].astype(F32) for k in range(4)]
    edges = [
        (
            edge_columns(lf[...], zero, ef[0, :, 0:256] * a),
            edge_columns(e1[0], zero, e1[2][:, 0:256] * a),
        ),
        (
            edge_columns(rf[...], ef[1, :, 256:512] * a_end, zero),
            edge_columns(e1[1], e1[3][:, 256:512] * a_end, zero),
        ),
    ]
    weights, other = ready(t), ready(cat1)
    value = matmul(jnp.concatenate([e[0] for e in edges]), weights[:, 0:COLS1B], True)
    value = value + matmul(jnp.concatenate([e[1] for e in edges]), weights[:, COLS1B : 2 * COLS1B], True)
    for k, half in ((0, 1), (1, 0)):
        at = slice(L * half, L * half + L)
        shf[:, at] = sigmoid(value[NJ * k : NJ * k + NJ, at] + bias)
    masks = (m0, m1, m2, m3)
    per = R // len(masks)
    for mask, (first, count) in zip(masks, quarter_blocks(index, len(masks))):
        rs = rows(lax.div(first, count), per)
        value = matmul(cat[rs, :], weights[:, 0:COLS1B], True)
        value = value + matmul(other[rs, :], weights[:, COLS1B : 2 * COLS1B], True)
        value = sigmoid(value + wide)
        sf[rs, :] = value
        mask[0:per, :] = value.astype(BF)
        ff[...] = jnp.zeros(ff.shape, F32)
        ff[0:count, :] = shf[rows(lax.div(first, count), count), :]
        mask[per : per + 16, :] = ff[...].astype(BF)


def ratio_terms(masks):
    squares = [m * m for m in masks]
    power = squares[0]
    for s in squares[1:]:
        power = power + s
    inverse = 1.0 / (power + RATIO_EPS)
    return [s * inverse for s in squares], inverse


def mask_back(masks, cots, mix):
    ratios, inverse = ratio_terms(masks)
    direct = cots[0] * ratios[0]
    for c, r in zip(cots[1:], ratios[1:]):
        direct = direct + c * r
    common = 2.0 * mix * inverse
    return [m * common * (c - direct) for m, c in zip(masks, cots)], direct


def mask_kernel(index, m0, m1, m2, m3, c0, x0, hx, g0, g1, g2, g3, df, ff):
    masks, grads = (m0, m1, m2, m3), (g0, g1, g2, g3)
    stems = len(masks)
    per, blocks = R // stems, NJ // stems
    mine = index[0]
    cots, mix, rim = ready(c0), ready(x0), ready(hx)

    def one(j):
        for at in tiles(256):
            m = [masks[s][rows(j), at].astype(F32) for s in range(stems)]
            c = [cots[rows((mine ^ s) * blocks + j), at].astype(F32) for s in range(stems)]
            x = mix[rows(mine * blocks + j), at].astype(F32)
            values, own = mask_back(m, c, x)
            df[rows(j), at] = own
            for s in range(stems):
                grads[s][rows(j), at] = values[s].astype(BF)

    for_blocks(one, blocks)
    m = [masks[s][per : per + 16, :].astype(F32)[0:blocks] for s in range(stems)]
    c = [rim[rows(stems + (mine ^ s), blocks), :] for s in range(stems)]
    values, _ = mask_back(m, c, rim[rows(mine, blocks), :])
    for s in range(stems):
        ff[...] = jnp.zeros(ff.shape, F32)
        ff[0:blocks, :] = values[s]
        grads[s][per : per + 16, :] = ff[...].astype(BF)


def estimate_kernel(index, m0, m1, m2, m3, x0, w1d, out, t, scr, est):
    masks = (m0, m1, m2, m3)
    stems = len(masks)
    blocks = NJ // stems
    mine = index[0]
    matrix_1_down(w1d.at[0], t, 0)
    matrix_1_down(w1d.at[1], t, 512)
    mix = ready(x0)

    def one(j):
        for at in tiles(256):
            m = [masks[s][rows(j), at].astype(F32) for s in range(stems)]
            x = mix[rows(mine * blocks + j), at].astype(F32)
            ratios, _ = ratio_terms(m)
            for s in range(stems):
                est[s, rows(j), at] = x * ratios[s]

    for_blocks(one, blocks)
    for s in range(stems):
        for t in range(blocks // 4):
            gather(
                lambda block, half, s=s, t=t: est[s, rows(4 * t + block), L * half : L * half + L], scr
            )
            for c in range(2):
                out[mine ^ s, c, :, L * t : L * t + L] = scr[c].astype(BF)


def down_one_back_kernel(
    index, q0, q1, q2, q3, sigh, sig, aux, mom1, mom3, rect, t,
    g3, cat, cross, core, mom, bias, gf, hf, zf, hw,
):
    grads = (q0, q1, q2, q3)
    blocks = quarter_blocks(index, len(grads))
    per = R // len(grads)
    rim = ready(sigh)
    for grad, (first, count) in zip(grads, blocks):
        span = rows(lax.div(first, count), count)
        value = grad[per : per + 16, :].astype(F32)[0:count]
        own = rim[span, :]
        hf[span, :] = value * own * (1.0 - own)
    zf[...] = jnp.zeros(zf.shape, F32)
    widen(hf, hw)
    sigs = ready(sig)

    def read(which, j, half):
        at = slice(L * half, L * half + L)
        own = sigs[rows(j), at]
        value = grads[which][rows(j - blocks[which][0]), at].astype(F32) * own * (1.0 - own)
        zf[...] = zf[...] + sum8(value)
        return value

    columns_0(cat, blocks, read, hw, hw, aux)
    bias[...] = zf[...]
    weights = ready(t)

    mean, scale = norm_terms(mom3, mom1[2:3])
    r = ready(rect)

    def use(j, k, at, value, s1, s2, stores):
        if k >= 4:
            stores.append((gf, rows(j), slice(L * k - 512, L * k - 384), value))
            return s1, s2
        stores.append((g3, rows(j), at, value))
        return s1 + sum8(value), s2 + sum8(value * (r[rows(j), at] - mean))

    s1, s2 = product_sums(cat, weights, False, use)
    pack_ends(g3, index, cross, core)
    pack_moments(mom, cross, fold(stack_rows([s1, s2 * scale]), 16))


def norm_back(g, xhat, kept, moments, count, factor):
    return factor * (g - kept * ((moments[0:1] + xhat * moments[1:2]) / count))


def up_two_back_kernel(
    index, g3, cross_in, core_in, mom4, mom1, mom3, mom2, prm, aux, kept, rect, h3, t, z2,
    g2, cat, cross, core, mom, lf, rf, lw, rw,
):
    count = mom1[2:3]
    mean, scale = norm_terms(mom3, count)
    factor = scale * prm[4:5]
    inverse = 1.0 / count

    def back(g, r, keep):
        xhat = (r - mean) * scale
        value = factor * (g - keep * ((mom4[0:1] + xhat * mom4[1:2]) * inverse))
        return value * softplus_slope(r)

    r, h = ready(rect), ready(h3)
    for k, at in enumerate(tiles(512)):
        left, right = sides(index, cross_in, core_in, at)
        row = k // 2
        lf[:, at] = back(left, h[0, :, at], kept[row : row + 1, :])
        rf[:, at] = back(right, h[1, :, at], kept[3 + row : 4 + row, :])
    widen(lf, lw)
    widen(rf, rw)
    a, a_next = aux[0], aux[1]

    def one(j, total):
        span, stores = rows(j), []
        for k, at in enumerate(tiles(512)):
            value = back(g3[span, at], r[span, at], aux[2 + k // 2])
            total = total + sum8(value)
            stores.append((cat, span, at, value.astype(BF)))
            if k >= 2:
                moved = from_prev(value, lw[rows(j, 8), at], a)
                stores.append((cat, span, slice(256 + L * k, 384 + L * k), moved.astype(BF)))
            start = 768 + L * k if k < 2 else 1280 + L * k
            moved = from_next(value, rw[rows(j, 8), at], a_next)
            stores.append((cat, span, slice(start, start + L), moved.astype(BF)))
        put_all(stores)
        return total

    def four(j, total):
        for i in range(UNROLL):
            total = one(j * UNROLL + i, total)
        return total

    bias = lax.fori_loop(0, NJ // UNROLL, four, jnp.zeros((8, L), F32))
    rims_1(cat, GROUPS1)
    weights = ready(t)

    mean2, scale2 = norm_terms(mom2, mom1[3:4])
    gain, shift = prm[2:3], prm[3:4]
    z = ready(z2)

    def use(j, k, at, value, s1, s2, stores):
        xhat = (z[rows(j), at] - mean2) * scale2
        value = value * silu_slope(xhat * gain + shift)
        stores.append((g2, rows(j), at, value))
        return s1 + sum8(value), s2 + sum8(value * xhat)

    stats = fold(stack_rows(product_sums(cat, weights, False, use)), 32)
    pack_ends(g2, index, cross, core)
    bias = fold(stack_rows([total_rows(bias)] * 3), 16)
    pack_moments(mom, cross, jnp.where(sub((8, L)) == 2, bias, stats))


def down_two_back_kernel(
    index, g2, cross_in, core_in, mom5, mom1, mom2, prm, aux, kept, z2, h2, t, gact, z1,
    g1, low2, cross, core, mom, cat, lf, rf, lw, rw,
):
    count = mom1[3:4]
    mean, scale = norm_terms(mom2, count)
    factor = scale * prm[2:3]
    inverse = 1.0 / count

    def back(g, z, keep):
        xhat = (z - mean) * scale
        return factor * (g - keep * ((mom5[0:1] + xhat * mom5[1:2]) * inverse))

    z, h = ready(z2), ready(h2)
    for at in tiles(256):
        left, right = sides(index, cross_in, core_in, at)
        lf[:, at] = back(left, h[0, :, at], kept[2:3, :])
        rf[:, at] = back(right, h[1, :, at], kept[5:6, :])
    widen(lf, lw)
    widen(rf, rw)
    columns_2(cat, lambda j, at: back(g2[rows(j), at], z[rows(j), at], aux[4]), lw, rw, aux)
    low2[...] = cat[:, 0:256]
    weights, added = ready(t), ready(gact)

    mean1, scale1 = norm_terms(mom1, mom1[2:3])
    gain, shift = prm[0:1], prm[1:2]
    z = ready(z1)

    def use(j, k, at, value, s1, s2, stores):
        xhat = (z[rows(j), at] - mean1) * scale1
        value = (value + added[rows(j), at]) * silu_slope(xhat * gain + shift)
        stores.append((g1, rows(j), at, value))
        return s1 + sum8(value), s2 + sum8(value * xhat)

    stats = fold(stack_rows(product_sums(cat, weights, True, use)), 16)
    pack_ends(g1, index, cross, core)
    pack_moments(mom, cross, stats)


def up_one_back_kernel(
    index, g1, cross_in, core_in, mom6, mom1, prm, aux, kept, z1, h1, t,
    n0, n1, n2, n3, low1, cat, lf, rf, lw, rw,
):
    count = mom1[2:3]
    mean, scale = norm_terms(mom1, count)
    factor = scale * prm[0:1]
    inverse = 1.0 / count

    def back(g, z, keep):
        xhat = (z - mean) * scale
        return factor * (g - keep * ((mom6[0:1] + xhat * mom6[1:2]) * inverse))

    z, h = ready(z1), ready(h1)
    for k, at in enumerate(tiles(512)):
        left, right = sides(index, cross_in, core_in, at)
        row = k // 2
        lf[:, at] = back(left, h[0, :, at], kept[row : row + 1, :])
        rf[:, at] = back(right, h[1, :, at], kept[3 + row : 4 + row, :])
    widen(lf, lw)
    widen(rf, rw)
    columns_1b(
        cat, lambda j, k, at: back(g1[rows(j), at], z[rows(j), at], aux[2 + k // 2]), lw, rw, aux
    )
    low1[...] = cat[:, 0:512]
    weights = ready(t)
    nets = (n0, n1, n2, n3)
    per = R // len(nets)
    for net, (first, blocks) in zip(nets, quarter_blocks(index, len(nets))):
        rs = rows(lax.div(first, blocks), per)
        net[...] = matmul(cat[rs, :], weights[...], True).astype(BF)


def mixture_kernel(p0, p1, p2, p3, direct, out, scr):
    parts = (p0, p1, p2, p3)
    own = ready(direct)

    def tile(t):
        def block(k, half):
            at = slice(L * half, L * half + L)
            value = own[rows(4 * t + k), at]
            for part in parts:
                value = value + part[rows(4 * t + k), at].astype(F32)
            return value

        gather(block, scr)
        for c in range(2):
            out[c, :, pl.ds(pl.multiple_of(t * L, L), L)] = scr[c]

    for_blocks(tile, NJ // len(parts) // 4)


def pairs(count, offset):
    there = [(i, (i + offset) % count) for i in range(0, count, 2)]
    return there + [(b, a) for a, b in there]


def flip(values, axis, bit):
    return lax.ppermute(values, axis, [(i, i ^ bit) for i in range(lax.axis_size(axis))])


def sum_over(values, axis):
    count = lax.axis_size(axis)
    if count & (count - 1):
        return lax.psum(values, axis)
    step = 1
    while step < count:
        radix = 2 if step == 1 or count // step == 2 else 4
        moved = [flip(values, axis, step * k) for k in range(1, radix)]
        for m in moved:
            values = values + m
        step *= radix
    return values


def sum_chips(low, axis, beside):
    count = lax.axis_size(axis)
    if count == 8:
        moved = [flip(low, axis, bit) for bit in (2, 4, 6)]
        made, low = beside(low)
        mine = low.astype(F32) + moved[0].astype(F32) + moved[1].astype(F32) + moved[2].astype(F32)
    else:
        made, low = beside(low)
        mine, step = low.astype(F32), 2
        while step < count:
            mine = mine + flip(mine, axis, step)
            step *= 2
    return mine, flip(mine, axis, 1), made


def exchange(cross, core, mom, axis, beside):
    count = lax.axis_size(axis)
    near = lax.ppermute(cross, axis, pairs(count, -1))
    if count == 8:
        far = lax.ppermute(mom, axis, pairs(count, 3))
        across = flip(mom, axis, 4)
        inside = flip(core, axis, 1)
        *made, mom = beside(mom)
        part = mom + near[NJ:, 0:L] + far + across
        return near, inside, part + flip(part, axis, 1), made
    inside = flip(core, axis, 1)
    *made, mom = beside(mom)
    return near, inside, sum_over(mom, axis), made


def swap(blocks, axis):
    return [blocks[0]] + [flip(blocks[k], axis, k) for k in range(1, len(blocks))]


def flags(seg_lengths, frame_mask, position, total):
    order = jnp.arange(seg_lengths.shape[0])
    earlier = order[None, :] < order[:, None]
    starts = 4 * jnp.sum(jnp.where(earlier, seg_lengths[None, :], 0), axis=1)
    frames = (position * M + jnp.arange(M + 1, dtype=jnp.int32)) * 4
    shut = jnp.any(frames[:, None] == starts[None, :], axis=1) | (frames == total)
    a = 1.0 - shut.astype(F32)
    keep_one = jnp.min(frame_mask.reshape(M, 2, 2), axis=2).astype(F32)
    keep_two = jnp.min(frame_mask.reshape(M, 4), axis=1).astype(F32)
    columns = jnp.stack([a[:M], a[1:], keep_one[:, 0], keep_one[:, 1], keep_two])
    return jnp.broadcast_to(columns[:, :, None], (5, M, L))


def per_device(
    mixture,
    seg_lengths,
    frame_mask,
    conv_first,
    encoder_gain_vector,
    shift_first,
    conv_second,
    gain_second,
    shift_second,
    deconv_second,
    bias_second,
    decoder_gain_vector,
    shift_third,
    deconv_first,
    bias_first,
    cotangent,
):
    position = lax.axis_index("tm")
    stems = lax.axis_size("stem")
    odd = position % 2
    index = jnp.stack([lax.axis_index("stem"), odd]).astype(jnp.int32)
    frames = mixture.shape[1]
    per, blocks = R // stems, NJ // stems
    aux = flags(seg_lengths, frame_mask, position, frames * lax.axis_size("tm"))
    prm = jnp.stack(
        [
            jnp.tile(encoder_gain_vector[0], 8),
            jnp.tile(shift_first[0], 8),
            jnp.tile(gain_second[0], 4),
            jnp.tile(shift_second[0], 4),
            jnp.tile(decoder_gain_vector[0], 8),
            jnp.tile(shift_third[0], 8),
            jnp.tile(bias_second[0], 8),
            jnp.tile(jnp.repeat(bias_first[0], 32), 2),
        ]
    )
    w1c = jnp.tile(conv_first[0].transpose(2, 3, 1, 0).reshape(50, 16).astype(F32), (1, 8))
    w1d = deconv_first[0].transpose(2, 3, 0, 1).reshape(50, 2, 16).astype(F32)
    w1d = jnp.tile(w1d.transpose(1, 0, 2), (1, 1, 8))
    w2c = conv_second[0].transpose(2, 3, 1, 0).reshape(400, 32)
    w2d = deconv_second[0].transpose(2, 3, 0, 1).reshape(400, 32)
    edge = 2 * NJ + 16

    def packet(lanes):
        return [((NJ + 8, lanes), F32), ((NJ, lanes), F32), ((8, L), F32)]

    def rim(lanes):
        return [((NJ, lanes), F32)] * 2

    def wide(lanes):
        return [((8 * NJ, lanes), F32)] * 2

    def far(*shape, kind=F32):
        return [(shape, kind, True)]

    cross, core, x0, c0 = run(
        layout_kernel,
        "layout",
        [((edge, 256), BF), ((edge, 256), BF), ((R, 256), BF), ((R, 256), BF)],
        [index, frame_mask, Far(mixture), Far(cotangent)],
        [((2, frames, L), F32), ((2 * R, 256), F32), ((2, edge, 256), F32)],
    )
    near = lax.ppermute(cross, "tm", pairs(lax.axis_size("tm"), -1))
    inside = flip(core, "tm", 1)
    t, x0_far, c0 = run(window_0, "window_0", [((COLS0, 512), BF)], [w1c], store=[x0, c0])
    cross, core, mom, kept, hx, cat0, z1 = run(
        conv_one_kernel,
        "conv_one",
        packet(512) + [((8, L), F32), ((2 * NJ, 256), F32), ((R, COLS0), BF)] + far(R, 512),
        [index, x0, near, inside, aux, t],
        [((R, 512), F32), ((edge, 256), F32), ((edge, 256), F32)] + wide(256),
        flops=2 * R * COLS0 * 512,
    )
    near, inside, mom1, (t, z1_here, hx, cat0) = exchange(
        cross, core, mom, "tm",
        lambda token: run(
            window_1,
            "window_1",
            [((COLS1, 256), BF)],
            [w2c],
            [((400, L), F32)],
            fetch=[Far(z1)],
            store=[hx, cat0],
            token=token,
        ),
    )
    cross, core, mom, ends1, h1, z2, cat1 = run(
        conv_two_kernel,
        "conv_two",
        packet(256) + [((4, NJ, 512), BF), ((2, NJ, 512), F32)] + far(R, 256) + far(R, COLS1, kind=BF),
        [index, z1_here, near, inside, mom1, prm, aux, t],
        [((R, 256), F32), ((R, COLS1), BF), ((4, NJ, 512), F32)] + wide(512),
        flops=2 * R * COLS1 * 256,
    )
    near, inside, mom2, (t, z2_here, ends1, h1) = exchange(
        cross, core, mom, "tm",
        lambda token: run(
            window_2,
            "window_2",
            [((512, COLS2), BF)],
            [w2d],
            [((400, L), F32)],
            fetch=[Far(z2)],
            store=[ends1, h1],
            token=token,
        ),
    )
    cross, core, mom, h2, act2, rect = run(
        up_two_kernel,
        "up_two",
        packet(512) + [((2, NJ, 256), F32), ((R, 256), BF)] + far(R, 512),
        [index, z2_here, near, inside, mom1, mom2, prm, aux, t],
        [((R, 512), F32), ((R, COLS2), BF)] + rim(256) + wide(256),
        flops=2 * R * COLS2 * 512,
    )
    near, inside, mom3, (t, rect_here, cat1_here, ends1_here, h2, act2) = exchange(
        cross, core, mom, "tm",
        lambda token: run(
            window_3,
            "window_3",
            [((256, 2 * COLS1B), BF)],
            [w1d],
            fetch=[Far(rect), Far(cat1, COLS1B), Far(ends1)],
            store=[h2, act2],
            token=token,
        ),
    )
    *masks, h3, low3, sig, sigh = run(
        up_one_kernel,
        "up_one",
        [((per + 16, 256), BF)] * stems
        + [((2, NJ, 512), F32), ((R, 512), BF), ((R, 256), F32), ((NJ, 256), F32)],
        [index, rect_here, near, inside, mom1, mom3, prm, aux, ends1_here, cat1_here, t],
        [((R, COLS1B), BF)] + rim(512) + [((2, NJ, 512), F32), ((16, 256), F32)] + wide(512),
        flops=2 * R * 2 * COLS1B * 256,
    )
    t2a_d, c0_here, x0_here, hx_here, h3, low3, sig, sigh = run(
        window_swap,
        "window_swap",
        far(COLS1, 256, kind=BF),
        [w2d],
        [((COLS1, 256), BF), ((400, L), F32)],
        fetch=[Far(c0), Far(x0_far), Far(hx)],
        store=[h3, low3, sig, sigh],
    )
    masks = swap(masks, "stem")
    *grads, direct = run(
        mask_kernel,
        "mask",
        [((per + 16, 256), BF)] * stems + [((per, 256), F32)],
        [index, *masks, c0_here, x0_here, hx_here],
        [((16, 256), F32)],
    )
    grads = swap(grads, "stem")
    estimates, t, sig_here, sigh_here, rect_here, direct = run(
        estimate_kernel,
        "estimate",
        [((stems, 2, frames, blocks * 32), BF), ((COLS0, 1024), BF)],
        [index, *masks, Far(x0_far), w1d],
        [((2, frames, L), F32), ((stems, per, 256), F32)],
        fetch=[Far(sig), Far(sigh), Far(rect)],
        store=[direct],
    )
    g3, cat0g, cross, core, mom, bias_one, gact = run(
        down_one_back_kernel,
        "down_one_back",
        [((R, 512), F32), ((R, COLS0), BF)] + packet(512) + [((8, L), F32), ((R, 512), F32)],
        [index, *grads, sigh_here, sig_here, aux, mom1, mom3, rect_here, t],
        [((NJ, 256), F32), ((8, L), F32), ((8 * NJ, 256), F32)],
        flops=2 * R * COLS0 * 1024,
    )
    near, inside, mom4, (w1d_grad, rect_here, t, h3_here, z2_here, gact) = exchange(
        cross, core, mom, "tm",
        lambda token: run(
            window_4,
            "window_4",
            far(32, L),
            [Far(low3, parts=2), Far(cat1, 512, parts=2), cat0g],
            [((512, COLS0), F32), ((32, L), F32)],
            flops=2 * R * COLS0 * 1024,
            fetch=[Far(rect), Far(t2a_d), Far(h3), Far(z2)],
            store=[gact],
            token=token,
        ),
    )
    g2, cat1g, cross, core, mom = run(
        up_two_back_kernel,
        "up_two_back",
        [((R, 256), F32), ((R, COLS1), BF)] + packet(256),
        [index, g3, near, inside, mom4, mom1, mom3, mom2, prm, aux, kept, rect_here, h3_here, t, z2_here],
        rim(512) + wide(512),
        flops=2 * R * COLS1 * 256,
    )
    near, inside, mom5, (t, w2d_grad, z2_here, h2_here, gact_here, z1_here) = exchange(
        cross, core, mom, "tm",
        lambda token: run(
            window_5,
            "window_5",
            [((512, COLS2), BF)] + far(128, L),
            [Far(act2), cat1g, w2c],
            [((256, COLS1), F32), ((400, L), F32), ((128, L), F32)],
            flops=2 * R * COLS1 * 256,
            fetch=[Far(z2), Far(h2), Far(gact), Far(z1)],
            token=token,
        ),
    )
    g1, low2, cross, core, mom = run(
        down_two_back_kernel,
        "down_two_back",
        [((R, 512), F32), ((R, 256), BF)] + packet(512),
        [index, g2, near, inside, mom5, mom1, mom2, prm, aux, kept, z2_here, h2_here, t, gact_here, z1_here],
        [((R, COLS2), BF)] + rim(256) + wide(256),
        flops=2 * R * COLS2 * 512,
    )
    near, inside, mom6, (t, keep, give, z1_here, h1_here, cat0_here) = exchange(
        cross, core, mom, "tm",
        lambda token: run(
            window_6,
            "window_6",
            [((256, COLS1B), BF), ((HALF, L), F32), ((HALF, L), F32)],
            [index, low2, Far(cat1, parts=2), w1c, Far(w1d_grad), Far(w2d_grad)],
            [((256, COLS1), F32), ((128, L), F32)],
            flops=2 * R * COLS1 * 256,
            fetch=[Far(z1), Far(h1), Far(cat0)],
            token=token,
        ),
    )
    got = flip(give, "tm", 1)
    *nets, low1 = run(
        up_one_back_kernel,
        "up_one_back",
        [((per, 256), BF)] * stems + [((R, 512), BF)],
        [index, g1, near, inside, mom6, mom1, prm, aux, kept, z1_here, h1_here, t],
        [((R, COLS1B), BF)] + rim(512) + wide(512),
        flops=2 * R * COLS1B * 256,
    )
    nets = swap(nets, "stem")
    low, direct_here = run(
        window_7,
        "window_7",
        [((HALF + 32, L), BF)],
        [low1, cat0_here, keep, got, bias_one],
        [((512, COLS0), F32), ((16, L), F32)],
        flops=2 * R * COLS0 * 512,
        fetch=[Far(direct)],
    )
    mine, other, mixture_grad = sum_chips(
        low,
        "tm",
        lambda token: run(
            mixture_kernel,
            "mixture",
            [((2, frames, blocks * 32), F32)],
            [*nets, direct_here],
            [((2, frames, L), F32)],
            token=token,
        ),
    )
    w1c_grad, w2c_grad, w2d_grad, w1d_grad, bias_one = run(
        unpack_kernel,
        "unpack",
        [((25, 2, 16), F32), ((25, 16, 32), F32), ((25, 16, 32), F32), ((25, 2, 32), F32), ((8, L), F32)],
        [index, mine, other],
    )

    def turned(grad, order):
        return grad.reshape((TAPS, TAPS) + grad.shape[1:]).transpose(order)[None]

    return (
        estimates,
        mixture_grad,
        turned(w1c_grad, (3, 2, 0, 1)),
        mom6[1, :16][None],
        mom6[0, :16][None],
        turned(w2c_grad, (3, 2, 0, 1)),
        mom5[1, :32][None],
        mom5[0, :32][None],
        turned(w2d_grad, (2, 3, 0, 1)),
        mom5[2, :16][None],
        mom4[1, :16][None],
        mom4[0, :16][None],
        turned(w1d_grad, (2, 3, 0, 1)),
        bias_one[0:1, 0:2],
    )


def solution(mesh):
    in_specs = (
        P(None, "tm", None),
        P(),
        P("tm"),
        P("stem", None, None, None, None),
        P("stem", None),
        P("stem", None),
        P("stem", None, None, None, None),
        P("stem", None),
        P("stem", None),
        P("stem", None, None, None, None),
        P("stem", None),
        P("stem", None),
        P("stem", None),
        P("stem", None, None, None, None),
        P("stem", None),
        P(None, None, "tm", "stem"),
    )
    out_specs = (
        P(None, None, "tm", "stem"),
        P(None, "tm", "stem"),
        P("stem", None, None, None, None),
        P("stem", None),
        P("stem", None),
        P("stem", None, None, None, None),
        P("stem", None),
        P("stem", None),
        P("stem", None, None, None, None),
        P("stem", None),
        P("stem", None),
        P("stem", None),
        P("stem", None, None, None, None),
        P("stem", None),
    )
    return jax.shard_map(
        per_device, mesh=mesh, in_specs=in_specs, out_specs=out_specs, check_vma=False
    )
```

```python
import jax
import jax.numpy as jnp
from jax import lax
from jax.experimental import pallas as pl
from jax.experimental.pallas import tpu as pltpu
from jax.sharding import PartitionSpec as P

NORM_EPS = 0.001
RATIO_EPS = 1e-10
BF = jnp.bfloat16
F32 = jnp.float32
TAPS = 5
L = 128
M = 32
NJ = 32
R = M * NJ
CHUNK = 512
UNROLL = 4
COLS0 = 1024
SPAN0 = (slice(0, 768), slice(256, 1024))
COLS1 = 1920
COLS1B = 1536
COLS2 = 1152
SPAN2 = (slice(0, 768), slice(0, 1152))
GROUPS2 = ((0, 512), (256, 640), (768, 1024))
GROUPS1 = ((0, 1024, 1), (256, 1152, 2), (512, 1280, 0), (768, 1408, 3), (1536, 1792, 4))
TILES0 = ((0, 128), (256, 512), (384, 640), (768, 896))
FULL = pl.BlockSpec(memory_space=pltpu.VMEM)
SCALAR = pl.BlockSpec(memory_space=pltpu.SMEM)
FAR = pl.BlockSpec(memory_space=pltpu.HBM)


class Far:
    def __init__(self, array, columns=None, parts=1):
        self.array, self.columns, self.parts = array, columns, parts


class Arriving:
    def __init__(self, source, target, sems, parts=1):
        self.target, self.waited, self.copies = target, 0, []
        size = target.shape[0] // parts
        for k in range(parts):
            span = pl.ds(k * size, size)
            here = (source, target) if parts == 1 else (source.at[span], target.at[span])
            self.copies.append(pltpu.make_async_copy(*here, sems.at[k]))
            self.copies[-1].start()

    def get(self, part=None):
        last = len(self.copies) if part is None else part + 1
        for copy in self.copies[self.waited : last]:
            copy.wait()
        self.waited = max(self.waited, last)
        return self.target


class Leaving:
    def __init__(self, target, sems):
        self.target, self.sems, self.copies = target, sems, []

    def put(self, source, part=None):
        target = self.target if part is None else self.target.at[part]
        source = source if part is None else source.at[part]
        copy = pltpu.make_async_copy(source, target, self.sems.at[len(self.copies)])
        copy.start()
        self.copies.append(copy)

    def wait(self):
        for copy in self.copies:
            copy.wait()


PARTS = 6


def run(kernel, name, outs, args, scratch=(), flops=0, fetch=(), store=(), token=None):
    n_args = len(args)
    args = list(args) + list(fetch) + list(store) + ([] if token is None else [token])
    n_made = len(outs)
    outs = list(outs)
    for f in fetch:
        outs.append(((f.array.shape[0], f.columns or f.array.shape[1]) + f.array.shape[2:], f.array.dtype))
    arrays = [a.array if isinstance(a, Far) else a for a in args]
    n_stored = len(outs)
    outs += [(a.shape, a.dtype, True) for a in store]
    if token is not None:
        outs.append((token.shape, token.dtype))
    far_in = [k for k, a in enumerate(args[:n_args]) if isinstance(a, Far)]
    far_out = [k for k, o in enumerate(outs) if len(o) == 3]
    n_in, n_out, n_own = len(args), len(outs), len(scratch)
    placed = [
        pltpu.with_memory_space_constraint(a.array, pltpu.HBM) if isinstance(a, Far) else a for a in args
    ]
    landing = []
    for k in far_in:
        shape = args[k].array.shape
        if args[k].columns is not None:
            shape = (shape[0], args[k].columns)
        space = pltpu.SMEM if args[k].array.dtype == jnp.int32 else pltpu.VMEM
        landing.append(space(shape, args[k].array.dtype))

    def body(*refs):
        ins, results = list(refs[:n_in]), list(refs[n_in : n_in + n_out])
        own = refs[n_in + n_out : n_in + n_out + n_own]
        targets = refs[n_in + n_out + n_own : n_in + n_out + n_own + len(far_in)]
        in_sems, out_sems = refs[-2:]

        def cut(k):
            return ins[k] if args[k].columns is None else ins[k].at[:, 0 : args[k].columns]

        for i, k in enumerate(far_in):
            ins[k] = Arriving(cut(k), targets[i], in_sems.at[i], args[k].parts)
        fetched = [
            Arriving(cut(n_args + i), results[n_made + i], in_sems.at[len(far_in) + i]) for i in range(len(fetch))
        ]
        for i, k in enumerate(far_out):
            results[k] = Leaving(results[k], out_sems.at[i])
        for i in range(len(store)):
            results[n_stored + i].put(ins[n_args + len(fetch) + i])
        if token is not None:
            results[-1][...] = ins[-1][...]
        kernel(*ins[:n_args], *results[:n_made], *own)
        for k in far_in:
            ins[k].get()
        for f in fetched:
            f.get()
        for k in far_out:
            results[k].wait()

    in_specs = []
    for a in args:
        if isinstance(a, Far):
            in_specs.append(FAR)
        else:
            in_specs.append(SCALAR if a.dtype == jnp.int32 and a.ndim == 1 else FULL)
    bytes_all = sum(a.size * a.dtype.itemsize for a in arrays)
    bytes_all += sum(jnp.zeros((), o[1]).dtype.itemsize * o[0][0] * o[0][-1] for o in outs)
    return pl.pallas_call(
        body,
        out_shape=[
            pltpu.HBM(o[0], o[1]) if len(o) == 3 else jax.ShapeDtypeStruct(o[0], o[1]) for o in outs
        ],
        in_specs=in_specs,
        out_specs=[FAR if len(o) == 3 else FULL for o in outs],
        scratch_shapes=[pltpu.VMEM(s, d) for s, d in scratch]
        + landing
        + [
            pltpu.SemaphoreType.DMA((max(1, len(far_in) + len(fetch)), PARTS)),
            pltpu.SemaphoreType.DMA((max(1, len(far_out)), PARTS)),
        ],
        compiler_params=pltpu.CompilerParams(vmem_limit_bytes=24 << 20),
        cost_estimate=pl.CostEstimate(flops=flops, bytes_accessed=bytes_all, transcendentals=0),
        name=name,
    )(*placed)


def lane(shape):
    return lax.broadcasted_iota(jnp.int32, shape, 1)


def sub(shape):
    return lax.broadcasted_iota(jnp.int32, shape, 0)


def rows(j, count=M):
    return pl.ds(pl.multiple_of(j * count, count), count)


def tiles(width):
    return [slice(L * k, L * k + L) for k in range(width // L)]


def for_blocks(fn, count=NJ):
    step = UNROLL if isinstance(count, int) and count % UNROLL == 0 else 1

    def body(j, carry):
        for i in range(step):
            fn(j * step + i)
        return carry

    lax.fori_loop(0, count // step, body, 0)


def put_all(stores):
    for ref, span, at, value in stores:
        ref[span, at] = value


def for_blocks_rims(fn):
    group = 5

    def several(first, count, has_prev, has_next):
        stores = []
        for i in range(count):
            stores += fn(first + i, has_prev, has_next)
        put_all(stores)

    def body(g, carry):
        several(group * g + 1, group, True, True)
        return carry

    several(0, 1, False, True)
    lax.fori_loop(0, (NJ - 2) // group, body, 0)
    several(NJ - 1, 1, True, False)


def from_prev(value, rim, flag):
    rim = jnp.concatenate([rim] * (M // 8), axis=0)
    return jnp.where(sub(value.shape) == 0, rim, pltpu.roll(value, 1, 0)) * flag


def from_next(value, rim, flag):
    rim = jnp.concatenate([rim] * (M // 8), axis=0)
    return jnp.where(sub(value.shape) == M - 1, rim, pltpu.roll(value, M - 1, 0)) * flag


def widen(source, out):
    def group(g):
        for at in tiles(source.shape[1]):
            tile = source[rows(g, 8), at]
            for i in range(8):
                out[rows(8 * g + i, 8), at] = jnp.broadcast_to(tile[i : i + 1], (8, L))

    for_blocks(group, NJ // 8)


def mask_bf(cond):
    return jnp.where(cond, 1.0, 0.0).astype(BF)


def fill_rims(cat, parts, low):
    zero = jnp.zeros((M, L), BF)
    cond = mask_bf(low) > 0.5

    def one(j, has_prev, has_next):
        stores = []
        for target, after, before in parts:
            value = cat[rows(j + 1), after : after + L] if has_next else zero
            other = cat[rows(j - 1), before : before + L] if has_prev else zero
            stores.append((cat, rows(j), slice(target, target + L), jnp.where(cond, value, other)))
        return stores

    for_blocks_rims(one)


def rims_1(cat, groups):
    fill_rims(cat, [(rim, base, base + L) for base, rim, _ in groups], lane((M, L)) < 32)


def rims_2(cat):
    fill_rims(cat, [(rim, base, base + L) for base, rim in GROUPS2], lane((M, L)) < 32)


def rims_0(cat):
    fill_rims(cat, [(rim, base, base) for base, rim in TILES0], lane((M, L)) % 32 < 2)


def matmul(left, right, transposed=False):
    return lax.dot_general(
        left, right, (((1,), (1 if transposed else 0,)), ((), ())), preferred_element_type=F32
    )


def quarters(fn):
    for k in range(4):
        fn(slice(R // 4 * k, R // 4 * (k + 1)))


def for_chunks(fn, size=CHUNK):
    def body(r, carry):
        fn(pl.ds(pl.multiple_of(r * size, size), size))
        return carry

    lax.fori_loop(0, R // size, body, 0)


def product_sums(product, use, done=None, size=256):
    sums = (jnp.zeros((8, L), F32), jnp.zeros((8, L), F32))

    def part(r, sums):
        rs = rows(r, size)
        value = [(piece, at) for piece in product(rs) for at in tiles(piece.shape[1])]
        for i in range(size // M):
            for k, (piece, at) in enumerate(value):
                if k % 4 == 0:
                    stores = []
                tile = piece[M * i : M * i + M, at]
                sums = use(r * (size // M) + i, k, slice(L * k, L * k + L), tile, *sums, stores)
                if k % 4 == 3 or k == len(value) - 1:
                    put_all(stores)
        if done is not None:
            done(rs)
        return sums

    if done is None:
        sums = lax.fori_loop(0, R // size, part, sums)
    else:
        for r in range(R // size):
            sums = part(r, sums)
    return [total_rows(v) for v in sums]


def rows_from_0(cat, weights):
    def product(rs):
        pieces = []
        for k in range(weights.shape[1] // 256):
            span = SPAN0[k % 2]
            pieces.append(matmul(cat[rs, span], weights[span, 256 * k : 256 * k + 256]))
        return pieces

    return product


def rows_from_2(cat, weights):
    def product(rs):
        return [
            matmul(cat[rs, span], weights[256 * k : 256 * k + 256, span], True) for k, span in enumerate(SPAN2)
        ]

    return product


def sum8(value):
    total = value[0:8]
    for k in range(1, value.shape[0] // 8):
        total = total + value[8 * k : 8 * k + 8]
    return total


def sum_blocks(fn):
    def body(j, carry):
        for i in range(UNROLL):
            carry = fn(j * UNROLL + i, *carry)
        return carry

    zero = jnp.zeros((8, L), F32)
    return [total_rows(s) for s in lax.fori_loop(0, NJ // UNROLL, body, (zero, zero))]


def fold(stats, period):
    step = L // 2
    while step >= period:
        stats = stats + pltpu.roll(stats, step, 1)
        step //= 2
    return stats


def stack_rows(values):
    at = sub((8, L))
    tile = jnp.zeros((8, L), F32)
    for k, value in enumerate(values):
        tile = jnp.where(at == k, value, tile)
    return tile


def total_rows(value):
    return jnp.sum(value, axis=0, keepdims=True)


def norm_terms(moments, count):
    mean = moments[0:1] / count
    return mean, lax.rsqrt(moments[1:2] / count - mean * mean + NORM_EPS)


def silu(v):
    return v / (1.0 + jnp.exp(-v))


def silu_slope(v):
    s = 1.0 / (1.0 + jnp.exp(-v))
    return s * (1.0 + v * (1.0 - s))


def sigmoid(v):
    return 1.0 / (1.0 + jnp.exp(-v))


def softplus(v):
    return jnp.maximum(v, 0.0) + jnp.log1p(jnp.exp(-jnp.abs(v)))


def softplus_slope(r):
    return jnp.where(r < 0.05, r * (1.0 - r * (0.5 - r * (1.0 / 6.0))), 1.0 - jnp.exp(-r))


def end_rows(z, group_out, blocks=NJ):
    def group(g):
        for at in tiles(z.shape[1]):
            place = sub((8, L))
            top = low = jnp.zeros((8, L), F32)
            for i in range(8):
                start = pl.multiple_of((8 * g + i) * M, M)
                top = jnp.where(place == i, z[pl.ds(start, 8), at][0:1], top)
                low = jnp.where(place == i, z[pl.ds(start + M - 8, 8), at][7:8], low)
            group_out(rows(g, 8), at, top, low)

    for_blocks(group, blocks // 8)


def pack_ends(z, index, cross, core, blocks=NJ):
    even = index[1] == 0

    def group_out(rs, at, top, low):
        cross[rs, at] = jnp.where(even, top, low)
        core[rs, at] = jnp.where(even, low, top)

    end_rows(z, group_out, blocks)


def pack_moments(mom, cross, value):
    mom[...] = value
    cross[NJ : NJ + 8, 0:L] = value


def sides(index, cross, core, at):
    even = index[1] == 0
    a, b = cross[0:NJ, at], core[0:NJ, at]
    return jnp.where(even, a, b), jnp.where(even, b, a)


def tile_2(w, tap, q, half):
    at = lane((16, L)) // 32
    tile = jnp.zeros((16, L), F32)
    for k in range(4):
        b = q - 2 * (4 * half + k) + 1
        if 0 <= b < TAPS:
            start = (tap * TAPS + b) * 16
            tile = jnp.where(at == k, w[start : start + 16, :], tile)
    return tile.astype(BF)


def repeat_lanes(w, out):
    for k in range(w.shape[0] // 16):
        span = slice(16 * k, 16 * k + 16)
        out[span, :] = jnp.concatenate([w[span, :].astype(F32)] * (L // 32), axis=1)


def matrix_2_down(narrow, t, w):
    repeat_lanes(narrow, w)
    zero = jnp.zeros((16, L), BF)
    for base, rim, tap in GROUPS1:
        for half in range(2):
            at = slice(L * half, L * half + L)
            for q in range(16):
                t[base + 16 * q : base + 16 * q + 16, at] = tile_2(w, tap, q, half)
            for part in range(8):
                q = {0: 16, 1: 17, 7: -1}.get(part)
                start = rim + 16 * part
                t[start : start + 16, at] = zero if q is None else tile_2(w, tap, q, half)


def matrix_2_up(narrow, t, w):
    repeat_lanes(narrow, w)
    zero = jnp.zeros((16, L), BF)
    at = lane((16, L))
    for row in range(2):
        for (base, edge), tap in zip(GROUPS2, (row + 1, row + 3, row - 1)):
            for q in range(16):
                span = slice(row * 256 + q * 16, row * 256 + q * 16 + 16)
                for half in range(2):
                    cols = slice(base + L * half, base + L * half + L)
                    t[span, cols] = tile_2(w, tap, q, half) if 0 <= tap < TAPS else zero
                rim = zero
                if 0 <= tap < TAPS and q in (0, 1, 15):
                    b = {0: 3, 1: 4, 15: 0}[q]
                    start = (tap * TAPS + b) * 16
                    cond = at < 32 if q == 15 else at >= 96
                    rim = jnp.where(cond, w[start : start + 16, :], 0.0).astype(BF)
                t[span, edge : edge + L] = rim


def band(w, tap, channel, offset):
    tile = jnp.zeros((32, L), F32)
    for b in range(TAPS):
        start = (tap * TAPS + b) * 2 + channel
        tile = jnp.where(offset == b, w[start : start + 1, :], tile)
    return tile.astype(BF)


def matrix_1_down(w, t, col):
    q, zero = sub((32, L)), jnp.zeros((32, L), BF)
    for half in range(2):
        p = 8 * half + lane((32, L)) // 16
        inner = q - 2 * p + 1
        rim = jnp.where(q == 31, -2 * p, jnp.where(q == 0, 33 - 2 * p, jnp.where(q == 1, 34 - 2 * p, -9)))
        for row in range(2):
            cols = slice(col + row * 256 + half * L, col + row * 256 + half * L + L)
            for (base, edge), frames in zip(TILES0, ((None, -1), (0, 1), (2, 3), (4, 5))):
                if not SPAN0[row].start <= base < SPAN0[row].stop:
                    continue
                for part, frame in enumerate(frames):
                    tap = -1 if frame is None else frame - 2 * row + 1
                    for c in range(2):
                        start = part * 64 + c * 32
                        ok = 0 <= tap < TAPS
                        for offset, bins in ((base, inner), (edge, rim)):
                            span = slice(offset + start, offset + start + 32)
                            t[span, cols] = band(w, tap, c, bins) if ok else zero


def matrix_1_up(w, t, col):
    q, zero = sub((32, L)), jnp.zeros((32, L), BF)
    at = lane((32, L))
    rim = jnp.where(at < 16, q - 31, jnp.where(at >= 112, q + 3, -9))
    for frame in range(4):
        taps = (frame + 1, frame - 1, frame + 3, frame - 3)
        for c in range(2):
            span = slice(frame * 64 + c * 32, frame * 64 + c * 32 + 32)
            for k, tap in enumerate(taps):
                ok = 0 <= tap < TAPS
                for half in range(2):
                    p = 8 * half + at // 16
                    start = col + 256 * k + L * half
                    t[span, start : start + L] = band(w, tap, c, q - 2 * p + 1) if ok else zero
                start = col + 1024 + L * k
                t[span, start : start + L] = band(w, tap, c, rim) if ok else zero


def double_lanes(value, first):
    while first < L:
        value = value + pltpu.roll(value, first, 1)
        first *= 2
    return value


def window_0(
    index, seg_lengths, frame_mask, raw_c, raw_d, gain1, shift1, gain2, shift2, gain3, shift3, bias2, bias1,
    t, w1c, w1d, aux, prm,
):
    w1c[...] = jnp.zeros(w1c.shape, F32)
    w1d[...] = jnp.zeros(w1d.shape, F32)
    for k in range(TAPS * TAPS):
        span = slice(2 * k, 2 * k + 2)
        w1c[span, 0:16] = raw_c[k].astype(F32)
        value = raw_d[k].astype(F32)
        w1d[0, span, 0:16] = value[:, 0:16]
        w1d[1, span, 0:16] = value[:, 16:32]
    w1c[...] = double_lanes(w1c[...], 16)
    for k in range(2):
        w1d[k] = double_lanes(w1d[k], 16)
    matrix_1_down(w1c, t, 0)
    prm[...] = jnp.zeros(prm.shape, F32)
    for k, value in enumerate((gain1, shift1, gain2, shift2, gain3, shift3, bias2)):
        prm[k : k + 1, 0 : value.shape[1]] = value[...]
    rows8, at = sub((8, L)), lane((8, L))
    value = prm[...]
    wide = (rows8 == 2) | (rows8 == 3)
    value = double_lanes(value + jnp.where(wide, 0.0, pltpu.roll(value, 16, 1)), 32)
    last = jnp.where(at // 32 % 2 == 0, bias1[0:1, 0:1], bias1[0:1, 1:2])
    prm[...] = jnp.where(rows8 == 7, last, value)
    row, at = sub((M, L)), lane((M, L))
    kept = jnp.broadcast_to(frame_mask[...].astype(F32), (8, L))
    kept = jnp.minimum(kept, pltpu.roll(kept, L - 1, 1))[0:1]
    keep = []
    for i in range(2):
        value = jnp.sum(jnp.where(at == 4 * row + 2 * i, kept, 0.0), axis=1, keepdims=True)
        keep.append(jnp.broadcast_to(value, (M, L)))
        aux[2 + i] = keep[i]
    aux[4] = keep[0] * keep[1]
    lengths = seg_lengths.get()
    start = jnp.int32(0)
    here = (index[2] * M + row) * 4
    shut = [here == index[3], here + 4 == index[3]]
    for k in range(lengths.shape[0]):
        shut = [shut[0] | (here == start), shut[1] | (here + 4 == start)]
        start = start + 4 * lengths[k]
    aux[0] = jnp.where(shut[0], 0.0, 1.0)
    aux[1] = jnp.where(shut[1], 0.0, 1.0)


def window_1(w2c, t, w):
    matrix_2_down(w2c, t, w)


def window_2(w2d, t, w):
    matrix_2_up(w2d, t, w)


def window_3(w1d, t):
    matrix_1_up(w1d.at[0], t, 0)
    matrix_1_up(w1d.at[1], t, COLS1B)


def window_swap(w2c, w2d, w1c, t2a, t2b, t1b, a, b, c, w):
    matrix_2_down(w2d, a, w)
    t2a.put(a)
    matrix_2_up(w2c, b, w)
    t2b.put(b)
    matrix_1_up(w1c, c, 0)
    t1b.put(c)


def correlate(coarse, fine, d, spans=(slice(None),)):
    for k in range(R // CHUNK):
        span = slice(CHUNK * k, CHUNK * k + CHUNK)
        left, right = ready(coarse, k), ready(fine, k)
        width = d.shape[0] // len(spans)
        for i, columns in enumerate(spans):
            out = slice(width * i, width * i + width)
            value = lax.dot_general(
                left[span, out], right[span, columns], (((0,), (0,)), ((), ())), preferred_element_type=F32
            )
            d[out, :] = value if k == 0 else d[out, :] + value


def weight_2(d, out):
    at = lane((32, L))
    sums = {}
    for base, rim, tap in GROUPS1:
        total = jnp.zeros((32, L), F32)
        for p in range(8):
            span = slice(32 * p, 32 * p + 32)
            parts = [d[span, base : base + L], d[span, base + L : base + 256], d[span, rim : rim + L]]
            if p == 0:
                value = jnp.where(at < 16, pltpu.roll(parts[2], 16, 1), pltpu.roll(parts[0], 16, 1))
            else:
                which, off = divmod(32 * p - 16, L)
                value = pltpu.roll(parts[which], L - off, 1)
                if off + 80 > L:
                    value = jnp.where(at < L - off, value, pltpu.roll(parts[which + 1], L - off, 1))
            total = total + value
        sums[tap] = total
    out[0:32, :] = jnp.where(at < 80, sums[0], pltpu.roll(sums[4], 80, 1))
    out[32:64, :] = jnp.where(at < 80, sums[1], pltpu.roll(sums[4], 32, 1))
    out[64:96, :] = sums[2]
    out[96:128, :] = sums[3]


def weight_1(d, out, start):
    at = lane((16, L)) % 32
    result = jnp.zeros((16, L), F32)
    for k in range(3):
        total = jnp.zeros((16, L), F32)
        for row in range(2):
            base, edge = TILES0[k + row]
            base, edge = base - SPAN0[row].start, edge - SPAN0[row].start
            for p in range(16):
                first = row * 256 + p * 16
                span = slice(first, first + 16)
                value = pltpu.roll(d[span, base : base + L], (1 - 2 * p) % L, 1)
                if p in (0, 15):
                    rim = pltpu.roll(d[span, edge : edge + L], L - 31 if p == 0 else 3, 1)
                    value = jnp.where(at == 0 if p == 0 else at >= 3, rim, value)
                total = total + value
        if k > 0:
            total = pltpu.roll(total, 8 * k, 1)
        result = jnp.where((at >= 8 * k) & (at < 8 * k + TAPS), total, result)
    out[start : start + 16, :] = result


def window_4(low, act, fine, out, d, kept):
    correlate(low, fine, d, SPAN0)
    weight_1(d, kept, 0)
    correlate(act, fine, d, SPAN0)
    weight_1(d, kept, 16)
    out.put(kept)


def window_5(coarse, fine, out, d, kept):
    correlate(coarse, fine, d)
    weight_2(d, kept)
    out.put(kept)


HALF = 144


def window_6(index, coarse, fine, w1d, w2d, keep, give, d, kept):
    correlate(coarse, fine, d)
    weight_2(d, kept)
    even = index[1] == 0
    up_two, up_one = ready(w2d), ready(w1d)

    def place(span, a, b):
        keep[span, :] = jnp.where(even, a, b)
        give[span, :] = jnp.where(even, b, a)

    place(slice(0, 128), up_two[...], kept[...])
    place(slice(128, 144), up_one[0:16, :], up_one[16:32, :])


def window_7(coarse, fine, keep, got, bias, low, d, first):
    correlate(coarse, fine, d, SPAN0)
    weight_1(d, first, 0)
    low[0:HALF, :] = (keep[...] + got[...]).astype(BF)
    low[HALF : HALF + 16, :] = first[...].astype(BF)
    low[HALF + 16 : HALF + 32, :] = jnp.concatenate([bias[...], jnp.zeros((8, L), F32)]).astype(BF)


def unpack_kernel(index, mine, other, w1c, w2c, w2d, w1d, bias):
    even = index[1] == 0
    a, b = mine[...], other[...]
    up, down = jnp.where(even, a, b), jnp.where(even, b, a)
    own = a[HALF:] + b[HALF:]
    for half, out in ((up, w2d), (down, w2c)):
        turned = half[0:128].T
        moved = [turned] + [pltpu.roll(turned, L - 32 * tap, 1) for tap in range(1, 4)]
        for tap in range(TAPS):
            for b in range(TAPS):
                if tap < 4:
                    value = moved[tap][16 * b : 16 * b + 16]
                else:
                    value = moved[b // 3][80 + 16 * (b % 3) : 96 + 16 * (b % 3)]
                out[tap * TAPS + b] = value[:, 0:32]
    tall = jnp.concatenate([up[128:144], down[128:144], own[0:16], jnp.zeros((80, L), F32)]).T
    other_tall = pltpu.roll(tall, L - 32, 1)
    for tap in range(TAPS):
        for b in range(TAPS):
            for c in range(2):
                row = (tap + 1) % 2 * 64 + c * 32 + (tap + 1) // 2 * 8 + b
                w1d[tap * TAPS + b, c : c + 1, :] = tall[row : row + 1, 0:32]
                w1c[tap * TAPS + b, c : c + 1, :] = other_tall[row : row + 1, 0:16]
    total = total_rows(own[16:24])
    total = jnp.broadcast_to(total, (8, L))
    total = total + pltpu.roll(total, 64, 1)
    for step in (16, 8, 4, 2, 1):
        total = total + pltpu.roll(total, L - step, 1)
    bias[...] = jnp.where(lane((8, L)) == 0, total, pltpu.roll(total, L - 31, 1))


def ready(ref, part=None):
    return ref.get(part) if isinstance(ref, Arriving) else ref


def spread(scr, store):
    at = lane((M, L)) // 32
    for half in range(2):
        parts = [scr[k % 2, pl.ds(2 * half + k // 2, M, stride=4), :] for k in range(4)]
        for block in range(4):
            value = parts[block]
            for k in range(4):
                if k != block:
                    value = jnp.where(at == k, pltpu.roll(parts[k], (32 * (k - block)) % L, 1), value)
            store(block, half, value)


def gather(blocks, scr):
    at = lane((M, L)) // 32
    for half in range(2):
        parts = [blocks(block, half) for block in range(4)]
        for k in range(4):
            value = parts[k]
            for block in range(4):
                if block != k:
                    value = jnp.where(
                        at == block, pltpu.roll(parts[block], (32 * (block - k)) % L, 1), value
                    )
            scr[k % 2, pl.ds(2 * half + k // 2, M, stride=4), :] = value


def layout_kernel(index, frame_mask, mix, cot, cross, core, x0, c0, scr, wide, ends):
    def place(out, block, row):
        def store(k, half, value):
            at = slice(L * half, L * half + L)
            out[rows(block + k), at] = value.astype(BF)
            wide[rows(row + k), at] = value

        return store

    m = mix.get()

    def mix_tile(t):
        for c in range(2):
            scr[c] = m[c, :, pl.ds(pl.multiple_of(t * L, L), L)].astype(F32)
        spread(scr, place(x0, 4 * t, 4 * t))

    for_blocks(mix_tile, NJ // 4)
    g = cot.get()
    per_stem = g.shape[3] // L

    def cot_tile(t):
        for c in range(2):
            lanes = pl.ds(pl.multiple_of((t % per_stem) * L, L), L)
            scr[c] = g[t // per_stem, c, :, lanes].astype(F32)
        spread(scr, place(c0, 4 * t, NJ + 4 * t))

    for_blocks(cot_tile, NJ // 4)
    ends[...] = jnp.zeros(ends.shape, F32)
    pack_ends(wide, index, ends.at[0], ends.at[1], 2 * NJ)
    even = index[1] == 0

    kept = frame_mask.get()

    def least(first, count):
        value = kept[first]
        for k in range(1, count):
            value = jnp.minimum(value, kept[first + k])
        return value.astype(F32)

    for i, (first, count) in enumerate(((0, 2), (2, 2), (0, 4))):
        top, low = least(first, count), least(4 * M - 4 + first, count)
        row = 2 * NJ + i
        ends[0, row : row + 1, :] = jnp.full((1, 2 * L), jnp.where(even, top, low))
        ends[1, row : row + 1, :] = jnp.full((1, 2 * L), jnp.where(even, low, top))
    cross[...] = ends[0].astype(BF)
    core[...] = ends[1].astype(BF)


def columns_0(cat, blocks, read, left, right, aux):
    a, a_next = aux[0], aux[1]
    for which, (first, count) in enumerate(blocks):

        def one(i, which=which, first=first):
            j = first + i
            span, stores = rows(j), []
            for half in range(2):
                value = read(which, j, half)
                stores.append((cat, span, slice(256 + L * half, 384 + L * half), value.astype(BF)))
                if half == 1:
                    moved = from_prev(value, left[rows(j, 8), L : 2 * L], a)
                    stores.append((cat, span, slice(0, 128), moved.astype(BF)))
                else:
                    moved = from_next(value, right[rows(j, 8), 0:L], a_next)
                    stores.append((cat, span, slice(768, 896), moved.astype(BF)))
            put_all(stores)

        for_blocks(one, count)
    rims_0(cat)


def conv_one_kernel(
    index, x0, cross_in, core_in, aux, t,
    cross, core, mom, kept, hx, cat, zfar, z, lf, rf, lw, rw,
):
    even = index[1] == 0
    a, b = cross_in[...].astype(F32), core_in[...].astype(F32)
    lf[...] = jnp.where(even, a, b)
    rf[...] = jnp.where(even, b, a)
    hx[:, 0:L] = rf[0 : 2 * NJ, 0:L]
    hx[:, L : 2 * L] = lf[0 : 2 * NJ, L : 2 * L]
    kept[...] = jnp.zeros(kept.shape, F32)
    kept[0:3, :] = lf[2 * NJ : 2 * NJ + 3, 0:L]
    kept[3:6, :] = rf[2 * NJ : 2 * NJ + 3, 0:L]
    widen(lf.at[0:NJ], lw)
    widen(rf.at[0:NJ], rw)
    x = ready(x0)
    read = lambda which, j, h: x[rows(j), L * h : L * h + L].astype(F32)
    columns_0(cat, [(0, NJ)], read, lw, rw, aux)
    weights = ready(t)

    def use(j, k, at, value, s1, s2, stores):
        stores.append((z, rows(j), at, value))
        part = value * aux[2 + k // 2]
        return s1 + sum8(part), s2 + sum8(part * value)

    stats = product_sums(rows_from_0(cat, weights), use, lambda rs: zfar.put(z, (rs, slice(None))))
    pack_ends(z, index, cross, core)
    stats = fold(stack_rows(stats), 16)
    at = sub((8, L))
    stats = jnp.where(at == 2, total_rows(aux[2] + aux[3]) * (NJ * 16.0), stats)
    stats = jnp.where(at == 3, total_rows(aux[4]) * (NJ * 8.0), stats)
    pack_moments(mom, cross, stats)


def conv_two_kernel(
    index, z1, cross_in, core_in, mom1, prm, aux, t,
    z2, cross, core, mom, eb, hf, zfar, catfar, cat, ef, lw, rw,
):
    mean, scale = norm_terms(mom1, mom1[2:3])
    gain, shift = prm[0:1], prm[1:2]

    def act(value):
        return silu((value - mean) * scale * gain + shift)

    a, a_next = aux[0], aux[1]
    for at in tiles(512):
        left, right = sides(index, cross_in, core_in, at)
        hf[0, :, at] = left
        hf[1, :, at] = right
        ef[0, :, at] = act(left)
        ef[1, :, at] = act(right)
    widen(ef.at[0], lw)
    widen(ef.at[1], rw)

    def one(j):
        span, stores = rows(j), []
        for k, at in enumerate(tiles(512)):
            value = act(z1[span, at])
            stores.append((cat, span, at, value.astype(BF)))
            if k >= 2:
                moved = from_prev(value, lw[rows(j, 8), at], a)
                stores.append((cat, span, slice(256 + L * k, 384 + L * k), moved.astype(BF)))
            start = 768 + L * k if k < 2 else 1280 + L * k
            moved = from_next(value, rw[rows(j, 8), at], a_next)
            stores.append((cat, span, slice(start, start + L), moved.astype(BF)))
        put_all(stores)

    for_blocks(one)
    catfar.put(cat, (slice(None), slice(0, 1024)))
    catfar.put(cat, (slice(None), slice(1536, 1792)))
    rims_1(cat, GROUPS1)
    catfar.put(cat, (slice(None), slice(1024, 1536)))
    catfar.put(cat, (slice(None), slice(1792, 1920)))
    def group_out(rs, at, top, low):
        ef[2, rs, at] = act(top)
        ef[3, rs, at] = act(low)

    end_rows(z1, group_out)
    eb[...] = ef[...].astype(BF)
    weights = ready(t)

    def use(j, k, at, value, s1, s2, stores):
        stores.append((z2, rows(j), at, value))
        part = value * aux[4]
        return s1 + sum8(part), s2 + sum8(part * value)

    stats = product_sums(
        lambda rs: [matmul(cat[rs, :], weights[...])], use, lambda rs: zfar.put(z2, (rs, slice(None)))
    )
    pack_ends(z2, index, cross, core)
    pack_moments(mom, cross, fold(stack_rows(stats), 32))


def columns_2(cat, read, left, right, aux):
    a, a_next = aux[0], aux[1]

    def one(j):
        span, stores = rows(j), []
        for k, at in enumerate(tiles(256)):
            value = read(j, at)
            stores.append((cat, span, at, value.astype(BF)))
            moved = from_prev(value, left[rows(j, 8), at], a)
            stores.append((cat, span, slice(256 + L * k, 384 + L * k), moved.astype(BF)))
            moved = from_next(value, right[rows(j, 8), at], a_next)
            stores.append((cat, span, slice(768 + L * k, 896 + L * k), moved.astype(BF)))
        put_all(stores)

    for_blocks(one)
    rims_2(cat)


def up_two_kernel(
    index, z2, cross_in, core_in, mom1, mom2, prm, aux, t,
    rect, cross, core, mom, hf, act2, rectfar, cat, lf, rf, lw, rw,
):
    mean, scale = norm_terms(mom2, mom1[3:4])
    gain, shift, bias = prm[2:3], prm[3:4], prm[6:7]

    def act(value):
        return silu((value - mean) * scale * gain + shift)

    for at in tiles(256):
        left, right = sides(index, cross_in, core_in, at)
        hf[0, :, at] = left
        hf[1, :, at] = right
        lf[:, at] = act(left)
        rf[:, at] = act(right)
    widen(lf, lw)
    widen(rf, rw)
    columns_2(cat, lambda j, at: act(z2[rows(j), at]), lw, rw, aux)
    act2[...] = cat[:, 0:256]
    weights = ready(t)

    def use(j, k, at, value, s1, s2, stores):
        value = softplus(value + bias)
        stores.append((rect, rows(j), at, value))
        part = value * aux[2 + k // 2]
        return s1 + sum8(part), s2 + sum8(part * value)

    stats = product_sums(rows_from_2(cat, weights), use, lambda rs: rectfar.put(rect, (rs, slice(None))))
    pack_moments(mom, cross, fold(stack_rows(stats), 16))
    pack_ends(rect, index, cross, core)


def columns_1b(cat, read, left, right, aux):
    a, a_next = aux[0], aux[1]

    def one(j):
        span, stores = rows(j), []
        for k, at in enumerate(tiles(512)):
            value = read(j, k, at)
            stores.append((cat, span, at, value.astype(BF)))
            if k >= 2:
                moved = from_prev(value, left[rows(j, 8), at], a)
                stores.append((cat, span, slice(256 + L * k, 384 + L * k), moved.astype(BF)))
            else:
                moved = from_next(value, right[rows(j, 8), at], a_next)
                stores.append((cat, span, slice(768 + L * k, 896 + L * k), moved.astype(BF)))
        put_all(stores)

    for_blocks(one)
    rims_1(cat, GROUPS1[:4])


def edge_columns(own, prev, after):
    at = lane((NJ, L))
    place = sub((NJ, L))
    parts = [own, prev, after]
    groups = [own[:, 0:256], own[:, 256:512], prev, after]
    for g in groups:
        low = jnp.where((place == NJ - 1) | (at >= 32), 0.0, pltpu.roll(g[:, 0:L], NJ - 1, 0))
        high = jnp.where((place == 0) | (at < 112), 0.0, pltpu.roll(g[:, L : 2 * L], 1, 0))
        parts.append(low + high)
    return jnp.concatenate(parts, axis=1).astype(BF)


def quarter_blocks(index, stems):
    count = NJ // stems
    return [((index[0] ^ k) * count, count) for k in range(stems)]


def up_one_kernel(
    index, rect, cross_in, core_in, mom1, mom3, prm, aux, ends1, cat1, t,
    m0, m1, m2, m3, hf, low3, sf, shf, cat, lf, rf, ef, ff, lw, rw,
):
    mean, scale = norm_terms(mom3, mom1[2:3])
    gain, shift, bias = prm[4:5], prm[5:6], prm[7:8]

    def norm(value):
        return (value - mean) * scale * gain + shift

    for at in tiles(512):
        left, right = sides(index, cross_in, core_in, at)
        hf[0, :, at] = left
        hf[1, :, at] = right
        lf[:, at] = norm(left)
        rf[:, at] = norm(right)
    widen(lf, lw)
    widen(rf, rw)
    columns_1b(cat, lambda j, k, at: norm(rect[rows(j), at]), lw, rw, aux)
    low3[...] = cat[:, 0:512]

    def group_out(rs, at, top, low):
        ef[0, rs, at] = norm(top)
        ef[1, rs, at] = norm(low)

    end_rows(rect, group_out)
    wide = jnp.concatenate([bias, bias], axis=1)
    zero = jnp.zeros((NJ, 256), F32)
    a, a_end = aux[0, 0:1, 0:1], aux[1, M - 1 : M, 0:1]
    e1 = [ends1[k].astype(F32) for k in range(4)]
    edges = [
        (
            edge_columns(lf[...], zero, ef[0, :, 0:256] * a),
            edge_columns(e1[0], zero, e1[2][:, 0:256] * a),
        ),
        (
            edge_columns(rf[...], ef[1, :, 256:512] * a_end, zero),
            edge_columns(e1[1], e1[3][:, 256:512] * a_end, zero),
        ),
    ]
    weights, other = ready(t), ready(cat1)
    value = matmul(jnp.concatenate([e[0] for e in edges]), weights[:, 0:COLS1B], True)
    value = value + matmul(jnp.concatenate([e[1] for e in edges]), weights[:, COLS1B : 2 * COLS1B], True)
    for k, half in ((0, 1), (1, 0)):
        at = slice(L * half, L * half + L)
        shf[:, at] = sigmoid(value[NJ * k : NJ * k + NJ, at] + bias)
    masks = (m0, m1, m2, m3)
    per = R // len(masks)
    for mask, (first, count) in zip(masks, quarter_blocks(index, len(masks))):
        rs = rows(lax.div(first, count), per)
        value = matmul(cat[rs, :], weights[:, 0:COLS1B], True)
        value = value + matmul(other[rs, :], weights[:, COLS1B : 2 * COLS1B], True)
        value = sigmoid(value + wide)
        sf[rs, :] = value
        mask[0:per, :] = value.astype(BF)
        ff[...] = jnp.zeros(ff.shape, F32)
        ff[0:count, :] = shf[rows(lax.div(first, count), count), :]
        mask[per : per + 16, :] = ff[...].astype(BF)


def ratio_terms(masks):
    squares = [m * m for m in masks]
    power = squares[0]
    for s in squares[1:]:
        power = power + s
    inverse = 1.0 / (power + RATIO_EPS)
    return [s * inverse for s in squares], inverse


def mask_back(masks, cots, mix):
    ratios, inverse = ratio_terms(masks)
    direct = cots[0] * ratios[0]
    for c, r in zip(cots[1:], ratios[1:]):
        direct = direct + c * r
    common = 2.0 * mix * inverse
    return [m * common * (c - direct) for m, c in zip(masks, cots)], direct


def mask_kernel(index, m0, m1, m2, m3, c0, x0, hx, g0, g1, g2, g3, df, ff):
    masks, grads = (m0, m1, m2, m3), (g0, g1, g2, g3)
    stems = len(masks)
    per, blocks = R // stems, NJ // stems
    mine = index[0]
    cots, mix, rim = ready(c0), ready(x0), ready(hx)

    def one(j):
        for at in tiles(256):
            m = [masks[s][rows(j), at].astype(F32) for s in range(stems)]
            c = [cots[rows((mine ^ s) * blocks + j), at].astype(F32) for s in range(stems)]
            x = mix[rows(mine * blocks + j), at].astype(F32)
            values, own = mask_back(m, c, x)
            df[rows(j), at] = own
            for s in range(stems):
                grads[s][rows(j), at] = values[s].astype(BF)

    for_blocks(one, blocks)
    m = [masks[s][per : per + 16, :].astype(F32)[0:blocks] for s in range(stems)]
    c = [rim[rows(stems + (mine ^ s), blocks), :] for s in range(stems)]
    values, _ = mask_back(m, c, rim[rows(mine, blocks), :])
    for s in range(stems):
        ff[...] = jnp.zeros(ff.shape, F32)
        ff[0:blocks, :] = values[s]
        grads[s][per : per + 16, :] = ff[...].astype(BF)


def estimate_kernel(index, m0, m1, m2, m3, x0, w1d, out, t, scr, est):
    masks = (m0, m1, m2, m3)
    stems = len(masks)
    blocks = NJ // stems
    mine = index[0]
    matrix_1_down(w1d.at[0], t, 0)
    matrix_1_down(w1d.at[1], t, 512)
    mix = ready(x0)

    def one(j):
        for at in tiles(256):
            m = [masks[s][rows(j), at].astype(F32) for s in range(stems)]
            x = mix[rows(mine * blocks + j), at].astype(F32)
            ratios, _ = ratio_terms(m)
            for s in range(stems):
                est[s, rows(j), at] = x * ratios[s]

    for_blocks(one, blocks)
    for s in range(stems):
        for t in range(blocks // 4):
            gather(
                lambda block, half, s=s, t=t: est[s, rows(4 * t + block), L * half : L * half + L], scr
            )
            for c in range(2):
                out[mine ^ s, c, :, L * t : L * t + L] = scr[c].astype(BF)


def down_one_back_kernel(
    index, q0, q1, q2, q3, sigh, sig, aux, mom1, mom3, rect, t,
    g3, cat, cross, core, mom, bias, gf, hf, zf, hw,
):
    grads = (q0, q1, q2, q3)
    blocks = quarter_blocks(index, len(grads))
    per = R // len(grads)
    rim = ready(sigh)
    for grad, (first, count) in zip(grads, blocks):
        span = rows(lax.div(first, count), count)
        value = grad[per : per + 16, :].astype(F32)[0:count]
        own = rim[span, :]
        hf[span, :] = value * own * (1.0 - own)
    zf[...] = jnp.zeros(zf.shape, F32)
    widen(hf, hw)
    sigs = ready(sig)

    def read(which, j, half):
        at = slice(L * half, L * half + L)
        own = sigs[rows(j), at]
        value = grads[which][rows(j - blocks[which][0]), at].astype(F32) * own * (1.0 - own)
        zf[...] = zf[...] + sum8(value)
        return value

    columns_0(cat, blocks, read, hw, hw, aux)
    bias[...] = zf[...]
    weights = ready(t)

    mean, scale = norm_terms(mom3, mom1[2:3])
    r = ready(rect)

    def use(j, k, at, value, s1, s2, stores):
        if k >= 4:
            stores.append((gf, rows(j), slice(L * k - 512, L * k - 384), value))
            return s1, s2
        stores.append((g3, rows(j), at, value))
        return s1 + sum8(value), s2 + sum8(value * (r[rows(j), at] - mean))

    s1, s2 = product_sums(rows_from_0(cat, weights), use)
    pack_ends(g3, index, cross, core)
    pack_moments(mom, cross, fold(stack_rows([s1, s2 * scale]), 16))


def norm_back(g, xhat, kept, moments, count, factor):
    return factor * (g - kept * ((moments[0:1] + xhat * moments[1:2]) / count))


def up_two_back_kernel(
    index, g3, cross_in, core_in, mom4, mom1, mom3, mom2, prm, aux, kept, rect, h3, t, z2,
    g2, cat, cross, core, mom, lf, rf, lw, rw,
):
    count = mom1[2:3]
    mean, scale = norm_terms(mom3, count)
    factor = scale * prm[4:5]
    inverse = 1.0 / count

    def back(g, r, keep):
        xhat = (r - mean) * scale
        value = factor * (g - keep * ((mom4[0:1] + xhat * mom4[1:2]) * inverse))
        return value * softplus_slope(r)

    r, h = ready(rect), ready(h3)
    for k, at in enumerate(tiles(512)):
        left, right = sides(index, cross_in, core_in, at)
        row = k // 2
        lf[:, at] = back(left, h[0, :, at], kept[row : row + 1, :])
        rf[:, at] = back(right, h[1, :, at], kept[3 + row : 4 + row, :])
    widen(lf, lw)
    widen(rf, rw)
    a, a_next = aux[0], aux[1]

    def one(j, total):
        span, stores = rows(j), []
        for k, at in enumerate(tiles(512)):
            value = back(g3[span, at], r[span, at], aux[2 + k // 2])
            total = total + sum8(value)
            stores.append((cat, span, at, value.astype(BF)))
            if k >= 2:
                moved = from_prev(value, lw[rows(j, 8), at], a)
                stores.append((cat, span, slice(256 + L * k, 384 + L * k), moved.astype(BF)))
            start = 768 + L * k if k < 2 else 1280 + L * k
            moved = from_next(value, rw[rows(j, 8), at], a_next)
            stores.append((cat, span, slice(start, start + L), moved.astype(BF)))
        put_all(stores)
        return total

    def four(j, total):
        for i in range(UNROLL):
            total = one(j * UNROLL + i, total)
        return total

    bias = lax.fori_loop(0, NJ // UNROLL, four, jnp.zeros((8, L), F32))
    rims_1(cat, GROUPS1)
    weights = ready(t)

    mean2, scale2 = norm_terms(mom2, mom1[3:4])
    gain, shift = prm[2:3], prm[3:4]
    z = ready(z2)

    def use(j, k, at, value, s1, s2, stores):
        xhat = (z[rows(j), at] - mean2) * scale2
        value = value * silu_slope(xhat * gain + shift)
        stores.append((g2, rows(j), at, value))
        return s1 + sum8(value), s2 + sum8(value * xhat)

    stats = fold(stack_rows(product_sums(lambda rs: [matmul(cat[rs, :], weights[...])], use)), 32)
    pack_ends(g2, index, cross, core)
    bias = fold(stack_rows([total_rows(bias)] * 3), 16)
    pack_moments(mom, cross, jnp.where(sub((8, L)) == 2, bias, stats))


def down_two_back_kernel(
    index, g2, cross_in, core_in, mom5, mom1, mom2, prm, aux, kept, z2, h2, t, gact, z1,
    g1, low2, cross, core, mom, cat, lf, rf, lw, rw,
):
    count = mom1[3:4]
    mean, scale = norm_terms(mom2, count)
    factor = scale * prm[2:3]
    inverse = 1.0 / count

    def back(g, z, keep):
        xhat = (z - mean) * scale
        return factor * (g - keep * ((mom5[0:1] + xhat * mom5[1:2]) * inverse))

    z, h = ready(z2), ready(h2)
    for at in tiles(256):
        left, right = sides(index, cross_in, core_in, at)
        lf[:, at] = back(left, h[0, :, at], kept[2:3, :])
        rf[:, at] = back(right, h[1, :, at], kept[5:6, :])
    widen(lf, lw)
    widen(rf, rw)
    columns_2(cat, lambda j, at: back(g2[rows(j), at], z[rows(j), at], aux[4]), lw, rw, aux)
    low2[...] = cat[:, 0:256]
    weights, added = ready(t), ready(gact)

    mean1, scale1 = norm_terms(mom1, mom1[2:3])
    gain, shift = prm[0:1], prm[1:2]
    z = ready(z1)

    def use(j, k, at, value, s1, s2, stores):
        xhat = (z[rows(j), at] - mean1) * scale1
        value = (value + added[rows(j), at]) * silu_slope(xhat * gain + shift)
        stores.append((g1, rows(j), at, value))
        return s1 + sum8(value), s2 + sum8(value * xhat)

    stats = fold(stack_rows(product_sums(rows_from_2(cat, weights), use)), 16)
    pack_ends(g1, index, cross, core)
    pack_moments(mom, cross, stats)


def up_one_back_kernel(
    index, g1, cross_in, core_in, mom6, mom1, prm, aux, kept, z1, h1, t,
    n0, n1, n2, n3, low1, cat, lf, rf, lw, rw,
):
    count = mom1[2:3]
    mean, scale = norm_terms(mom1, count)
    factor = scale * prm[0:1]
    inverse = 1.0 / count

    def back(g, z, keep):
        xhat = (z - mean) * scale
        return factor * (g - keep * ((mom6[0:1] + xhat * mom6[1:2]) * inverse))

    z, h = ready(z1), ready(h1)
    for k, at in enumerate(tiles(512)):
        left, right = sides(index, cross_in, core_in, at)
        row = k // 2
        lf[:, at] = back(left, h[0, :, at], kept[row : row + 1, :])
        rf[:, at] = back(right, h[1, :, at], kept[3 + row : 4 + row, :])
    widen(lf, lw)
    widen(rf, rw)
    columns_1b(
        cat, lambda j, k, at: back(g1[rows(j), at], z[rows(j), at], aux[2 + k // 2]), lw, rw, aux
    )
    low1[...] = cat[:, 0:512]
    weights = ready(t)
    nets = (n0, n1, n2, n3)
    per = R // len(nets)
    for net, (first, blocks) in zip(nets, quarter_blocks(index, len(nets))):
        rs = rows(lax.div(first, blocks), per)
        net[...] = matmul(cat[rs, :], weights[...], True).astype(BF)


def mixture_kernel(p0, p1, p2, p3, direct, out, scr):
    parts = (p0, p1, p2, p3)
    own = ready(direct)

    def tile(t):
        def block(k, half):
            at = slice(L * half, L * half + L)
            value = own[rows(4 * t + k), at]
            for part in parts:
                value = value + part[rows(4 * t + k), at].astype(F32)
            return value

        gather(block, scr)
        for c in range(2):
            out[c, :, pl.ds(pl.multiple_of(t * L, L), L)] = scr[c]

    for_blocks(tile, NJ // len(parts) // 4)


def pairs(count, offset):
    there = [(i, (i + offset) % count) for i in range(0, count, 2)]
    return there + [(b, a) for a, b in there]


def flip(values, axis, bit):
    return lax.ppermute(values, axis, [(i, i ^ bit) for i in range(lax.axis_size(axis))])


def sum_over(values, axis):
    count = lax.axis_size(axis)
    if count & (count - 1):
        return lax.psum(values, axis)
    step = 1
    while step < count:
        radix = 2 if step == 1 or count // step == 2 else 4
        moved = [flip(values, axis, step * k) for k in range(1, radix)]
        for m in moved:
            values = values + m
        step *= radix
    return values


def sum_chips(low, axis, beside):
    count = lax.axis_size(axis)
    if count == 8:
        moved = [flip(low, axis, bit) for bit in (2, 4, 6)]
        made, low = beside(low)
        mine = low.astype(F32) + moved[0].astype(F32) + moved[1].astype(F32) + moved[2].astype(F32)
    else:
        made, low = beside(low)
        mine, step = low.astype(F32), 2
        while step < count:
            mine = mine + flip(mine, axis, step)
            step *= 2
    return mine, flip(mine, axis, 1), made


def exchange(cross, core, mom, axis, beside):
    count = lax.axis_size(axis)
    near = lax.ppermute(cross, axis, pairs(count, -1))
    if count == 8:
        far = lax.ppermute(mom, axis, pairs(count, 3))
        across = flip(mom, axis, 4)
        inside = flip(core, axis, 1)
        *made, mom = beside(mom)
        part = mom + near[NJ:, 0:L] + far + across
        return near, inside, part + flip(part, axis, 1), made
    inside = flip(core, axis, 1)
    *made, mom = beside(mom)
    return near, inside, sum_over(mom, axis), made


def swap(blocks, axis):
    return [blocks[0]] + [flip(blocks[k], axis, k) for k in range(1, len(blocks))]


def per_device(
    mixture,
    seg_lengths,
    frame_mask,
    conv_first,
    encoder_gain_vector,
    shift_first,
    conv_second,
    gain_second,
    shift_second,
    deconv_second,
    bias_second,
    decoder_gain_vector,
    shift_third,
    deconv_first,
    bias_first,
    cotangent,
):
    position = lax.axis_index("tm")
    stems = lax.axis_size("stem")
    odd = position % 2
    total = mixture.shape[1] * lax.axis_size("tm")
    index = jnp.stack([lax.axis_index("stem"), odd, position, total]).astype(jnp.int32)
    frames = mixture.shape[1]
    per, blocks = R // stems, NJ // stems
    w2c = conv_second[0].transpose(2, 3, 1, 0).reshape(400, 32)
    w2d = deconv_second[0].transpose(2, 3, 0, 1).reshape(400, 32)
    edge = 2 * NJ + 16

    def packet(lanes):
        return [((NJ + 8, lanes), F32), ((NJ, lanes), F32), ((8, L), F32)]

    def rim(lanes):
        return [((NJ, lanes), F32)] * 2

    def wide(lanes):
        return [((8 * NJ, lanes), F32)] * 2

    def far(*shape, kind=F32):
        return [(shape, kind, True)]

    raw = [conv_first[0].transpose(2, 3, 1, 0).reshape(25, 2, 16)]
    raw += [deconv_first[0].transpose(2, 3, 0, 1).reshape(25, 2, 32)]
    raw += [encoder_gain_vector, shift_first, gain_second, shift_second]
    raw += [decoder_gain_vector, shift_third, bias_second, bias_first]
    cross, core, x0, c0, *raw = run(
        layout_kernel,
        "layout",
        [((edge, 256), BF), ((edge, 256), BF), ((R, 256), BF), ((R, 256), BF)],
        [index, Far(frame_mask), Far(mixture), Far(cotangent)],
        [((2, frames, L), F32), ((2 * R, 256), F32), ((2, edge, 256), F32)],
        fetch=[Far(frame_mask.reshape(1, 4 * M))] + [Far(v) for v in raw],
    )
    near = lax.ppermute(cross, "tm", pairs(lax.axis_size("tm"), -1))
    inside = flip(core, "tm", 1)
    t, w1c, w1d, aux, prm, x0_far, c0 = run(
        window_0,
        "window_0",
        [((COLS0, 512), BF), ((56, L), F32), ((2, 56, L), F32), ((5, M, L), F32), ((8, L), F32)],
        [index, Far(seg_lengths), *raw],
        store=[x0, c0],
    )
    cross, core, mom, kept, hx, cat0, z1 = run(
        conv_one_kernel,
        "conv_one",
        packet(512) + [((8, L), F32), ((2 * NJ, 256), F32), ((R, COLS0), BF)] + far(R, 512),
        [index, x0, near, inside, aux, t],
        [((R, 512), F32), ((edge, 256), F32), ((edge, 256), F32)] + wide(256),
        flops=2 * R * COLS0 * 512,
    )
    near, inside, mom1, (t, z1_here, hx, cat0) = exchange(
        cross, core, mom, "tm",
        lambda token: run(
            window_1,
            "window_1",
            [((COLS1, 256), BF)],
            [w2c],
            [((400, L), F32)],
            fetch=[Far(z1)],
            store=[hx, cat0],
            token=token,
        ),
    )
    z2_here, cross, core, mom, ends1, h1, z2, cat1 = run(
        conv_two_kernel,
        "conv_two",
        [((R, 256), F32)] + packet(256) + [((4, NJ, 512), BF), ((2, NJ, 512), F32)] + far(R, 256) + far(R, COLS1, kind=BF),
        [index, z1_here, near, inside, mom1, prm, aux, t],
        [((R, COLS1), BF), ((4, NJ, 512), F32)] + wide(512),
        flops=2 * R * COLS1 * 256,
    )
    near, inside, mom2, (t, ends1, h1) = exchange(
        cross, core, mom, "tm",
        lambda token: run(
            window_2,
            "window_2",
            [((512, COLS2), BF)],
            [w2d],
            [((400, L), F32)],
            store=[ends1, h1],
            token=token,
        ),
    )
    rect_here, cross, core, mom, h2, act2, rect = run(
        up_two_kernel,
        "up_two",
        [((R, 512), F32)] + packet(512) + [((2, NJ, 256), F32), ((R, 256), BF)] + far(R, 512),
        [index, z2_here, near, inside, mom1, mom2, prm, aux, t],
        [((R, COLS2), BF)] + rim(256) + wide(256),
        flops=2 * R * COLS2 * 512,
    )
    near, inside, mom3, (t, cat1_here, ends1_here, h2, act2) = exchange(
        cross, core, mom, "tm",
        lambda token: run(
            window_3,
            "window_3",
            [((256, 2 * COLS1B), BF)],
            [w1d],
            fetch=[Far(cat1, COLS1B), Far(ends1)],
            store=[h2, act2],
            token=token,
        ),
    )
    *masks, h3, low3, sig, sigh = run(
        up_one_kernel,
        "up_one",
        [((per + 16, 256), BF)] * stems
        + [((2, NJ, 512), F32), ((R, 512), BF), ((R, 256), F32), ((NJ, 256), F32)],
        [index, rect_here, near, inside, mom1, mom3, prm, aux, ends1_here, cat1_here, t],
        [((R, COLS1B), BF)] + rim(512) + [((2, NJ, 512), F32), ((16, 256), F32)] + wide(512),
        flops=2 * R * 2 * COLS1B * 256,
    )
    t2a_d, t2b_c, t1b_c, c0_here, x0_here, hx_here, h3, low3, sig, sigh = run(
        window_swap,
        "window_swap",
        far(COLS1, 256, kind=BF) + far(512, COLS2, kind=BF) + far(256, COLS1B, kind=BF),
        [w2c, w2d, w1c],
        [((COLS1, 256), BF), ((512, COLS2), BF), ((256, COLS1B), BF), ((400, L), F32)],
        fetch=[Far(c0), Far(x0_far), Far(hx)],
        store=[h3, low3, sig, sigh],
    )
    masks = swap(masks, "stem")
    *grads, direct = run(
        mask_kernel,
        "mask",
        [((per + 16, 256), BF)] * stems + [((per, 256), F32)],
        [index, *masks, c0_here, x0_here, hx_here],
        [((16, 256), F32)],
    )
    grads = swap(grads, "stem")
    estimates, t, sig_here, sigh_here, rect_here, direct = run(
        estimate_kernel,
        "estimate",
        [((stems, 2, frames, blocks * 32), BF), ((COLS0, 1024), BF)],
        [index, *masks, Far(x0_far), w1d],
        [((2, frames, L), F32), ((stems, per, 256), F32)],
        fetch=[Far(sig), Far(sigh), Far(rect)],
        store=[direct],
    )
    g3, cat0g, cross, core, mom, bias_one, gact = run(
        down_one_back_kernel,
        "down_one_back",
        [((R, 512), F32), ((R, COLS0), BF)] + packet(512) + [((8, L), F32), ((R, 512), F32)],
        [index, *grads, sigh_here, sig_here, aux, mom1, mom3, rect_here, t],
        [((NJ, 256), F32), ((8, L), F32), ((8 * NJ, 256), F32)],
        flops=2 * R * COLS0 * 1024,
    )
    near, inside, mom4, (w1d_grad, rect_here, t, h3_here, z2_here, gact) = exchange(
        cross, core, mom, "tm",
        lambda token: run(
            window_4,
            "window_4",
            far(32, L),
            [Far(low3, parts=2), Far(cat1, 512, parts=2), cat0g],
            [((512, 768), F32), ((32, L), F32)],
            flops=2 * R * COLS0 * 1024,
            fetch=[Far(rect), Far(t2a_d), Far(h3), Far(z2)],
            store=[gact],
            token=token,
        ),
    )
    g2, cat1g, cross, core, mom = run(
        up_two_back_kernel,
        "up_two_back",
        [((R, 256), F32), ((R, COLS1), BF)] + packet(256),
        [index, g3, near, inside, mom4, mom1, mom3, mom2, prm, aux, kept, rect_here, h3_here, t, z2_here],
        rim(512) + wide(512),
        flops=2 * R * COLS1 * 256,
    )
    near, inside, mom5, (w2d_grad, z2_here, t, h2_here, gact_here, z1_here) = exchange(
        cross, core, mom, "tm",
        lambda token: run(
            window_5,
            "window_5",
            far(128, L),
            [Far(act2, parts=2), cat1g],
            [((256, COLS1), F32), ((128, L), F32)],
            flops=2 * R * COLS1 * 256,
            fetch=[Far(z2), Far(t2b_c), Far(h2), Far(gact), Far(z1)],
            token=token,
        ),
    )
    g1, low2, cross, core, mom = run(
        down_two_back_kernel,
        "down_two_back",
        [((R, 512), F32), ((R, 256), BF)] + packet(512),
        [index, g2, near, inside, mom5, mom1, mom2, prm, aux, kept, z2_here, h2_here, t, gact_here, z1_here],
        [((R, COLS2), BF)] + rim(256) + wide(256),
        flops=2 * R * COLS2 * 512,
    )
    near, inside, mom6, (keep, give, t, z1_here, h1_here, cat0_here) = exchange(
        cross, core, mom, "tm",
        lambda token: run(
            window_6,
            "window_6",
            [((HALF, L), F32), ((HALF, L), F32)],
            [index, low2, Far(cat1, parts=2), Far(w1d_grad), Far(w2d_grad)],
            [((256, COLS1), F32), ((128, L), F32)],
            flops=2 * R * COLS1 * 256,
            fetch=[Far(t1b_c), Far(z1), Far(h1), Far(cat0)],
            token=token,
        ),
    )
    got = flip(give, "tm", 1)
    *nets, low1 = run(
        up_one_back_kernel,
        "up_one_back",
        [((per, 256), BF)] * stems + [((R, 512), BF)],
        [index, g1, near, inside, mom6, mom1, prm, aux, kept, z1_here, h1_here, t],
        [((R, COLS1B), BF)] + rim(512) + wide(512),
        flops=2 * R * COLS1B * 256,
    )
    nets = swap(nets, "stem")
    low, direct_here = run(
        window_7,
        "window_7",
        [((HALF + 32, L), BF)],
        [low1, cat0_here, keep, got, bias_one],
        [((512, 768), F32), ((16, L), F32)],
        flops=2 * R * COLS0 * 512,
        fetch=[Far(direct)],
    )
    mine, other, mixture_grad = sum_chips(
        low,
        "tm",
        lambda token: run(
            mixture_kernel,
            "mixture",
            [((2, frames, blocks * 32), F32)],
            [*nets, direct_here],
            [((2, frames, L), F32)],
            token=token,
        ),
    )
    w1c_grad, w2c_grad, w2d_grad, w1d_grad, bias_one = run(
        unpack_kernel,
        "unpack",
        [((25, 2, 16), F32), ((25, 16, 32), F32), ((25, 16, 32), F32), ((25, 2, 32), F32), ((8, L), F32)],
        [index, mine, other],
    )

    def turned(grad, order):
        return grad.reshape((TAPS, TAPS) + grad.shape[1:]).transpose(order)[None]

    return (
        estimates,
        mixture_grad,
        turned(w1c_grad, (3, 2, 0, 1)),
        mom6[1, :16][None],
        mom6[0, :16][None],
        turned(w2c_grad, (3, 2, 0, 1)),
        mom5[1, :32][None],
        mom5[0, :32][None],
        turned(w2d_grad, (2, 3, 0, 1)),
        mom5[2, :16][None],
        mom4[1, :16][None],
        mom4[0, :16][None],
        turned(w1d_grad, (2, 3, 0, 1)),
        bias_one[0:1, 0:2],
    )


def solution(mesh):
    in_specs = (
        P(None, "tm", None),
        P(),
        P("tm"),
        P("stem", None, None, None, None),
        P("stem", None),
        P("stem", None),
        P("stem", None, None, None, None),
        P("stem", None),
        P("stem", None),
        P("stem", None, None, None, None),
        P("stem", None),
        P("stem", None),
        P("stem", None),
        P("stem", None, None, None, None),
        P("stem", None),
        P(None, None, "tm", "stem"),
    )
    out_specs = (
        P(None, None, "tm", "stem"),
        P(None, "tm", "stem"),
        P("stem", None, None, None, None),
        P("stem", None),
        P("stem", None),
        P("stem", None, None, None, None),
        P("stem", None),
        P("stem", None),
        P("stem", None, None, None, None),
        P("stem", None),
        P("stem", None),
        P("stem", None),
        P("stem", None, None, None, None),
        P("stem", None),
    )
    return jax.shard_map(
        per_device, mesh=mesh, in_specs=in_specs, out_specs=out_specs, check_vma=False
    )
```

```python
import jax
import jax.numpy as jnp
from jax import lax
from jax.experimental import pallas as pl
from jax.experimental.pallas import tpu as pltpu
from jax.sharding import PartitionSpec as P

NORM_EPS = 0.001
RATIO_EPS = 1e-10
BF = jnp.bfloat16
F32 = jnp.float32
TAPS = 5
L = 128
M = 32
NJ = 32
R = M * NJ
CHUNK = 512
UNROLL = 4
COLS0 = 1024
SPAN0 = (slice(0, 768), slice(256, 1024))
COLS1 = 1920
COLS1B = 1536
COLS2 = 1152
SPAN2 = (slice(0, 768), slice(0, 1152))
GROUPS2 = ((0, 512), (256, 640), (768, 1024))
GROUPS1 = ((0, 1024, 1), (256, 1152, 2), (512, 1280, 0), (768, 1408, 3), (1536, 1792, 4))
TILES0 = ((0, 128), (256, 512), (384, 640), (768, 896))
FULL = pl.BlockSpec(memory_space=pltpu.VMEM)
SCALAR = pl.BlockSpec(memory_space=pltpu.SMEM)
FAR = pl.BlockSpec(memory_space=pltpu.HBM)


class Far:
    def __init__(self, array, columns=None, parts=1):
        self.array, self.columns, self.parts = array, columns, parts


class Arriving:
    def __init__(self, source, target, sems, parts=1):
        self.target, self.waited, self.copies = target, 0, []
        size = target.shape[0] // parts
        for k in range(parts):
            span = pl.ds(k * size, size)
            here = (source, target) if parts == 1 else (source.at[span], target.at[span])
            self.copies.append(pltpu.make_async_copy(*here, sems.at[k]))
            self.copies[-1].start()

    def get(self, part=None):
        last = len(self.copies) if part is None else part + 1
        for copy in self.copies[self.waited : last]:
            copy.wait()
        self.waited = max(self.waited, last)
        return self.target


class Leaving:
    def __init__(self, target, sems):
        self.target, self.sems, self.copies = target, sems, []

    def put(self, source, part=None):
        target = self.target if part is None else self.target.at[part]
        source = source if part is None else source.at[part]
        copy = pltpu.make_async_copy(source, target, self.sems.at[len(self.copies)])
        copy.start()
        self.copies.append(copy)

    def wait(self):
        for copy in self.copies:
            copy.wait()


PARTS = 6


def run(kernel, name, outs, args, scratch=(), flops=0, fetch=(), store=(), token=None, carry=()):
    n_args = len(args)
    args = list(args) + list(fetch) + list(store) + ([] if token is None else [token])
    n_made = len(outs)
    outs = list(outs)
    for f in fetch:
        outs.append(((f.array.shape[0], f.columns or f.array.shape[1]) + f.array.shape[2:], f.array.dtype))
    arrays = [a.array if isinstance(a, Far) else a for a in args]
    n_stored = len(outs)
    outs += [(a.shape, a.dtype, True) for a in store]
    if token is not None:
        outs.append((token.shape, token.dtype))
    aliases = {}
    for value in carry:
        at = [k for k, a in enumerate(args) if a is value]
        if not at:
            at = [len(args)]
            args.append(value)
        aliases[at[0]] = len(outs)
        outs.append((value.shape, value.dtype))
    n_token = n_args + len(fetch) + len(store)
    far_in = [k for k, a in enumerate(args[:n_args]) if isinstance(a, Far)]
    far_out = [k for k, o in enumerate(outs) if len(o) == 3]
    n_in, n_out, n_own = len(args), len(outs), len(scratch)
    placed = [
        pltpu.with_memory_space_constraint(a.array, pltpu.HBM) if isinstance(a, Far) else a for a in args
    ]
    landing = []
    for k in far_in:
        shape = args[k].array.shape
        if args[k].columns is not None:
            shape = (shape[0], args[k].columns)
        space = pltpu.SMEM if args[k].array.dtype == jnp.int32 else pltpu.VMEM
        landing.append(space(shape, args[k].array.dtype))

    def body(*refs):
        ins, results = list(refs[:n_in]), list(refs[n_in : n_in + n_out])
        own = refs[n_in + n_out : n_in + n_out + n_own]
        targets = refs[n_in + n_out + n_own : n_in + n_out + n_own + len(far_in)]
        in_sems, out_sems = refs[-2:]

        def cut(k):
            return ins[k] if args[k].columns is None else ins[k].at[:, 0 : args[k].columns]

        for i, k in enumerate(far_in):
            ins[k] = Arriving(cut(k), targets[i], in_sems.at[i], args[k].parts)
        fetched = [
            Arriving(cut(n_args + i), results[n_made + i], in_sems.at[len(far_in) + i]) for i in range(len(fetch))
        ]
        for i, k in enumerate(far_out):
            results[k] = Leaving(results[k], out_sems.at[i])
        for i in range(len(store)):
            results[n_stored + i].put(ins[n_args + len(fetch) + i])
        if token is not None:
            results[n_stored + len(store)][...] = ins[n_token][...]
        kernel(*ins[:n_args], *results[:n_made], *own)
        for k in far_in:
            ins[k].get()
        for f in fetched:
            f.get()
        for k in far_out:
            results[k].wait()

    in_specs = []
    for a in args:
        if isinstance(a, Far):
            in_specs.append(FAR)
        else:
            in_specs.append(SCALAR if a.dtype == jnp.int32 and a.ndim == 1 else FULL)
    bytes_all = sum(a.size * a.dtype.itemsize for a in arrays)
    bytes_all += sum(jnp.zeros((), o[1]).dtype.itemsize * o[0][0] * o[0][-1] for o in outs)
    return pl.pallas_call(
        body,
        out_shape=[
            pltpu.HBM(o[0], o[1]) if len(o) == 3 else jax.ShapeDtypeStruct(o[0], o[1]) for o in outs
        ],
        in_specs=in_specs,
        out_specs=[FAR if len(o) == 3 else FULL for o in outs],
        input_output_aliases=aliases,
        scratch_shapes=[pltpu.VMEM(s, d) for s, d in scratch]
        + landing
        + [
            pltpu.SemaphoreType.DMA((max(1, len(far_in) + len(fetch)), PARTS)),
            pltpu.SemaphoreType.DMA((max(1, len(far_out)), PARTS)),
        ],
        compiler_params=pltpu.CompilerParams(vmem_limit_bytes=24 << 20),
        cost_estimate=pl.CostEstimate(flops=flops, bytes_accessed=bytes_all, transcendentals=0),
        name=name,
    )(*placed)


def lane(shape):
    return lax.broadcasted_iota(jnp.int32, shape, 1)


def sub(shape):
    return lax.broadcasted_iota(jnp.int32, shape, 0)


def rows(j, count=M):
    return pl.ds(pl.multiple_of(j * count, count), count)


def tiles(width):
    return [slice(L * k, L * k + L) for k in range(width // L)]


def for_blocks(fn, count=NJ):
    step = UNROLL if isinstance(count, int) and count % UNROLL == 0 else 1

    def body(j, carry):
        for i in range(step):
            fn(j * step + i)
        return carry

    lax.fori_loop(0, count // step, body, 0)


def put_all(stores):
    for ref, span, at, value in stores:
        ref[span, at] = value


def for_blocks_rims(fn):
    group = 5

    def several(first, count, has_prev, has_next):
        stores = []
        for i in range(count):
            stores += fn(first + i, has_prev, has_next)
        put_all(stores)

    def body(g, carry):
        several(group * g + 1, group, True, True)
        return carry

    several(0, 1, False, True)
    lax.fori_loop(0, (NJ - 2) // group, body, 0)
    several(NJ - 1, 1, True, False)


def from_prev(value, rim, flag):
    rim = jnp.concatenate([rim] * (M // 8), axis=0)
    return jnp.where(sub(value.shape) == 0, rim, pltpu.roll(value, 1, 0)) * flag


def from_next(value, rim, flag):
    rim = jnp.concatenate([rim] * (M // 8), axis=0)
    return jnp.where(sub(value.shape) == M - 1, rim, pltpu.roll(value, M - 1, 0)) * flag


def widen(source, out):
    def group(g):
        for at in tiles(source.shape[1]):
            tile = source[rows(g, 8), at]
            for i in range(8):
                out[rows(8 * g + i, 8), at] = jnp.broadcast_to(tile[i : i + 1], (8, L))

    for_blocks(group, NJ // 8)


def mask_bf(cond):
    return jnp.where(cond, 1.0, 0.0).astype(BF)


def fill_rims(cat, parts, low):
    zero = jnp.zeros((M, L), BF)
    cond = mask_bf(low) > 0.5

    def one(j, has_prev, has_next):
        stores = []
        for target, after, before in parts:
            value = cat[rows(j + 1), after : after + L] if has_next else zero
            other = cat[rows(j - 1), before : before + L] if has_prev else zero
            stores.append((cat, rows(j), slice(target, target + L), jnp.where(cond, value, other)))
        return stores

    for_blocks_rims(one)


def rims_1(cat, groups):
    fill_rims(cat, [(rim, base, base + L) for base, rim, _ in groups], lane((M, L)) < 32)


def rims_2(cat):
    fill_rims(cat, [(rim, base, base + L) for base, rim in GROUPS2], lane((M, L)) < 32)


def rims_0(cat):
    fill_rims(cat, [(rim, base, base) for base, rim in TILES0], lane((M, L)) % 32 < 2)


def matmul(left, right, transposed=False):
    return lax.dot_general(
        left, right, (((1,), (1 if transposed else 0,)), ((), ())), preferred_element_type=F32
    )


def quarters(fn):
    for k in range(4):
        fn(slice(R // 4 * k, R // 4 * (k + 1)))


def for_chunks(fn, size=CHUNK):
    def body(r, carry):
        fn(pl.ds(pl.multiple_of(r * size, size), size))
        return carry

    lax.fori_loop(0, R // size, body, 0)


def product_sums(product, use, done=None, size=256):
    sums = (jnp.zeros((8, L), F32), jnp.zeros((8, L), F32))

    def part(r, sums):
        rs = rows(r, size)
        value = [(piece, at) for piece in product(rs) for at in tiles(piece.shape[1])]
        for i in range(size // M):
            for k, (piece, at) in enumerate(value):
                if k % 4 == 0:
                    stores = []
                tile = piece[M * i : M * i + M, at]
                sums = use(r * (size // M) + i, k, slice(L * k, L * k + L), tile, *sums, stores)
                if k % 4 == 3 or k == len(value) - 1:
                    put_all(stores)
        if done is not None:
            done(rs)
        return sums

    if done is None:
        sums = lax.fori_loop(0, R // size, part, sums)
    else:
        for r in range(R // size):
            sums = part(r, sums)
    return [total_rows(v) for v in sums]


def rows_from_0(cat, weights):
    def product(rs):
        pieces = []
        for k in range(weights.shape[1] // 256):
            span = SPAN0[k % 2]
            pieces.append(matmul(cat[rs, span], weights[span, 256 * k : 256 * k + 256]))
        return pieces

    return product


def rows_from_2(cat, weights):
    def product(rs):
        return [
            matmul(cat[rs, span], weights[256 * k : 256 * k + 256, span], True) for k, span in enumerate(SPAN2)
        ]

    return product


def sum8(value):
    total = value[0:8]
    for k in range(1, value.shape[0] // 8):
        total = total + value[8 * k : 8 * k + 8]
    return total


def sum_blocks(fn):
    def body(j, carry):
        for i in range(UNROLL):
            carry = fn(j * UNROLL + i, *carry)
        return carry

    zero = jnp.zeros((8, L), F32)
    return [total_rows(s) for s in lax.fori_loop(0, NJ // UNROLL, body, (zero, zero))]


def fold(stats, period):
    step = L // 2
    while step >= period:
        stats = stats + pltpu.roll(stats, step, 1)
        step //= 2
    return stats


def stack_rows(values):
    at = sub((8, L))
    tile = jnp.zeros((8, L), F32)
    for k, value in enumerate(values):
        tile = jnp.where(at == k, value, tile)
    return tile


def total_rows(value):
    return jnp.sum(value, axis=0, keepdims=True)


def norm_terms(moments, count):
    mean = moments[0:1] / count
    return mean, lax.rsqrt(moments[1:2] / count - mean * mean + NORM_EPS)


def silu(v):
    return v / (1.0 + jnp.exp(-v))


def silu_slope(v):
    s = 1.0 / (1.0 + jnp.exp(-v))
    return s * (1.0 + v * (1.0 - s))


def sigmoid(v):
    return 1.0 / (1.0 + jnp.exp(-v))


def softplus(v):
    return jnp.maximum(v, 0.0) + jnp.log1p(jnp.exp(-jnp.abs(v)))


def softplus_slope(r):
    return jnp.where(r < 0.05, r * (1.0 - r * (0.5 - r * (1.0 / 6.0))), 1.0 - jnp.exp(-r))


def end_rows(z, group_out, blocks=NJ):
    def group(g):
        for at in tiles(z.shape[1]):
            place = sub((8, L))
            top = low = jnp.zeros((8, L), F32)
            for i in range(8):
                start = pl.multiple_of((8 * g + i) * M, M)
                top = jnp.where(place == i, z[pl.ds(start, 8), at][0:1], top)
                low = jnp.where(place == i, z[pl.ds(start + M - 8, 8), at][7:8], low)
            group_out(rows(g, 8), at, top, low)

    for_blocks(group, blocks // 8)


def pack_ends(z, index, cross, core, blocks=NJ):
    even = index[1] == 0

    def group_out(rs, at, top, low):
        cross[rs, at] = jnp.where(even, top, low)
        core[rs, at] = jnp.where(even, low, top)

    end_rows(z, group_out, blocks)


def pack_moments(mom, cross, value):
    mom[...] = value
    cross[NJ : NJ + 8, 0:L] = value


def sides(index, cross, core, at):
    even = index[1] == 0
    a, b = cross[0:NJ, at], core[0:NJ, at]
    return jnp.where(even, a, b), jnp.where(even, b, a)


def tile_2(w, tap, q, half):
    at = lane((16, L)) // 32
    tile = jnp.zeros((16, L), F32)
    for k in range(4):
        b = q - 2 * (4 * half + k) + 1
        if 0 <= b < TAPS:
            start = (tap * TAPS + b) * 16
            tile = jnp.where(at == k, w[start : start + 16, :], tile)
    return tile.astype(BF)


def repeat_lanes(w, out):
    for k in range(w.shape[0] // 16):
        span = slice(16 * k, 16 * k + 16)
        out[span, :] = jnp.concatenate([w[span, :].astype(F32)] * (L // 32), axis=1)


def matrix_2_down(narrow, t, w):
    repeat_lanes(narrow, w)
    zero = jnp.zeros((16, L), BF)
    for base, rim, tap in GROUPS1:
        for half in range(2):
            at = slice(L * half, L * half + L)
            for q in range(16):
                t[base + 16 * q : base + 16 * q + 16, at] = tile_2(w, tap, q, half)
            for part in range(8):
                q = {0: 16, 1: 17, 7: -1}.get(part)
                start = rim + 16 * part
                t[start : start + 16, at] = zero if q is None else tile_2(w, tap, q, half)


def matrix_2_up(narrow, t, w):
    repeat_lanes(narrow, w)
    zero = jnp.zeros((16, L), BF)
    at = lane((16, L))
    for row in range(2):
        for (base, edge), tap in zip(GROUPS2, (row + 1, row + 3, row - 1)):
            for q in range(16):
                span = slice(row * 256 + q * 16, row * 256 + q * 16 + 16)
                for half in range(2):
                    cols = slice(base + L * half, base + L * half + L)
                    t[span, cols] = tile_2(w, tap, q, half) if 0 <= tap < TAPS else zero
                rim = zero
                if 0 <= tap < TAPS and q in (0, 1, 15):
                    b = {0: 3, 1: 4, 15: 0}[q]
                    start = (tap * TAPS + b) * 16
                    cond = at < 32 if q == 15 else at >= 96
                    rim = jnp.where(cond, w[start : start + 16, :], 0.0).astype(BF)
                t[span, edge : edge + L] = rim


def band(w, tap, channel, offset):
    tile = jnp.zeros((32, L), F32)
    for b in range(TAPS):
        start = (tap * TAPS + b) * 2 + channel
        tile = jnp.where(offset == b, w[start : start + 1, :], tile)
    return tile.astype(BF)


def matrix_1_down(w, t, col):
    q, zero = sub((32, L)), jnp.zeros((32, L), BF)
    for half in range(2):
        p = 8 * half + lane((32, L)) // 16
        inner = q - 2 * p + 1
        rim = jnp.where(q == 31, -2 * p, jnp.where(q == 0, 33 - 2 * p, jnp.where(q == 1, 34 - 2 * p, -9)))
        for row in range(2):
            cols = slice(col + row * 256 + half * L, col + row * 256 + half * L + L)
            for (base, edge), frames in zip(TILES0, ((None, -1), (0, 1), (2, 3), (4, 5))):
                if not SPAN0[row].start <= base < SPAN0[row].stop:
                    continue
                for part, frame in enumerate(frames):
                    tap = -1 if frame is None else frame - 2 * row + 1
                    for c in range(2):
                        start = part * 64 + c * 32
                        ok = 0 <= tap < TAPS
                        for offset, bins in ((base, inner), (edge, rim)):
                            span = slice(offset + start, offset + start + 32)
                            t[span, cols] = band(w, tap, c, bins) if ok else zero


def matrix_1_up(w, t, col):
    q, zero = sub((32, L)), jnp.zeros((32, L), BF)
    at = lane((32, L))
    rim = jnp.where(at < 16, q - 31, jnp.where(at >= 112, q + 3, -9))
    for frame in range(4):
        taps = (frame + 1, frame - 1, frame + 3, frame - 3)
        for c in range(2):
            span = slice(frame * 64 + c * 32, frame * 64 + c * 32 + 32)
            for k, tap in enumerate(taps):
                ok = 0 <= tap < TAPS
                for half in range(2):
                    p = 8 * half + at // 16
                    start = col + 256 * k + L * half
                    t[span, start : start + L] = band(w, tap, c, q - 2 * p + 1) if ok else zero
                start = col + 1024 + L * k
                t[span, start : start + L] = band(w, tap, c, rim) if ok else zero


def double_lanes(value, first):
    while first < L:
        value = value + pltpu.roll(value, first, 1)
        first *= 2
    return value


def window_0(
    index, seg_lengths, frame_mask, raw_c, raw_d, gain1, shift1, gain2, shift2, gain3, shift3, bias2, bias1,
    t, w1c, w1d, aux, prm,
):
    w1c[...] = jnp.zeros(w1c.shape, F32)
    w1d[...] = jnp.zeros(w1d.shape, F32)
    for k in range(TAPS * TAPS):
        span = slice(2 * k, 2 * k + 2)
        w1c[span, 0:16] = raw_c[k].astype(F32)
        value = raw_d[k].astype(F32)
        w1d[0, span, 0:16] = value[:, 0:16]
        w1d[1, span, 0:16] = value[:, 16:32]
    w1c[...] = double_lanes(w1c[...], 16)
    for k in range(2):
        w1d[k] = double_lanes(w1d[k], 16)
    matrix_1_down(w1c, t, 0)
    prm[...] = jnp.zeros(prm.shape, F32)
    for k, value in enumerate((gain1, shift1, gain2, shift2, gain3, shift3, bias2)):
        prm[k : k + 1, 0 : value.shape[1]] = value[...]
    rows8, at = sub((8, L)), lane((8, L))
    value = prm[...]
    wide = (rows8 == 2) | (rows8 == 3)
    value = double_lanes(value + jnp.where(wide, 0.0, pltpu.roll(value, 16, 1)), 32)
    last = jnp.where(at // 32 % 2 == 0, bias1[0:1, 0:1], bias1[0:1, 1:2])
    prm[...] = jnp.where(rows8 == 7, last, value)
    row, at = sub((M, L)), lane((M, L))
    kept = jnp.broadcast_to(frame_mask[...].astype(F32), (8, L))
    kept = jnp.minimum(kept, pltpu.roll(kept, L - 1, 1))[0:1]
    keep = []
    for i in range(2):
        value = jnp.sum(jnp.where(at == 4 * row + 2 * i, kept, 0.0), axis=1, keepdims=True)
        keep.append(jnp.broadcast_to(value, (M, L)))
        aux[2 + i] = keep[i]
    aux[4] = keep[0] * keep[1]
    lengths = seg_lengths.get()
    start = jnp.int32(0)
    here = (index[2] * M + row) * 4
    shut = [here == index[3], here + 4 == index[3]]
    for k in range(lengths.shape[0]):
        shut = [shut[0] | (here == start), shut[1] | (here + 4 == start)]
        start = start + 4 * lengths[k]
    aux[0] = jnp.where(shut[0], 0.0, 1.0)
    aux[1] = jnp.where(shut[1], 0.0, 1.0)


def window_1(w2c, t, w):
    matrix_2_down(w2c, t, w)


def window_2(w2d, t, w):
    matrix_2_up(w2d, t, w)


def window_3(w1d, t):
    matrix_1_up(w1d.at[0], t, 0)
    matrix_1_up(w1d.at[1], t, COLS1B)


def window_swap(w2c, w2d, w1c, t2a, t2b, t1b, a, b, c, w):
    matrix_2_down(w2d, a, w)
    t2a.put(a)
    matrix_2_up(w2c, b, w)
    t2b.put(b)
    matrix_1_up(w1c, c, 0)
    t1b.put(c)


def correlate(coarse, fine, d, spans=(slice(None),)):
    for k in range(R // CHUNK):
        span = slice(CHUNK * k, CHUNK * k + CHUNK)
        left, right = ready(coarse, k), ready(fine, k)
        width = d.shape[0] // len(spans)
        for i, columns in enumerate(spans):
            out = slice(width * i, width * i + width)
            value = lax.dot_general(
                left[span, out], right[span, columns], (((0,), (0,)), ((), ())), preferred_element_type=F32
            )
            d[out, :] = value if k == 0 else d[out, :] + value


def weight_2(d, out):
    at = lane((32, L))
    sums = {}
    for base, rim, tap in GROUPS1:
        total = jnp.zeros((32, L), F32)
        for p in range(8):
            span = slice(32 * p, 32 * p + 32)
            parts = [d[span, base : base + L], d[span, base + L : base + 256], d[span, rim : rim + L]]
            if p == 0:
                value = jnp.where(at < 16, pltpu.roll(parts[2], 16, 1), pltpu.roll(parts[0], 16, 1))
            else:
                which, off = divmod(32 * p - 16, L)
                value = pltpu.roll(parts[which], L - off, 1)
                if off + 80 > L:
                    value = jnp.where(at < L - off, value, pltpu.roll(parts[which + 1], L - off, 1))
            total = total + value
        sums[tap] = total
    out[0:32, :] = jnp.where(at < 80, sums[0], pltpu.roll(sums[4], 80, 1))
    out[32:64, :] = jnp.where(at < 80, sums[1], pltpu.roll(sums[4], 32, 1))
    out[64:96, :] = sums[2]
    out[96:128, :] = sums[3]


def weight_1(d, out, start):
    at = lane((16, L)) % 32
    result = jnp.zeros((16, L), F32)
    for k in range(3):
        total = jnp.zeros((16, L), F32)
        for row in range(2):
            base, edge = TILES0[k + row]
            base, edge = base - SPAN0[row].start, edge - SPAN0[row].start
            for p in range(16):
                first = row * 256 + p * 16
                span = slice(first, first + 16)
                value = pltpu.roll(d[span, base : base + L], (1 - 2 * p) % L, 1)
                if p in (0, 15):
                    rim = pltpu.roll(d[span, edge : edge + L], L - 31 if p == 0 else 3, 1)
                    value = jnp.where(at == 0 if p == 0 else at >= 3, rim, value)
                total = total + value
        if k > 0:
            total = pltpu.roll(total, 8 * k, 1)
        result = jnp.where((at >= 8 * k) & (at < 8 * k + TAPS), total, result)
    out[start : start + 16, :] = result


def window_4(low, act, fine, out, d):
    correlate(low, fine, d, SPAN0)
    weight_1(d, out, 0)
    correlate(act, fine, d, SPAN0)
    weight_1(d, out, 16)


def window_5(coarse, fine, out, d):
    correlate(coarse, fine, d)
    weight_2(d, out)


HALF = 144


def window_6(index, coarse, fine, w1d, w2d, keep, give, d, kept):
    correlate(coarse, fine, d)
    weight_2(d, kept)
    even = index[1] == 0
    up_two, up_one = ready(w2d), ready(w1d)

    def place(span, a, b):
        keep[span, :] = jnp.where(even, a, b)
        give[span, :] = jnp.where(even, b, a)

    place(slice(0, 128), up_two[...], kept[...])
    place(slice(128, 144), up_one[0:16, :], up_one[16:32, :])


def window_7(coarse, fine, keep, got, bias, low, d, first):
    correlate(coarse, fine, d, SPAN0)
    weight_1(d, first, 0)
    low[0:HALF, :] = (keep[...] + got[...]).astype(BF)
    low[HALF : HALF + 16, :] = first[...].astype(BF)
    low[HALF + 16 : HALF + 32, :] = jnp.concatenate([bias[...], jnp.zeros((8, L), F32)]).astype(BF)


def unpack_kernel(
    index, mine, other, mom4, mom5, mom6,
    w1c, w2c, w2d, w1d, bias1, gain1, shift1, gain2, shift2, bias2, gain3, shift3,
):
    even = index[1] == 0
    a, b = mine[...], other[...]
    up, down = jnp.where(even, a, b), jnp.where(even, b, a)
    own = a[HALF:] + b[HALF:]
    for half, out in ((up, w2d), (down, w2c)):
        turned = half[0:128].T
        moved = [turned] + [pltpu.roll(turned, L - 32 * tap, 1) for tap in range(1, 4)]
        for tap in range(TAPS):
            for b in range(TAPS):
                if tap < 4:
                    value = moved[tap][16 * b : 16 * b + 16]
                else:
                    value = moved[b // 3][80 + 16 * (b % 3) : 96 + 16 * (b % 3)]
                out[tap * TAPS + b] = value[:, 0:32]
    tall = jnp.concatenate([up[128:144], down[128:144], own[0:16], jnp.zeros((80, L), F32)]).T
    other_tall = pltpu.roll(tall, L - 32, 1)
    for tap in range(TAPS):
        for b in range(TAPS):
            for c in range(2):
                row = (tap + 1) % 2 * 64 + c * 32 + (tap + 1) // 2 * 8 + b
                w1d[tap * TAPS + b, c : c + 1, :] = tall[row : row + 1, 0:32]
                w1c[tap * TAPS + b, c : c + 1, :] = other_tall[row : row + 1, 0:16]
    total = total_rows(own[16:24])
    total = jnp.broadcast_to(total, (8, L))
    total = total + pltpu.roll(total, 64, 1)
    for step in (16, 8, 4, 2, 1):
        total = total + pltpu.roll(total, L - step, 1)
    total = jnp.where(lane((8, L)) == 0, total, pltpu.roll(total, L - 31, 1))
    bias1[...] = total[0:1, 0:2]
    for out, mom, row in (
        (gain1, mom6, 1), (shift1, mom6, 0), (gain2, mom5, 1), (shift2, mom5, 0),
        (bias2, mom5, 2), (gain3, mom4, 1), (shift3, mom4, 0),
    ):
        out[...] = mom[row : row + 1, 0 : out.shape[1]]


def ready(ref, part=None):
    return ref.get(part) if isinstance(ref, Arriving) else ref


def spread(scr, store):
    at = lane((M, L)) // 32
    for half in range(2):
        parts = [scr[k % 2, pl.ds(2 * half + k // 2, M, stride=4), :] for k in range(4)]
        for block in range(4):
            value = parts[block]
            for k in range(4):
                if k != block:
                    value = jnp.where(at == k, pltpu.roll(parts[k], (32 * (k - block)) % L, 1), value)
            store(block, half, value)


def gather(blocks, scr):
    at = lane((M, L)) // 32
    for half in range(2):
        parts = [blocks(block, half) for block in range(4)]
        for k in range(4):
            value = parts[k]
            for block in range(4):
                if block != k:
                    value = jnp.where(
                        at == block, pltpu.roll(parts[block], (32 * (block - k)) % L, 1), value
                    )
            scr[k % 2, pl.ds(2 * half + k // 2, M, stride=4), :] = value


def layout_kernel(index, frame_mask, mix, cot, cross, core, x0, c0, scr, wide, ends):
    def place(out, block, row):
        def store(k, half, value):
            at = slice(L * half, L * half + L)
            out[rows(block + k), at] = value.astype(BF)
            wide[rows(row + k), at] = value

        return store

    m = mix.get()

    def mix_tile(t):
        for c in range(2):
            scr[c] = m[c, :, pl.ds(pl.multiple_of(t * L, L), L)].astype(F32)
        spread(scr, place(x0, 4 * t, 4 * t))

    for_blocks(mix_tile, NJ // 4)
    g = cot.get()
    per_stem = g.shape[3] // L

    def cot_tile(t):
        for c in range(2):
            lanes = pl.ds(pl.multiple_of((t % per_stem) * L, L), L)
            scr[c] = g[t // per_stem, c, :, lanes].astype(F32)
        spread(scr, place(c0, 4 * t, NJ + 4 * t))

    for_blocks(cot_tile, NJ // 4)
    ends[...] = jnp.zeros(ends.shape, F32)
    pack_ends(wide, index, ends.at[0], ends.at[1], 2 * NJ)
    even = index[1] == 0

    kept = frame_mask.get()

    def least(first, count):
        value = kept[first]
        for k in range(1, count):
            value = jnp.minimum(value, kept[first + k])
        return value.astype(F32)

    for i, (first, count) in enumerate(((0, 2), (2, 2), (0, 4))):
        top, low = least(first, count), least(4 * M - 4 + first, count)
        row = 2 * NJ + i
        ends[0, row : row + 1, :] = jnp.full((1, 2 * L), jnp.where(even, top, low))
        ends[1, row : row + 1, :] = jnp.full((1, 2 * L), jnp.where(even, low, top))
    cross[...] = ends[0].astype(BF)
    core[...] = ends[1].astype(BF)


def columns_0(cat, blocks, read, left, right, aux):
    a, a_next = aux[0], aux[1]
    for which, (first, count) in enumerate(blocks):

        def one(i, which=which, first=first):
            j = first + i
            span, stores = rows(j), []
            for half in range(2):
                value = read(which, j, half)
                stores.append((cat, span, slice(256 + L * half, 384 + L * half), value.astype(BF)))
                if half == 1:
                    moved = from_prev(value, left[rows(j, 8), L : 2 * L], a)
                    stores.append((cat, span, slice(0, 128), moved.astype(BF)))
                else:
                    moved = from_next(value, right[rows(j, 8), 0:L], a_next)
                    stores.append((cat, span, slice(768, 896), moved.astype(BF)))
            put_all(stores)

        for_blocks(one, count)
    rims_0(cat)


def conv_one_kernel(
    index, x0, cross_in, core_in, aux, t,
    cross, core, mom, kept, hx, cat, zfar, z, lf, rf, lw, rw,
):
    even = index[1] == 0
    a, b = cross_in[...].astype(F32), core_in[...].astype(F32)
    lf[...] = jnp.where(even, a, b)
    rf[...] = jnp.where(even, b, a)
    hx[:, 0:L] = rf[0 : 2 * NJ, 0:L]
    hx[:, L : 2 * L] = lf[0 : 2 * NJ, L : 2 * L]
    kept[...] = jnp.zeros(kept.shape, F32)
    kept[0:3, :] = lf[2 * NJ : 2 * NJ + 3, 0:L]
    kept[3:6, :] = rf[2 * NJ : 2 * NJ + 3, 0:L]
    widen(lf.at[0:NJ], lw)
    widen(rf.at[0:NJ], rw)
    x = ready(x0)
    read = lambda which, j, h: x[rows(j), L * h : L * h + L].astype(F32)
    columns_0(cat, [(0, NJ)], read, lw, rw, aux)
    weights = ready(t)

    def use(j, k, at, value, s1, s2, stores):
        stores.append((z, rows(j), at, value))
        part = value * aux[2 + k // 2]
        return s1 + sum8(part), s2 + sum8(part * value)

    stats = product_sums(rows_from_0(cat, weights), use, lambda rs: zfar.put(z, (rs, slice(None))))
    pack_ends(z, index, cross, core)
    stats = fold(stack_rows(stats), 16)
    at = sub((8, L))
    stats = jnp.where(at == 2, total_rows(aux[2] + aux[3]) * (NJ * 16.0), stats)
    stats = jnp.where(at == 3, total_rows(aux[4]) * (NJ * 8.0), stats)
    pack_moments(mom, cross, stats)


def conv_two_kernel(
    index, z1, cross_in, core_in, mom1, prm, aux, t,
    z2, cross, core, mom, eb, hf, zfar, catfar, cat, ef, lw, rw,
):
    mean, scale = norm_terms(mom1, mom1[2:3])
    gain, shift = prm[0:1], prm[1:2]

    def act(value):
        return silu((value - mean) * scale * gain + shift)

    a, a_next = aux[0], aux[1]
    for at in tiles(512):
        left, right = sides(index, cross_in, core_in, at)
        hf[0, :, at] = left
        hf[1, :, at] = right
        ef[0, :, at] = act(left)
        ef[1, :, at] = act(right)
    widen(ef.at[0], lw)
    widen(ef.at[1], rw)

    def one(j):
        span, stores = rows(j), []
        for k, at in enumerate(tiles(512)):
            value = act(z1[span, at])
            stores.append((cat, span, at, value.astype(BF)))
            if k >= 2:
                moved = from_prev(value, lw[rows(j, 8), at], a)
                stores.append((cat, span, slice(256 + L * k, 384 + L * k), moved.astype(BF)))
            start = 768 + L * k if k < 2 else 1280 + L * k
            moved = from_next(value, rw[rows(j, 8), at], a_next)
            stores.append((cat, span, slice(start, start + L), moved.astype(BF)))
        put_all(stores)

    for_blocks(one)
    catfar.put(cat, (slice(None), slice(0, 1024)))
    catfar.put(cat, (slice(None), slice(1536, 1792)))
    rims_1(cat, GROUPS1)
    catfar.put(cat, (slice(None), slice(1024, 1536)))
    catfar.put(cat, (slice(None), slice(1792, 1920)))
    def group_out(rs, at, top, low):
        ef[2, rs, at] = act(top)
        ef[3, rs, at] = act(low)

    end_rows(z1, group_out)
    eb[...] = ef[...].astype(BF)
    weights = ready(t)

    def use(j, k, at, value, s1, s2, stores):
        stores.append((z2, rows(j), at, value))
        part = value * aux[4]
        return s1 + sum8(part), s2 + sum8(part * value)

    stats = product_sums(
        lambda rs: [matmul(cat[rs, :], weights[...])], use, lambda rs: zfar.put(z2, (rs, slice(None)))
    )
    pack_ends(z2, index, cross, core)
    pack_moments(mom, cross, fold(stack_rows(stats), 32))


def columns_2(cat, read, left, right, aux):
    a, a_next = aux[0], aux[1]

    def one(j):
        span, stores = rows(j), []
        for k, at in enumerate(tiles(256)):
            value = read(j, at)
            stores.append((cat, span, at, value.astype(BF)))
            moved = from_prev(value, left[rows(j, 8), at], a)
            stores.append((cat, span, slice(256 + L * k, 384 + L * k), moved.astype(BF)))
            moved = from_next(value, right[rows(j, 8), at], a_next)
            stores.append((cat, span, slice(768 + L * k, 896 + L * k), moved.astype(BF)))
        put_all(stores)

    for_blocks(one)
    rims_2(cat)


def up_two_kernel(
    index, z2, cross_in, core_in, mom1, mom2, prm, aux, t,
    rect, cross, core, mom, hf, act2, rectfar, cat, lf, rf, lw, rw,
):
    mean, scale = norm_terms(mom2, mom1[3:4])
    gain, shift, bias = prm[2:3], prm[3:4], prm[6:7]

    def act(value):
        return silu((value - mean) * scale * gain + shift)

    for at in tiles(256):
        left, right = sides(index, cross_in, core_in, at)
        hf[0, :, at] = left
        hf[1, :, at] = right
        lf[:, at] = act(left)
        rf[:, at] = act(right)
    widen(lf, lw)
    widen(rf, rw)
    columns_2(cat, lambda j, at: act(z2[rows(j), at]), lw, rw, aux)
    act2[...] = cat[:, 0:256]
    weights = ready(t)

    def use(j, k, at, value, s1, s2, stores):
        value = softplus(value + bias)
        stores.append((rect, rows(j), at, value))
        part = value * aux[2 + k // 2]
        return s1 + sum8(part), s2 + sum8(part * value)

    stats = product_sums(rows_from_2(cat, weights), use, lambda rs: rectfar.put(rect, (rs, slice(None))))
    pack_moments(mom, cross, fold(stack_rows(stats), 16))
    pack_ends(rect, index, cross, core)


def columns_1b(cat, read, left, right, aux):
    a, a_next = aux[0], aux[1]

    def one(j):
        span, stores = rows(j), []
        for k, at in enumerate(tiles(512)):
            value = read(j, k, at)
            stores.append((cat, span, at, value.astype(BF)))
            if k >= 2:
                moved = from_prev(value, left[rows(j, 8), at], a)
                stores.append((cat, span, slice(256 + L * k, 384 + L * k), moved.astype(BF)))
            else:
                moved = from_next(value, right[rows(j, 8), at], a_next)
                stores.append((cat, span, slice(768 + L * k, 896 + L * k), moved.astype(BF)))
        put_all(stores)

    for_blocks(one)
    rims_1(cat, GROUPS1[:4])


def edge_columns(own, prev, after):
    at = lane((NJ, L))
    place = sub((NJ, L))
    parts = [own, prev, after]
    groups = [own[:, 0:256], own[:, 256:512], prev, after]
    for g in groups:
        low = jnp.where((place == NJ - 1) | (at >= 32), 0.0, pltpu.roll(g[:, 0:L], NJ - 1, 0))
        high = jnp.where((place == 0) | (at < 112), 0.0, pltpu.roll(g[:, L : 2 * L], 1, 0))
        parts.append(low + high)
    return jnp.concatenate(parts, axis=1).astype(BF)


def quarter_blocks(index, stems):
    count = NJ // stems
    return [((index[0] ^ k) * count, count) for k in range(stems)]


def up_one_kernel(
    index, rect, cross_in, core_in, mom1, mom3, prm, aux, ends1, cat1, t,
    m0, m1, m2, m3, hf, low3, sf, shf, cat, lf, rf, ef, ff, lw, rw,
):
    mean, scale = norm_terms(mom3, mom1[2:3])
    gain, shift, bias = prm[4:5], prm[5:6], prm[7:8]

    def norm(value):
        return (value - mean) * scale * gain + shift

    for at in tiles(512):
        left, right = sides(index, cross_in, core_in, at)
        hf[0, :, at] = left
        hf[1, :, at] = right
        lf[:, at] = norm(left)
        rf[:, at] = norm(right)
    widen(lf, lw)
    widen(rf, rw)
    columns_1b(cat, lambda j, k, at: norm(rect[rows(j), at]), lw, rw, aux)
    low3[...] = cat[:, 0:512]

    def group_out(rs, at, top, low):
        ef[0, rs, at] = norm(top)
        ef[1, rs, at] = norm(low)

    end_rows(rect, group_out)
    wide = jnp.concatenate([bias, bias], axis=1)
    zero = jnp.zeros((NJ, 256), F32)
    a, a_end = aux[0, 0:1, 0:1], aux[1, M - 1 : M, 0:1]
    e1 = [ends1[k].astype(F32) for k in range(4)]
    edges = [
        (
            edge_columns(lf[...], zero, ef[0, :, 0:256] * a),
            edge_columns(e1[0], zero, e1[2][:, 0:256] * a),
        ),
        (
            edge_columns(rf[...], ef[1, :, 256:512] * a_end, zero),
            edge_columns(e1[1], e1[3][:, 256:512] * a_end, zero),
        ),
    ]
    weights, other = ready(t), ready(cat1)
    value = matmul(jnp.concatenate([e[0] for e in edges]), weights[:, 0:COLS1B], True)
    value = value + matmul(jnp.concatenate([e[1] for e in edges]), weights[:, COLS1B : 2 * COLS1B], True)
    for k, half in ((0, 1), (1, 0)):
        at = slice(L * half, L * half + L)
        shf[:, at] = sigmoid(value[NJ * k : NJ * k + NJ, at] + bias)
    masks = (m0, m1, m2, m3)
    per = R // len(masks)
    for mask, (first, count) in zip(masks, quarter_blocks(index, len(masks))):
        rs = rows(lax.div(first, count), per)
        value = matmul(cat[rs, :], weights[:, 0:COLS1B], True)
        value = value + matmul(other[rs, :], weights[:, COLS1B : 2 * COLS1B], True)
        value = sigmoid(value + wide)
        sf[rs, :] = value
        mask[0:per, :] = value.astype(BF)
        ff[...] = jnp.zeros(ff.shape, F32)
        ff[0:count, :] = shf[rows(lax.div(first, count), count), :]
        mask[per : per + 16, :] = ff[...].astype(BF)


def ratio_terms(masks):
    squares = [m * m for m in masks]
    power = squares[0]
    for s in squares[1:]:
        power = power + s
    inverse = 1.0 / (power + RATIO_EPS)
    return [s * inverse for s in squares], inverse


def mask_back(masks, cots, mix):
    ratios, inverse = ratio_terms(masks)
    direct = cots[0] * ratios[0]
    for c, r in zip(cots[1:], ratios[1:]):
        direct = direct + c * r
    common = 2.0 * mix * inverse
    return [m * common * (c - direct) for m, c in zip(masks, cots)], direct


def mask_kernel(index, m0, m1, m2, m3, c0, x0, hx, g0, g1, g2, g3, df, ff):
    masks, grads = (m0, m1, m2, m3), (g0, g1, g2, g3)
    stems = len(masks)
    per, blocks = R // stems, NJ // stems
    mine = index[0]
    cots, mix, rim = ready(c0), ready(x0), ready(hx)

    def one(j):
        for at in tiles(256):
            m = [masks[s][rows(j), at].astype(F32) for s in range(stems)]
            c = [cots[rows((mine ^ s) * blocks + j), at].astype(F32) for s in range(stems)]
            x = mix[rows(mine * blocks + j), at].astype(F32)
            values, own = mask_back(m, c, x)
            df[rows(j), at] = own
            for s in range(stems):
                grads[s][rows(j), at] = values[s].astype(BF)

    for_blocks(one, blocks)
    m = [masks[s][per : per + 16, :].astype(F32)[0:blocks] for s in range(stems)]
    c = [rim[rows(stems + (mine ^ s), blocks), :] for s in range(stems)]
    values, _ = mask_back(m, c, rim[rows(mine, blocks), :])
    for s in range(stems):
        ff[...] = jnp.zeros(ff.shape, F32)
        ff[0:blocks, :] = values[s]
        grads[s][per : per + 16, :] = ff[...].astype(BF)


def estimate_kernel(index, m0, m1, m2, m3, x0, w1d, out, t, scr, est):
    masks = (m0, m1, m2, m3)
    stems = len(masks)
    blocks = NJ // stems
    mine = index[0]
    matrix_1_down(w1d.at[0], t, 0)
    matrix_1_down(w1d.at[1], t, 512)
    mix = ready(x0)

    def one(j):
        for at in tiles(256):
            m = [masks[s][rows(j), at].astype(F32) for s in range(stems)]
            x = mix[rows(mine * blocks + j), at].astype(F32)
            ratios, _ = ratio_terms(m)
            for s in range(stems):
                est[s, rows(j), at] = x * ratios[s]

    for_blocks(one, blocks)
    for s in range(stems):
        for t in range(blocks // 4):
            gather(
                lambda block, half, s=s, t=t: est[s, rows(4 * t + block), L * half : L * half + L], scr
            )
            for c in range(2):
                out[mine ^ s, c, :, L * t : L * t + L] = scr[c].astype(BF)


def down_one_back_kernel(
    index, q0, q1, q2, q3, sigh, sig, aux, mom1, mom3, rect, t,
    g3, cat, cross, core, mom, bias, gf, hf, zf, hw,
):
    grads = (q0, q1, q2, q3)
    blocks = quarter_blocks(index, len(grads))
    per = R // len(grads)
    rim = ready(sigh)
    for grad, (first, count) in zip(grads, blocks):
        span = rows(lax.div(first, count), count)
        value = grad[per : per + 16, :].astype(F32)[0:count]
        own = rim[span, :]
        hf[span, :] = value * own * (1.0 - own)
    zf[...] = jnp.zeros(zf.shape, F32)
    widen(hf, hw)
    sigs = ready(sig)

    def read(which, j, half):
        at = slice(L * half, L * half + L)
        own = sigs[rows(j), at]
        value = grads[which][rows(j - blocks[which][0]), at].astype(F32) * own * (1.0 - own)
        zf[...] = zf[...] + sum8(value)
        return value

    columns_0(cat, blocks, read, hw, hw, aux)
    bias[...] = zf[...]
    weights = ready(t)

    mean, scale = norm_terms(mom3, mom1[2:3])
    r = ready(rect)

    def use(j, k, at, value, s1, s2, stores):
        if k >= 4:
            stores.append((gf, rows(j), slice(L * k - 512, L * k - 384), value))
            return s1, s2
        stores.append((g3, rows(j), at, value))
        return s1 + sum8(value), s2 + sum8(value * (r[rows(j), at] - mean))

    s1, s2 = product_sums(rows_from_0(cat, weights), use)
    pack_ends(g3, index, cross, core)
    pack_moments(mom, cross, fold(stack_rows([s1, s2 * scale]), 16))


def norm_back(g, xhat, kept, moments, count, factor):
    return factor * (g - kept * ((moments[0:1] + xhat * moments[1:2]) / count))


def up_two_back_kernel(
    index, g3, cross_in, core_in, mom4, mom1, mom3, mom2, prm, aux, kept, rect, h3, t, z2,
    g2, cat, cross, core, mom, lf, rf, lw, rw,
):
    count = mom1[2:3]
    mean, scale = norm_terms(mom3, count)
    factor = scale * prm[4:5]
    inverse = 1.0 / count

    def back(g, r, keep):
        xhat = (r - mean) * scale
        value = factor * (g - keep * ((mom4[0:1] + xhat * mom4[1:2]) * inverse))
        return value * softplus_slope(r)

    r, h = ready(rect), ready(h3)
    for k, at in enumerate(tiles(512)):
        left, right = sides(index, cross_in, core_in, at)
        row = k // 2
        lf[:, at] = back(left, h[0, :, at], kept[row : row + 1, :])
        rf[:, at] = back(right, h[1, :, at], kept[3 + row : 4 + row, :])
    widen(lf, lw)
    widen(rf, rw)
    a, a_next = aux[0], aux[1]

    def one(j, total):
        span, stores = rows(j), []
        for k, at in enumerate(tiles(512)):
            value = back(g3[span, at], r[span, at], aux[2 + k // 2])
            total = total + sum8(value)
            stores.append((cat, span, at, value.astype(BF)))
            if k >= 2:
                moved = from_prev(value, lw[rows(j, 8), at], a)
                stores.append((cat, span, slice(256 + L * k, 384 + L * k), moved.astype(BF)))
            start = 768 + L * k if k < 2 else 1280 + L * k
            moved = from_next(value, rw[rows(j, 8), at], a_next)
            stores.append((cat, span, slice(start, start + L), moved.astype(BF)))
        put_all(stores)
        return total

    def four(j, total):
        for i in range(UNROLL):
            total = one(j * UNROLL + i, total)
        return total

    bias = lax.fori_loop(0, NJ // UNROLL, four, jnp.zeros((8, L), F32))
    rims_1(cat, GROUPS1)
    weights = ready(t)

    mean2, scale2 = norm_terms(mom2, mom1[3:4])
    gain, shift = prm[2:3], prm[3:4]
    z = ready(z2)

    def use(j, k, at, value, s1, s2, stores):
        xhat = (z[rows(j), at] - mean2) * scale2
        value = value * silu_slope(xhat * gain + shift)
        stores.append((g2, rows(j), at, value))
        return s1 + sum8(value), s2 + sum8(value * xhat)

    stats = fold(stack_rows(product_sums(lambda rs: [matmul(cat[rs, :], weights[...])], use)), 32)
    pack_ends(g2, index, cross, core)
    bias = fold(stack_rows([total_rows(bias)] * 3), 16)
    pack_moments(mom, cross, jnp.where(sub((8, L)) == 2, bias, stats))


def down_two_back_kernel(
    index, g2, cross_in, core_in, mom5, mom1, mom2, prm, aux, kept, z2, h2, t, gact, z1,
    g1, low2, cross, core, mom, cat, lf, rf, lw, rw,
):
    count = mom1[3:4]
    mean, scale = norm_terms(mom2, count)
    factor = scale * prm[2:3]
    inverse = 1.0 / count

    def back(g, z, keep):
        xhat = (z - mean) * scale
        return factor * (g - keep * ((mom5[0:1] + xhat * mom5[1:2]) * inverse))

    z, h = ready(z2), ready(h2)
    for at in tiles(256):
        left, right = sides(index, cross_in, core_in, at)
        lf[:, at] = back(left, h[0, :, at], kept[2:3, :])
        rf[:, at] = back(right, h[1, :, at], kept[5:6, :])
    widen(lf, lw)
    widen(rf, rw)
    columns_2(cat, lambda j, at: back(g2[rows(j), at], z[rows(j), at], aux[4]), lw, rw, aux)
    low2[...] = cat[:, 0:256]
    weights, added = ready(t), ready(gact)

    mean1, scale1 = norm_terms(mom1, mom1[2:3])
    gain, shift = prm[0:1], prm[1:2]
    z = ready(z1)

    def use(j, k, at, value, s1, s2, stores):
        xhat = (z[rows(j), at] - mean1) * scale1
        value = (value + added[rows(j), at]) * silu_slope(xhat * gain + shift)
        stores.append((g1, rows(j), at, value))
        return s1 + sum8(value), s2 + sum8(value * xhat)

    stats = fold(stack_rows(product_sums(rows_from_2(cat, weights), use)), 16)
    pack_ends(g1, index, cross, core)
    pack_moments(mom, cross, stats)


def up_one_back_kernel(
    index, g1, cross_in, core_in, mom6, mom1, prm, aux, kept, z1, h1, t,
    n0, n1, n2, n3, low1, cat, lf, rf, lw, rw,
):
    count = mom1[2:3]
    mean, scale = norm_terms(mom1, count)
    factor = scale * prm[0:1]
    inverse = 1.0 / count

    def back(g, z, keep):
        xhat = (z - mean) * scale
        return factor * (g - keep * ((mom6[0:1] + xhat * mom6[1:2]) * inverse))

    z, h = ready(z1), ready(h1)
    for k, at in enumerate(tiles(512)):
        left, right = sides(index, cross_in, core_in, at)
        row = k // 2
        lf[:, at] = back(left, h[0, :, at], kept[row : row + 1, :])
        rf[:, at] = back(right, h[1, :, at], kept[3 + row : 4 + row, :])
    widen(lf, lw)
    widen(rf, rw)
    columns_1b(
        cat, lambda j, k, at: back(g1[rows(j), at], z[rows(j), at], aux[2 + k // 2]), lw, rw, aux
    )
    low1[...] = cat[:, 0:512]
    weights = ready(t)
    nets = (n0, n1, n2, n3)
    per = R // len(nets)
    for net, (first, blocks) in zip(nets, quarter_blocks(index, len(nets))):
        rs = rows(lax.div(first, blocks), per)
        net[...] = matmul(cat[rs, :], weights[...], True).astype(BF)


def mixture_kernel(p0, p1, p2, p3, direct, out, scr):
    parts = (p0, p1, p2, p3)
    own = ready(direct)

    def tile(t):
        def block(k, half):
            at = slice(L * half, L * half + L)
            value = own[rows(4 * t + k), at]
            for part in parts:
                value = value + part[rows(4 * t + k), at].astype(F32)
            return value

        gather(block, scr)
        for c in range(2):
            out[c, :, pl.ds(pl.multiple_of(t * L, L), L)] = scr[c]

    for_blocks(tile, NJ // len(parts) // 4)


def pairs(count, offset):
    there = [(i, (i + offset) % count) for i in range(0, count, 2)]
    return there + [(b, a) for a, b in there]


def flip(values, axis, bit):
    return lax.ppermute(values, axis, [(i, i ^ bit) for i in range(lax.axis_size(axis))])


def sum_over(values, axis):
    count = lax.axis_size(axis)
    if count & (count - 1):
        return lax.psum(values, axis)
    step = 1
    while step < count:
        radix = 2 if step == 1 or count // step == 2 else 4
        moved = [flip(values, axis, step * k) for k in range(1, radix)]
        for m in moved:
            values = values + m
        step *= radix
    return values


def sum_chips(low, axis, beside):
    count = lax.axis_size(axis)
    if count == 8:
        moved = [flip(low, axis, bit) for bit in (2, 4, 6)]
        made, low = beside(low)
        mine = low.astype(F32) + moved[0].astype(F32) + moved[1].astype(F32) + moved[2].astype(F32)
    else:
        made, low = beside(low)
        mine, step = low.astype(F32), 2
        while step < count:
            mine = mine + flip(mine, axis, step)
            step *= 2
    return mine, flip(mine, axis, 1), made


def exchange(cross, core, mom, axis, beside):
    count = lax.axis_size(axis)
    near = lax.ppermute(cross, axis, pairs(count, -1))
    if count == 8:
        far = lax.ppermute(mom, axis, pairs(count, 3))
        across = flip(mom, axis, 4)
        inside = flip(core, axis, 1)
        *made, mom = beside(mom)
        part = mom + near[NJ:, 0:L] + far + across
        return near, inside, part + flip(part, axis, 1), made
    inside = flip(core, axis, 1)
    *made, mom = beside(mom)
    return near, inside, sum_over(mom, axis), made


def swap(blocks, axis):
    return [blocks[0]] + [flip(blocks[k], axis, k) for k in range(1, len(blocks))]


def per_device(
    mixture,
    seg_lengths,
    frame_mask,
    conv_first,
    encoder_gain_vector,
    shift_first,
    conv_second,
    gain_second,
    shift_second,
    deconv_second,
    bias_second,
    decoder_gain_vector,
    shift_third,
    deconv_first,
    bias_first,
    cotangent,
):
    position = lax.axis_index("tm")
    stems = lax.axis_size("stem")
    odd = position % 2
    total = mixture.shape[1] * lax.axis_size("tm")
    index = jnp.stack([lax.axis_index("stem"), odd, position, total]).astype(jnp.int32)
    frames = mixture.shape[1]
    per, blocks = R // stems, NJ // stems
    w2c = conv_second[0].transpose(2, 3, 1, 0).reshape(400, 32)
    w2d = deconv_second[0].transpose(2, 3, 0, 1).reshape(400, 32)
    edge = 2 * NJ + 16

    def packet(lanes):
        return [((NJ + 8, lanes), F32), ((NJ, lanes), F32), ((8, L), F32)]

    def rim(lanes):
        return [((NJ, lanes), F32)] * 2

    def wide(lanes):
        return [((8 * NJ, lanes), F32)] * 2

    def far(*shape, kind=F32):
        return [(shape, kind, True)]

    raw = [conv_first[0].transpose(2, 3, 1, 0).reshape(25, 2, 16)]
    raw += [deconv_first[0].transpose(2, 3, 0, 1).reshape(25, 2, 32)]
    raw += [encoder_gain_vector, shift_first, gain_second, shift_second]
    raw += [decoder_gain_vector, shift_third, bias_second, bias_first]
    cross, core, x0, c0, *raw = run(
        layout_kernel,
        "layout",
        [((edge, 256), BF), ((edge, 256), BF), ((R, 256), BF), ((R, 256), BF)],
        [index, Far(frame_mask), Far(mixture), Far(cotangent)],
        [((2, frames, L), F32), ((2 * R, 256), F32), ((2, edge, 256), F32)],
        fetch=[Far(frame_mask.reshape(1, 4 * M))] + [Far(v) for v in raw],
    )
    near = lax.ppermute(cross, "tm", pairs(lax.axis_size("tm"), -1))
    inside = flip(core, "tm", 1)
    t, w1c, w1d, aux, prm, x0_far, c0 = run(
        window_0,
        "window_0",
        [((COLS0, 512), BF), ((56, L), F32), ((2, 56, L), F32), ((5, M, L), F32), ((8, L), F32)],
        [index, Far(seg_lengths), *raw],
        store=[x0, c0],
    )
    cross, core, mom, kept, hx, cat0, z1 = run(
        conv_one_kernel,
        "conv_one",
        packet(512) + [((8, L), F32), ((2 * NJ, 256), F32), ((R, COLS0), BF)] + far(R, 512),
        [index, x0, near, inside, aux, t],
        [((R, 512), F32), ((edge, 256), F32), ((edge, 256), F32)] + wide(256),
        flops=2 * R * COLS0 * 512,
    )
    near, inside, mom1, (t, z1_here, hx, cat0) = exchange(
        cross, core, mom, "tm",
        lambda token: run(
            window_1,
            "window_1",
            [((COLS1, 256), BF)],
            [w2c],
            [((400, L), F32)],
            fetch=[Far(z1)],
            store=[hx, cat0],
            token=token,
        ),
    )
    z2_here, cross, core, mom, ends1, h1, z2, cat1 = run(
        conv_two_kernel,
        "conv_two",
        [((R, 256), F32)] + packet(256) + [((4, NJ, 512), BF), ((2, NJ, 512), F32)] + far(R, 256) + far(R, COLS1, kind=BF),
        [index, z1_here, near, inside, mom1, prm, aux, t],
        [((R, COLS1), BF), ((4, NJ, 512), F32)] + wide(512),
        flops=2 * R * COLS1 * 256,
    )
    near, inside, mom2, (t, ends1, h1) = exchange(
        cross, core, mom, "tm",
        lambda token: run(
            window_2,
            "window_2",
            [((512, COLS2), BF)],
            [w2d],
            [((400, L), F32)],
            store=[ends1, h1],
            token=token,
        ),
    )
    rect_here, cross, core, mom, h2, act2, rect = run(
        up_two_kernel,
        "up_two",
        [((R, 512), F32)] + packet(512) + [((2, NJ, 256), F32), ((R, 256), BF)] + far(R, 512),
        [index, z2_here, near, inside, mom1, mom2, prm, aux, t],
        [((R, COLS2), BF)] + rim(256) + wide(256),
        flops=2 * R * COLS2 * 512,
    )
    near, inside, mom3, (t, cat1_here, ends1_here, h2, act2) = exchange(
        cross, core, mom, "tm",
        lambda token: run(
            window_3,
            "window_3",
            [((256, 2 * COLS1B), BF)],
            [w1d],
            fetch=[Far(cat1, COLS1B), Far(ends1)],
            store=[h2, act2],
            token=token,
        ),
    )
    *masks, h3, low3, sig, sigh = run(
        up_one_kernel,
        "up_one",
        [((per + 16, 256), BF)] * stems
        + [((2, NJ, 512), F32), ((R, 512), BF), ((R, 256), F32), ((NJ, 256), F32)],
        [index, rect_here, near, inside, mom1, mom3, prm, aux, ends1_here, cat1_here, t],
        [((R, COLS1B), BF)] + rim(512) + [((2, NJ, 512), F32), ((16, 256), F32)] + wide(512),
        flops=2 * R * 2 * COLS1B * 256,
    )
    t2a_d, t2b_c, t1b_c, c0_here, x0_here, hx_here, h3, low3, sig, sigh = run(
        window_swap,
        "window_swap",
        far(COLS1, 256, kind=BF) + far(512, COLS2, kind=BF) + far(256, COLS1B, kind=BF),
        [w2c, w2d, w1c],
        [((COLS1, 256), BF), ((512, COLS2), BF), ((256, COLS1B), BF), ((400, L), F32)],
        fetch=[Far(c0), Far(x0_far), Far(hx)],
        store=[h3, low3, sig, sigh],
    )
    masks = swap(masks, "stem")
    *grads, direct = run(
        mask_kernel,
        "mask",
        [((per + 16, 256), BF)] * stems + [((per, 256), F32)],
        [index, *masks, c0_here, x0_here, hx_here],
        [((16, 256), F32)],
    )
    grads = swap(grads, "stem")
    estimates, t, sig_here, sigh_here, rect_here, low3_here, act_here, direct = run(
        estimate_kernel,
        "estimate",
        [((stems, 2, frames, blocks * 32), BF), ((COLS0, 1024), BF)],
        [index, *masks, Far(x0_far), w1d],
        [((2, frames, L), F32), ((stems, per, 256), F32)],
        fetch=[Far(sig), Far(sigh), Far(rect), Far(low3), Far(cat1, 512)],
        store=[direct],
    )
    g3, cat0g, cross, core, mom, bias_one, gact, rect_here, low3_here, act_here = run(
        down_one_back_kernel,
        "down_one_back",
        [((R, 512), F32), ((R, COLS0), BF)] + packet(512) + [((8, L), F32), ((R, 512), F32)],
        [index, *grads, sigh_here, sig_here, aux, mom1, mom3, rect_here, t],
        [((NJ, 256), F32), ((8, L), F32), ((8 * NJ, 256), F32)],
        flops=2 * R * COLS0 * 1024,
        carry=[rect_here, low3_here, act_here],
    )
    near, inside, mom4, (w1d_grad, t, h3_here, z2_here, act2_here) = exchange(
        cross, core, mom, "tm",
        lambda token: run(
            window_4,
            "window_4",
            [((32, L), F32)],
            [low3_here, act_here, cat0g],
            [((512, 768), F32)],
            flops=2 * R * COLS0 * 1024,
            fetch=[Far(t2a_d), Far(h3), Far(z2), Far(act2)],
            token=token,
        ),
    )
    g2, cat1g, cross, core, mom, gact, z2_here, act2_here, w1d_grad = run(
        up_two_back_kernel,
        "up_two_back",
        [((R, 256), F32), ((R, COLS1), BF)] + packet(256),
        [index, g3, near, inside, mom4, mom1, mom3, mom2, prm, aux, kept, rect_here, h3_here, t, z2_here],
        rim(512) + wide(512),
        flops=2 * R * COLS1 * 256,
        carry=[gact, z2_here, act2_here, w1d_grad],
    )
    near, inside, mom5, (w2d_grad, t, h2_here, z1_here) = exchange(
        cross, core, mom, "tm",
        lambda token: run(
            window_5,
            "window_5",
            [((128, L), F32)],
            [act2_here, cat1g],
            [((256, COLS1), F32)],
            flops=2 * R * COLS1 * 256,
            fetch=[Far(t2b_c), Far(h2), Far(z1)],
            token=token,
        ),
    )
    g1, low2, cross, core, mom, z1_here, w1d_grad, w2d_grad = run(
        down_two_back_kernel,
        "down_two_back",
        [((R, 512), F32), ((R, 256), BF)] + packet(512),
        [index, g2, near, inside, mom5, mom1, mom2, prm, aux, kept, z2_here, h2_here, t, gact, z1_here],
        [((R, COLS2), BF)] + rim(256) + wide(256),
        flops=2 * R * COLS2 * 512,
        carry=[z1_here, w1d_grad, w2d_grad],
    )
    near, inside, mom6, (keep, give, t, h1_here, cat0_here) = exchange(
        cross, core, mom, "tm",
        lambda token: run(
            window_6,
            "window_6",
            [((HALF, L), F32), ((HALF, L), F32)],
            [index, low2, Far(cat1, parts=2), w1d_grad, w2d_grad],
            [((256, COLS1), F32), ((128, L), F32)],
            flops=2 * R * COLS1 * 256,
            fetch=[Far(t1b_c), Far(h1), Far(cat0)],
            token=token,
        ),
    )
    got = flip(give, "tm", 1)
    *nets, low1 = run(
        up_one_back_kernel,
        "up_one_back",
        [((per, 256), BF)] * stems + [((R, 512), BF)],
        [index, g1, near, inside, mom6, mom1, prm, aux, kept, z1_here, h1_here, t],
        [((R, COLS1B), BF)] + rim(512) + wide(512),
        flops=2 * R * COLS1B * 256,
    )
    nets = swap(nets, "stem")
    low, direct_here = run(
        window_7,
        "window_7",
        [((HALF + 32, L), BF)],
        [low1, cat0_here, keep, got, bias_one],
        [((512, 768), F32), ((16, L), F32)],
        flops=2 * R * COLS0 * 512,
        fetch=[Far(direct)],
    )
    mine, other, mixture_grad = sum_chips(
        low,
        "tm",
        lambda token: run(
            mixture_kernel,
            "mixture",
            [((2, frames, blocks * 32), F32)],
            [*nets, direct_here],
            [((2, frames, L), F32)],
            token=token,
        ),
    )
    w1c_grad, w2c_grad, w2d_grad, w1d_grad, bias1, gain1, shift1, gain2, shift2, bias2, gain3, shift3 = run(
        unpack_kernel,
        "unpack",
        [((25, 2, 16), F32), ((25, 16, 32), F32), ((25, 16, 32), F32), ((25, 2, 32), F32), ((1, 2), F32)]
        + [((1, n), F32) for n in (16, 16, 32, 32, 16, 16, 16)],
        [index, mine, other, mom4, mom5, mom6],
    )

    def turned(grad, order):
        return grad.reshape((TAPS, TAPS) + grad.shape[1:]).transpose(order)[None]

    return (
        estimates,
        mixture_grad,
        turned(w1c_grad, (3, 2, 0, 1)),
        gain1,
        shift1,
        turned(w2c_grad, (3, 2, 0, 1)),
        gain2,
        shift2,
        turned(w2d_grad, (2, 3, 0, 1)),
        bias2,
        gain3,
        shift3,
        turned(w1d_grad, (2, 3, 0, 1)),
        bias1,
    )


def solution(mesh):
    in_specs = (
        P(None, "tm", None),
        P(),
        P("tm"),
        P("stem", None, None, None, None),
        P("stem", None),
        P("stem", None),
        P("stem", None, None, None, None),
        P("stem", None),
        P("stem", None),
        P("stem", None, None, None, None),
        P("stem", None),
        P("stem", None),
        P("stem", None),
        P("stem", None, None, None, None),
        P("stem", None),
        P(None, None, "tm", "stem"),
    )
    out_specs = (
        P(None, None, "tm", "stem"),
        P(None, "tm", "stem"),
        P("stem", None, None, None, None),
        P("stem", None),
        P("stem", None),
        P("stem", None, None, None, None),
        P("stem", None),
        P("stem", None),
        P("stem", None, None, None, None),
        P("stem", None),
        P("stem", None),
        P("stem", None),
        P("stem", None, None, None, None),
        P("stem", None),
    )
    return jax.shard_map(
        per_device, mesh=mesh, in_specs=in_specs, out_specs=out_specs, check_vma=False
    )
```

```python
import jax
import jax.numpy as jnp
from jax import lax
from jax.experimental import pallas as pl
from jax.experimental.pallas import tpu as pltpu
from jax.sharding import PartitionSpec as P

NORM_EPS = 0.001
RATIO_EPS = 1e-10
BF = jnp.bfloat16
F32 = jnp.float32
TAPS = 5
L = 128
M = 32
NJ = 32
R = M * NJ
CHUNK = 512
UNROLL = 4
COLS0 = 1024
SPAN0 = (slice(0, 768), slice(256, 1024))
COLS1 = 1920
COLS1B = 1536
COLS2 = 1152
SPAN2 = (slice(0, 768), slice(0, 1152))
GROUPS2 = ((0, 512), (256, 640), (768, 1024))
GROUPS1 = ((0, 1024, 1), (256, 1152, 2), (512, 1280, 0), (768, 1408, 3), (1536, 1792, 4))
TILES0 = ((0, 128), (256, 512), (384, 640), (768, 896))
FULL = pl.BlockSpec(memory_space=pltpu.VMEM)
SCALAR = pl.BlockSpec(memory_space=pltpu.SMEM)
FAR = pl.BlockSpec(memory_space=pltpu.HBM)


class Far:
    def __init__(self, array, columns=None, parts=1):
        self.array, self.columns, self.parts = array, columns, parts


class Arriving:
    def __init__(self, source, target, sems, parts=1):
        self.target, self.waited, self.copies = target, 0, []
        size = target.shape[0] // parts
        for k in range(parts):
            span = pl.ds(k * size, size)
            here = (source, target) if parts == 1 else (source.at[span], target.at[span])
            self.copies.append(pltpu.make_async_copy(*here, sems.at[k]))
            self.copies[-1].start()

    def get(self, part=None):
        last = len(self.copies) if part is None else part + 1
        for copy in self.copies[self.waited : last]:
            copy.wait()
        self.waited = max(self.waited, last)
        return self.target


class Leaving:
    def __init__(self, target, sems):
        self.target, self.sems, self.copies = target, sems, []

    def put(self, source, part=None):
        target = self.target if part is None else self.target.at[part]
        source = source if part is None else source.at[part]
        copy = pltpu.make_async_copy(source, target, self.sems.at[len(self.copies)])
        copy.start()
        self.copies.append(copy)

    def wait(self):
        for copy in self.copies:
            copy.wait()


PARTS = 8


def run(kernel, name, outs, args, scratch=(), flops=0, fetch=(), store=(), token=None, carry=()):
    n_args = len(args)
    args = list(args) + list(fetch) + list(store)
    n_made = len(outs)
    outs = list(outs)
    for f in fetch:
        outs.append(((f.array.shape[0], f.columns or f.array.shape[1]) + f.array.shape[2:], f.array.dtype))
    arrays = [a.array if isinstance(a, Far) else a for a in args]
    n_stored = len(outs)
    outs += [(a.shape, a.dtype, True) for a in store]
    aliases = {}
    for value in carry:
        at = [k for k, a in enumerate(args) if a is value]
        if not at:
            at = [len(args)]
            args.append(value)
        aliases[at[0]] = len(outs)
        outs.append((value.shape, value.dtype))
    if token is not None:
        args.append(token)
        outs.append((token.shape, token.dtype))
    far_in = [k for k, a in enumerate(args[:n_args]) if isinstance(a, Far)]
    far_out = [k for k, o in enumerate(outs) if len(o) == 3]
    n_in, n_out, n_own = len(args), len(outs), len(scratch)
    placed = [
        pltpu.with_memory_space_constraint(a.array, pltpu.HBM) if isinstance(a, Far) else a for a in args
    ]
    landing = []
    for k in far_in:
        shape = args[k].array.shape
        if args[k].columns is not None:
            shape = (shape[0], args[k].columns)
        space = pltpu.SMEM if args[k].array.dtype == jnp.int32 else pltpu.VMEM
        landing.append(space(shape, args[k].array.dtype))

    def body(*refs):
        ins, results = list(refs[:n_in]), list(refs[n_in : n_in + n_out])
        own = refs[n_in + n_out : n_in + n_out + n_own]
        targets = refs[n_in + n_out + n_own : n_in + n_out + n_own + len(far_in)]
        in_sems, out_sems = refs[-2:]

        def cut(k):
            return ins[k] if args[k].columns is None else ins[k].at[:, 0 : args[k].columns]

        for i, k in enumerate(far_in):
            ins[k] = Arriving(cut(k), targets[i], in_sems.at[i], args[k].parts)
        fetched = [
            Arriving(cut(n_args + i), results[n_made + i], in_sems.at[len(far_in) + i]) for i in range(len(fetch))
        ]
        for i, k in enumerate(far_out):
            results[k] = Leaving(results[k], out_sems.at[i])
        for i in range(len(store)):
            results[n_stored + i].put(ins[n_args + len(fetch) + i])
        if token is not None:
            results[-1][...] = ins[-1][...]
        kernel(*ins[:n_args], *results[:n_made], *own)
        for k in far_in:
            ins[k].get()
        for f in fetched:
            f.get()
        for k in far_out:
            results[k].wait()

    in_specs = []
    for a in args:
        if isinstance(a, Far):
            in_specs.append(FAR)
        else:
            in_specs.append(SCALAR if a.dtype == jnp.int32 and a.ndim == 1 else FULL)
    bytes_all = sum(a.size * a.dtype.itemsize for a in arrays)
    bytes_all += sum(jnp.zeros((), o[1]).dtype.itemsize * o[0][0] * o[0][-1] for o in outs)
    return pl.pallas_call(
        body,
        out_shape=[
            pltpu.HBM(o[0], o[1]) if len(o) == 3 else jax.ShapeDtypeStruct(o[0], o[1]) for o in outs
        ],
        in_specs=in_specs,
        out_specs=[FAR if len(o) == 3 else FULL for o in outs],
        input_output_aliases=aliases,
        scratch_shapes=[pltpu.VMEM(s, d) for s, d in scratch]
        + landing
        + [
            pltpu.SemaphoreType.DMA((max(1, len(far_in) + len(fetch)), PARTS)),
            pltpu.SemaphoreType.DMA((max(1, len(far_out)), PARTS)),
        ],
        compiler_params=pltpu.CompilerParams(vmem_limit_bytes=24 << 20),
        cost_estimate=pl.CostEstimate(flops=flops, bytes_accessed=bytes_all, transcendentals=0),
        name=name,
    )(*placed)


def lane(shape):
    return lax.broadcasted_iota(jnp.int32, shape, 1)


def sub(shape):
    return lax.broadcasted_iota(jnp.int32, shape, 0)


def rows(j, count=M):
    return pl.ds(pl.multiple_of(j * count, count), count)


def tiles(width):
    return [slice(L * k, L * k + L) for k in range(width // L)]


def for_blocks(fn, count=NJ):
    step = UNROLL if isinstance(count, int) and count % UNROLL == 0 else 1

    def body(j, carry):
        for i in range(step):
            fn(j * step + i)
        return carry

    lax.fori_loop(0, count // step, body, 0)


def put_all(stores):
    for ref, span, at, value in stores:
        ref[span, at] = value


def for_blocks_rims(fn):
    group = 5

    def several(first, count, has_prev, has_next):
        stores = []
        for i in range(count):
            stores += fn(first + i, has_prev, has_next)
        put_all(stores)

    def body(g, carry):
        several(group * g + 1, group, True, True)
        return carry

    several(0, 1, False, True)
    lax.fori_loop(0, (NJ - 2) // group, body, 0)
    several(NJ - 1, 1, True, False)


def from_prev(value, rim, flag):
    rim = jnp.concatenate([rim] * (M // 8), axis=0)
    return jnp.where(sub(value.shape) == 0, rim, pltpu.roll(value, 1, 0)) * flag


def from_next(value, rim, flag):
    rim = jnp.concatenate([rim] * (M // 8), axis=0)
    return jnp.where(sub(value.shape) == M - 1, rim, pltpu.roll(value, M - 1, 0)) * flag


def widen(source, out):
    def group(g):
        for at in tiles(source.shape[1]):
            tile = source[rows(g, 8), at]
            for i in range(8):
                out[rows(8 * g + i, 8), at] = jnp.broadcast_to(tile[i : i + 1], (8, L))

    for_blocks(group, NJ // 8)


def mask_bf(cond):
    return jnp.where(cond, 1.0, 0.0).astype(BF)


def fill_rims(cat, parts, low):
    zero = jnp.zeros((M, L), BF)
    cond = mask_bf(low) > 0.5

    def one(j, has_prev, has_next):
        stores = []
        for target, after, before in parts:
            value = cat[rows(j + 1), after : after + L] if has_next else zero
            other = cat[rows(j - 1), before : before + L] if has_prev else zero
            stores.append((cat, rows(j), slice(target, target + L), jnp.where(cond, value, other)))
        return stores

    for_blocks_rims(one)


def rims_1(cat, groups):
    fill_rims(cat, [(rim, base, base + L) for base, rim, _ in groups], lane((M, L)) < 32)


def rims_2(cat):
    fill_rims(cat, [(rim, base, base + L) for base, rim in GROUPS2], lane((M, L)) < 32)


def rims_0(cat):
    fill_rims(cat, [(rim, base, base) for base, rim in TILES0], lane((M, L)) % 32 < 2)


def matmul(left, right, transposed=False):
    return lax.dot_general(
        left, right, (((1,), (1 if transposed else 0,)), ((), ())), preferred_element_type=F32
    )


def quarters(fn):
    for k in range(4):
        fn(slice(R // 4 * k, R // 4 * (k + 1)))


def for_chunks(fn, size=CHUNK):
    def body(r, carry):
        fn(pl.ds(pl.multiple_of(r * size, size), size))
        return carry

    lax.fori_loop(0, R // size, body, 0)


def product_sums(product, use, done=None, size=R):
    sums = (jnp.zeros((8, L), F32), jnp.zeros((8, L), F32))

    def part(r, sums):
        rs = rows(r, size)
        value = [(piece, at) for piece in product(rs) for at in tiles(piece.shape[1])]
        for i in range(size // M):
            for k, (piece, at) in enumerate(value):
                if k % 4 == 0:
                    stores = []
                tile = piece[M * i : M * i + M, at]
                sums = use(r * (size // M) + i, k, slice(L * k, L * k + L), tile, *sums, stores)
                if k % 4 == 3 or k == len(value) - 1:
                    put_all(stores)
        if done is not None:
            done(rs)
        return sums

    if done is None:
        sums = lax.fori_loop(0, R // size, part, sums)
    else:
        for r in range(R // size):
            sums = part(r, sums)
    return [total_rows(v) for v in sums]


def rows_from_0(cat, weights):
    def product(rs):
        pieces = []
        for k in range(weights.shape[1] // 256):
            span = SPAN0[k % 2]
            pieces.append(matmul(cat[rs, span], weights[span, 256 * k : 256 * k + 256]))
        return pieces

    return product


def rows_from_2(cat, weights):
    def product(rs):
        return [
            matmul(cat[rs, span], weights[256 * k : 256 * k + 256, span], True) for k, span in enumerate(SPAN2)
        ]

    return product


def sum8(value):
    total = value[0:8]
    for k in range(1, value.shape[0] // 8):
        total = total + value[8 * k : 8 * k + 8]
    return total


def sum_blocks(fn):
    def body(j, carry):
        for i in range(UNROLL):
            carry = fn(j * UNROLL + i, *carry)
        return carry

    zero = jnp.zeros((8, L), F32)
    return [total_rows(s) for s in lax.fori_loop(0, NJ // UNROLL, body, (zero, zero))]


def fold(stats, period):
    step = L // 2
    while step >= period:
        stats = stats + pltpu.roll(stats, step, 1)
        step //= 2
    return stats


def stack_rows(values):
    at = sub((8, L))
    tile = jnp.zeros((8, L), F32)
    for k, value in enumerate(values):
        tile = jnp.where(at == k, value, tile)
    return tile


def total_rows(value):
    return jnp.sum(value, axis=0, keepdims=True)


def norm_terms(moments, count):
    mean = moments[0:1] / count
    return mean, lax.rsqrt(moments[1:2] / count - mean * mean + NORM_EPS)


def silu(v):
    return v / (1.0 + jnp.exp(-v))


def silu_slope(v):
    s = 1.0 / (1.0 + jnp.exp(-v))
    return s * (1.0 + v * (1.0 - s))


def sigmoid(v):
    return 1.0 / (1.0 + jnp.exp(-v))


def softplus(v):
    return jnp.maximum(v, 0.0) + jnp.log1p(jnp.exp(-jnp.abs(v)))


def softplus_slope(r):
    return jnp.where(r < 0.05, r * (1.0 - r * (0.5 - r * (1.0 / 6.0))), 1.0 - jnp.exp(-r))


def end_rows(z, group_out, blocks=NJ):
    def group(g):
        for at in tiles(z.shape[1]):
            place = sub((8, L))
            top = low = jnp.zeros((8, L), F32)
            for i in range(8):
                start = pl.multiple_of((8 * g + i) * M, M)
                top = jnp.where(place == i, z[pl.ds(start, 8), at][0:1], top)
                low = jnp.where(place == i, z[pl.ds(start + M - 8, 8), at][7:8], low)
            group_out(rows(g, 8), at, top, low)

    for_blocks(group, blocks // 8)


def pack_ends(z, index, cross, core, blocks=NJ):
    even = index[1] == 0

    def group_out(rs, at, top, low):
        cross[rs, at] = jnp.where(even, top, low)
        core[rs, at] = jnp.where(even, low, top)

    end_rows(z, group_out, blocks)


def pack_moments(mom, cross, value):
    mom[...] = value
    cross[NJ : NJ + 8, 0:L] = value


def sides(index, cross, core, at):
    even = index[1] == 0
    a, b = cross[0:NJ, at], core[0:NJ, at]
    return jnp.where(even, a, b), jnp.where(even, b, a)


def tile_2(w, tap, q, half):
    at = lane((16, L)) // 32
    tile = jnp.zeros((16, L), F32)
    for k in range(4):
        b = q - 2 * (4 * half + k) + 1
        if 0 <= b < TAPS:
            start = (tap * TAPS + b) * 16
            tile = jnp.where(at == k, w[start : start + 16, :], tile)
    return tile.astype(BF)


def repeat_lanes(w, out):
    for k in range(w.shape[0] // 16):
        span = slice(16 * k, 16 * k + 16)
        out[span, :] = jnp.concatenate([w[span, :].astype(F32)] * (L // 32), axis=1)


def matrix_2_down(narrow, t, w):
    repeat_lanes(narrow, w)
    zero = jnp.zeros((16, L), BF)
    for base, rim, tap in GROUPS1:
        for half in range(2):
            at = slice(L * half, L * half + L)
            for q in range(16):
                t[base + 16 * q : base + 16 * q + 16, at] = tile_2(w, tap, q, half)
            for part in range(8):
                q = {0: 16, 1: 17, 7: -1}.get(part)
                start = rim + 16 * part
                t[start : start + 16, at] = zero if q is None else tile_2(w, tap, q, half)


def matrix_2_up(narrow, t, w):
    repeat_lanes(narrow, w)
    zero = jnp.zeros((16, L), BF)
    at = lane((16, L))
    for row in range(2):
        for (base, edge), tap in zip(GROUPS2, (row + 1, row + 3, row - 1)):
            for q in range(16):
                span = slice(row * 256 + q * 16, row * 256 + q * 16 + 16)
                for half in range(2):
                    cols = slice(base + L * half, base + L * half + L)
                    t[span, cols] = tile_2(w, tap, q, half) if 0 <= tap < TAPS else zero
                rim = zero
                if 0 <= tap < TAPS and q in (0, 1, 15):
                    b = {0: 3, 1: 4, 15: 0}[q]
                    start = (tap * TAPS + b) * 16
                    cond = at < 32 if q == 15 else at >= 96
                    rim = jnp.where(cond, w[start : start + 16, :], 0.0).astype(BF)
                t[span, edge : edge + L] = rim


def band(w, tap, channel, offset):
    tile = jnp.zeros((32, L), F32)
    for b in range(TAPS):
        start = (tap * TAPS + b) * 2 + channel
        tile = jnp.where(offset == b, w[start : start + 1, :], tile)
    return tile.astype(BF)


def matrix_1_down(w, t, col):
    q, zero = sub((32, L)), jnp.zeros((32, L), BF)
    for half in range(2):
        p = 8 * half + lane((32, L)) // 16
        inner = q - 2 * p + 1
        rim = jnp.where(q == 31, -2 * p, jnp.where(q == 0, 33 - 2 * p, jnp.where(q == 1, 34 - 2 * p, -9)))
        for row in range(2):
            cols = slice(col + row * 256 + half * L, col + row * 256 + half * L + L)
            for (base, edge), frames in zip(TILES0, ((None, -1), (0, 1), (2, 3), (4, 5))):
                if not SPAN0[row].start <= base < SPAN0[row].stop:
                    continue
                for part, frame in enumerate(frames):
                    tap = -1 if frame is None else frame - 2 * row + 1
                    for c in range(2):
                        start = part * 64 + c * 32
                        ok = 0 <= tap < TAPS
                        for offset, bins in ((base, inner), (edge, rim)):
                            span = slice(offset + start, offset + start + 32)
                            t[span, cols] = band(w, tap, c, bins) if ok else zero


def matrix_1_up(w, t, col):
    q, zero = sub((32, L)), jnp.zeros((32, L), BF)
    at = lane((32, L))
    rim = jnp.where(at < 16, q - 31, jnp.where(at >= 112, q + 3, -9))
    for frame in range(4):
        taps = (frame + 1, frame - 1, frame + 3, frame - 3)
        for c in range(2):
            span = slice(frame * 64 + c * 32, frame * 64 + c * 32 + 32)
            for k, tap in enumerate(taps):
                ok = 0 <= tap < TAPS
                for half in range(2):
                    p = 8 * half + at // 16
                    start = col + 256 * k + L * half
                    t[span, start : start + L] = band(w, tap, c, q - 2 * p + 1) if ok else zero
                start = col + 1024 + L * k
                t[span, start : start + L] = band(w, tap, c, rim) if ok else zero


def double_lanes(value, first):
    while first < L:
        value = value + pltpu.roll(value, first, 1)
        first *= 2
    return value


def window_0(
    index, seg_lengths, frame_mask, raw_c, raw_d, gain1, shift1, gain2, shift2, gain3, shift3, bias2, bias1,
    t, w1c, w1d, aux, prm,
):
    w1c[...] = jnp.zeros(w1c.shape, F32)
    w1d[...] = jnp.zeros(w1d.shape, F32)
    for k in range(TAPS * TAPS):
        span = slice(2 * k, 2 * k + 2)
        w1c[span, 0:16] = raw_c[k].astype(F32)
        value = raw_d[k].astype(F32)
        w1d[0, span, 0:16] = value[:, 0:16]
        w1d[1, span, 0:16] = value[:, 16:32]
    w1c[...] = double_lanes(w1c[...], 16)
    for k in range(2):
        w1d[k] = double_lanes(w1d[k], 16)
    matrix_1_down(w1c, t, 0)
    prm[...] = jnp.zeros(prm.shape, F32)
    for k, value in enumerate((gain1, shift1, gain2, shift2, gain3, shift3, bias2)):
        prm[k : k + 1, 0 : value.shape[1]] = value[...]
    rows8, at = sub((8, L)), lane((8, L))
    value = prm[...]
    wide = (rows8 == 2) | (rows8 == 3)
    value = double_lanes(value + jnp.where(wide, 0.0, pltpu.roll(value, 16, 1)), 32)
    last = jnp.where(at // 32 % 2 == 0, bias1[0:1, 0:1], bias1[0:1, 1:2])
    prm[...] = jnp.where(rows8 == 7, last, value)
    row, at = sub((M, L)), lane((M, L))
    kept = jnp.broadcast_to(frame_mask[...].astype(F32), (8, L))
    kept = jnp.minimum(kept, pltpu.roll(kept, L - 1, 1))[0:1]
    keep = []
    for i in range(2):
        value = jnp.sum(jnp.where(at == 4 * row + 2 * i, kept, 0.0), axis=1, keepdims=True)
        keep.append(jnp.broadcast_to(value, (M, L)))
        aux[2 + i] = keep[i]
    aux[4] = keep[0] * keep[1]
    lengths = seg_lengths.get()
    start = jnp.int32(0)
    here = (index[2] * M + row) * 4
    shut = [here == index[3], here + 4 == index[3]]
    for k in range(lengths.shape[0]):
        shut = [shut[0] | (here == start), shut[1] | (here + 4 == start)]
        start = start + 4 * lengths[k]
    aux[0] = jnp.where(shut[0], 0.0, 1.0)
    aux[1] = jnp.where(shut[1], 0.0, 1.0)


def window_1(w2c, t, w):
    matrix_2_down(w2c, t, w)


def window_2(w2d, t, w):
    matrix_2_up(w2d, t, w)


def window_3(w1d, t):
    matrix_1_up(w1d.at[0], t, 0)
    matrix_1_up(w1d.at[1], t, COLS1B)


def window_swap(w2c, w2d, w1c, t2a, t2b, t1b, a, b, c, w):
    matrix_2_down(w2d, a, w)
    t2a.put(a)
    matrix_2_up(w2c, b, w)
    t2b.put(b)
    matrix_1_up(w1c, c, 0)
    t1b.put(c)


def correlate(coarse, fine, d, spans=(slice(None),)):
    for k in range(R // CHUNK):
        span = slice(CHUNK * k, CHUNK * k + CHUNK)
        left, right = ready(coarse, k), ready(fine, k)
        width = d.shape[0] // len(spans)
        for i, columns in enumerate(spans):
            out = slice(width * i, width * i + width)
            value = lax.dot_general(
                left[span, out], right[span, columns], (((0,), (0,)), ((), ())), preferred_element_type=F32
            )
            d[out, :] = value if k == 0 else d[out, :] + value


def weight_2(d, out):
    at = lane((32, L))
    sums = {}
    for base, rim, tap in GROUPS1:
        total = jnp.zeros((32, L), F32)
        for p in range(8):
            span = slice(32 * p, 32 * p + 32)
            parts = [d[span, base : base + L], d[span, base + L : base + 256], d[span, rim : rim + L]]
            if p == 0:
                value = jnp.where(at < 16, pltpu.roll(parts[2], 16, 1), pltpu.roll(parts[0], 16, 1))
            else:
                which, off = divmod(32 * p - 16, L)
                value = pltpu.roll(parts[which], L - off, 1)
                if off + 80 > L:
                    value = jnp.where(at < L - off, value, pltpu.roll(parts[which + 1], L - off, 1))
            total = total + value
        sums[tap] = total
    out[0:32, :] = jnp.where(at < 80, sums[0], pltpu.roll(sums[4], 80, 1))
    out[32:64, :] = jnp.where(at < 80, sums[1], pltpu.roll(sums[4], 32, 1))
    out[64:96, :] = sums[2]
    out[96:128, :] = sums[3]


def weight_1(d, out, start):
    at = lane((16, L)) % 32
    result = jnp.zeros((16, L), F32)
    for k in range(3):
        total = jnp.zeros((16, L), F32)
        for row in range(2):
            base, edge = TILES0[k + row]
            base, edge = base - SPAN0[row].start, edge - SPAN0[row].start
            for p in range(16):
                first = row * 256 + p * 16
                span = slice(first, first + 16)
                value = pltpu.roll(d[span, base : base + L], (1 - 2 * p) % L, 1)
                if p in (0, 15):
                    rim = pltpu.roll(d[span, edge : edge + L], L - 31 if p == 0 else 3, 1)
                    value = jnp.where(at == 0 if p == 0 else at >= 3, rim, value)
                total = total + value
        if k > 0:
            total = pltpu.roll(total, 8 * k, 1)
        result = jnp.where((at >= 8 * k) & (at < 8 * k + TAPS), total, result)
    out[start : start + 16, :] = result


def window_4(low, act, fine, out, d):
    correlate(low, fine, d, SPAN0)
    weight_1(d, out, 0)
    correlate(act, fine, d, SPAN0)
    weight_1(d, out, 16)


def window_5(coarse, fine, out, d):
    correlate(coarse, fine, d)
    weight_2(d, out)


HALF = 144


def window_6(index, coarse, fine, w1d, w2d, keep, give, d, kept):
    correlate(coarse, fine, d)
    weight_2(d, kept)
    even = index[1] == 0
    up_two, up_one = ready(w2d), ready(w1d)

    def place(span, a, b):
        keep[span, :] = jnp.where(even, a, b)
        give[span, :] = jnp.where(even, b, a)

    place(slice(0, 128), up_two[...], kept[...])
    place(slice(128, 144), up_one[0:16, :], up_one[16:32, :])


def window_7(coarse, fine, keep, got, bias, low, d, first):
    correlate(coarse, fine, d, SPAN0)
    weight_1(d, first, 0)
    low[0:HALF, :] = (keep[...] + got[...]).astype(BF)
    low[HALF : HALF + 16, :] = first[...].astype(BF)
    low[HALF + 16 : HALF + 32, :] = jnp.concatenate([bias[...], jnp.zeros((8, L), F32)]).astype(BF)


def unpack_kernel(
    index, mine, other, mom4, mom5, mom6,
    w1c, w2c, w2d, w1d, bias1, gain1, shift1, gain2, shift2, bias2, gain3, shift3,
):
    even = index[1] == 0
    a, b = mine[...], other[...]
    up, down = jnp.where(even, a, b), jnp.where(even, b, a)
    own = a[HALF:] + b[HALF:]
    for half, out in ((up, w2d), (down, w2c)):
        turned = half[0:128].T
        moved = [turned] + [pltpu.roll(turned, L - 32 * tap, 1) for tap in range(1, 4)]
        for tap in range(TAPS):
            for b in range(TAPS):
                if tap < 4:
                    value = moved[tap][16 * b : 16 * b + 16]
                else:
                    value = moved[b // 3][80 + 16 * (b % 3) : 96 + 16 * (b % 3)]
                out[tap * TAPS + b] = value[:, 0:32]
    tall = jnp.concatenate([up[128:144], down[128:144], own[0:16], jnp.zeros((80, L), F32)]).T
    other_tall = pltpu.roll(tall, L - 32, 1)
    for tap in range(TAPS):
        for b in range(TAPS):
            for c in range(2):
                row = (tap + 1) % 2 * 64 + c * 32 + (tap + 1) // 2 * 8 + b
                w1d[tap * TAPS + b, c : c + 1, :] = tall[row : row + 1, 0:32]
                w1c[tap * TAPS + b, c : c + 1, :] = other_tall[row : row + 1, 0:16]
    total = total_rows(own[16:24])
    total = jnp.broadcast_to(total, (8, L))
    total = total + pltpu.roll(total, 64, 1)
    for step in (16, 8, 4, 2, 1):
        total = total + pltpu.roll(total, L - step, 1)
    total = jnp.where(lane((8, L)) == 0, total, pltpu.roll(total, L - 31, 1))
    bias1[...] = total[0:1, 0:2]
    for out, mom, row in (
        (gain1, mom6, 1), (shift1, mom6, 0), (gain2, mom5, 1), (shift2, mom5, 0),
        (bias2, mom5, 2), (gain3, mom4, 1), (shift3, mom4, 0),
    ):
        out[...] = mom[row : row + 1, 0 : out.shape[1]]


def ready(ref, part=None):
    return ref.get(part) if isinstance(ref, Arriving) else ref


def spread(scr, store):
    at = lane((M, L)) // 32
    for half in range(2):
        parts = [scr[k % 2, pl.ds(2 * half + k // 2, M, stride=4), :] for k in range(4)]
        for block in range(4):
            value = parts[block]
            for k in range(4):
                if k != block:
                    value = jnp.where(at == k, pltpu.roll(parts[k], (32 * (k - block)) % L, 1), value)
            store(block, half, value)


def gather(blocks, scr):
    at = lane((M, L)) // 32
    for half in range(2):
        parts = [blocks(block, half) for block in range(4)]
        for k in range(4):
            value = parts[k]
            for block in range(4):
                if block != k:
                    value = jnp.where(
                        at == block, pltpu.roll(parts[block], (32 * (block - k)) % L, 1), value
                    )
            scr[k % 2, pl.ds(2 * half + k // 2, M, stride=4), :] = value


def layout_kernel(index, frame_mask, mix, cot, cross, core, x0, c0, scr, wide, ends):
    def place(out, block, row):
        def store(k, half, value):
            at = slice(L * half, L * half + L)
            out[rows(block + k), at] = value.astype(BF)
            wide[rows(row + k), at] = value

        return store

    m = mix.get()

    def mix_tile(t):
        for c in range(2):
            scr[c] = m[c, :, pl.ds(pl.multiple_of(t * L, L), L)].astype(F32)
        spread(scr, place(x0, 4 * t, 4 * t))

    for_blocks(mix_tile, NJ // 4)
    g = cot.get()
    per_stem = g.shape[3] // L

    def cot_tile(t):
        for c in range(2):
            lanes = pl.ds(pl.multiple_of((t % per_stem) * L, L), L)
            scr[c] = g[t // per_stem, c, :, lanes].astype(F32)
        spread(scr, place(c0, 4 * t, NJ + 4 * t))

    for_blocks(cot_tile, NJ // 4)
    ends[...] = jnp.zeros(ends.shape, F32)
    pack_ends(wide, index, ends.at[0], ends.at[1], 2 * NJ)
    even = index[1] == 0

    kept = frame_mask.get()

    def least(first, count):
        value = kept[first]
        for k in range(1, count):
            value = jnp.minimum(value, kept[first + k])
        return value.astype(F32)

    for i, (first, count) in enumerate(((0, 2), (2, 2), (0, 4))):
        top, low = least(first, count), least(4 * M - 4 + first, count)
        row = 2 * NJ + i
        ends[0, row : row + 1, :] = jnp.full((1, 2 * L), jnp.where(even, top, low))
        ends[1, row : row + 1, :] = jnp.full((1, 2 * L), jnp.where(even, low, top))
    cross[...] = ends[0].astype(BF)
    core[...] = ends[1].astype(BF)


def columns_0(cat, blocks, read, left, right, aux):
    a, a_next = aux[0], aux[1]
    for which, (first, count) in enumerate(blocks):

        def one(i, which=which, first=first):
            j = first + i
            span, stores = rows(j), []
            for half in range(2):
                value = read(which, j, half)
                stores.append((cat, span, slice(256 + L * half, 384 + L * half), value.astype(BF)))
                if half == 1:
                    moved = from_prev(value, left[rows(j, 8), L : 2 * L], a)
                    stores.append((cat, span, slice(0, 128), moved.astype(BF)))
                else:
                    moved = from_next(value, right[rows(j, 8), 0:L], a_next)
                    stores.append((cat, span, slice(768, 896), moved.astype(BF)))
            put_all(stores)

        for_blocks(one, count)
    rims_0(cat)


def conv_one_kernel(
    index, x0, cross_in, core_in, aux, t,
    z, cross, core, mom, kept, hx, cat, lf, rf, lw, rw,
):
    even = index[1] == 0
    a, b = cross_in[...].astype(F32), core_in[...].astype(F32)
    lf[...] = jnp.where(even, a, b)
    rf[...] = jnp.where(even, b, a)
    hx[:, 0:L] = rf[0 : 2 * NJ, 0:L]
    hx[:, L : 2 * L] = lf[0 : 2 * NJ, L : 2 * L]
    kept[...] = jnp.zeros(kept.shape, F32)
    kept[0:3, :] = lf[2 * NJ : 2 * NJ + 3, 0:L]
    kept[3:6, :] = rf[2 * NJ : 2 * NJ + 3, 0:L]
    widen(lf.at[0:NJ], lw)
    widen(rf.at[0:NJ], rw)
    x = ready(x0)
    read = lambda which, j, h: x[rows(j), L * h : L * h + L].astype(F32)
    columns_0(cat, [(0, NJ)], read, lw, rw, aux)
    weights = ready(t)

    def use(j, k, at, value, s1, s2, stores):
        stores.append((z, rows(j), at, value))
        part = value * aux[2 + k // 2]
        return s1 + sum8(part), s2 + sum8(part * value)

    stats = product_sums(rows_from_0(cat, weights), use)
    pack_ends(z, index, cross, core)
    stats = fold(stack_rows(stats), 16)
    at = sub((8, L))
    stats = jnp.where(at == 2, total_rows(aux[2] + aux[3]) * (NJ * 16.0), stats)
    stats = jnp.where(at == 3, total_rows(aux[4]) * (NJ * 8.0), stats)
    pack_moments(mom, cross, stats)


def conv_two_kernel(
    index, z1, cross_in, core_in, mom1, prm, aux, t,
    z2, cross, core, mom, eb, hf, cat, ef, lw, rw,
):
    mean, scale = norm_terms(mom1, mom1[2:3])
    gain, shift = prm[0:1], prm[1:2]

    def act(value):
        return silu((value - mean) * scale * gain + shift)

    a, a_next = aux[0], aux[1]
    for at in tiles(512):
        left, right = sides(index, cross_in, core_in, at)
        hf[0, :, at] = left
        hf[1, :, at] = right
        ef[0, :, at] = act(left)
        ef[1, :, at] = act(right)
    widen(ef.at[0], lw)
    widen(ef.at[1], rw)

    def one(j):
        span, stores = rows(j), []
        for k, at in enumerate(tiles(512)):
            value = act(z1[span, at])
            stores.append((cat, span, at, value.astype(BF)))
            if k >= 2:
                moved = from_prev(value, lw[rows(j, 8), at], a)
                stores.append((cat, span, slice(256 + L * k, 384 + L * k), moved.astype(BF)))
            start = 768 + L * k if k < 2 else 1280 + L * k
            moved = from_next(value, rw[rows(j, 8), at], a_next)
            stores.append((cat, span, slice(start, start + L), moved.astype(BF)))
        put_all(stores)

    for_blocks(one)
    rims_1(cat, GROUPS1)
    def group_out(rs, at, top, low):
        ef[2, rs, at] = act(top)
        ef[3, rs, at] = act(low)

    end_rows(z1, group_out)
    eb[...] = ef[...].astype(BF)
    weights = ready(t)

    def use(j, k, at, value, s1, s2, stores):
        stores.append((z2, rows(j), at, value))
        part = value * aux[4]
        return s1 + sum8(part), s2 + sum8(part * value)

    stats = product_sums(lambda rs: [matmul(cat[rs, :], weights[...])], use)
    pack_ends(z2, index, cross, core)
    pack_moments(mom, cross, fold(stack_rows(stats), 32))


def columns_2(cat, read, left, right, aux):
    a, a_next = aux[0], aux[1]

    def one(j):
        span, stores = rows(j), []
        for k, at in enumerate(tiles(256)):
            value = read(j, at)
            stores.append((cat, span, at, value.astype(BF)))
            moved = from_prev(value, left[rows(j, 8), at], a)
            stores.append((cat, span, slice(256 + L * k, 384 + L * k), moved.astype(BF)))
            moved = from_next(value, right[rows(j, 8), at], a_next)
            stores.append((cat, span, slice(768 + L * k, 896 + L * k), moved.astype(BF)))
        put_all(stores)

    for_blocks(one)
    rims_2(cat)


def up_two_kernel(
    index, z2, cross_in, core_in, mom1, mom2, prm, aux, t,
    rect, cross, core, mom, hf, act2, cat, lf, rf, lw, rw,
):
    mean, scale = norm_terms(mom2, mom1[3:4])
    gain, shift, bias = prm[2:3], prm[3:4], prm[6:7]

    def act(value):
        return silu((value - mean) * scale * gain + shift)

    for at in tiles(256):
        left, right = sides(index, cross_in, core_in, at)
        hf[0, :, at] = left
        hf[1, :, at] = right
        lf[:, at] = act(left)
        rf[:, at] = act(right)
    widen(lf, lw)
    widen(rf, rw)
    columns_2(cat, lambda j, at: act(z2[rows(j), at]), lw, rw, aux)
    act2[...] = cat[:, 0:256]
    weights = ready(t)

    def use(j, k, at, value, s1, s2, stores):
        value = softplus(value + bias)
        stores.append((rect, rows(j), at, value))
        part = value * aux[2 + k // 2]
        return s1 + sum8(part), s2 + sum8(part * value)

    stats = product_sums(rows_from_2(cat, weights), use)
    pack_moments(mom, cross, fold(stack_rows(stats), 16))
    pack_ends(rect, index, cross, core)


def columns_1b(cat, read, left, right, aux):
    a, a_next = aux[0], aux[1]

    def one(j):
        span, stores = rows(j), []
        for k, at in enumerate(tiles(512)):
            value = read(j, k, at)
            stores.append((cat, span, at, value.astype(BF)))
            if k >= 2:
                moved = from_prev(value, left[rows(j, 8), at], a)
                stores.append((cat, span, slice(256 + L * k, 384 + L * k), moved.astype(BF)))
            else:
                moved = from_next(value, right[rows(j, 8), at], a_next)
                stores.append((cat, span, slice(768 + L * k, 896 + L * k), moved.astype(BF)))
        put_all(stores)

    for_blocks(one)
    rims_1(cat, GROUPS1[:4])


def edge_columns(own, prev, after):
    at = lane((NJ, L))
    place = sub((NJ, L))
    parts = [own, prev, after]
    groups = [own[:, 0:256], own[:, 256:512], prev, after]
    for g in groups:
        low = jnp.where((place == NJ - 1) | (at >= 32), 0.0, pltpu.roll(g[:, 0:L], NJ - 1, 0))
        high = jnp.where((place == 0) | (at < 112), 0.0, pltpu.roll(g[:, L : 2 * L], 1, 0))
        parts.append(low + high)
    return jnp.concatenate(parts, axis=1).astype(BF)


def quarter_blocks(index, stems):
    count = NJ // stems
    return [((index[0] ^ k) * count, count) for k in range(stems)]


def up_one_kernel(
    index, rect, cross_in, core_in, mom1, mom3, prm, aux, ends1, cat1, t,
    m0, m1, m2, m3, hf, low3, sf, shf, cat, lf, rf, ef, ff, lw, rw,
):
    mean, scale = norm_terms(mom3, mom1[2:3])
    gain, shift, bias = prm[4:5], prm[5:6], prm[7:8]

    def norm(value):
        return (value - mean) * scale * gain + shift

    for at in tiles(512):
        left, right = sides(index, cross_in, core_in, at)
        hf[0, :, at] = left
        hf[1, :, at] = right
        lf[:, at] = norm(left)
        rf[:, at] = norm(right)
    widen(lf, lw)
    widen(rf, rw)
    columns_1b(cat, lambda j, k, at: norm(rect[rows(j), at]), lw, rw, aux)
    low3[...] = cat[:, 0:512]

    def group_out(rs, at, top, low):
        ef[0, rs, at] = norm(top)
        ef[1, rs, at] = norm(low)

    end_rows(rect, group_out)
    wide = jnp.concatenate([bias, bias], axis=1)
    zero = jnp.zeros((NJ, 256), F32)
    a, a_end = aux[0, 0:1, 0:1], aux[1, M - 1 : M, 0:1]
    e1 = [ends1[k].astype(F32) for k in range(4)]
    edges = [
        (
            edge_columns(lf[...], zero, ef[0, :, 0:256] * a),
            edge_columns(e1[0], zero, e1[2][:, 0:256] * a),
        ),
        (
            edge_columns(rf[...], ef[1, :, 256:512] * a_end, zero),
            edge_columns(e1[1], e1[3][:, 256:512] * a_end, zero),
        ),
    ]
    weights, other = ready(t), ready(cat1)
    value = matmul(jnp.concatenate([e[0] for e in edges]), weights[:, 0:COLS1B], True)
    value = value + matmul(jnp.concatenate([e[1] for e in edges]), weights[:, COLS1B : 2 * COLS1B], True)
    for k, half in ((0, 1), (1, 0)):
        at = slice(L * half, L * half + L)
        shf[:, at] = sigmoid(value[NJ * k : NJ * k + NJ, at] + bias)
    masks = (m0, m1, m2, m3)
    per = R // len(masks)
    for mask, (first, count) in zip(masks, quarter_blocks(index, len(masks))):
        rs = rows(lax.div(first, count), per)
        value = matmul(cat[rs, :], weights[:, 0:COLS1B], True)
        value = value + matmul(other[rs, :], weights[:, COLS1B : 2 * COLS1B], True)
        value = sigmoid(value + wide)
        sf[rs, :] = value
        mask[0:per, :] = value.astype(BF)
        ff[...] = jnp.zeros(ff.shape, F32)
        ff[0:count, :] = shf[rows(lax.div(first, count), count), :]
        mask[per : per + 16, :] = ff[...].astype(BF)


def ratio_terms(masks):
    squares = [m * m for m in masks]
    power = squares[0]
    for s in squares[1:]:
        power = power + s
    inverse = 1.0 / (power + RATIO_EPS)
    return [s * inverse for s in squares], inverse


def mask_back(masks, cots, mix):
    ratios, inverse = ratio_terms(masks)
    direct = cots[0] * ratios[0]
    for c, r in zip(cots[1:], ratios[1:]):
        direct = direct + c * r
    common = 2.0 * mix * inverse
    return [m * common * (c - direct) for m, c in zip(masks, cots)], direct


def mask_kernel(index, m0, m1, m2, m3, c0, x0, hx, g0, g1, g2, g3, df, ff):
    masks, grads = (m0, m1, m2, m3), (g0, g1, g2, g3)
    stems = len(masks)
    per, blocks = R // stems, NJ // stems
    mine = index[0]
    cots, mix, rim = ready(c0), ready(x0), ready(hx)

    def one(j):
        for at in tiles(256):
            m = [masks[s][rows(j), at].astype(F32) for s in range(stems)]
            c = [cots[rows((mine ^ s) * blocks + j), at].astype(F32) for s in range(stems)]
            x = mix[rows(mine * blocks + j), at].astype(F32)
            values, own = mask_back(m, c, x)
            df[rows(j), at] = own
            for s in range(stems):
                grads[s][rows(j), at] = values[s].astype(BF)

    for_blocks(one, blocks)
    m = [masks[s][per : per + 16, :].astype(F32)[0:blocks] for s in range(stems)]
    c = [rim[rows(stems + (mine ^ s), blocks), :] for s in range(stems)]
    values, _ = mask_back(m, c, rim[rows(mine, blocks), :])
    for s in range(stems):
        ff[...] = jnp.zeros(ff.shape, F32)
        ff[0:blocks, :] = values[s]
        grads[s][per : per + 16, :] = ff[...].astype(BF)


def estimate_kernel(index, m0, m1, m2, m3, x0, w1d, out, t, scr, est):
    masks = (m0, m1, m2, m3)
    stems = len(masks)
    blocks = NJ // stems
    mine = index[0]
    matrix_1_down(w1d.at[0], t, 0)
    matrix_1_down(w1d.at[1], t, 512)
    mix = ready(x0)

    def one(j):
        for at in tiles(256):
            m = [masks[s][rows(j), at].astype(F32) for s in range(stems)]
            x = mix[rows(mine * blocks + j), at].astype(F32)
            ratios, _ = ratio_terms(m)
            for s in range(stems):
                est[s, rows(j), at] = x * ratios[s]

    for_blocks(one, blocks)
    for s in range(stems):
        for t in range(blocks // 4):
            gather(
                lambda block, half, s=s, t=t: est[s, rows(4 * t + block), L * half : L * half + L], scr
            )
            for c in range(2):
                out[mine ^ s, c, :, L * t : L * t + L] = scr[c].astype(BF)


def down_one_back_kernel(
    index, q0, q1, q2, q3, sigh, sig, aux, mom1, mom3, rect, t,
    g3, cat, cross, core, mom, bias, gf, hf, zf, hw,
):
    grads = (q0, q1, q2, q3)
    blocks = quarter_blocks(index, len(grads))
    per = R // len(grads)
    rim = ready(sigh)
    for grad, (first, count) in zip(grads, blocks):
        span = rows(lax.div(first, count), count)
        value = grad[per : per + 16, :].astype(F32)[0:count]
        own = rim[span, :]
        hf[span, :] = value * own * (1.0 - own)
    zf[...] = jnp.zeros(zf.shape, F32)
    widen(hf, hw)
    sigs = ready(sig)

    def read(which, j, half):
        at = slice(L * half, L * half + L)
        own = sigs[rows(j), at]
        value = grads[which][rows(j - blocks[which][0]), at].astype(F32) * own * (1.0 - own)
        zf[...] = zf[...] + sum8(value)
        return value

    columns_0(cat, blocks, read, hw, hw, aux)
    bias[...] = zf[...]
    weights = ready(t)

    mean, scale = norm_terms(mom3, mom1[2:3])
    r = ready(rect)

    def use(j, k, at, value, s1, s2, stores):
        if k >= 4:
            stores.append((gf, rows(j), slice(L * k - 512, L * k - 384), value))
            return s1, s2
        stores.append((g3, rows(j), at, value))
        return s1 + sum8(value), s2 + sum8(value * (r[rows(j), at] - mean))

    s1, s2 = product_sums(rows_from_0(cat, weights), use)
    pack_ends(g3, index, cross, core)
    pack_moments(mom, cross, fold(stack_rows([s1, s2 * scale]), 16))


def norm_back(g, xhat, kept, moments, count, factor):
    return factor * (g - kept * ((moments[0:1] + xhat * moments[1:2]) / count))


def up_two_back_kernel(
    index, g3, cross_in, core_in, mom4, mom1, mom3, mom2, prm, aux, kept, rect, h3, t, z2,
    g2, cat, cross, core, mom, lf, rf, lw, rw,
):
    count = mom1[2:3]
    mean, scale = norm_terms(mom3, count)
    factor = scale * prm[4:5]
    inverse = 1.0 / count

    def back(g, r, keep):
        xhat = (r - mean) * scale
        value = factor * (g - keep * ((mom4[0:1] + xhat * mom4[1:2]) * inverse))
        return value * softplus_slope(r)

    r, h = ready(rect), ready(h3)
    for k, at in enumerate(tiles(512)):
        left, right = sides(index, cross_in, core_in, at)
        row = k // 2
        lf[:, at] = back(left, h[0, :, at], kept[row : row + 1, :])
        rf[:, at] = back(right, h[1, :, at], kept[3 + row : 4 + row, :])
    widen(lf, lw)
    widen(rf, rw)
    a, a_next = aux[0], aux[1]

    def one(j, total):
        span, stores = rows(j), []
        for k, at in enumerate(tiles(512)):
            value = back(g3[span, at], r[span, at], aux[2 + k // 2])
            total = total + sum8(value)
            stores.append((cat, span, at, value.astype(BF)))
            if k >= 2:
                moved = from_prev(value, lw[rows(j, 8), at], a)
                stores.append((cat, span, slice(256 + L * k, 384 + L * k), moved.astype(BF)))
            start = 768 + L * k if k < 2 else 1280 + L * k
            moved = from_next(value, rw[rows(j, 8), at], a_next)
            stores.append((cat, span, slice(start, start + L), moved.astype(BF)))
        put_all(stores)
        return total

    def four(j, total):
        for i in range(UNROLL):
            total = one(j * UNROLL + i, total)
        return total

    bias = lax.fori_loop(0, NJ // UNROLL, four, jnp.zeros((8, L), F32))
    rims_1(cat, GROUPS1)
    weights = ready(t)

    mean2, scale2 = norm_terms(mom2, mom1[3:4])
    gain, shift = prm[2:3], prm[3:4]
    z = ready(z2)

    def use(j, k, at, value, s1, s2, stores):
        xhat = (z[rows(j), at] - mean2) * scale2
        value = value * silu_slope(xhat * gain + shift)
        stores.append((g2, rows(j), at, value))
        return s1 + sum8(value), s2 + sum8(value * xhat)

    stats = fold(stack_rows(product_sums(lambda rs: [matmul(cat[rs, :], weights[...])], use)), 32)
    pack_ends(g2, index, cross, core)
    bias = fold(stack_rows([total_rows(bias)] * 3), 16)
    pack_moments(mom, cross, jnp.where(sub((8, L)) == 2, bias, stats))


def down_two_back_kernel(
    index, g2, cross_in, core_in, mom5, mom1, mom2, prm, aux, kept, z2, h2, t, gact, z1,
    g1, low2, cross, core, mom, cat, lf, rf, lw, rw,
):
    count = mom1[3:4]
    mean, scale = norm_terms(mom2, count)
    factor = scale * prm[2:3]
    inverse = 1.0 / count

    def back(g, z, keep):
        xhat = (z - mean) * scale
        return factor * (g - keep * ((mom5[0:1] + xhat * mom5[1:2]) * inverse))

    z, h = ready(z2), ready(h2)
    for at in tiles(256):
        left, right = sides(index, cross_in, core_in, at)
        lf[:, at] = back(left, h[0, :, at], kept[2:3, :])
        rf[:, at] = back(right, h[1, :, at], kept[5:6, :])
    widen(lf, lw)
    widen(rf, rw)
    columns_2(cat, lambda j, at: back(g2[rows(j), at], z[rows(j), at], aux[4]), lw, rw, aux)
    low2[...] = cat[:, 0:256]
    weights, added = ready(t), ready(gact)

    mean1, scale1 = norm_terms(mom1, mom1[2:3])
    gain, shift = prm[0:1], prm[1:2]
    z = ready(z1)

    def use(j, k, at, value, s1, s2, stores):
        xhat = (z[rows(j), at] - mean1) * scale1
        value = (value + added[rows(j), at]) * silu_slope(xhat * gain + shift)
        stores.append((g1, rows(j), at, value))
        return s1 + sum8(value), s2 + sum8(value * xhat)

    stats = fold(stack_rows(product_sums(rows_from_2(cat, weights), use)), 16)
    pack_ends(g1, index, cross, core)
    pack_moments(mom, cross, stats)


def up_one_back_kernel(
    index, g1, cross_in, core_in, mom6, mom1, prm, aux, kept, z1, h1, t,
    n0, n1, n2, n3, low1, cat, lf, rf, lw, rw,
):
    count = mom1[2:3]
    mean, scale = norm_terms(mom1, count)
    factor = scale * prm[0:1]
    inverse = 1.0 / count

    def back(g, z, keep):
        xhat = (z - mean) * scale
        return factor * (g - keep * ((mom6[0:1] + xhat * mom6[1:2]) * inverse))

    z, h = ready(z1), ready(h1)
    for k, at in enumerate(tiles(512)):
        left, right = sides(index, cross_in, core_in, at)
        row = k // 2
        lf[:, at] = back(left, h[0, :, at], kept[row : row + 1, :])
        rf[:, at] = back(right, h[1, :, at], kept[3 + row : 4 + row, :])
    widen(lf, lw)
    widen(rf, rw)
    columns_1b(
        cat, lambda j, k, at: back(g1[rows(j), at], z[rows(j), at], aux[2 + k // 2]), lw, rw, aux
    )
    low1[...] = cat[:, 0:512]
    weights = ready(t)
    nets = (n0, n1, n2, n3)
    per = R // len(nets)
    for net, (first, blocks) in zip(nets, quarter_blocks(index, len(nets))):
        rs = rows(lax.div(first, blocks), per)
        net[...] = matmul(cat[rs, :], weights[...], True).astype(BF)


def mixture_kernel(p0, p1, p2, p3, direct, out, scr):
    parts = (p0, p1, p2, p3)
    own = ready(direct)

    def tile(t):
        def block(k, half):
            at = slice(L * half, L * half + L)
            value = own[rows(4 * t + k), at]
            for part in parts:
                value = value + part[rows(4 * t + k), at].astype(F32)
            return value

        gather(block, scr)
        for c in range(2):
            out[c, :, pl.ds(pl.multiple_of(t * L, L), L)] = scr[c]

    for_blocks(tile, NJ // len(parts) // 4)


def pairs(count, offset):
    there = [(i, (i + offset) % count) for i in range(0, count, 2)]
    return there + [(b, a) for a, b in there]


def flip(values, axis, bit):
    return lax.ppermute(values, axis, [(i, i ^ bit) for i in range(lax.axis_size(axis))])


def sum_over(values, axis):
    count = lax.axis_size(axis)
    if count & (count - 1):
        return lax.psum(values, axis)
    step = 1
    while step < count:
        radix = 2 if step == 1 or count // step == 2 else 4
        moved = [flip(values, axis, step * k) for k in range(1, radix)]
        for m in moved:
            values = values + m
        step *= radix
    return values


def sum_chips(low, axis, beside):
    count = lax.axis_size(axis)
    if count == 8:
        moved = [flip(low, axis, bit) for bit in (2, 4, 6)]
        made, low = beside(low)
        mine = low.astype(F32) + moved[0].astype(F32) + moved[1].astype(F32) + moved[2].astype(F32)
    else:
        made, low = beside(low)
        mine, step = low.astype(F32), 2
        while step < count:
            mine = mine + flip(mine, axis, step)
            step *= 2
    return mine, flip(mine, axis, 1), made


def exchange(cross, core, mom, axis, beside):
    count = lax.axis_size(axis)
    near = lax.ppermute(cross, axis, pairs(count, -1))
    if count == 8:
        far = lax.ppermute(mom, axis, pairs(count, 3))
        across = flip(mom, axis, 4)
        inside = flip(core, axis, 1)
        *made, mom = beside(mom)
        part = mom + near[NJ:, 0:L] + far + across
        return near, inside, part + flip(part, axis, 1), made
    inside = flip(core, axis, 1)
    *made, mom = beside(mom)
    return near, inside, sum_over(mom, axis), made


def swap(blocks, axis):
    return [blocks[0]] + [flip(blocks[k], axis, k) for k in range(1, len(blocks))]


def per_device(
    mixture,
    seg_lengths,
    frame_mask,
    conv_first,
    encoder_gain_vector,
    shift_first,
    conv_second,
    gain_second,
    shift_second,
    deconv_second,
    bias_second,
    decoder_gain_vector,
    shift_third,
    deconv_first,
    bias_first,
    cotangent,
):
    position = lax.axis_index("tm")
    stems = lax.axis_size("stem")
    odd = position % 2
    total = mixture.shape[1] * lax.axis_size("tm")
    index = jnp.stack([lax.axis_index("stem"), odd, position, total]).astype(jnp.int32)
    frames = mixture.shape[1]
    per, blocks = R // stems, NJ // stems
    w2c = conv_second[0].transpose(2, 3, 1, 0).reshape(400, 32)
    w2d = deconv_second[0].transpose(2, 3, 0, 1).reshape(400, 32)
    edge = 2 * NJ + 16

    def packet(lanes):
        return [((NJ + 8, lanes), F32), ((NJ, lanes), F32), ((8, L), F32)]

    def rim(lanes):
        return [((NJ, lanes), F32)] * 2

    def wide(lanes):
        return [((8 * NJ, lanes), F32)] * 2

    def far(*shape, kind=F32):
        return [(shape, kind, True)]

    raw = [conv_first[0].transpose(2, 3, 1, 0).reshape(25, 2, 16)]
    raw += [deconv_first[0].transpose(2, 3, 0, 1).reshape(25, 2, 32)]
    raw += [encoder_gain_vector, shift_first, gain_second, shift_second]
    raw += [decoder_gain_vector, shift_third, bias_second, bias_first]
    cross, core, x0, c0, *raw = run(
        layout_kernel,
        "layout",
        [((edge, 256), BF), ((edge, 256), BF), ((R, 256), BF), ((R, 256), BF)],
        [index, Far(frame_mask), Far(mixture), Far(cotangent)],
        [((2, frames, L), F32), ((2 * R, 256), F32), ((2, edge, 256), F32)],
        fetch=[Far(frame_mask.reshape(1, 4 * M))] + [Far(v) for v in raw],
    )
    near = lax.ppermute(cross, "tm", pairs(lax.axis_size("tm"), -1))
    inside = flip(core, "tm", 1)
    t, w1c, w1d, aux, prm, x0_far, c0 = run(
        window_0,
        "window_0",
        [((COLS0, 512), BF), ((56, L), F32), ((2, 56, L), F32), ((5, M, L), F32), ((8, L), F32)],
        [index, Far(seg_lengths), *raw],
        store=[x0, c0],
    )
    z1_here, cross, core, mom, kept, hx, cat0 = run(
        conv_one_kernel,
        "conv_one",
        [((R, 512), F32)] + packet(512) + [((8, L), F32), ((2 * NJ, 256), F32), ((R, COLS0), BF)],
        [index, x0, near, inside, aux, t],
        [((edge, 256), F32), ((edge, 256), F32)] + wide(256),
        flops=2 * R * COLS0 * 512,
    )
    near, inside, mom1, (t, z1, hx, cat0, z1_here) = exchange(
        cross, core, mom, "tm",
        lambda token: run(
            window_1,
            "window_1",
            [((COLS1, 256), BF)],
            [w2c],
            [((400, L), F32)],
            store=[z1_here, hx, cat0],
            carry=[z1_here],
            token=token,
        ),
    )
    z2_here, cross, core, mom, ends1, h1, cat1 = run(
        conv_two_kernel,
        "conv_two",
        [((R, 256), F32)] + packet(256) + [((4, NJ, 512), BF), ((2, NJ, 512), F32), ((R, COLS1), BF)],
        [index, z1_here, near, inside, mom1, prm, aux, t],
        [((4, NJ, 512), F32)] + wide(512),
        flops=2 * R * COLS1 * 256,
    )
    near, inside, mom2, (t, cat1, z2, ends1, h1, z2_here) = exchange(
        cross, core, mom, "tm",
        lambda token: run(
            window_2,
            "window_2",
            [((512, COLS2), BF)],
            [w2d],
            [((400, L), F32)],
            store=[cat1, z2_here, ends1, h1],
            carry=[z2_here],
            token=token,
        ),
    )
    rect_here, cross, core, mom, h2, act2 = run(
        up_two_kernel,
        "up_two",
        [((R, 512), F32)] + packet(512) + [((2, NJ, 256), F32), ((R, 256), BF)],
        [index, z2_here, near, inside, mom1, mom2, prm, aux, t],
        [((R, COLS2), BF)] + rim(256) + wide(256),
        flops=2 * R * COLS2 * 512,
    )
    near, inside, mom3, (t, cat1_here, ends1_here, rect, h2, act2, rect_here) = exchange(
        cross, core, mom, "tm",
        lambda token: run(
            window_3,
            "window_3",
            [((256, 2 * COLS1B), BF)],
            [w1d],
            fetch=[Far(cat1, COLS1B), Far(ends1)],
            store=[rect_here, h2, act2],
            carry=[rect_here],
            token=token,
        ),
    )
    *masks, h3, low3, sig, sigh = run(
        up_one_kernel,
        "up_one",
        [((per + 16, 256), BF)] * stems
        + [((2, NJ, 512), F32), ((R, 512), BF), ((R, 256), F32), ((NJ, 256), F32)],
        [index, rect_here, near, inside, mom1, mom3, prm, aux, ends1_here, cat1_here, t],
        [((R, COLS1B), BF)] + rim(512) + [((2, NJ, 512), F32), ((16, 256), F32)] + wide(512),
        flops=2 * R * 2 * COLS1B * 256,
    )
    t2a_d, t2b_c, t1b_c, c0_here, x0_here, hx_here, h3, low3, sig, sigh = run(
        window_swap,
        "window_swap",
        far(COLS1, 256, kind=BF) + far(512, COLS2, kind=BF) + far(256, COLS1B, kind=BF),
        [w2c, w2d, w1c],
        [((COLS1, 256), BF), ((512, COLS2), BF), ((256, COLS1B), BF), ((400, L), F32)],
        fetch=[Far(c0), Far(x0_far), Far(hx)],
        store=[h3, low3, sig, sigh],
    )
    masks = swap(masks, "stem")
    *grads, direct = run(
        mask_kernel,
        "mask",
        [((per + 16, 256), BF)] * stems + [((per, 256), F32)],
        [index, *masks, c0_here, x0_here, hx_here],
        [((16, 256), F32)],
    )
    grads = swap(grads, "stem")
    estimates, t, sig_here, sigh_here, rect_here, low3_here, act_here, direct = run(
        estimate_kernel,
        "estimate",
        [((stems, 2, frames, blocks * 32), BF), ((COLS0, 1024), BF)],
        [index, *masks, Far(x0_far), w1d],
        [((2, frames, L), F32), ((stems, per, 256), F32)],
        fetch=[Far(sig), Far(sigh), Far(rect), Far(low3), Far(cat1, 512)],
        store=[direct],
    )
    g3, cat0g, cross, core, mom, bias_one, gact, rect_here, low3_here, act_here = run(
        down_one_back_kernel,
        "down_one_back",
        [((R, 512), F32), ((R, COLS0), BF)] + packet(512) + [((8, L), F32), ((R, 512), F32)],
        [index, *grads, sigh_here, sig_here, aux, mom1, mom3, rect_here, t],
        [((NJ, 256), F32), ((8, L), F32), ((8 * NJ, 256), F32)],
        flops=2 * R * COLS0 * 1024,
        carry=[rect_here, low3_here, act_here],
    )
    near, inside, mom4, (w1d_grad, t, h3_here, z2_here, act2_here) = exchange(
        cross, core, mom, "tm",
        lambda token: run(
            window_4,
            "window_4",
            [((32, L), F32)],
            [low3_here, act_here, cat0g],
            [((512, 768), F32)],
            flops=2 * R * COLS0 * 1024,
            fetch=[Far(t2a_d), Far(h3), Far(z2), Far(act2)],
            token=token,
        ),
    )
    g2, cat1g, cross, core, mom, gact, z2_here, act2_here, w1d_grad = run(
        up_two_back_kernel,
        "up_two_back",
        [((R, 256), F32), ((R, COLS1), BF)] + packet(256),
        [index, g3, near, inside, mom4, mom1, mom3, mom2, prm, aux, kept, rect_here, h3_here, t, z2_here],
        rim(512) + wide(512),
        flops=2 * R * COLS1 * 256,
        carry=[gact, z2_here, act2_here, w1d_grad],
    )
    near, inside, mom5, (w2d_grad, t, h2_here, z1_here) = exchange(
        cross, core, mom, "tm",
        lambda token: run(
            window_5,
            "window_5",
            [((128, L), F32)],
            [act2_here, cat1g],
            [((256, COLS1), F32)],
            flops=2 * R * COLS1 * 256,
            fetch=[Far(t2b_c), Far(h2), Far(z1)],
            token=token,
        ),
    )
    g1, low2, cross, core, mom, z1_here, w1d_grad, w2d_grad = run(
        down_two_back_kernel,
        "down_two_back",
        [((R, 512), F32), ((R, 256), BF)] + packet(512),
        [index, g2, near, inside, mom5, mom1, mom2, prm, aux, kept, z2_here, h2_here, t, gact, z1_here],
        [((R, COLS2), BF)] + rim(256) + wide(256),
        flops=2 * R * COLS2 * 512,
        carry=[z1_here, w1d_grad, w2d_grad],
    )
    near, inside, mom6, (keep, give, t, h1_here, cat0_here) = exchange(
        cross, core, mom, "tm",
        lambda token: run(
            window_6,
            "window_6",
            [((HALF, L), F32), ((HALF, L), F32)],
            [index, low2, Far(cat1, parts=2), w1d_grad, w2d_grad],
            [((256, COLS1), F32), ((128, L), F32)],
            flops=2 * R * COLS1 * 256,
            fetch=[Far(t1b_c), Far(h1), Far(cat0)],
            token=token,
        ),
    )
    got = flip(give, "tm", 1)
    *nets, low1 = run(
        up_one_back_kernel,
        "up_one_back",
        [((per, 256), BF)] * stems + [((R, 512), BF)],
        [index, g1, near, inside, mom6, mom1, prm, aux, kept, z1_here, h1_here, t],
        [((R, COLS1B), BF)] + rim(512) + wide(512),
        flops=2 * R * COLS1B * 256,
    )
    nets = swap(nets, "stem")
    low, direct_here = run(
        window_7,
        "window_7",
        [((HALF + 32, L), BF)],
        [low1, cat0_here, keep, got, bias_one],
        [((512, 768), F32), ((16, L), F32)],
        flops=2 * R * COLS0 * 512,
        fetch=[Far(direct)],
    )
    mine, other, mixture_grad = sum_chips(
        low,
        "tm",
        lambda token: run(
            mixture_kernel,
            "mixture",
            [((2, frames, blocks * 32), F32)],
            [*nets, direct_here],
            [((2, frames, L), F32)],
            token=token,
        ),
    )
    w1c_grad, w2c_grad, w2d_grad, w1d_grad, bias1, gain1, shift1, gain2, shift2, bias2, gain3, shift3 = run(
        unpack_kernel,
        "unpack",
        [((25, 2, 16), F32), ((25, 16, 32), F32), ((25, 16, 32), F32), ((25, 2, 32), F32), ((1, 2), F32)]
        + [((1, n), F32) for n in (16, 16, 32, 32, 16, 16, 16)],
        [index, mine, other, mom4, mom5, mom6],
    )

    def turned(grad, order):
        return grad.reshape((TAPS, TAPS) + grad.shape[1:]).transpose(order)[None]

    return (
        estimates,
        mixture_grad,
        turned(w1c_grad, (3, 2, 0, 1)),
        gain1,
        shift1,
        turned(w2c_grad, (3, 2, 0, 1)),
        gain2,
        shift2,
        turned(w2d_grad, (2, 3, 0, 1)),
        bias2,
        gain3,
        shift3,
        turned(w1d_grad, (2, 3, 0, 1)),
        bias1,
    )


def solution(mesh):
    in_specs = (
        P(None, "tm", None),
        P(),
        P("tm"),
        P("stem", None, None, None, None),
        P("stem", None),
        P("stem", None),
        P("stem", None, None, None, None),
        P("stem", None),
        P("stem", None),
        P("stem", None, None, None, None),
        P("stem", None),
        P("stem", None),
        P("stem", None),
        P("stem", None, None, None, None),
        P("stem", None),
        P(None, None, "tm", "stem"),
    )
    out_specs = (
        P(None, None, "tm", "stem"),
        P(None, "tm", "stem"),
        P("stem", None, None, None, None),
        P("stem", None),
        P("stem", None),
        P("stem", None, None, None, None),
        P("stem", None),
        P("stem", None),
        P("stem", None, None, None, None),
        P("stem", None),
        P("stem", None),
        P("stem", None),
        P("stem", None, None, None, None),
        P("stem", None),
    )
    return jax.shard_map(
        per_device, mesh=mesh, in_specs=in_specs, out_specs=out_specs, check_vma=False
    )
```

```python
import jax
import jax.numpy as jnp
from jax import lax
from jax.experimental import pallas as pl
from jax.experimental.pallas import tpu as pltpu
from jax.sharding import PartitionSpec as P

NORM_EPS = 0.001
RATIO_EPS = 1e-10
BF = jnp.bfloat16
F32 = jnp.float32
TAPS = 5
L = 128
M = 32
NJ = 32
R = M * NJ
CHUNK = 512
UNROLL = 4
COLS0 = 1024
SPAN0 = (slice(0, 768), slice(256, 1024))
COLS1 = 1920
COLS1B = 1536
COLS2 = 1152
SPAN2 = (slice(0, 768), slice(0, 1152))
GROUPS2 = ((0, 512), (256, 640), (768, 1024))
GROUPS1 = ((0, 1024, 1), (256, 1152, 2), (512, 1280, 0), (768, 1408, 3), (1536, 1792, 4))
TILES0 = ((0, 128), (256, 512), (384, 640), (768, 896))
FULL = pl.BlockSpec(memory_space=pltpu.VMEM)
SCALAR = pl.BlockSpec(memory_space=pltpu.SMEM)
FAR = pl.BlockSpec(memory_space=pltpu.HBM)


class Far:
    def __init__(self, array, columns=None, parts=1):
        self.array, self.columns, self.parts = array, columns, parts


class Arriving:
    def __init__(self, source, target, sems, parts=1):
        self.target, self.waited, self.copies = target, 0, []
        size = target.shape[0] // parts
        for k in range(parts):
            span = pl.ds(k * size, size)
            here = (source, target) if parts == 1 else (source.at[span], target.at[span])
            self.copies.append(pltpu.make_async_copy(*here, sems.at[k]))
            self.copies[-1].start()

    def get(self, part=None):
        last = len(self.copies) if part is None else part + 1
        for copy in self.copies[self.waited : last]:
            copy.wait()
        self.waited = max(self.waited, last)
        return self.target


class Leaving:
    def __init__(self, target, sems):
        self.target, self.sems, self.copies = target, sems, []

    def put(self, source, part=None):
        target = self.target if part is None else self.target.at[part]
        source = source if part is None else source.at[part]
        copy = pltpu.make_async_copy(source, target, self.sems.at[len(self.copies)])
        copy.start()
        self.copies.append(copy)

    def wait(self):
        for copy in self.copies:
            copy.wait()


PARTS = 8


def run(kernel, name, outs, args, scratch=(), flops=0, fetch=(), store=(), token=None, carry=()):
    n_args = len(args)
    args = list(args) + list(fetch) + list(store)
    n_made = len(outs)
    outs = list(outs)
    for f in fetch:
        outs.append(((f.array.shape[0], f.columns or f.array.shape[1]) + f.array.shape[2:], f.array.dtype))
    arrays = [a.array if isinstance(a, Far) else a for a in args]
    n_stored = len(outs)
    outs += [(a.shape, a.dtype, True) for a in store]
    aliases = {}
    for value in carry:
        at = [k for k, a in enumerate(args) if a is value]
        if not at:
            at = [len(args)]
            args.append(value)
        aliases[at[0]] = len(outs)
        outs.append((value.shape, value.dtype))
    if token is not None:
        args.append(token)
        outs.append((token.shape, token.dtype))
    far_in = [k for k, a in enumerate(args[:n_args]) if isinstance(a, Far)]
    far_out = [k for k, o in enumerate(outs) if len(o) == 3]
    n_in, n_out, n_own = len(args), len(outs), len(scratch)
    placed = [
        pltpu.with_memory_space_constraint(a.array, pltpu.HBM) if isinstance(a, Far) else a for a in args
    ]
    landing = []
    for k in far_in:
        shape = args[k].array.shape
        if args[k].columns is not None:
            shape = (shape[0], args[k].columns)
        space = pltpu.SMEM if args[k].array.dtype == jnp.int32 else pltpu.VMEM
        landing.append(space(shape, args[k].array.dtype))

    def body(*refs):
        ins, results = list(refs[:n_in]), list(refs[n_in : n_in + n_out])
        own = refs[n_in + n_out : n_in + n_out + n_own]
        targets = refs[n_in + n_out + n_own : n_in + n_out + n_own + len(far_in)]
        in_sems, out_sems = refs[-2:]

        def cut(k):
            return ins[k] if args[k].columns is None else ins[k].at[:, 0 : args[k].columns]

        for i, k in enumerate(far_in):
            ins[k] = Arriving(cut(k), targets[i], in_sems.at[i], args[k].parts)
        fetched = [
            Arriving(cut(n_args + i), results[n_made + i], in_sems.at[len(far_in) + i]) for i in range(len(fetch))
        ]
        for i, k in enumerate(far_out):
            results[k] = Leaving(results[k], out_sems.at[i])
        for i in range(len(store)):
            results[n_stored + i].put(ins[n_args + len(fetch) + i])
        if token is not None:
            results[-1][...] = ins[-1][...]
        kernel(*ins[:n_args], *results[:n_made], *own)
        for k in far_in:
            ins[k].get()
        for f in fetched:
            f.get()
        for k in far_out:
            results[k].wait()

    in_specs = []
    for a in args:
        if isinstance(a, Far):
            in_specs.append(FAR)
        else:
            in_specs.append(SCALAR if a.dtype == jnp.int32 and a.ndim == 1 else FULL)
    bytes_all = sum(a.size * a.dtype.itemsize for a in arrays)
    bytes_all += sum(jnp.zeros((), o[1]).dtype.itemsize * o[0][0] * o[0][-1] for o in outs)
    return pl.pallas_call(
        body,
        out_shape=[
            pltpu.HBM(o[0], o[1]) if len(o) == 3 else jax.ShapeDtypeStruct(o[0], o[1]) for o in outs
        ],
        in_specs=in_specs,
        out_specs=[FAR if len(o) == 3 else FULL for o in outs],
        input_output_aliases=aliases,
        scratch_shapes=[pltpu.VMEM(s, d) for s, d in scratch]
        + landing
        + [
            pltpu.SemaphoreType.DMA((max(1, len(far_in) + len(fetch)), PARTS)),
            pltpu.SemaphoreType.DMA((max(1, len(far_out)), PARTS)),
        ],
        compiler_params=pltpu.CompilerParams(vmem_limit_bytes=24 << 20),
        cost_estimate=pl.CostEstimate(flops=flops, bytes_accessed=bytes_all, transcendentals=0),
        name=name,
    )(*placed)


def lane(shape):
    return lax.broadcasted_iota(jnp.int32, shape, 1)


def sub(shape):
    return lax.broadcasted_iota(jnp.int32, shape, 0)


def rows(j, count=M):
    return pl.ds(pl.multiple_of(j * count, count), count)


def tiles(width):
    return [slice(L * k, L * k + L) for k in range(width // L)]


def for_blocks(fn, count=NJ):
    step = UNROLL if isinstance(count, int) and count % UNROLL == 0 else 1

    def body(j, carry):
        for i in range(step):
            fn(j * step + i)
        return carry

    lax.fori_loop(0, count // step, body, 0)


def put_all(stores):
    for ref, span, at, value in stores:
        ref[span, at] = value


def for_blocks_rims(fn):
    group = 10

    def several(first, count, has_prev, has_next):
        stores = []
        for i in range(count):
            stores += fn(first + i, has_prev, has_next)
        put_all(stores)

    def body(g, carry):
        several(group * g + 1, group, True, True)
        return carry

    several(0, 1, False, True)
    lax.fori_loop(0, (NJ - 2) // group, body, 0)
    several(NJ - 1, 1, True, False)


def from_prev(value, rim, flag):
    rim = jnp.concatenate([rim] * (M // 8), axis=0)
    return jnp.where(sub(value.shape) == 0, rim, pltpu.roll(value, 1, 0)) * flag


def from_next(value, rim, flag):
    rim = jnp.concatenate([rim] * (M // 8), axis=0)
    return jnp.where(sub(value.shape) == M - 1, rim, pltpu.roll(value, M - 1, 0)) * flag


def widen(source, out):
    def group(g):
        for at in tiles(source.shape[1]):
            tile = source[rows(g, 8), at]
            for i in range(8):
                out[rows(8 * g + i, 8), at] = jnp.broadcast_to(tile[i : i + 1], (8, L))

    for_blocks(group, NJ // 8)


def mask_bf(cond):
    return jnp.where(cond, 1.0, 0.0).astype(BF)


def fill_rims(cat, parts, low):
    zero = jnp.zeros((M, L), BF)
    cond = mask_bf(low) > 0.5

    def one(j, has_prev, has_next):
        stores = []
        for target, after, before in parts:
            value = cat[rows(j + 1), after : after + L] if has_next else zero
            other = cat[rows(j - 1), before : before + L] if has_prev else zero
            stores.append((cat, rows(j), slice(target, target + L), jnp.where(cond, value, other)))
        return stores

    for_blocks_rims(one)


def rims_1(cat, groups):
    fill_rims(cat, [(rim, base, base + L) for base, rim, _ in groups], lane((M, L)) < 32)


def rims_2(cat):
    fill_rims(cat, [(rim, base, base + L) for base, rim in GROUPS2], lane((M, L)) < 32)


def rims_0(cat):
    fill_rims(cat, [(rim, base, base) for base, rim in TILES0], lane((M, L)) % 32 < 2)


def matmul(left, right, transposed=False):
    return lax.dot_general(
        left, right, (((1,), (1 if transposed else 0,)), ((), ())), preferred_element_type=F32
    )


def quarters(fn):
    for k in range(4):
        fn(slice(R // 4 * k, R // 4 * (k + 1)))


def for_chunks(fn, size=CHUNK):
    def body(r, carry):
        fn(pl.ds(pl.multiple_of(r * size, size), size))
        return carry

    lax.fori_loop(0, R // size, body, 0)


def product_sums(product, use, done=None, size=R):
    sums = (jnp.zeros((8, L), F32), jnp.zeros((8, L), F32))

    def part(r, sums):
        rs = rows(r, size)
        value = [(piece, at) for piece in product(rs) for at in tiles(piece.shape[1])]
        for i in range(size // M):
            for k, (piece, at) in enumerate(value):
                if k % 4 == 0:
                    stores = []
                tile = piece[M * i : M * i + M, at]
                sums = use(r * (size // M) + i, k, slice(L * k, L * k + L), tile, *sums, stores)
                if k % 4 == 3 or k == len(value) - 1:
                    put_all(stores)
        if done is not None:
            done(rs)
        return sums

    if done is None:
        sums = lax.fori_loop(0, R // size, part, sums)
    else:
        for r in range(R // size):
            sums = part(r, sums)
    return [total_rows(v) for v in sums]


def rows_from_0(cat, weights):
    def product(rs):
        pieces = []
        for k in range(weights.shape[1] // 256):
            span = SPAN0[k % 2]
            pieces.append(matmul(cat[rs, span], weights[span, 256 * k : 256 * k + 256]))
        return pieces

    return product


def rows_from_2(cat, weights):
    def product(rs):
        return [
            matmul(cat[rs, span], weights[256 * k : 256 * k + 256, span], True) for k, span in enumerate(SPAN2)
        ]

    return product


def sum8(value):
    total = value[0:8]
    for k in range(1, value.shape[0] // 8):
        total = total + value[8 * k : 8 * k + 8]
    return total


def sum_blocks(fn):
    def body(j, carry):
        for i in range(UNROLL):
            carry = fn(j * UNROLL + i, *carry)
        return carry

    zero = jnp.zeros((8, L), F32)
    return [total_rows(s) for s in lax.fori_loop(0, NJ // UNROLL, body, (zero, zero))]


def fold(stats, period):
    step = L // 2
    while step >= period:
        stats = stats + pltpu.roll(stats, step, 1)
        step //= 2
    return stats


def stack_rows(values):
    at = sub((8, L))
    tile = jnp.zeros((8, L), F32)
    for k, value in enumerate(values):
        tile = jnp.where(at == k, value, tile)
    return tile


def total_rows(value):
    return jnp.sum(value, axis=0, keepdims=True)


def norm_terms(moments, count):
    mean = moments[0:1] / count
    return mean, lax.rsqrt(moments[1:2] / count - mean * mean + NORM_EPS)


def silu(v):
    return v / (1.0 + jnp.exp(-v))


def silu_slope(v):
    s = 1.0 / (1.0 + jnp.exp(-v))
    return s * (1.0 + v * (1.0 - s))


def sigmoid(v):
    return 1.0 / (1.0 + jnp.exp(-v))


def softplus(v):
    return jnp.maximum(v, 0.0) + jnp.log1p(jnp.exp(-jnp.abs(v)))


def softplus_slope(r):
    return jnp.where(r < 0.05, r * (1.0 - r * (0.5 - r * (1.0 / 6.0))), 1.0 - jnp.exp(-r))


def end_rows(z, group_out, blocks=NJ):
    def group(g):
        for at in tiles(z.shape[1]):
            place = sub((8, L))
            top = low = jnp.zeros((8, L), F32)
            for i in range(8):
                start = pl.multiple_of((8 * g + i) * M, M)
                top = jnp.where(place == i, z[pl.ds(start, 8), at][0:1], top)
                low = jnp.where(place == i, z[pl.ds(start + M - 8, 8), at][7:8], low)
            group_out(rows(g, 8), at, top, low)

    for_blocks(group, blocks // 8)


def pack_ends(z, index, cross, core, blocks=NJ):
    even = index[1] == 0

    def group_out(rs, at, top, low):
        cross[rs, at] = jnp.where(even, top, low)
        core[rs, at] = jnp.where(even, low, top)

    end_rows(z, group_out, blocks)


def pack_moments(mom, cross, value):
    mom[...] = value
    cross[NJ : NJ + 8, 0:L] = value


def sides(index, cross, core, at):
    even = index[1] == 0
    a, b = cross[0:NJ, at], core[0:NJ, at]
    return jnp.where(even, a, b), jnp.where(even, b, a)


def tile_2(w, tap, q, half):
    at = lane((16, L)) // 32
    tile = jnp.zeros((16, L), F32)
    for k in range(4):
        b = q - 2 * (4 * half + k) + 1
        if 0 <= b < TAPS:
            start = (tap * TAPS + b) * 16
            tile = jnp.where(at == k, w[start : start + 16, :], tile)
    return tile.astype(BF)


def repeat_lanes(w, out):
    for k in range(w.shape[0] // 16):
        span = slice(16 * k, 16 * k + 16)
        out[span, :] = jnp.concatenate([w[span, :].astype(F32)] * (L // 32), axis=1)


def matrix_2_down(narrow, t, w):
    repeat_lanes(narrow, w)
    zero = jnp.zeros((16, L), BF)
    for base, rim, tap in GROUPS1:
        for half in range(2):
            at = slice(L * half, L * half + L)
            for q in range(16):
                t[base + 16 * q : base + 16 * q + 16, at] = tile_2(w, tap, q, half)
            for part in range(8):
                q = {0: 16, 1: 17, 7: -1}.get(part)
                start = rim + 16 * part
                t[start : start + 16, at] = zero if q is None else tile_2(w, tap, q, half)


def matrix_2_up(narrow, t, w):
    repeat_lanes(narrow, w)
    zero = jnp.zeros((16, L), BF)
    at = lane((16, L))
    for row in range(2):
        for (base, edge), tap in zip(GROUPS2, (row + 1, row + 3, row - 1)):
            for q in range(16):
                span = slice(row * 256 + q * 16, row * 256 + q * 16 + 16)
                for half in range(2):
                    cols = slice(base + L * half, base + L * half + L)
                    t[span, cols] = tile_2(w, tap, q, half) if 0 <= tap < TAPS else zero
                rim = zero
                if 0 <= tap < TAPS and q in (0, 1, 15):
                    b = {0: 3, 1: 4, 15: 0}[q]
                    start = (tap * TAPS + b) * 16
                    cond = at < 32 if q == 15 else at >= 96
                    rim = jnp.where(cond, w[start : start + 16, :], 0.0).astype(BF)
                t[span, edge : edge + L] = rim


def band(w, tap, channel, offset):
    tile = jnp.zeros((32, L), F32)
    for b in range(TAPS):
        start = (tap * TAPS + b) * 2 + channel
        tile = jnp.where(offset == b, w[start : start + 1, :], tile)
    return tile.astype(BF)


def matrix_1_down(w, t, col):
    q, zero = sub((32, L)), jnp.zeros((32, L), BF)
    for half in range(2):
        p = 8 * half + lane((32, L)) // 16
        inner = q - 2 * p + 1
        rim = jnp.where(q == 31, -2 * p, jnp.where(q == 0, 33 - 2 * p, jnp.where(q == 1, 34 - 2 * p, -9)))
        for row in range(2):
            cols = slice(col + row * 256 + half * L, col + row * 256 + half * L + L)
            for (base, edge), frames in zip(TILES0, ((None, -1), (0, 1), (2, 3), (4, 5))):
                if not SPAN0[row].start <= base < SPAN0[row].stop:
                    continue
                for part, frame in enumerate(frames):
                    tap = -1 if frame is None else frame - 2 * row + 1
                    for c in range(2):
                        start = part * 64 + c * 32
                        ok = 0 <= tap < TAPS
                        for offset, bins in ((base, inner), (edge, rim)):
                            span = slice(offset + start, offset + start + 32)
                            t[span, cols] = band(w, tap, c, bins) if ok else zero


def matrix_1_up(w, t, col):
    q, zero = sub((32, L)), jnp.zeros((32, L), BF)
    at = lane((32, L))
    rim = jnp.where(at < 16, q - 31, jnp.where(at >= 112, q + 3, -9))
    for frame in range(4):
        taps = (frame + 1, frame - 1, frame + 3, frame - 3)
        for c in range(2):
            span = slice(frame * 64 + c * 32, frame * 64 + c * 32 + 32)
            for k, tap in enumerate(taps):
                ok = 0 <= tap < TAPS
                for half in range(2):
                    p = 8 * half + at // 16
                    start = col + 256 * k + L * half
                    t[span, start : start + L] = band(w, tap, c, q - 2 * p + 1) if ok else zero
                start = col + 1024 + L * k
                t[span, start : start + L] = band(w, tap, c, rim) if ok else zero


def double_lanes(value, first):
    while first < L:
        value = value + pltpu.roll(value, first, 1)
        first *= 2
    return value


def window_0(
    index, seg_lengths, frame_mask, raw_c, raw_d, gain1, shift1, gain2, shift2, gain3, shift3, bias2, bias1,
    t, w1c, w1d, aux, prm,
):
    w1c[...] = jnp.zeros(w1c.shape, F32)
    w1d[...] = jnp.zeros(w1d.shape, F32)
    for k in range(TAPS * TAPS):
        span = slice(2 * k, 2 * k + 2)
        w1c[span, 0:16] = raw_c[k].astype(F32)
        value = raw_d[k].astype(F32)
        w1d[0, span, 0:16] = value[:, 0:16]
        w1d[1, span, 0:16] = value[:, 16:32]
    w1c[...] = double_lanes(w1c[...], 16)
    for k in range(2):
        w1d[k] = double_lanes(w1d[k], 16)
    matrix_1_down(w1c, t, 0)
    prm[...] = jnp.zeros(prm.shape, F32)
    for k, value in enumerate((gain1, shift1, gain2, shift2, gain3, shift3, bias2)):
        prm[k : k + 1, 0 : value.shape[1]] = value[...]
    rows8, at = sub((8, L)), lane((8, L))
    value = prm[...]
    wide = (rows8 == 2) | (rows8 == 3)
    value = double_lanes(value + jnp.where(wide, 0.0, pltpu.roll(value, 16, 1)), 32)
    last = jnp.where(at // 32 % 2 == 0, bias1[0:1, 0:1], bias1[0:1, 1:2])
    prm[...] = jnp.where(rows8 == 7, last, value)
    row, at = sub((M, L)), lane((M, L))
    kept = jnp.broadcast_to(frame_mask[...].astype(F32), (8, L))
    kept = jnp.minimum(kept, pltpu.roll(kept, L - 1, 1))[0:1]
    keep = []
    for i in range(2):
        value = jnp.sum(jnp.where(at == 4 * row + 2 * i, kept, 0.0), axis=1, keepdims=True)
        keep.append(jnp.broadcast_to(value, (M, L)))
        aux[2 + i] = keep[i]
    aux[4] = keep[0] * keep[1]
    lengths = seg_lengths.get()
    start = jnp.int32(0)
    here = (index[2] * M + row) * 4
    shut = [here == index[3], here + 4 == index[3]]
    for k in range(lengths.shape[0]):
        shut = [shut[0] | (here == start), shut[1] | (here + 4 == start)]
        start = start + 4 * lengths[k]
    aux[0] = jnp.where(shut[0], 0.0, 1.0)
    aux[1] = jnp.where(shut[1], 0.0, 1.0)


def window_1(w2c, t, w):
    matrix_2_down(w2c, t, w)


def window_2(w2d, t, w):
    matrix_2_up(w2d, t, w)


def window_3(w1d, t):
    matrix_1_up(w1d.at[0], t, 0)
    matrix_1_up(w1d.at[1], t, COLS1B)


def window_swap(w2c, w2d, w1c, t2a, t2b, t1b, a, b, c, w):
    matrix_2_down(w2d, a, w)
    t2a.put(a)
    matrix_2_up(w2c, b, w)
    t2b.put(b)
    matrix_1_up(w1c, c, 0)
    t1b.put(c)


def correlate(coarse, fine, d, spans=(slice(None),)):
    for k in range(R // CHUNK):
        span = slice(CHUNK * k, CHUNK * k + CHUNK)
        left, right = ready(coarse, k), ready(fine, k)
        width = d.shape[0] // len(spans)
        for i, columns in enumerate(spans):
            out = slice(width * i, width * i + width)
            value = lax.dot_general(
                left[span, out], right[span, columns], (((0,), (0,)), ((), ())), preferred_element_type=F32
            )
            d[out, :] = value if k == 0 else d[out, :] + value


def weight_2(d, out):
    at = lane((32, L))
    sums = {}
    for base, rim, tap in GROUPS1:
        total = jnp.zeros((32, L), F32)
        for p in range(8):
            span = slice(32 * p, 32 * p + 32)
            parts = [d[span, base : base + L], d[span, base + L : base + 256], d[span, rim : rim + L]]
            if p == 0:
                value = jnp.where(at < 16, pltpu.roll(parts[2], 16, 1), pltpu.roll(parts[0], 16, 1))
            else:
                which, off = divmod(32 * p - 16, L)
                value = pltpu.roll(parts[which], L - off, 1)
                if off + 80 > L:
                    value = jnp.where(at < L - off, value, pltpu.roll(parts[which + 1], L - off, 1))
            total = total + value
        sums[tap] = total
    out[0:32, :] = jnp.where(at < 80, sums[0], pltpu.roll(sums[4], 80, 1))
    out[32:64, :] = jnp.where(at < 80, sums[1], pltpu.roll(sums[4], 32, 1))
    out[64:96, :] = sums[2]
    out[96:128, :] = sums[3]


def weight_1(d, out, start):
    at = lane((16, L)) % 32
    result = jnp.zeros((16, L), F32)
    for k in range(3):
        total = jnp.zeros((16, L), F32)
        for row in range(2):
            base, edge = TILES0[k + row]
            base, edge = base - SPAN0[row].start, edge - SPAN0[row].start
            for p in range(16):
                first = row * 256 + p * 16
                span = slice(first, first + 16)
                value = pltpu.roll(d[span, base : base + L], (1 - 2 * p) % L, 1)
                if p in (0, 15):
                    rim = pltpu.roll(d[span, edge : edge + L], L - 31 if p == 0 else 3, 1)
                    value = jnp.where(at == 0 if p == 0 else at >= 3, rim, value)
                total = total + value
        if k > 0:
            total = pltpu.roll(total, 8 * k, 1)
        result = jnp.where((at >= 8 * k) & (at < 8 * k + TAPS), total, result)
    out[start : start + 16, :] = result


def window_4(low, act, fine, out, d):
    correlate(low, fine, d, SPAN0)
    weight_1(d, out, 0)
    correlate(act, fine, d, SPAN0)
    weight_1(d, out, 16)


def window_5(coarse, fine, out, d):
    correlate(coarse, fine, d)
    weight_2(d, out)


HALF = 144


def window_6(index, coarse, fine, w1d, w2d, keep, give, d, kept):
    correlate(coarse, fine, d)
    weight_2(d, kept)
    even = index[1] == 0
    up_two, up_one = ready(w2d), ready(w1d)

    def place(span, a, b):
        keep[span, :] = jnp.where(even, a, b)
        give[span, :] = jnp.where(even, b, a)

    place(slice(0, 128), up_two[...], kept[...])
    place(slice(128, 144), up_one[0:16, :], up_one[16:32, :])


def window_7(coarse, fine, keep, got, bias, low, d, first):
    correlate(coarse, fine, d, SPAN0)
    weight_1(d, first, 0)
    low[0:HALF, :] = (keep[...] + got[...]).astype(BF)
    low[HALF : HALF + 16, :] = first[...].astype(BF)
    low[HALF + 16 : HALF + 32, :] = jnp.concatenate([bias[...], jnp.zeros((8, L), F32)]).astype(BF)


def unpack_kernel(
    index, mine, other, mom4, mom5, mom6,
    w1c, w2c, w2d, w1d, bias1, gain1, shift1, gain2, shift2, bias2, gain3, shift3,
):
    even = index[1] == 0
    a, b = mine[...], other[...]
    up, down = jnp.where(even, a, b), jnp.where(even, b, a)
    own = a[HALF:] + b[HALF:]
    for half, out in ((up, w2d), (down, w2c)):
        turned = half[0:128].T
        moved = [turned] + [pltpu.roll(turned, L - 32 * tap, 1) for tap in range(1, 4)]
        for tap in range(TAPS):
            for b in range(TAPS):
                if tap < 4:
                    value = moved[tap][16 * b : 16 * b + 16]
                else:
                    value = moved[b // 3][80 + 16 * (b % 3) : 96 + 16 * (b % 3)]
                out[tap * TAPS + b] = value[:, 0:32]
    tall = jnp.concatenate([up[128:144], down[128:144], own[0:16], jnp.zeros((80, L), F32)]).T
    other_tall = pltpu.roll(tall, L - 32, 1)
    for tap in range(TAPS):
        for b in range(TAPS):
            for c in range(2):
                row = (tap + 1) % 2 * 64 + c * 32 + (tap + 1) // 2 * 8 + b
                w1d[tap * TAPS + b, c : c + 1, :] = tall[row : row + 1, 0:32]
                w1c[tap * TAPS + b, c : c + 1, :] = other_tall[row : row + 1, 0:16]
    total = total_rows(own[16:24])
    total = jnp.broadcast_to(total, (8, L))
    total = total + pltpu.roll(total, 64, 1)
    for step in (16, 8, 4, 2, 1):
        total = total + pltpu.roll(total, L - step, 1)
    total = jnp.where(lane((8, L)) == 0, total, pltpu.roll(total, L - 31, 1))
    bias1[...] = total[0:1, 0:2]
    for out, mom, row in (
        (gain1, mom6, 1), (shift1, mom6, 0), (gain2, mom5, 1), (shift2, mom5, 0),
        (bias2, mom5, 2), (gain3, mom4, 1), (shift3, mom4, 0),
    ):
        out[...] = mom[row : row + 1, 0 : out.shape[1]]


def ready(ref, part=None):
    return ref.get(part) if isinstance(ref, Arriving) else ref


def spread(scr, store):
    at = lane((M, L)) // 32
    for half in range(2):
        parts = [scr[k % 2, pl.ds(2 * half + k // 2, M, stride=4), :] for k in range(4)]
        for block in range(4):
            value = parts[block]
            for k in range(4):
                if k != block:
                    value = jnp.where(at == k, pltpu.roll(parts[k], (32 * (k - block)) % L, 1), value)
            store(block, half, value)


def gather(blocks, scr):
    at = lane((M, L)) // 32
    for half in range(2):
        parts = [blocks(block, half) for block in range(4)]
        for k in range(4):
            value = parts[k]
            for block in range(4):
                if block != k:
                    value = jnp.where(
                        at == block, pltpu.roll(parts[block], (32 * (block - k)) % L, 1), value
                    )
            scr[k % 2, pl.ds(2 * half + k // 2, M, stride=4), :] = value


def layout_kernel(index, frame_mask, mix, cot, cross, core, x0, c0, scr, wide, ends):
    def place(out, block, row):
        def store(k, half, value):
            at = slice(L * half, L * half + L)
            out[rows(block + k), at] = value.astype(BF)
            wide[rows(row + k), at] = value

        return store

    m = mix.get()

    def mix_tile(t):
        for c in range(2):
            scr[c] = m[c, :, pl.ds(pl.multiple_of(t * L, L), L)].astype(F32)
        spread(scr, place(x0, 4 * t, 4 * t))

    for_blocks(mix_tile, NJ // 4)
    g = cot.get()
    per_stem = g.shape[3] // L

    def cot_tile(t):
        for c in range(2):
            lanes = pl.ds(pl.multiple_of((t % per_stem) * L, L), L)
            scr[c] = g[t // per_stem, c, :, lanes].astype(F32)
        spread(scr, place(c0, 4 * t, NJ + 4 * t))

    for_blocks(cot_tile, NJ // 4)
    ends[...] = jnp.zeros(ends.shape, F32)
    pack_ends(wide, index, ends.at[0], ends.at[1], 2 * NJ)
    even = index[1] == 0

    kept = frame_mask.get()

    def least(first, count):
        value = kept[first]
        for k in range(1, count):
            value = jnp.minimum(value, kept[first + k])
        return value.astype(F32)

    for i, (first, count) in enumerate(((0, 2), (2, 2), (0, 4))):
        top, low = least(first, count), least(4 * M - 4 + first, count)
        row = 2 * NJ + i
        ends[0, row : row + 1, :] = jnp.full((1, 2 * L), jnp.where(even, top, low))
        ends[1, row : row + 1, :] = jnp.full((1, 2 * L), jnp.where(even, low, top))
    cross[...] = ends[0].astype(BF)
    core[...] = ends[1].astype(BF)


def columns_0(cat, blocks, read, left, right, aux):
    a, a_next = aux[0], aux[1]
    for which, (first, count) in enumerate(blocks):

        def one(i, which=which, first=first):
            j = first + i
            span, stores = rows(j), []
            for half in range(2):
                value = read(which, j, half)
                stores.append((cat, span, slice(256 + L * half, 384 + L * half), value.astype(BF)))
                if half == 1:
                    moved = from_prev(value, left[rows(j, 8), L : 2 * L], a)
                    stores.append((cat, span, slice(0, 128), moved.astype(BF)))
                else:
                    moved = from_next(value, right[rows(j, 8), 0:L], a_next)
                    stores.append((cat, span, slice(768, 896), moved.astype(BF)))
            put_all(stores)

        for_blocks(one, count)
    rims_0(cat)


def conv_one_kernel(
    index, x0, cross_in, core_in, aux, t,
    z, cross, core, mom, kept, hx, cat, lf, rf, lw, rw,
):
    even = index[1] == 0
    a, b = cross_in[...].astype(F32), core_in[...].astype(F32)
    lf[...] = jnp.where(even, a, b)
    rf[...] = jnp.where(even, b, a)
    hx[:, 0:L] = rf[0 : 2 * NJ, 0:L]
    hx[:, L : 2 * L] = lf[0 : 2 * NJ, L : 2 * L]
    kept[...] = jnp.zeros(kept.shape, F32)
    kept[0:3, :] = lf[2 * NJ : 2 * NJ + 3, 0:L]
    kept[3:6, :] = rf[2 * NJ : 2 * NJ + 3, 0:L]
    widen(lf.at[0:NJ], lw)
    widen(rf.at[0:NJ], rw)
    x = ready(x0)
    read = lambda which, j, h: x[rows(j), L * h : L * h + L].astype(F32)
    columns_0(cat, [(0, NJ)], read, lw, rw, aux)
    weights = ready(t)

    def use(j, k, at, value, s1, s2, stores):
        stores.append((z, rows(j), at, value))
        part = value * aux[2 + k // 2]
        return s1 + sum8(part), s2 + sum8(part * value)

    stats = product_sums(rows_from_0(cat, weights), use)
    pack_ends(z, index, cross, core)
    stats = fold(stack_rows(stats), 16)
    at = sub((8, L))
    stats = jnp.where(at == 2, total_rows(aux[2] + aux[3]) * (NJ * 16.0), stats)
    stats = jnp.where(at == 3, total_rows(aux[4]) * (NJ * 8.0), stats)
    pack_moments(mom, cross, stats)


def conv_two_kernel(
    index, z1, cross_in, core_in, mom1, prm, aux, t,
    z2, cross, core, mom, eb, hf, cat, ef, lw, rw,
):
    mean, scale = norm_terms(mom1, mom1[2:3])
    gain, shift = prm[0:1], prm[1:2]

    def act(value):
        return silu((value - mean) * scale * gain + shift)

    a, a_next = aux[0], aux[1]
    for at in tiles(512):
        left, right = sides(index, cross_in, core_in, at)
        hf[0, :, at] = left
        hf[1, :, at] = right
        ef[0, :, at] = act(left)
        ef[1, :, at] = act(right)
    widen(ef.at[0], lw)
    widen(ef.at[1], rw)

    def one(j):
        span, stores = rows(j), []
        for k, at in enumerate(tiles(512)):
            value = act(z1[span, at])
            stores.append((cat, span, at, value.astype(BF)))
            if k >= 2:
                moved = from_prev(value, lw[rows(j, 8), at], a)
                stores.append((cat, span, slice(256 + L * k, 384 + L * k), moved.astype(BF)))
            start = 768 + L * k if k < 2 else 1280 + L * k
            moved = from_next(value, rw[rows(j, 8), at], a_next)
            stores.append((cat, span, slice(start, start + L), moved.astype(BF)))
        put_all(stores)

    for_blocks(one)
    rims_1(cat, GROUPS1)
    def group_out(rs, at, top, low):
        ef[2, rs, at] = act(top)
        ef[3, rs, at] = act(low)

    end_rows(z1, group_out)
    eb[...] = ef[...].astype(BF)
    weights = ready(t)

    def use(j, k, at, value, s1, s2, stores):
        stores.append((z2, rows(j), at, value))
        part = value * aux[4]
        return s1 + sum8(part), s2 + sum8(part * value)

    stats = product_sums(lambda rs: [matmul(cat[rs, :], weights[...])], use)
    pack_ends(z2, index, cross, core)
    pack_moments(mom, cross, fold(stack_rows(stats), 32))


def columns_2(cat, read, left, right, aux):
    a, a_next = aux[0], aux[1]

    def one(j):
        span, stores = rows(j), []
        for k, at in enumerate(tiles(256)):
            value = read(j, at)
            stores.append((cat, span, at, value.astype(BF)))
            moved = from_prev(value, left[rows(j, 8), at], a)
            stores.append((cat, span, slice(256 + L * k, 384 + L * k), moved.astype(BF)))
            moved = from_next(value, right[rows(j, 8), at], a_next)
            stores.append((cat, span, slice(768 + L * k, 896 + L * k), moved.astype(BF)))
        put_all(stores)

    for_blocks(one)
    rims_2(cat)


def up_two_kernel(
    index, z2, cross_in, core_in, mom1, mom2, prm, aux, t,
    rect, cross, core, mom, hf, act2, cat, lf, rf, lw, rw,
):
    mean, scale = norm_terms(mom2, mom1[3:4])
    gain, shift, bias = prm[2:3], prm[3:4], prm[6:7]

    def act(value):
        return silu((value - mean) * scale * gain + shift)

    for at in tiles(256):
        left, right = sides(index, cross_in, core_in, at)
        hf[0, :, at] = left
        hf[1, :, at] = right
        lf[:, at] = act(left)
        rf[:, at] = act(right)
    widen(lf, lw)
    widen(rf, rw)
    columns_2(cat, lambda j, at: act(z2[rows(j), at]), lw, rw, aux)
    act2[...] = cat[:, 0:256]
    weights = ready(t)

    def use(j, k, at, value, s1, s2, stores):
        value = softplus(value + bias)
        stores.append((rect, rows(j), at, value))
        part = value * aux[2 + k // 2]
        return s1 + sum8(part), s2 + sum8(part * value)

    stats = product_sums(rows_from_2(cat, weights), use)
    pack_moments(mom, cross, fold(stack_rows(stats), 16))
    pack_ends(rect, index, cross, core)


def columns_1b(cat, read, left, right, aux):
    a, a_next = aux[0], aux[1]

    def one(j):
        span, stores = rows(j), []
        for k, at in enumerate(tiles(512)):
            value = read(j, k, at)
            stores.append((cat, span, at, value.astype(BF)))
            if k >= 2:
                moved = from_prev(value, left[rows(j, 8), at], a)
                stores.append((cat, span, slice(256 + L * k, 384 + L * k), moved.astype(BF)))
            else:
                moved = from_next(value, right[rows(j, 8), at], a_next)
                stores.append((cat, span, slice(768 + L * k, 896 + L * k), moved.astype(BF)))
        put_all(stores)

    for_blocks(one)
    rims_1(cat, GROUPS1[:4])


def edge_columns(own, prev, after):
    at = lane((NJ, L))
    place = sub((NJ, L))
    parts = [own, prev, after]
    groups = [own[:, 0:256], own[:, 256:512], prev, after]
    for g in groups:
        low = jnp.where((place == NJ - 1) | (at >= 32), 0.0, pltpu.roll(g[:, 0:L], NJ - 1, 0))
        high = jnp.where((place == 0) | (at < 112), 0.0, pltpu.roll(g[:, L : 2 * L], 1, 0))
        parts.append(low + high)
    return jnp.concatenate(parts, axis=1).astype(BF)


def quarter_blocks(index, stems):
    count = NJ // stems
    return [((index[0] ^ k) * count, count) for k in range(stems)]


def up_one_kernel(
    index, rect, cross_in, core_in, mom1, mom3, prm, aux, ends1, cat1, t,
    m0, m1, m2, m3, hf, low3, sf, shf, cat, lf, rf, ef, ff, lw, rw,
):
    mean, scale = norm_terms(mom3, mom1[2:3])
    gain, shift, bias = prm[4:5], prm[5:6], prm[7:8]

    def norm(value):
        return (value - mean) * scale * gain + shift

    for at in tiles(512):
        left, right = sides(index, cross_in, core_in, at)
        hf[0, :, at] = left
        hf[1, :, at] = right
        lf[:, at] = norm(left)
        rf[:, at] = norm(right)
    widen(lf, lw)
    widen(rf, rw)
    columns_1b(cat, lambda j, k, at: norm(rect[rows(j), at]), lw, rw, aux)
    low3[...] = cat[:, 0:512]

    def group_out(rs, at, top, low):
        ef[0, rs, at] = norm(top)
        ef[1, rs, at] = norm(low)

    end_rows(rect, group_out)
    wide = jnp.concatenate([bias, bias], axis=1)
    zero = jnp.zeros((NJ, 256), F32)
    a, a_end = aux[0, 0:1, 0:1], aux[1, M - 1 : M, 0:1]
    e1 = [ends1[k].astype(F32) for k in range(4)]
    edges = [
        (
            edge_columns(lf[...], zero, ef[0, :, 0:256] * a),
            edge_columns(e1[0], zero, e1[2][:, 0:256] * a),
        ),
        (
            edge_columns(rf[...], ef[1, :, 256:512] * a_end, zero),
            edge_columns(e1[1], e1[3][:, 256:512] * a_end, zero),
        ),
    ]
    weights, other = ready(t), ready(cat1)
    value = matmul(jnp.concatenate([e[0] for e in edges]), weights[:, 0:COLS1B], True)
    value = value + matmul(jnp.concatenate([e[1] for e in edges]), weights[:, COLS1B : 2 * COLS1B], True)
    for k, half in ((0, 1), (1, 0)):
        at = slice(L * half, L * half + L)
        shf[:, at] = sigmoid(value[NJ * k : NJ * k + NJ, at] + bias)
    masks = (m0, m1, m2, m3)
    per = R // len(masks)
    for mask, (first, count) in zip(masks, quarter_blocks(index, len(masks))):
        rs = rows(lax.div(first, count), per)
        value = matmul(cat[rs, :], weights[:, 0:COLS1B], True)
        value = value + matmul(other[rs, :], weights[:, COLS1B : 2 * COLS1B], True)
        value = sigmoid(value + wide)
        sf[rs, :] = value
        mask[0:per, :] = value.astype(BF)
        ff[...] = jnp.zeros(ff.shape, F32)
        ff[0:count, :] = shf[rows(lax.div(first, count), count), :]
        mask[per : per + 16, :] = ff[...].astype(BF)


def ratio_terms(masks):
    squares = [m * m for m in masks]
    power = squares[0]
    for s in squares[1:]:
        power = power + s
    inverse = 1.0 / (power + RATIO_EPS)
    return [s * inverse for s in squares], inverse


def mask_back(masks, cots, mix):
    ratios, inverse = ratio_terms(masks)
    direct = cots[0] * ratios[0]
    for c, r in zip(cots[1:], ratios[1:]):
        direct = direct + c * r
    common = 2.0 * mix * inverse
    return [m * common * (c - direct) for m, c in zip(masks, cots)], direct


def mask_kernel(index, m0, m1, m2, m3, c0, x0, hx, g0, g1, g2, g3, df, ff):
    masks, grads = (m0, m1, m2, m3), (g0, g1, g2, g3)
    stems = len(masks)
    per, blocks = R // stems, NJ // stems
    mine = index[0]
    cots, mix, rim = ready(c0), ready(x0), ready(hx)

    def one(j):
        for at in tiles(256):
            m = [masks[s][rows(j), at].astype(F32) for s in range(stems)]
            c = [cots[rows((mine ^ s) * blocks + j), at].astype(F32) for s in range(stems)]
            x = mix[rows(mine * blocks + j), at].astype(F32)
            values, own = mask_back(m, c, x)
            df[rows(j), at] = own
            for s in range(stems):
                grads[s][rows(j), at] = values[s].astype(BF)

    for_blocks(one, blocks)
    m = [masks[s][per : per + 16, :].astype(F32)[0:blocks] for s in range(stems)]
    c = [rim[rows(stems + (mine ^ s), blocks), :] for s in range(stems)]
    values, _ = mask_back(m, c, rim[rows(mine, blocks), :])
    for s in range(stems):
        ff[...] = jnp.zeros(ff.shape, F32)
        ff[0:blocks, :] = values[s]
        grads[s][per : per + 16, :] = ff[...].astype(BF)


def estimate_kernel(index, m0, m1, m2, m3, x0, w1d, out, t, scr, est):
    masks = (m0, m1, m2, m3)
    stems = len(masks)
    blocks = NJ // stems
    mine = index[0]
    matrix_1_down(w1d.at[0], t, 0)
    matrix_1_down(w1d.at[1], t, 512)
    mix = ready(x0)

    def one(j):
        for at in tiles(256):
            m = [masks[s][rows(j), at].astype(F32) for s in range(stems)]
            x = mix[rows(mine * blocks + j), at].astype(F32)
            ratios, _ = ratio_terms(m)
            for s in range(stems):
                est[s, rows(j), at] = x * ratios[s]

    for_blocks(one, blocks)
    for s in range(stems):
        for t in range(blocks // 4):
            gather(
                lambda block, half, s=s, t=t: est[s, rows(4 * t + block), L * half : L * half + L], scr
            )
            for c in range(2):
                out[mine ^ s, c, :, L * t : L * t + L] = scr[c].astype(BF)


def down_one_back_kernel(
    index, q0, q1, q2, q3, sigh, sig, aux, mom1, mom3, rect, t,
    g3, cat, cross, core, mom, bias, gf, hf, zf, hw,
):
    grads = (q0, q1, q2, q3)
    blocks = quarter_blocks(index, len(grads))
    per = R // len(grads)
    rim = ready(sigh)
    for grad, (first, count) in zip(grads, blocks):
        span = rows(lax.div(first, count), count)
        value = grad[per : per + 16, :].astype(F32)[0:count]
        own = rim[span, :]
        hf[span, :] = value * own * (1.0 - own)
    zf[...] = jnp.zeros(zf.shape, F32)
    widen(hf, hw)
    sigs = ready(sig)

    def read(which, j, half):
        at = slice(L * half, L * half + L)
        own = sigs[rows(j), at]
        value = grads[which][rows(j - blocks[which][0]), at].astype(F32) * own * (1.0 - own)
        zf[...] = zf[...] + sum8(value)
        return value

    columns_0(cat, blocks, read, hw, hw, aux)
    bias[...] = zf[...]
    weights = ready(t)

    mean, scale = norm_terms(mom3, mom1[2:3])
    r = ready(rect)

    def use(j, k, at, value, s1, s2, stores):
        if k >= 4:
            stores.append((gf, rows(j), slice(L * k - 512, L * k - 384), value))
            return s1, s2
        stores.append((g3, rows(j), at, value))
        return s1 + sum8(value), s2 + sum8(value * (r[rows(j), at] - mean))

    s1, s2 = product_sums(rows_from_0(cat, weights), use)
    pack_ends(g3, index, cross, core)
    pack_moments(mom, cross, fold(stack_rows([s1, s2 * scale]), 16))


def norm_back(g, xhat, kept, moments, count, factor):
    return factor * (g - kept * ((moments[0:1] + xhat * moments[1:2]) / count))


def up_two_back_kernel(
    index, g3, cross_in, core_in, mom4, mom1, mom3, mom2, prm, aux, kept, rect, h3, t, z2,
    g2, cat, cross, core, mom, lf, rf, lw, rw,
):
    count = mom1[2:3]
    mean, scale = norm_terms(mom3, count)
    factor = scale * prm[4:5]
    inverse = 1.0 / count

    def back(g, r, keep):
        xhat = (r - mean) * scale
        value = factor * (g - keep * ((mom4[0:1] + xhat * mom4[1:2]) * inverse))
        return value * softplus_slope(r)

    r, h = ready(rect), ready(h3)
    for k, at in enumerate(tiles(512)):
        left, right = sides(index, cross_in, core_in, at)
        row = k // 2
        lf[:, at] = back(left, h[0, :, at], kept[row : row + 1, :])
        rf[:, at] = back(right, h[1, :, at], kept[3 + row : 4 + row, :])
    widen(lf, lw)
    widen(rf, rw)
    a, a_next = aux[0], aux[1]

    def one(j, total):
        span, stores = rows(j), []
        for k, at in enumerate(tiles(512)):
            value = back(g3[span, at], r[span, at], aux[2 + k // 2])
            total = total + sum8(value)
            stores.append((cat, span, at, value.astype(BF)))
            if k >= 2:
                moved = from_prev(value, lw[rows(j, 8), at], a)
                stores.append((cat, span, slice(256 + L * k, 384 + L * k), moved.astype(BF)))
            start = 768 + L * k if k < 2 else 1280 + L * k
            moved = from_next(value, rw[rows(j, 8), at], a_next)
            stores.append((cat, span, slice(start, start + L), moved.astype(BF)))
        put_all(stores)
        return total

    def four(j, total):
        for i in range(UNROLL):
            total = one(j * UNROLL + i, total)
        return total

    bias = lax.fori_loop(0, NJ // UNROLL, four, jnp.zeros((8, L), F32))
    rims_1(cat, GROUPS1)
    weights = ready(t)

    mean2, scale2 = norm_terms(mom2, mom1[3:4])
    gain, shift = prm[2:3], prm[3:4]
    z = ready(z2)

    def use(j, k, at, value, s1, s2, stores):
        xhat = (z[rows(j), at] - mean2) * scale2
        value = value * silu_slope(xhat * gain + shift)
        stores.append((g2, rows(j), at, value))
        return s1 + sum8(value), s2 + sum8(value * xhat)

    stats = fold(stack_rows(product_sums(lambda rs: [matmul(cat[rs, :], weights[...])], use)), 32)
    pack_ends(g2, index, cross, core)
    bias = fold(stack_rows([total_rows(bias)] * 3), 16)
    pack_moments(mom, cross, jnp.where(sub((8, L)) == 2, bias, stats))


def down_two_back_kernel(
    index, g2, cross_in, core_in, mom5, mom1, mom2, prm, aux, kept, z2, h2, t, gact, z1,
    g1, low2, cross, core, mom, cat, lf, rf, lw, rw,
):
    count = mom1[3:4]
    mean, scale = norm_terms(mom2, count)
    factor = scale * prm[2:3]
    inverse = 1.0 / count

    def back(g, z, keep):
        xhat = (z - mean) * scale
        return factor * (g - keep * ((mom5[0:1] + xhat * mom5[1:2]) * inverse))

    z, h = ready(z2), ready(h2)
    for at in tiles(256):
        left, right = sides(index, cross_in, core_in, at)
        lf[:, at] = back(left, h[0, :, at], kept[2:3, :])
        rf[:, at] = back(right, h[1, :, at], kept[5:6, :])
    widen(lf, lw)
    widen(rf, rw)
    columns_2(cat, lambda j, at: back(g2[rows(j), at], z[rows(j), at], aux[4]), lw, rw, aux)
    low2[...] = cat[:, 0:256]
    weights, added = ready(t), ready(gact)

    mean1, scale1 = norm_terms(mom1, mom1[2:3])
    gain, shift = prm[0:1], prm[1:2]
    z = ready(z1)

    def use(j, k, at, value, s1, s2, stores):
        xhat = (z[rows(j), at] - mean1) * scale1
        value = (value + added[rows(j), at]) * silu_slope(xhat * gain + shift)
        stores.append((g1, rows(j), at, value))
        return s1 + sum8(value), s2 + sum8(value * xhat)

    stats = fold(stack_rows(product_sums(rows_from_2(cat, weights), use)), 16)
    pack_ends(g1, index, cross, core)
    pack_moments(mom, cross, stats)


def up_one_back_kernel(
    index, g1, cross_in, core_in, mom6, mom1, prm, aux, kept, z1, h1, t,
    n0, n1, n2, n3, low1, cat, lf, rf, lw, rw,
):
    count = mom1[2:3]
    mean, scale = norm_terms(mom1, count)
    factor = scale * prm[0:1]
    inverse = 1.0 / count

    def back(g, z, keep):
        xhat = (z - mean) * scale
        return factor * (g - keep * ((mom6[0:1] + xhat * mom6[1:2]) * inverse))

    z, h = ready(z1), ready(h1)
    for k, at in enumerate(tiles(512)):
        left, right = sides(index, cross_in, core_in, at)
        row = k // 2
        lf[:, at] = back(left, h[0, :, at], kept[row : row + 1, :])
        rf[:, at] = back(right, h[1, :, at], kept[3 + row : 4 + row, :])
    widen(lf, lw)
    widen(rf, rw)
    columns_1b(
        cat, lambda j, k, at: back(g1[rows(j), at], z[rows(j), at], aux[2 + k // 2]), lw, rw, aux
    )
    low1[...] = cat[:, 0:512]
    weights = ready(t)
    nets = (n0, n1, n2, n3)
    per = R // len(nets)
    for net, (first, blocks) in zip(nets, quarter_blocks(index, len(nets))):
        rs = rows(lax.div(first, blocks), per)
        net[...] = matmul(cat[rs, :], weights[...], True).astype(BF)


def mixture_kernel(p0, p1, p2, p3, direct, out, scr):
    parts = (p0, p1, p2, p3)
    own = ready(direct)

    def tile(t):
        def block(k, half):
            at = slice(L * half, L * half + L)
            value = own[rows(4 * t + k), at]
            for part in parts:
                value = value + part[rows(4 * t + k), at].astype(F32)
            return value

        gather(block, scr)
        for c in range(2):
            out[c, :, pl.ds(pl.multiple_of(t * L, L), L)] = scr[c]

    for_blocks(tile, NJ // len(parts) // 4)


def pairs(count, offset):
    there = [(i, (i + offset) % count) for i in range(0, count, 2)]
    return there + [(b, a) for a, b in there]


def flip(values, axis, bit):
    return lax.ppermute(values, axis, [(i, i ^ bit) for i in range(lax.axis_size(axis))])


def sum_over(values, axis):
    count = lax.axis_size(axis)
    if count & (count - 1):
        return lax.psum(values, axis)
    step = 1
    while step < count:
        radix = 2 if step == 1 or count // step == 2 else 4
        moved = [flip(values, axis, step * k) for k in range(1, radix)]
        for m in moved:
            values = values + m
        step *= radix
    return values


def sum_chips(low, axis, beside):
    count = lax.axis_size(axis)
    if count == 8:
        moved = [flip(low, axis, bit) for bit in (2, 4, 6)]
        made, low = beside(low)
        mine = low.astype(F32) + moved[0].astype(F32) + moved[1].astype(F32) + moved[2].astype(F32)
    else:
        made, low = beside(low)
        mine, step = low.astype(F32), 2
        while step < count:
            mine = mine + flip(mine, axis, step)
            step *= 2
    return mine, flip(mine, axis, 1), made


def exchange(cross, core, mom, axis, beside):
    count = lax.axis_size(axis)
    near = lax.ppermute(cross, axis, pairs(count, -1))
    if count == 8:
        far = lax.ppermute(mom, axis, pairs(count, 3))
        across = flip(mom, axis, 4)
        inside = flip(core, axis, 1)
        *made, mom = beside(mom)
        part = mom + near[NJ:, 0:L] + far + across
        return near, inside, part + flip(part, axis, 1), made
    inside = flip(core, axis, 1)
    *made, mom = beside(mom)
    return near, inside, sum_over(mom, axis), made


def swap(blocks, axis):
    return [blocks[0]] + [flip(blocks[k], axis, k) for k in range(1, len(blocks))]


def per_device(
    mixture,
    seg_lengths,
    frame_mask,
    conv_first,
    encoder_gain_vector,
    shift_first,
    conv_second,
    gain_second,
    shift_second,
    deconv_second,
    bias_second,
    decoder_gain_vector,
    shift_third,
    deconv_first,
    bias_first,
    cotangent,
):
    position = lax.axis_index("tm")
    stems = lax.axis_size("stem")
    odd = position % 2
    total = mixture.shape[1] * lax.axis_size("tm")
    index = jnp.stack([lax.axis_index("stem"), odd, position, total]).astype(jnp.int32)
    frames = mixture.shape[1]
    per, blocks = R // stems, NJ // stems
    w2c = conv_second[0].transpose(2, 3, 1, 0).reshape(400, 32)
    w2d = deconv_second[0].transpose(2, 3, 0, 1).reshape(400, 32)
    edge = 2 * NJ + 16

    def packet(lanes):
        return [((NJ + 8, lanes), F32), ((NJ, lanes), F32), ((8, L), F32)]

    def rim(lanes):
        return [((NJ, lanes), F32)] * 2

    def wide(lanes):
        return [((8 * NJ, lanes), F32)] * 2

    def far(*shape, kind=F32):
        return [(shape, kind, True)]

    raw = [conv_first[0].transpose(2, 3, 1, 0).reshape(25, 2, 16)]
    raw += [deconv_first[0].transpose(2, 3, 0, 1).reshape(25, 2, 32)]
    raw += [encoder_gain_vector, shift_first, gain_second, shift_second]
    raw += [decoder_gain_vector, shift_third, bias_second, bias_first]
    cross, core, x0, c0, *raw = run(
        layout_kernel,
        "layout",
        [((edge, 256), BF), ((edge, 256), BF), ((R, 256), BF), ((R, 256), BF)],
        [index, Far(frame_mask), Far(mixture), Far(cotangent)],
        [((2, frames, L), F32), ((2 * R, 256), F32), ((2, edge, 256), F32)],
        fetch=[Far(frame_mask.reshape(1, 4 * M))] + [Far(v) for v in raw],
    )
    near = lax.ppermute(cross, "tm", pairs(lax.axis_size("tm"), -1))
    inside = flip(core, "tm", 1)
    t, w1c, w1d, aux, prm, x0_far, c0 = run(
        window_0,
        "window_0",
        [((COLS0, 512), BF), ((56, L), F32), ((2, 56, L), F32), ((5, M, L), F32), ((8, L), F32)],
        [index, Far(seg_lengths), *raw],
        store=[x0, c0],
    )
    z1_here, cross, core, mom, kept, hx, cat0 = run(
        conv_one_kernel,
        "conv_one",
        [((R, 512), F32)] + packet(512) + [((8, L), F32), ((2 * NJ, 256), F32), ((R, COLS0), BF)],
        [index, x0, near, inside, aux, t],
        [((edge, 256), F32), ((edge, 256), F32)] + wide(256),
        flops=2 * R * COLS0 * 512,
    )
    near, inside, mom1, (t, z1, hx, cat0, z1_here) = exchange(
        cross, core, mom, "tm",
        lambda token: run(
            window_1,
            "window_1",
            [((COLS1, 256), BF)],
            [w2c],
            [((400, L), F32)],
            store=[z1_here, hx, cat0],
            carry=[z1_here],
            token=token,
        ),
    )
    z2_here, cross, core, mom, ends1, h1, cat1 = run(
        conv_two_kernel,
        "conv_two",
        [((R, 256), F32)] + packet(256) + [((4, NJ, 512), BF), ((2, NJ, 512), F32), ((R, COLS1), BF)],
        [index, z1_here, near, inside, mom1, prm, aux, t],
        [((4, NJ, 512), F32)] + wide(512),
        flops=2 * R * COLS1 * 256,
    )
    near, inside, mom2, (t, cat1, z2, ends1, h1, z2_here) = exchange(
        cross, core, mom, "tm",
        lambda token: run(
            window_2,
            "window_2",
            [((512, COLS2), BF)],
            [w2d],
            [((400, L), F32)],
            store=[cat1, z2_here, ends1, h1],
            carry=[z2_here],
            token=token,
        ),
    )
    rect_here, cross, core, mom, h2, act2 = run(
        up_two_kernel,
        "up_two",
        [((R, 512), F32)] + packet(512) + [((2, NJ, 256), F32), ((R, 256), BF)],
        [index, z2_here, near, inside, mom1, mom2, prm, aux, t],
        [((R, COLS2), BF)] + rim(256) + wide(256),
        flops=2 * R * COLS2 * 512,
    )
    near, inside, mom3, (t, cat1_here, ends1_here, rect, h2, act2, rect_here) = exchange(
        cross, core, mom, "tm",
        lambda token: run(
            window_3,
            "window_3",
            [((256, 2 * COLS1B), BF)],
            [w1d],
            fetch=[Far(cat1, COLS1B), Far(ends1)],
            store=[rect_here, h2, act2],
            carry=[rect_here],
            token=token,
        ),
    )
    *masks, h3, low3, sig, sigh = run(
        up_one_kernel,
        "up_one",
        [((per + 16, 256), BF)] * stems
        + [((2, NJ, 512), F32), ((R, 512), BF), ((R, 256), F32), ((NJ, 256), F32)],
        [index, rect_here, near, inside, mom1, mom3, prm, aux, ends1_here, cat1_here, t],
        [((R, COLS1B), BF)] + rim(512) + [((2, NJ, 512), F32), ((16, 256), F32)] + wide(512),
        flops=2 * R * 2 * COLS1B * 256,
    )
    t2a_d, t2b_c, t1b_c, c0_here, x0_here, hx_here, h3, low3, sig, sigh = run(
        window_swap,
        "window_swap",
        far(COLS1, 256, kind=BF) + far(512, COLS2, kind=BF) + far(256, COLS1B, kind=BF),
        [w2c, w2d, w1c],
        [((COLS1, 256), BF), ((512, COLS2), BF), ((256, COLS1B), BF), ((400, L), F32)],
        fetch=[Far(c0), Far(x0_far), Far(hx)],
        store=[h3, low3, sig, sigh],
    )
    masks = swap(masks, "stem")
    *grads, direct = run(
        mask_kernel,
        "mask",
        [((per + 16, 256), BF)] * stems + [((per, 256), F32)],
        [index, *masks, c0_here, x0_here, hx_here],
        [((16, 256), F32)],
    )
    grads = swap(grads, "stem")
    estimates, t, sig_here, sigh_here, rect_here, low3_here, act_here, direct = run(
        estimate_kernel,
        "estimate",
        [((stems, 2, frames, blocks * 32), BF), ((COLS0, 1024), BF)],
        [index, *masks, Far(x0_far), w1d],
        [((2, frames, L), F32), ((stems, per, 256), F32)],
        fetch=[Far(sig), Far(sigh), Far(rect), Far(low3), Far(cat1, 512)],
        store=[direct],
    )
    g3, cat0g, cross, core, mom, bias_one, gact, rect_here, low3_here, act_here = run(
        down_one_back_kernel,
        "down_one_back",
        [((R, 512), F32), ((R, COLS0), BF)] + packet(512) + [((8, L), F32), ((R, 512), F32)],
        [index, *grads, sigh_here, sig_here, aux, mom1, mom3, rect_here, t],
        [((NJ, 256), F32), ((8, L), F32), ((8 * NJ, 256), F32)],
        flops=2 * R * COLS0 * 1024,
        carry=[rect_here, low3_here, act_here],
    )
    near, inside, mom4, (w1d_grad, t, h3_here, z2_here, act2_here) = exchange(
        cross, core, mom, "tm",
        lambda token: run(
            window_4,
            "window_4",
            [((32, L), F32)],
            [low3_here, act_here, cat0g],
            [((512, 768), F32)],
            flops=2 * R * COLS0 * 1024,
            fetch=[Far(t2a_d), Far(h3), Far(z2), Far(act2)],
            token=token,
        ),
    )
    g2, cat1g, cross, core, mom, gact, z2_here, act2_here, w1d_grad = run(
        up_two_back_kernel,
        "up_two_back",
        [((R, 256), F32), ((R, COLS1), BF)] + packet(256),
        [index, g3, near, inside, mom4, mom1, mom3, mom2, prm, aux, kept, rect_here, h3_here, t, z2_here],
        rim(512) + wide(512),
        flops=2 * R * COLS1 * 256,
        carry=[gact, z2_here, act2_here, w1d_grad],
    )
    near, inside, mom5, (w2d_grad, t, h2_here, z1_here) = exchange(
        cross, core, mom, "tm",
        lambda token: run(
            window_5,
            "window_5",
            [((128, L), F32)],
            [act2_here, cat1g],
            [((256, COLS1), F32)],
            flops=2 * R * COLS1 * 256,
            fetch=[Far(t2b_c), Far(h2), Far(z1)],
            token=token,
        ),
    )
    g1, low2, cross, core, mom, z1_here, w1d_grad, w2d_grad = run(
        down_two_back_kernel,
        "down_two_back",
        [((R, 512), F32), ((R, 256), BF)] + packet(512),
        [index, g2, near, inside, mom5, mom1, mom2, prm, aux, kept, z2_here, h2_here, t, gact, z1_here],
        [((R, COLS2), BF)] + rim(256) + wide(256),
        flops=2 * R * COLS2 * 512,
        carry=[z1_here, w1d_grad, w2d_grad],
    )
    near, inside, mom6, (keep, give, t, h1_here, cat0_here) = exchange(
        cross, core, mom, "tm",
        lambda token: run(
            window_6,
            "window_6",
            [((HALF, L), F32), ((HALF, L), F32)],
            [index, low2, Far(cat1, parts=2), w1d_grad, w2d_grad],
            [((256, COLS1), F32), ((128, L), F32)],
            flops=2 * R * COLS1 * 256,
            fetch=[Far(t1b_c), Far(h1), Far(cat0)],
            token=token,
        ),
    )
    got = flip(give, "tm", 1)
    *nets, low1 = run(
        up_one_back_kernel,
        "up_one_back",
        [((per, 256), BF)] * stems + [((R, 512), BF)],
        [index, g1, near, inside, mom6, mom1, prm, aux, kept, z1_here, h1_here, t],
        [((R, COLS1B), BF)] + rim(512) + wide(512),
        flops=2 * R * COLS1B * 256,
    )
    nets = swap(nets, "stem")
    low, direct_here = run(
        window_7,
        "window_7",
        [((HALF + 32, L), BF)],
        [low1, cat0_here, keep, got, bias_one],
        [((512, 768), F32), ((16, L), F32)],
        flops=2 * R * COLS0 * 512,
        fetch=[Far(direct)],
    )
    mine, other, mixture_grad = sum_chips(
        low,
        "tm",
        lambda token: run(
            mixture_kernel,
            "mixture",
            [((2, frames, blocks * 32), F32)],
            [*nets, direct_here],
            [((2, frames, L), F32)],
            token=token,
        ),
    )
    w1c_grad, w2c_grad, w2d_grad, w1d_grad, bias1, gain1, shift1, gain2, shift2, bias2, gain3, shift3 = run(
        unpack_kernel,
        "unpack",
        [((25, 2, 16), F32), ((25, 16, 32), F32), ((25, 16, 32), F32), ((25, 2, 32), F32), ((1, 2), F32)]
        + [((1, n), F32) for n in (16, 16, 32, 32, 16, 16, 16)],
        [index, mine, other, mom4, mom5, mom6],
    )

    def turned(grad, order):
        return grad.reshape((TAPS, TAPS) + grad.shape[1:]).transpose(order)[None]

    return (
        estimates,
        mixture_grad,
        turned(w1c_grad, (3, 2, 0, 1)),
        gain1,
        shift1,
        turned(w2c_grad, (3, 2, 0, 1)),
        gain2,
        shift2,
        turned(w2d_grad, (2, 3, 0, 1)),
        bias2,
        gain3,
        shift3,
        turned(w1d_grad, (2, 3, 0, 1)),
        bias1,
    )


def solution(mesh):
    in_specs = (
        P(None, "tm", None),
        P(),
        P("tm"),
        P("stem", None, None, None, None),
        P("stem", None),
        P("stem", None),
        P("stem", None, None, None, None),
        P("stem", None),
        P("stem", None),
        P("stem", None, None, None, None),
        P("stem", None),
        P("stem", None),
        P("stem", None),
        P("stem", None, None, None, None),
        P("stem", None),
        P(None, None, "tm", "stem"),
    )
    out_specs = (
        P(None, None, "tm", "stem"),
        P(None, "tm", "stem"),
        P("stem", None, None, None, None),
        P("stem", None),
        P("stem", None),
        P("stem", None, None, None, None),
        P("stem", None),
        P("stem", None),
        P("stem", None, None, None, None),
        P("stem", None),
        P("stem", None),
        P("stem", None),
        P("stem", None, None, None, None),
        P("stem", None),
    )
    return jax.shard_map(
        per_device, mesh=mesh, in_specs=in_specs, out_specs=out_specs, check_vma=False
    )
```
